32 devices in a mesh: tower: 2 (over core), dp: 8 (over z, x), mp: 2 (over y).
Axes of the slice: x: 2, y: 2, z: 4, core: 2. Of those that a mesh axis runs over, the one named last changes fastest.
Arguments:
- token_ids: int32 [2, 8192], P('tower', 'dp'), may hold values from 0 to 30527
- seq_lengths: int32 [2, 8, 16], replicated, may hold values from 0 to 1024, as said below
- positives: int32 [8, 16], replicated, may hold values from 0 to 127, as said below
- embedding: float32 [30528, 768], P('dp', 'mp'), may hold values from -0.21875 to 0.21875
- attn_in: float32 [768, 3, 768], P(('tower', 'dp'), None, 'mp'), may hold values from -0.21875 to 0.21875
- attn_out: float32 [768, 768], P(('tower', 'dp'), 'mp'), may hold values from -0.875 to 0.875
- ffn_in: float32 [768, 2, 3072], P(('tower', 'dp'), None, 'mp'), may hold values from -0.21875 to 0.21875
- ffn_out: float32 [768, 3072], P(('tower', 'dp'), 'mp'), may hold values from -0.109375 to 0.109375
- norm_params: float32 [6, 768], replicated, as said below
- logit_scale: float32 [1], replicated, may hold values from 2.6 to 3.6
- embed_m: float32 [30528, 768], P('dp', 'mp'), as said below
- embed_v: float32 [30528, 768], P('dp', 'mp'), as said below
- attn_in_m: float32 [768, 3, 768], P(('tower', 'dp'), None, 'mp'), as said below
- attn_in_v: float32 [768, 3, 768], P(('tower', 'dp'), None, 'mp'), as said below
- attn_out_m: float32 [768, 768], P(('tower', 'dp'), 'mp'), as said below
- attn_out_v: float32 [768, 768], P(('tower', 'dp'), 'mp'), as said below
- ffn_in_m: float32 [768, 2, 3072], P(('tower', 'dp'), None, 'mp'), as said below
- ffn_in_v: float32 [768, 2, 3072], P(('tower', 'dp'), None, 'mp'), as said below
- ffn_out_m: float32 [768, 3072], P(('tower', 'dp'), 'mp'), as said below
- ffn_out_v: float32 [768, 3072], P(('tower', 'dp'), 'mp'), as said below
- norm_m: float32 [6, 768], replicated, as said below
- norm_v: float32 [6, 768], replicated, as said below
- scale_m: float32 [1], replicated, as said below
- scale_v: float32 [1], replicated, as said below
Outputs:
- new_embedding: float32 [30528, 768], P('dp', 'mp')
- new_embed_m: float32 [30528, 768], P('dp', 'mp')
- new_embed_v: float32 [30528, 768], P('dp', 'mp')
- new_attn_in: float32 [768, 3, 768], P(('tower', 'dp'), None, 'mp')
- new_attn_in_m: float32 [768, 3, 768], P(('tower', 'dp'), None, 'mp')
- new_attn_in_v: float32 [768, 3, 768], P(('tower', 'dp'), None, 'mp')
- new_attn_out: float32 [768, 768], P(('tower', 'dp'), 'mp')
- new_attn_out_m: float32 [768, 768], P(('tower', 'dp'), 'mp')
- new_attn_out_v: float32 [768, 768], P(('tower', 'dp'), 'mp')
- new_ffn_in: float32 [768, 2, 3072], P(('tower', 'dp'), None, 'mp')
- new_ffn_in_m: float32 [768, 2, 3072], P(('tower', 'dp'), None, 'mp')
- new_ffn_in_v: float32 [768, 2, 3072], P(('tower', 'dp'), None, 'mp')
- new_ffn_out: float32 [768, 3072], P(('tower', 'dp'), 'mp')
- new_ffn_out_m: float32 [768, 3072], P(('tower', 'dp'), 'mp')
- new_ffn_out_v: float32 [768, 3072], P(('tower', 'dp'), 'mp')
- new_norms: float32 [6, 768], replicated
- new_norm_m: float32 [6, 768], replicated
- new_norm_v: float32 [6, 768], replicated
- new_scale: float32 [1], replicated
- new_scale_m: float32 [1], replicated
- new_scale_v: float32 [1], replicated
- loss_sum: float32 [1], replicated
- query_count: float32 [1], replicated
- grad_norm: float32 [1], replicated
The draws below stay inside these ranges and needn't reach their ends.
Inputs may be any that keep to these rules, and one draw needn't show every extreme that they name: seq_lengths[0] are query lengths of 4 to 64 tokens, at least 8 per row; seq_lengths[1] are document lengths; in every row the slots of positive length come first and sum to at most 1024; every row of seq_lengths[1] holds a document, one row holds a single document of exactly 1024 tokens, and the last row holds 16 documents of 64 tokens. `positives`: each entry is i * 16 + s for a slot s of positive length in seq_lengths[1, i]. `norm_params`: rows 0, 2, 4 are gains, rows 1, 3, 5 biases. `embed_m`: moments of both signs. `embed_v`: positive. `attn_in_m`: moments of both signs. `attn_in_v`: positive. `attn_out_m`: moments of both signs. `attn_out_v`: positive. `ffn_in_m`: moments of both signs. `ffn_in_v`: positive. `ffn_out_m`: moments of both signs. `ffn_out_v`: positive. `norm_m`: moments of both signs. `norm_v`: positive. `scale_m`: a moment. `scale_v`: positive.
All inputs are finite; a program needn't handle non-finite values.
Results may differ from the reference program's by a relative error of at most 0.019.
The reference program's roundings to bfloat16 on the way count: a program that leaves them out, or rounds other values in their place, can miss the bound.
Values may be sent and summed in bfloat16 or wider, within the bound.
A program may use at most 320 MiB of HBM per device.

```python
import math
import jax
import jax.numpy as jnp
import numpy as np
from jax import lax

D = 768
HEADS = 12
HDIM = 64
FF = 3072
VOCAB = 30528
TOK_DEV = 1024
SEG_DEV = 16
STEP = 5
TOKENS = 8192
N_DP = 8


def layout_draw(key):
    query_most = TOK_DEV // SEG_DEV
    slot_ids = jnp.arange(SEG_DEV, dtype=jnp.int32)[None, :]
    row_ids = jnp.arange(N_DP, dtype=jnp.int32)[:, None]
    query_len = jax.random.randint(jax.random.fold_in(key, 1), (N_DP, SEG_DEV), 4, query_most + 1)
    query_num = jax.random.randint(jax.random.fold_in(key, 2), (N_DP, 1), SEG_DEV // 2, SEG_DEV + 1)
    query_len = jnp.where(slot_ids < query_num, query_len, 0)
    levels = int(math.log2(TOK_DEV)) - 3
    shifts = jax.random.randint(jax.random.fold_in(key, 3), (N_DP, SEG_DEV), 1, levels + 1)
    floor_len = jnp.right_shift(jnp.full((N_DP, SEG_DEV), TOK_DEV, jnp.int32), shifts)
    extra_len = jax.random.randint(jax.random.fold_in(key, 4), (N_DP, SEG_DEV), 0, floor_len)
    doc_len = floor_len + extra_len
    doc_len = jnp.where(jnp.cumsum(doc_len, 1) <= TOK_DEV, doc_len, 0)
    doc_len = jnp.where(row_ids == N_DP - 1, TOK_DEV // SEG_DEV, doc_len)
    chosen = jax.random.randint(jax.random.fold_in(key, 5), (), 0, N_DP - 1)
    full_row = jnp.where(slot_ids == 0, TOK_DEV, 0)
    doc_len = jnp.where(row_ids == chosen, full_row, doc_len)
    return jnp.stack([query_len, doc_len]).astype(jnp.int32)


def draw_seq_lengths(key, part):
    return layout_draw(key)


def draw_positives(key, part):
    lengths = layout_draw(key)
    doc_num = jnp.sum((lengths[1] > 0).astype(jnp.int32), 1)
    device = jax.random.randint(jax.random.fold_in(key, 6), (N_DP, SEG_DEV), 0, N_DP)
    slot_pick = jax.random.randint(jax.random.fold_in(key, 7), (N_DP, SEG_DEV), 0, doc_num[device])
    picks = device * SEG_DEV + slot_pick
    row_ids = jnp.arange(N_DP, dtype=jnp.int32)[:, None]
    slot_ids = jnp.arange(SEG_DEV, dtype=jnp.int32)[None, :]
    picks = jnp.where((row_ids == 0) & (slot_ids == 0), 0, picks)
    picks = jnp.where((row_ids == N_DP - 1) & (slot_ids == SEG_DEV - 1), N_DP * SEG_DEV - 1, picks)
    return picks.astype(jnp.int32)


def draw_norm_params(key, part):
    ramp = jnp.arange(D, dtype=jnp.float32) / (D - 1)
    rising = 0.5 + 1.5 * ramp
    gains = rising[None, :] * (1.0 + 0.1 * jax.random.uniform(key, (3, D), jnp.float32, -1.0, 1.0))
    biases = 0.1 * jax.random.normal(jax.random.fold_in(key, 1), (3, D), jnp.float32)
    return jnp.stack([gains, biases], 1).reshape(6, D)


def grad_size():
    return 0.01 / math.sqrt(VOCAB * D + 4 * D * D + 3 * D * FF)


def first_moment(key, shape, size):
    return size / 9.0 * jax.random.normal(key, shape, jnp.float32)


def second_moment(key, shape, size):
    spread = jnp.exp(jax.random.uniform(key, shape, jnp.float32, math.log(0.5), math.log(8.0)))
    return 0.001 * size * size * spread


def draw_embed_m(key, part):
    return first_moment(key, (VOCAB, D), 0.3 * grad_size())


def draw_embed_v(key, part):
    return second_moment(key, (VOCAB, D), 0.3 * grad_size())


def draw_attn_in_m(key, part):
    return first_moment(key, (D, 3, D), grad_size())


def draw_attn_in_v(key, part):
    return second_moment(key, (D, 3, D), grad_size())


def draw_attn_out_m(key, part):
    return first_moment(key, (D, D), grad_size())


def draw_attn_out_v(key, part):
    return second_moment(key, (D, D), grad_size())


def draw_ffn_in_m(key, part):
    return first_moment(key, (D, 2, FF), grad_size())


def draw_ffn_in_v(key, part):
    return second_moment(key, (D, 2, FF), grad_size())


def draw_ffn_out_m(key, part):
    return first_moment(key, (D, FF), grad_size())


def draw_ffn_out_v(key, part):
    return second_moment(key, (D, FF), grad_size())


def draw_norm_m(key, part):
    return first_moment(key, (6, D), 10.0 * grad_size())


def draw_norm_v(key, part):
    return second_moment(key, (6, D), 10.0 * grad_size())


def draw_scale_m(key, part):
    return first_moment(key, (1,), 0.003)


def draw_scale_v(key, part):
    return second_moment(key, (1,), 0.003)


def set_ends(array, stream_key, smallest, top_value):
    shape = array.shape
    place = [jax.random.randint(jax.random.fold_in(stream_key, axis), (), 0, shape[axis]) for axis in range(len(shape))]
    array = array.at[tuple(place)].set(smallest)
    longest = shape.index(max(shape))
    place[longest] = (place[longest] + 1) % shape[longest]
    return array.at[tuple(place)].set(top_value)


def steps_of(own_key, shape, shards, smallest, top_value):
    loudness, own = 1.0, jax.random.fold_in(own_key, 6)
    for dim, parts in shards:
        heights = jnp.exp(jax.random.uniform(jax.random.fold_in(own, dim), (parts,), jnp.float32, smallest / len(shards), top_value / len(shards)))
        loudness = loudness * jnp.repeat(heights, shape[dim] // parts).reshape([-1 if axis == dim else 1 for axis in range(len(shape))])
    return loudness


def rank_bounds(amount, skew):
    portions = [(1 << 20) // math.isqrt(standing ** skew) + 1 for standing in range(1, amount + 1)]
    deviation = 1 + sum(portions) // (1 << 30)
    return np.cumsum(np.array([max(1, weight // deviation) for weight in portions]))


def skewed_ids(key, shape, amount, skew):
    listing = rank_bounds(amount, skew)
    pick = jax.random.randint(jax.random.fold_in(key, 1), shape, 0, int(listing[amount - 1]))
    standing = jnp.searchsorted(jnp.asarray(listing, jnp.int32), pick, side="right")
    return jax.random.permutation(jax.random.fold_in(key, 2), amount)[standing].astype(jnp.int32)


def gaussian(own_key, shape, scale, limit, split=(), kind=jnp.bfloat16):
    array = scale * jax.random.normal(own_key, shape, jnp.float32)
    if split:
        array = array * steps_of(own_key, shape, split, -0.22, 0.18)
    return jnp.clip(array, -limit, limit).astype(kind)


def setup_inputs(seed: int = 0) -> dict:
    keys = jax.random.split(jax.random.key(seed), 25)
    return {
        "token_ids": set_ends(skewed_ids(keys[0], (2, TOKENS), VOCAB, 2), jax.random.fold_in(keys[0], 3), 0, VOCAB - 1).astype(jnp.int32),
        "seq_lengths": draw_seq_lengths(jax.random.fold_in(keys[24], 71), 0),
        "positives": draw_positives(jax.random.fold_in(keys[24], 71), 0),
        "embedding": gaussian(keys[3], (VOCAB, D), D ** -0.5, 0.21875, ((0, 8), (1, 2)), jnp.float32),
        "attn_in": gaussian(keys[4], (D, 3, D), D ** -0.5, 0.21875, ((0, 16), (2, 2)), jnp.float32),
        "attn_out": gaussian(keys[5], (D, D), (D // 16) ** -0.5, 0.875, ((0, 16), (1, 2)), jnp.float32),
        "ffn_in": gaussian(keys[6], (D, 2, FF), D ** -0.5, 0.21875, ((0, 16), (2, 2)), jnp.float32),
        "ffn_out": gaussian(keys[7], (D, FF), FF ** -0.5, 0.109375, ((0, 16), (1, 2)), jnp.float32),
        "norm_params": draw_norm_params(jax.random.fold_in(keys[24], 71), 0),
        "logit_scale": jnp.clip(jax.random.uniform(keys[9], (1,), jnp.float32, 2.6, 3.6), 2.6, 3.6),
        "embed_m": draw_embed_m(jax.random.fold_in(keys[24], 71), 0),
        "embed_v": draw_embed_v(jax.random.fold_in(keys[24], 71), 0),
        "attn_in_m": draw_attn_in_m(jax.random.fold_in(keys[24], 71), 0),
        "attn_in_v": draw_attn_in_v(jax.random.fold_in(keys[24], 71), 0),
        "attn_out_m": draw_attn_out_m(jax.random.fold_in(keys[24], 71), 0),
        "attn_out_v": draw_attn_out_v(jax.random.fold_in(keys[24], 71), 0),
        "ffn_in_m": draw_ffn_in_m(jax.random.fold_in(keys[24], 71), 0),
        "ffn_in_v": draw_ffn_in_v(jax.random.fold_in(keys[24], 71), 0),
        "ffn_out_m": draw_ffn_out_m(jax.random.fold_in(keys[24], 71), 0),
        "ffn_out_v": draw_ffn_out_v(jax.random.fold_in(keys[24], 71), 0),
        "norm_m": draw_norm_m(jax.random.fold_in(keys[24], 71), 0),
        "norm_v": draw_norm_v(jax.random.fold_in(keys[24], 71), 0),
        "scale_m": draw_scale_m(jax.random.fold_in(keys[24], 71), 0),
        "scale_v": draw_scale_v(jax.random.fold_in(keys[24], 71), 0),
    }


@jax.custom_vjp
def low(v):
    return lax.optimization_barrier(v.astype(jnp.bfloat16)).astype(jnp.float32)

@jax.custom_vjp
def low_back(v):
    return v

def low_keep(v):
    return (low(v), None)

def low_pass(kept, grad):
    return (grad,)

def back_keep(v):
    return (v, None)

def back_low(kept, grad):
    return (low(grad),)
low.defvjp(low_keep, low_pass)
low_back.defvjp(back_keep, back_low)
norm_eps = 1e-06
cap_value = 3.4
clip_max = 0.01
beta_one = 0.9
beta_two = 0.999
learn_rate = 0.02
out_rate = 0.05
norm_rate = 0.3
decay_rate = 0.01
adam_eps = 1e-08
neg_large = -1e+30
highest = lax.Precision.HIGHEST

def layer_norm(stream, gain_row, bias_row):
    average = lax.optimization_barrier(jnp.mean(stream, -1, keepdims=True))
    centered = stream - average
    variance = lax.optimization_barrier(jnp.mean(centered * centered, -1, keepdims=True))
    return centered * lax.rsqrt(variance + norm_eps) * gain_row + bias_row

def rotate(values, cosine, sine_table):
    half_dim = values.shape[-1] // 2
    turned = jnp.concatenate([-values[..., half_dim:], values[..., :half_dim]], -1)
    return values * cosine + turned * sine_table

def rotary_tables(positions):
    half_dim = HDIM // 2
    inverse = 1000.0 ** (-2.0 * jnp.arange(half_dim, dtype=jnp.float32) / HDIM)
    angles = positions.astype(jnp.float32)[:, None] * inverse[None, :]
    angles = jnp.concatenate([angles, angles], 1)[:, None, :]
    return (jnp.cos(angles), jnp.sin(angles))

def layout(lengths):
    end_points = jnp.cumsum(lengths)
    places = jnp.arange(TOK_DEV, dtype=jnp.int32)
    segment = lax.optimization_barrier(jnp.sum((places[:, None] >= end_points[None, :]).astype(jnp.int32), 1))
    starts = jnp.concatenate([jnp.zeros((1,), jnp.int32), end_points.astype(jnp.int32)])
    slot_ids = jnp.arange(SEG_DEV + 1, dtype=jnp.int32)
    segment_start = lax.optimization_barrier(jnp.sum(jnp.where(segment[:, None] == slot_ids[None, :], starts[None, :], 0), 1))
    return (segment, places - segment_start)

def encode(token_row, lengths, table, weights):
    w_qkv, w_out, w_ffn, w_down, norm_rows = weights
    segment, positions = layout(lengths)
    embed_rows = low_back(jnp.take(table, token_row, axis=0))
    stream_zero = layer_norm(embed_rows, norm_rows[0], norm_rows[1])
    input_zero = low(stream_zero)
    projected = low_back(jnp.einsum('td,dcf->tcf', input_zero, w_qkv, precision=highest))
    heads_view = projected.reshape(TOK_DEV, 3, HEADS, HDIM)
    cosine, sine_table = rotary_tables(positions)
    query_low = low(rotate(heads_view[:, 0], cosine, sine_table))
    key_low = low(rotate(heads_view[:, 1], cosine, sine_table))
    value_low = low(heads_view[:, 2])
    scores = low_back(jnp.einsum('thd,shd->hts', query_low, key_low, precision=highest) * HDIM ** (-0.5))
    same_seg = (segment[:, None] == segment[None, :])[None]
    soft_rows = jax.nn.softmax(jnp.where(same_seg, scores, neg_large), axis=-1)
    attended = jnp.einsum('hts,shd->thd', low(soft_rows), value_low, precision=highest).reshape(TOK_DEV, D)
    attended = low_back(low(attended))
    attn_branch = low_back(jnp.einsum('tf,df->td', attended, w_out, precision=highest))
    stream_one = layer_norm(stream_zero + attn_branch, norm_rows[2], norm_rows[3])
    input_one = low(stream_one)
    gate_up = jnp.einsum('td,dcf->tcf', input_one, w_ffn, precision=highest)
    gate_vals = low_back(gate_up[:, 0])
    up_vals = low_back(gate_up[:, 1])
    hidden = low(jax.nn.silu(gate_vals) * up_vals)
    ffn_branch = low_back(jnp.einsum('tf,df->td', hidden, w_down, precision=highest))
    stream_two = layer_norm(stream_one + ffn_branch, norm_rows[4], norm_rows[5])
    member = (segment[None, :] == jnp.arange(SEG_DEV, dtype=jnp.int32)[:, None]).astype(jnp.float32)
    counts = jnp.maximum(lengths, 1).astype(jnp.float32)
    pooled = jnp.dot(member, stream_two, precision=highest) / counts[:, None]
    return low(pooled * lax.rsqrt(lax.optimization_barrier(jnp.sum(pooled * pooled, 1, keepdims=True)) + 1e-06))

def total_loss(params, token_ids, seq_lengths, positives):
    embedding, attn_in, attn_out, ffn_in, ffn_out, norm_params, logit_scale = params
    table = low(embedding)
    weights = (low(attn_in), low(attn_out), low(ffn_in), low(ffn_out), norm_params)
    token_rows = token_ids.reshape(2 * N_DP, TOK_DEV)
    length_rows = seq_lengths.reshape(2 * N_DP, SEG_DEV)

    def encode_pair(operands):
        return encode(operands[0], operands[1], table, weights)
    embeds = lax.map(jax.checkpoint(encode_pair), (token_rows, length_rows))
    embeds = embeds.reshape(2, N_DP * SEG_DEV, D)
    cosines = low_back(jnp.dot(embeds[0], embeds[1].T, precision=highest))
    logit_factor = jnp.exp(jnp.minimum(logit_scale[0], cap_value))
    doc_ok = seq_lengths[1].reshape(-1) > 0
    query_ok = seq_lengths[0].reshape(-1) > 0
    logits = jnp.where(doc_ok[None, :], logit_factor * cosines, neg_large)
    log_total = jax.nn.logsumexp(logits, axis=1)
    target_mask = jnp.arange(N_DP * SEG_DEV, dtype=jnp.int32)[None, :] == positives.reshape(-1)[:, None]
    picked = lax.optimization_barrier(jnp.sum(jnp.where(target_mask, logits, 0.0), 1))
    query_count = jnp.sum(query_ok.astype(jnp.float32))
    loss_sum = jnp.sum(jnp.where(query_ok, log_total - picked, 0.0))
    return (loss_sum / query_count, (loss_sum, query_count))

def adamw(weight_in, gradient, first_mom, second, factor, step_num, rate):
    gradient = gradient * factor
    first_new = beta_one * first_mom + (1.0 - beta_one) * gradient
    second_new = beta_two * second + (1.0 - beta_two) * gradient * gradient
    first_hat = first_new / (1.0 - beta_one ** step_num)
    second_hat = second_new / (1.0 - beta_two ** step_num)
    weight_new = weight_in - rate * (first_hat / (jnp.sqrt(second_hat) + adam_eps) + decay_rate * weight_in)
    return (weight_new, first_new, second_new)

def reference(token_ids, seq_lengths, positives, embedding, attn_in, attn_out, ffn_in, ffn_out, norm_params, logit_scale, embed_m, embed_v, attn_in_m, attn_in_v, attn_out_m, attn_out_v, ffn_in_m, ffn_in_v, ffn_out_m, ffn_out_v, norm_m, norm_v, scale_m, scale_v):
    params = (embedding, attn_in, attn_out, ffn_in, ffn_out, norm_params, logit_scale)

    def loss_of(*weights_all):
        return total_loss(weights_all, token_ids, seq_lengths, positives)
    loss_value, pullback, extras = jax.vjp(loss_of, *params, has_aux=True)
    grads = pullback(jnp.ones_like(loss_value))
    total_sq = sum((jnp.sum(gradient * gradient) for gradient in grads))
    grad_norm = jnp.sqrt(total_sq)
    factor = jnp.minimum(1.0, clip_max / (grad_norm + 1e-06))
    step_num = float(STEP)
    firsts = (embed_m, attn_in_m, attn_out_m, ffn_in_m, ffn_out_m, norm_m, scale_m)
    seconds = (embed_v, attn_in_v, attn_out_v, ffn_in_v, ffn_out_v, norm_v, scale_v)
    rates = (learn_rate, learn_rate, out_rate, learn_rate, learn_rate, norm_rate, learn_rate)
    updates = [adamw(params[index], grads[index], firsts[index], seconds[index], factor, step_num, rates[index]) for index in range(7)]
    return (updates[0][0], updates[0][1], updates[0][2], updates[1][0], updates[1][1], updates[1][2], updates[2][0], updates[2][1], updates[2][2], updates[3][0], updates[3][1], updates[3][2], updates[4][0], updates[4][1], updates[4][2], updates[5][0], updates[5][1], updates[5][2], updates[6][0], updates[6][1], updates[6][2], extras[0].reshape(1), extras[1].reshape(1), grad_norm.reshape(1))
```

```python
import jax
import jax.numpy as jnp
from jax import lax
from jax.sharding import PartitionSpec as P
from jax.experimental import pallas as pl
from jax.experimental.pallas import tpu as pltpu

HDIM = 64
STEP = 5

norm_eps = 1e-06
cap_value = 3.4
clip_max = 0.01
beta_one = 0.9
beta_two = 0.999
learn_rate = 0.02
out_rate = 0.05
norm_rate = 0.3
decay_rate = 0.01
adam_eps = 1e-08
neg_large = -1e30
highest = lax.Precision.HIGHEST
f32 = jnp.float32
bf16 = jnp.bfloat16
MESH = pl.DeviceIdType.MESH
ANY = pl.BlockSpec(memory_space=pl.ANY)
VM = pl.BlockSpec(memory_space=pltpu.VMEM)


def sds(shape, dtype):
    return jax.ShapeDtypeStruct(shape, dtype)


def params(ident, limit=58):
    return pltpu.CompilerParams(
        collective_id=ident, has_side_effects=True, vmem_limit_bytes=limit << 20
    )


class Place:
    def __init__(self):
        self.n_dp = lax.axis_size("dp")
        self.count = self.n_dp.bit_length() - 1
        self.t = lax.axis_index("tower")
        self.d = lax.axis_index("dp")
        self.m = lax.axis_index("mp")
        self.bits = [(self.d // (1 << (self.count - 1 - j))) % 2 for j in range(self.count)]

    def across(self, dim):
        if dim == "t":
            return {"tower": 1 - self.t}
        if dim == "y":
            return {"mp": 1 - self.m}
        step = 1 << (self.count - 1 - dim)
        return {"dp": self.d + (1 - 2 * self.bits[dim]) * step}

    def mixed(self, rel):
        out = self.d
        for j in range(self.count):
            step = 1 << (self.count - 1 - j)
            if rel & step:
                out = out + (1 - 2 * self.bits[j]) * step
        return out


def remote(src, dst, send, recv, where):
    return pltpu.make_async_remote_copy(
        src_ref=src, dst_ref=dst, send_sem=send, recv_sem=recv, device_id=where, device_id_type=MESH
    )


def greet(peers):
    barrier = pltpu.get_barrier_semaphore()
    for where in peers:
        pl.semaphore_signal(barrier, inc=1, device_id=where, device_id_type=MESH)
    pl.semaphore_wait(barrier, len(peers))


def tdot(lhs, rhs):
    return lax.dot_general(lhs, rhs, (((1,), (1,)), ((), ())), preferred_element_type=f32)


def mdot(lhs, rhs):
    return jnp.dot(lhs, rhs, preferred_element_type=f32)


class Gather:
    def __init__(self, here, shard, full, other, order, sems, local_sem):
        self.here, self.shard, self.full, self.other = here, shard, full, other
        self.order, self.sems, self.local_sem = order, sems, local_sem
        self.done = set()
        self.live = []
        self.arrays = [full]
        self.slot = 0

    def view(self):
        here = self.here
        return (here.t,) + tuple(
            slice(None) if j in self.done else here.bits[j] for j in range(here.count)
        )

    def begin(self):
        self.place = pltpu.make_async_copy(
            self.shard, self.full.at[self.view()], self.local_sem
        )
        self.place.start()
        self.sent = []

    def stage(self, step):
        here = self.here
        if step > 0:
            for copy in self.live:
                copy.wait_recv()
        if step == 1:
            self.place.wait()
        self.sent += self.live
        self.live = []
        if step == len(self.order):
            for copy in self.sent:
                copy.wait_send()
            return
        dim = self.order[step]
        pairs = []
        if dim == "y":
            pairs = [(self.full.at[self.view()], self.other.at[self.view()])]
            self.arrays = [self.full, self.other]
        elif dim == "t":
            pairs = [(ref.at[here.t], ref.at[here.t]) for ref in self.arrays]
        elif step == 0:
            pairs = [(self.shard, self.full.at[self.view()])]
        else:
            pairs = [(ref.at[self.view()], ref.at[self.view()]) for ref in self.arrays]
        for src, dst in pairs:
            copy = remote(
                src, dst, self.sems[0].at[self.slot], self.sems[1].at[self.slot], here.across(dim)
            )
            copy.start()
            self.live.append(copy)
            self.slot += 1
        if dim not in ("t", "y"):
            self.done.add(dim)


def run_gathers(gathers):
    longest = max(len(g.order) for g in gathers)
    for tick in range(longest + len(gathers)):
        for lag, g in enumerate(gathers):
            step = tick - lag
            if 0 <= step <= len(g.order):
                g.stage(step)


def gather_orders(count):
    far = list(range(count - 1))
    near = [count - 1]
    return {
        "plain": far + near + ["t"],
        "late": far + near + ["y", "t"],
        "early": far + ["y"] + near + ["t"],
    }


def fetch_body(kinds, room, *refs):
    here = Place()
    n, count = here.n_dp, here.count
    refs = list(refs)
    table, lists = refs[0], refs[1]
    shards = refs[2 : 2 + len(kinds)]
    pos = 2 + len(kinds)
    rows, heard, flag = refs[pos : pos + 3]
    pos += 3
    fulls = []
    for kind in kinds:
        if kind == "plain":
            fulls.append((refs[pos], None))
            pos += 1
        else:
            fulls.append((refs[pos], refs[pos + 1]))
            pos += 2
    low_table, served, flags = refs[pos : pos + 3]
    pos += 3
    lows = refs[pos : pos + len(kinds)]
    pos += len(kinds)
    lsem, rsem, ysem, fsem, wsend, wrecv, wlocal = refs[pos:]

    peers = [{"dp": here.mixed(k)} for k in range(1, n)]
    greet(peers + [here.across("t"), here.across("y")])

    list_copies = []
    for k in range(1, n):
        copy = remote(lists.at[k], heard.at[k], lsem.at[0, k], lsem.at[1, k], {"dp": here.mixed(k)})
        copy.start()
        list_copies.append(copy)
    orders = gather_orders(count)
    gathers = []
    for j, kind in enumerate(kinds):
        lows[j][...] = shards[j][...].astype(bf16)
        gathers.append(
            Gather(
                here, lows[j], fulls[j][0], fulls[j][1], orders[kind],
                (wsend.at[j], wrecv.at[j]), wlocal.at[j],
            )
        )
        gathers[-1].begin()
    heard[0] = lists[0]
    low_table[...] = table[...].astype(bf16)
    row_count = table.shape[0]
    out_copies = []
    y_copies = []
    for k in range(n):
        if k > 0:
            list_copies[k - 1].wait_recv()
        column = jnp.transpose(heard[k])[:room, 0:1]
        hot = (lax.broadcasted_iota(jnp.int32, (room, row_count), 1) == column).astype(f32)
        found = mdot(hot.astype(bf16), low_table[...]).astype(bf16)
        if k == 0:
            rows[here.m, 0] = found
            copy = remote(
                rows.at[here.m, 0], rows.at[here.m, 0], ysem.at[0, 0], ysem.at[1, 0], here.across("y")
            )
            copy.start()
            y_copies.append(copy)
        else:
            served[k] = found
            copy = remote(
                served.at[k], rows.at[here.m, k], rsem.at[0, k], rsem.at[1, k],
                {"dp": here.mixed(k)},
            )
            copy.start()
            out_copies.append(copy)
    own_flag = jnp.max(heard[...], axis=0)
    flags[0] = own_flag
    flag_copy = remote(flags.at[0], flags.at[1], fsem.at[0], fsem.at[1], here.across("t"))
    flag_copy.start()
    for k in range(1, n):
        out_copies[k - 1].wait_recv()
        copy = remote(
            rows.at[here.m, k], rows.at[here.m, k], ysem.at[0, k], ysem.at[1, k], here.across("y")
        )
        copy.start()
        y_copies.append(copy)
    run_gathers(gathers)
    flag_copy.wait()
    flag[...] = jnp.maximum(flags[0], flags[1])
    for copy in list_copies + out_copies:
        copy.wait_send()
    for copy in y_copies:
        copy.wait()


def fetch(table, lists, shards, kinds, room):
    n_dp = lists.shape[0]
    count = n_dp.bit_length() - 1
    halves = (2,) + (2,) * count
    width = table.shape[1]
    outs = [
        sds((2, n_dp, room, width), bf16),
        sds(lists.shape, jnp.int32),
        sds(lists.shape[1:], jnp.int32),
    ]
    specs = [VM, VM, VM]
    for shard, kind in zip(shards, kinds):
        full = sds(halves + shard.shape, bf16)
        outs += [full] if kind == "plain" else [full, full]
        specs += [ANY] if kind == "plain" else [ANY, ANY]
    dma = pltpu.SemaphoreType.DMA
    steps = count + 6
    scratch = (
        [
            pltpu.VMEM(table.shape, bf16),
            pltpu.VMEM((n_dp, room, width), bf16),
            pltpu.VMEM((2,) + lists.shape[1:], jnp.int32),
        ]
        + [pltpu.VMEM(shard.shape, bf16) for shard in shards]
        + [dma((2, n_dp)), dma((2, n_dp)), dma((2, n_dp)), dma((2,))]
        + [dma((len(kinds), steps)), dma((len(kinds), steps)), dma((len(kinds),))]
    )
    out = pl.pallas_call(
        lambda *refs: fetch_body(kinds, room, *refs),
        out_shape=outs,
        in_specs=[VM] * (2 + len(shards)),
        out_specs=specs,
        scratch_shapes=scratch,
        compiler_params=params(1),
        name="fetch",
    )(table, lists, *shards)
    rows, heard, flag = out[:3]
    weights, pos = [], 3
    for shard, kind in zip(shards, kinds):
        whole = (2 * n_dp * shard.shape[0], shard.shape[1])
        if kind == "plain":
            weights.append(out[pos].reshape(whole))
            pos += 1
        else:
            weights.append((out[pos].reshape(whole), out[pos + 1].reshape(whole)))
            pos += 2
    return rows, heard, flag, weights


def turned(values):
    lanes = lax.broadcasted_iota(jnp.int32, values.shape, 1) % HDIM
    size = values.shape[1]
    return jnp.where(
        lanes < HDIM // 2,
        -pltpu.roll(values, size - HDIM // 2, 1),
        pltpu.roll(values, HDIM // 2, 1),
    )


def norm_parts(stream):
    average = jnp.mean(stream, -1, keepdims=True)
    centered = stream - average
    variance = jnp.mean(centered * centered, -1, keepdims=True)
    scale = lax.rsqrt(variance + norm_eps)
    return centered * scale, scale


def forward_body(rows, pos, norm_rows, w_qkv, cosine, sine, seg_row, seg_col,
                 emb_out, zero_out, input_out, q_out, k_out, v_out, lse_out, att_out, vt):
    tok = pos.shape[0]
    half = tok // 2
    width = rows.shape[3]
    slots = rows.shape[1] * rows.shape[2]
    feats = q_out.shape[1]
    block = 256

    @pl.loop(0, tok // block)
    def _(i):
        at = pl.ds(pl.multiple_of(i * block, block), block)
        hot = (lax.broadcasted_iota(jnp.int32, (block, slots), 1) == pos[at, :]).astype(f32)
        hot = hot.astype(bf16)
        emb = jnp.concatenate(
            [mdot(hot, rows[h].reshape(slots, width)) for h in range(2)], 1
        )
        hat, _scale = norm_parts(emb)
        stream = hat * norm_rows[0:1, :] + norm_rows[1:2, :]
        low = stream.astype(bf16)
        input_out[at, :] = low

        @pl.when(i < half // block)
        def _():
            emb_out[at, :] = emb.astype(bf16)
            zero_out[at, :] = stream

        cos, sin = cosine[at, :], sine[at, :]
        for c in range(3):
            proj = mdot(low, w_qkv[:, c * feats : (c + 1) * feats])
            for g in range(feats // 128):
                cols = slice(g * 128, (g + 1) * 128)
                part = proj[:, cols]
                if c < 2:
                    part = part * cos + turned(part) * sin
                part = part.astype(bf16)
                if c == 0:
                    q_out[at, cols] = part * bf16(HDIM**-0.5)
                elif c == 1:
                    k_out[at, cols] = part
                else:
                    v_out[at, cols] = part

    lane = lax.broadcasted_iota(jnp.int32, (1, 128), 1)
    for g in range(feats // 128):
        cols = slice(g * 128, (g + 1) * 128)
        vt[...] = jnp.transpose(v_out[:, cols].astype(f32)).astype(bf16)
        keys = [
            jnp.where((lane // HDIM) == h, k_out[:, cols], bf16(0)) for h in range(2)
        ]

        @pl.loop(0, tok // block)
        def _(i):
            at = pl.ds(pl.multiple_of(i * block, block), block)
            query = q_out[at, cols]
            same = seg_col[...] == seg_row[:, at]
            outs = []
            for h in range(2):
                scores = jnp.where(same, tdot(keys[h], query), neg_large)
                peak = jnp.max(scores, 0, keepdims=True)
                soft = jnp.exp(scores - peak)
                total = jnp.sum(soft, 0, keepdims=True)
                lse_out[2 * g + h, :, at] = peak + jnp.log(total)
                soft = (soft * (1.0 / total)).astype(bf16)
                outs.append(mdot(vt[h * HDIM : (h + 1) * HDIM, :], soft))
            att_out[at, cols] = jnp.transpose(jnp.concatenate(outs, 0)).astype(bf16)


def forward_attention(rows, pos, norm_rows, w_qkv, cosine, sine, seg_row, seg_col):
    tok = pos.shape[0]
    width = 2 * rows.shape[3]
    feats = w_qkv.shape[1] // 3
    half = tok // 2
    return pl.pallas_call(
        forward_body,
        out_shape=[
            sds((half, width), bf16),
            sds((half, width), f32),
            sds((tok, width), bf16),
            sds((tok, feats), bf16),
            sds((tok, feats), bf16),
            sds((tok, feats), bf16),
            sds((feats // HDIM, 1, tok), f32),
            sds((tok, feats), bf16),
        ],
        in_specs=[VM] * 8,
        out_specs=[VM] * 8,
        scratch_shapes=[pltpu.VMEM((128, tok), bf16)],
        compiler_params=pltpu.CompilerParams(vmem_limit_bytes=58 << 20),
        name="forward",
    )(rows, pos, norm_rows, w_qkv, cosine, sine, seg_row, seg_col)


def backward_body(query, key, value, grad_att, lse, cosine, sine, seg_row, seg_col,
                  out, kt, dq, dk, dv):
    tok, feats = query.shape
    block = 256
    lane = lax.broadcasted_iota(jnp.int32, (1, 128), 1)
    for g in range(feats // 128):
        cols = slice(g * 128, (g + 1) * 128)
        kt[...] = jnp.transpose(key[:, cols].astype(f32)).astype(bf16)
        keys = [jnp.where((lane // HDIM) == h, key[:, cols], bf16(0)) for h in range(2)]
        values = [jnp.where((lane // HDIM) == h, value[:, cols], bf16(0)) for h in range(2)]
        dk[...] = jnp.zeros_like(dk)
        dv[...] = jnp.zeros_like(dv)

        @pl.loop(0, tok // block)
        def _(i):
            at = pl.ds(pl.multiple_of(i * block, block), block)
            q_part = query[at, cols]
            g_part = grad_att[at, cols]
            same = seg_col[...] == seg_row[:, at]
            turns = []
            for h in range(2):
                mine = (lane // HDIM) == h
                scores = jnp.where(same, tdot(keys[h], q_part), neg_large)
                soft = jnp.exp(scores - lse[2 * g + h, :, at])
                grad_soft = tdot(values[h], g_part)
                inner = jnp.sum(soft * grad_soft, 0, keepdims=True)
                grad_scores = (soft * (grad_soft - inner)).astype(bf16)
                dv[...] += mdot(soft.astype(bf16), jnp.where(mine, g_part, bf16(0)))
                dk[...] += mdot(grad_scores, jnp.where(mine, q_part, bf16(0)))
                turns.append(mdot(kt[h * HDIM : (h + 1) * HDIM, :], grad_scores))
            dq[at, :] = jnp.transpose(jnp.concatenate(turns, 0)) * (HDIM**-0.5)

        cos, sin = cosine[...], sine[...]
        for c, grad in ((0, dq), (1, dk)):
            whole = grad[...]
            back = whole * cos - turned(whole) * sin
            out[:, c * feats + g * 128 : c * feats + (g + 1) * 128] = back.astype(bf16)
        out[:, 2 * feats + g * 128 : 2 * feats + (g + 1) * 128] = dv[...].astype(bf16)


def backward_attention(query, key, value, grad_att, lse, cosine, sine, seg_row, seg_col):
    tok, feats = query.shape
    return pl.pallas_call(
        backward_body,
        out_shape=sds((tok, 3 * feats), bf16),
        in_specs=[VM] * 9,
        out_specs=VM,
        scratch_shapes=[pltpu.VMEM((128, tok), bf16)] + [pltpu.VMEM((tok, 128), f32)] * 3,
        compiler_params=pltpu.CompilerParams(vmem_limit_bytes=58 << 20),
        name="backward",
    )(query, key, value, grad_att, lse, cosine, sine, seg_row, seg_col)


def loss_body(part, counts, doc_ok, query_ok, target, scale, grad_out, stats, other, low_all, turn,
              psend, precv, esend, erecv):
    here = Place()
    n = here.n_dp
    slots, width = part.shape
    peers = []
    for rt in range(2):
        for rd in range(n):
            if rt or rd:
                peers.append(
                    (rt * n + rd, {"tower": here.t + rt * (1 - 2 * here.t), "dp": here.mixed(rd)})
                )
    greet([where for _, where in peers] + [here.across("y")])
    copy = remote(part, other, psend, precv, here.across("y"))
    copy.start()
    copy.wait()
    pooled = (part[...] + other[...]) / counts[...]
    scale_row = lax.rsqrt(jnp.sum(pooled * pooled, 1, keepdims=True) + 1e-06)
    unit = pooled * scale_row
    low_all[here.t, here.d] = unit.astype(bf16)
    copies = []
    for rel, where in peers:
        copy = remote(
            low_all.at[here.t, here.d], low_all.at[here.t, here.d], esend.at[rel], erecv.at[rel], where
        )
        copy.start()
        copies.append(copy)
    for copy in copies:
        copy.wait()
    total = n * slots
    queries = low_all[0].reshape(total, width)
    documents = low_all[1].reshape(total, width)
    cosines = tdot(queries, documents)
    factor = jnp.exp(jnp.minimum(scale[...], cap_value))
    logits = jnp.where(doc_ok[...] > 0, factor * cosines, neg_large)
    peak = jnp.max(logits, 1, keepdims=True)
    log_total = peak + jnp.log(jnp.sum(jnp.exp(logits - peak), 1, keepdims=True))
    soft = jnp.exp(logits - log_total)
    mask = lax.broadcasted_iota(jnp.int32, (total, total), 1) == target[...]
    picked = jnp.sum(jnp.where(mask, logits, 0.0), 1, keepdims=True)
    valid = query_ok[...] > 0
    query_count = jnp.sum(valid.astype(f32), axis=0, keepdims=True)
    loss_sum = jnp.sum(jnp.where(valid, log_total - picked, 0.0), axis=0, keepdims=True)
    grad_logits = jnp.where(valid, soft - mask.astype(f32), 0.0) / query_count
    by_row = jnp.sum(grad_logits * cosines, 1, keepdims=True)
    grad_scale = (
        jnp.sum(by_row, 0, keepdims=True) * factor * (scale[...] < cap_value).astype(f32)
    )
    grad_cos = factor * grad_logits
    at = pl.ds(pl.multiple_of(here.d * slots, slots), slots)
    turn[0] = grad_cos
    turn[1] = jnp.transpose(grad_cos)
    left = turn[here.t, at, :].astype(bf16)
    right = low_all[1 - here.t].reshape(total, width)
    grad_unit = mdot(left, right)
    grad_pooled = scale_row * (
        grad_unit - unit * jnp.sum(unit * grad_unit, 1, keepdims=True)
    )
    grad_out[...] = grad_pooled / counts[...]
    row = lax.broadcasted_iota(jnp.int32, stats.shape, 0)
    stats[...] = jnp.where(row == 0, loss_sum, jnp.where(row == 1, query_count, grad_scale))


def loss_step(part, counts, doc_ok, query_ok, target, scale):
    n_dp = lax.axis_size("dp")
    slots, width = part.shape
    total = n_dp * slots
    dma = pltpu.SemaphoreType.DMA
    return pl.pallas_call(
        loss_body,
        out_shape=[sds(part.shape, f32), sds((8, 128), f32)],
        in_specs=[VM] * 6,
        out_specs=[VM] * 2,
        scratch_shapes=[
            pltpu.VMEM(part.shape, f32),
            pltpu.VMEM((2, n_dp, slots, width), bf16),
            pltpu.VMEM((2, total, total), f32),
            dma, dma, dma((2 * n_dp,)), dma((2 * n_dp,)),
        ],
        compiler_params=params(2),
        name="loss",
    )(part, counts, doc_ok, query_ok, target, scale)


class Scatter:
    def __init__(self, here, own, other, order, held, landed, out, sems):
        self.here, self.own, self.other, self.order = here, own, other, order
        self.held, self.landed, self.out, self.sems = held, landed, out, sems
        self.fixed = {}
        self.live = []
        self.sent = []
        self.slot = 0
        self.land = 0
        self.arrays = [0] if other is None else [0, 1]

    def view(self, extra=None):
        fixed = dict(self.fixed)
        if extra:
            fixed.update(extra)
        return tuple(fixed.get(j, slice(None)) for j in range(self.here.count))

    def send(self, src, where, index):
        here = self.here
        dst = self.landed[self.land]
        copy = remote(src, dst, self.sems[0].at[self.slot], self.sems[1].at[self.slot], where)
        copy.start()
        self.slot += 1
        self.live.append((copy, self.land, index))
        self.land += 1

    def start(self, step):
        here = self.here
        dim = self.order[step]
        if dim == "t":
            for index in self.arrays:
                src = (self.own, self.other)[index]
                self.send(src.at[1 - here.t], here.across("t"), index)
        elif dim == "y":
            self.send(self.held[1].at[self.view()], here.across("y"), 0)
            self.arrays = [0]
        else:
            bit = here.bits[dim]
            for index in self.arrays:
                self.send(self.held[index].at[self.view({dim: 1 - bit})], here.across(dim), index)

    def finish(self, step):
        here = self.here
        dim = self.order[step]
        if dim not in ("t", "y"):
            self.fixed[dim] = here.bits[dim]
        view = self.view()
        last = step == len(self.order) - 1
        for copy, land, index in self.live:
            copy.wait()
            got = self.landed[land][...].astype(f32)
            if dim == "t":
                mine = (self.own, self.other)[index][here.t]
            else:
                mine = self.held[index][view]
            total = mine.astype(f32) + got
            if last:
                self.out[...] = total
            elif dim == "t":
                self.held[index][...] = total.astype(bf16)
            else:
                self.held[index][view] = total.astype(bf16)
        self.live = []


def scatter_lands(order, count, pair, rows, cols):
    shapes, free, live = [], count, 2 if pair else 1
    for dim in order:
        if dim == "y":
            live = 1
        elif dim != "t":
            free -= 1
        shapes += [(2,) * free + (rows, cols)] * live
    return shapes


def scatter_orders(count):
    near = [count - 1]
    far = list(range(count - 2, -1, -1))
    return {
        "plain": ["t"] + near + far,
        "early": ["t", "y"] + near + far,
        "late": ["t"] + near + ["y"] + far,
    }


def run_scatters(scatters):
    longest = max(len(s.order) for s in scatters)
    for tick in range(longest + len(scatters)):
        for lag, s in enumerate(scatters):
            step = tick - lag
            if 0 < step <= len(s.order):
                s.finish(step - 1)
            if 0 <= step < len(s.order):
                s.start(step)


def reduce_body(kinds, sizes, *refs):
    here = Place()
    count = here.count
    orders = scatter_orders(count)
    refs = list(refs)
    ins, pos = [], 0
    for kind in kinds:
        if kind == "plain":
            ins.append((refs[pos], None))
            pos += 1
        else:
            ins.append((refs[pos], refs[pos + 1]))
            pos += 2
    outs = refs[pos : pos + len(kinds)]
    pos += len(kinds)
    scatters = []
    held_all, land_all = [], []
    for kind in kinds:
        width = 1 if kind == "plain" else 2
        held_all.append(refs[pos : pos + width])
        pos += width
    for kind, (rows, cols) in zip(kinds, sizes):
        amount = len(scatter_lands(orders[kind], count, kind != "plain", rows, cols))
        land_all.append(refs[pos : pos + amount])
        pos += amount
    send, recv = refs[pos:]
    greet([here.across("t"), here.across("y")] + [here.across(j) for j in range(count)])
    for j, kind in enumerate(kinds):
        scatters.append(
            Scatter(
                here, ins[j][0], ins[j][1], orders[kind], held_all[j], land_all[j], outs[j],
                (send.at[j], recv.at[j]),
            )
        )
    run_scatters(scatters)


def reduce_grads(grads, kinds, ident):
    n_dp = lax.axis_size("dp")
    count = n_dp.bit_length() - 1
    orders = scatter_orders(count)
    args, sizes, held, lands, outs = [], [], [], [], []
    for grad, kind in zip(grads, kinds):
        pair = [grad] if kind == "plain" else list(grad)
        rows, cols = pair[0].shape[0] // (2 * n_dp), pair[0].shape[1]
        sizes.append((rows, cols))
        args += [g.reshape((2,) + (2,) * count + (rows, cols)) for g in pair]
        held += [pltpu.VMEM((2,) * count + (rows, cols), bf16)] * len(pair)
        lands += [
            pltpu.VMEM(shape, bf16)
            for shape in scatter_lands(orders[kind], count, len(pair) == 2, rows, cols)
        ]
        outs.append(sds((rows, cols), f32))
    dma = pltpu.SemaphoreType.DMA
    steps = 2 * count + 6
    return pl.pallas_call(
        lambda *refs: reduce_body(kinds, sizes, *refs),
        out_shape=outs,
        in_specs=[VM] * len(args),
        out_specs=[VM] * len(outs),
        scratch_shapes=held + lands + [dma((len(kinds), steps)), dma((len(kinds), steps))],
        compiler_params=params(ident),
        name="reduce",
    )(*args)


def spread_body(room, grad, pos, heard, norm_grad, out, lists_out, norms_out,
                other, packed, mine, theirs, heard_o, norms,
                ysem, rsem, csem, lsem, nsem):
    here = Place()
    n = here.n_dp
    width = grad.shape[1] // 2
    half = grad.shape[0]
    slots = n * room
    peers = []
    for rt in range(2):
        for rd in range(n):
            for rm in range(2):
                if rt or rd or rm:
                    peers.append(
                        (
                            (rt * n + rd) * 2 + rm,
                            {
                                "tower": here.t + rt * (1 - 2 * here.t),
                                "dp": here.mixed(rd),
                                "mp": here.m + rm * (1 - 2 * here.m),
                            },
                        )
                    )
    greet([where for _, where in peers])
    theirs_at = pl.ds(pl.multiple_of((1 - here.m) * width, 128), width)
    mine_at = pl.ds(pl.multiple_of(here.m * width, 128), width)
    swap = remote(grad.at[:, theirs_at], other, ysem.at[0], ysem.at[1], here.across("y"))
    swap.start()
    list_copy = remote(heard, heard_o, lsem.at[0], lsem.at[1], here.across("t"))
    list_copy.start()
    me = (here.t * n + here.d) * 2 + here.m
    norm_copies = []
    for rel, where in peers:
        copy = remote(norm_grad, norms.at[me], nsem.at[0, rel], nsem.at[1, rel], where)
        copy.start()
        norm_copies.append(copy)
    norms[me] = norm_grad[...]
    swap.wait()
    both = jnp.concatenate([grad[:, mine_at], other[...]], 0)
    copies = []
    for k in list(range(1, n)) + [0]:
        hot = (
            lax.broadcasted_iota(jnp.int32, (room, pos.shape[1]), 0) + k * room == pos[...]
        ).astype(f32)
        packed[k] = mdot(hot.astype(bf16), both).astype(bf16)
        if k:
            copy = remote(
                packed.at[k], mine.at[k], rsem.at[0, k], rsem.at[1, k], {"dp": here.mixed(k)}
            )
        else:
            mine[0] = packed[0]
            copy = remote(mine.at[0], theirs.at[0], csem.at[0, 0], csem.at[1, 0], here.across("t"))
        copy.start()
        copies.append(copy)
    passed = [copies.pop()]
    for k in range(1, n):
        copies[k - 1].wait_recv()
        copy = remote(mine.at[k], theirs.at[k], csem.at[0, k], csem.at[1, k], here.across("t"))
        copy.start()
        passed.append(copy)
    for copy in copies:
        copy.wait_send()
    for copy in passed:
        copy.wait()
    list_copy.wait()
    row_count = out.shape[0]
    block = row_count
    for size in range(512, 255, -8):
        if row_count % size == 0:
            block = size
            break

    @pl.loop(0, row_count // block)
    def _(i):
        at = pl.ds(pl.multiple_of(i * block, 8) if block != row_count else 0, block)
        base = lax.broadcasted_iota(jnp.int32, (block, room), 0) + i * block
        hots = []
        for source in (heard, heard_o):
            for k in range(n):
                hots.append((base == source[k, 0:1, :room]).astype(f32).astype(bf16))
        whole = jnp.concatenate(hots, 1)
        data = jnp.concatenate(
            [mine[...].reshape(slots, width), theirs[...].reshape(slots, width)], 0
        )
        out[at, :] = mdot(whole, data)

    for copy in norm_copies:
        copy.wait()
    total = norms[0]
    for j in range(1, 4 * n):
        total = total + norms[j]
    norms_out[...] = total


def spread_rows(grad, pos_row, heard, norm_grad, row_count, room):
    n_dp = lax.axis_size("dp")
    width = grad.shape[1] // 2
    half = grad.shape[0]
    dma = pltpu.SemaphoreType.DMA

    def body(grad, pos, heard, norm_grad, out, norms_out, *scratch):
        spread_body(room, grad, pos, heard, norm_grad, out, None, norms_out, *scratch)

    return pl.pallas_call(
        body,
        out_shape=[sds((row_count, width), f32), sds(norm_grad.shape, f32)],
        in_specs=[VM] * 4,
        out_specs=[VM] * 2,
        scratch_shapes=[
            pltpu.VMEM((half, width), bf16),
            pltpu.VMEM((n_dp, room, width), bf16),
            pltpu.VMEM((n_dp, room, width), bf16),
            pltpu.VMEM((n_dp, room, width), bf16),
            pltpu.VMEM(heard.shape, jnp.int32),
            pltpu.VMEM((4 * n_dp,) + norm_grad.shape, f32),
            dma((2,)), dma((2, n_dp)), dma((2, n_dp)), dma((2,)), dma((2, 4 * n_dp)),
        ],
        compiler_params=params(5),
        name="spread",
    )(grad, pos_row, heard, norm_grad)


def total_body(value, out, parts, send, recv):
    here = Place()
    n = here.n_dp
    peers = []
    for rt in range(2):
        for rd in range(n):
            for rm in range(2):
                if rt or rd or rm:
                    where = {
                        "tower": here.t + rt * (1 - 2 * here.t),
                        "dp": here.mixed(rd),
                        "mp": here.m + rm * (1 - 2 * here.m),
                    }
                    peers.append(((rt * n + rd) * 2 + rm, where))
    greet([where for _, where in peers])
    me = (here.t * n + here.d) * 2 + here.m
    copies = []
    for rel, where in peers:
        copy = remote(value, parts.at[me], send.at[rel], recv.at[rel], where)
        copy.start()
        copies.append(copy)
    parts[me] = value[...]
    for copy in copies:
        copy.wait()
    out[...] = jnp.sum(parts[...], 0)


def total_of(value):
    n_dp = lax.axis_size("dp")
    dma = pltpu.SemaphoreType.DMA
    return pl.pallas_call(
        total_body,
        out_shape=sds(value.shape, f32),
        in_specs=[VM],
        out_specs=VM,
        scratch_shapes=[
            pltpu.VMEM((4 * n_dp,) + value.shape, f32), dma((4 * n_dp,)), dma((4 * n_dp,))
        ],
        compiler_params=params(6),
        name="total",
    )(value)


def swap(values):
    return lax.ppermute(values, "mp", [(0, 1), (1, 0)])


def rotary_tables(positions):
    half_dim = HDIM // 2
    inverse = 1000.0 ** (-2.0 * jnp.arange(half_dim, dtype=f32) / HDIM)
    angles = positions.astype(f32)[:, None] * inverse[None, :]
    angles = jnp.concatenate([angles] * 4, 1)
    return jnp.cos(angles), jnp.sin(angles)


def layout(lengths, places, slot_count):
    end_points = jnp.cumsum(lengths)
    segment = jnp.sum((places[:, None] >= end_points[None, :]).astype(jnp.int32), 1)
    starts = jnp.concatenate([jnp.zeros((1,), jnp.int32), end_points])
    slot_ids = jnp.arange(slot_count + 1, dtype=jnp.int32)
    segment_start = jnp.sum(jnp.where(segment[:, None] == slot_ids[None, :], starts[None, :], 0), 1)
    return segment, places - segment_start


def norm_back(grad, hat, scale, gain):
    grad_hat = grad * gain
    first = jnp.mean(grad_hat, -1, keepdims=True)
    second = jnp.mean(grad_hat * hat, -1, keepdims=True)
    return (
        scale * (grad_hat - first - hat * second),
        jnp.sum(grad * hat, 0),
        jnp.sum(grad, 0),
    )


def glu(gate_vals, up_vals):
    return jax.nn.silu(gate_vals) * up_vals


def adamw(weight_in, gradient, first_mom, second, factor, step_num, rate):
    gradient = gradient * factor
    first_new = beta_one * first_mom + (1.0 - beta_one) * gradient
    second_new = beta_two * second + (1.0 - beta_two) * gradient * gradient
    first_hat = first_new / (1.0 - beta_one**step_num)
    second_hat = second_new / (1.0 - beta_two**step_num)
    weight_new = weight_in - rate * (
        first_hat / (jnp.sqrt(second_hat) + adam_eps) + decay_rate * weight_in
    )
    return (weight_new, first_new, second_new)


def name_rows(ids, d, n_dp, row_count, room):
    tok = ids.shape[0]
    owner = ids // row_count
    local = ids - owner * row_count
    order = jnp.bitwise_xor(owner, d)
    places = jnp.arange(tok, dtype=jnp.int32)
    first_at = jnp.min(
        jnp.where(ids[:, None] == ids[None, :], places[None, :], tok), 1
    )
    is_first = first_at == places
    slot = jnp.sum(
        (
            (places[None, :] < first_at[:, None])
            & is_first[None, :]
            & (owner[None, :] == owner[:, None])
        ).astype(jnp.int32),
        1,
    )
    over = jnp.max(slot) >= room
    pos = order * room + slot
    wanted = jnp.arange(n_dp * room, dtype=jnp.int32)
    listed = jnp.max(
        jnp.where((pos[None, :] == wanted[:, None]) & is_first[None, :], local[None, :], -1), 1
    ).reshape(n_dp, 1, room)
    listed = jnp.pad(listed, ((0, 0), (0, 0), (0, 128 - room)), constant_values=-1)
    flag = jnp.broadcast_to(over.astype(jnp.int32), (n_dp, 7, 128))
    return pos, jnp.concatenate([listed, flag], 1)


def local(
    token_ids, seq_lengths, positives, embedding, attn_in, attn_out, ffn_in, ffn_out, norm_params,
    logit_scale, embed_m, embed_v, attn_in_m, attn_in_v, attn_out_m, attn_out_v, ffn_in_m, ffn_in_v,
    ffn_out_m, ffn_out_v, norm_m, norm_v, scale_m, scale_v,
):
    n_dp = lax.axis_size("dp")
    tower_idx = lax.axis_index("tower")
    data_idx = lax.axis_index("dp")
    model_idx = lax.axis_index("mp")
    slot_count = seq_lengths.shape[2]
    ids = token_ids[0]
    tok = ids.shape[0]
    half = tok // 2
    row_count, width = embedding.shape
    room = max(32, tok // n_dp)
    heads_cols = attn_out.shape[1]
    ff = ffn_out.shape[1]

    pos, lists = name_rows(ids, data_idx, n_dp, row_count, room)
    kinds = ("plain", "late", "late", "early", "late")
    shards = (
        attn_in.reshape(attn_in.shape[0], -1), attn_out, ffn_in[:, 0], ffn_in[:, 1], ffn_out,
    )
    rows, heard, flag, weights = fetch(embedding, lists, shards, kinds, room)
    w_qkv, w_out, w_gate, w_up, w_down = weights
    crowded = flag[1, 0] > 0

    def whole_table(_):
        table = lax.all_gather(embedding.astype(bf16), "dp", axis=0, tiled=True)
        mine = jnp.take(table, jnp.clip(ids, 0, table.shape[0] - 1), axis=0)
        both = lax.all_gather(mine, "mp", axis=0)
        extra = n_dp * room - tok
        both = jnp.pad(both, ((0, 0), (0, extra), (0, 0)))
        return both.reshape(rows.shape), jnp.arange(tok, dtype=jnp.int32)

    rows, pos_used = lax.cond(crowded, whole_table, lambda _: (rows, pos), None)
    shift = model_idx * half
    places = (jnp.arange(tok, dtype=jnp.int32) + shift) % tok
    pos_rel = jnp.where(
        model_idx == 0, pos_used, jnp.concatenate([pos_used[half:], pos_used[:half]])
    )
    pos_back = jnp.where(model_idx == 0, pos, jnp.concatenate([pos[half:], pos[:half]]))
    lengths_row = seq_lengths[tower_idx, data_idx]
    segment, positions = layout(lengths_row, places, slot_count)
    cosine, sine = rotary_tables(positions)
    seg_row, seg_col = segment[None, :], segment[:, None]
    emb, stream_zero, input_zero, query, key, value, lse, attended = forward_attention(
        rows, pos_rel[:, None], norm_params[0:2], w_qkv, cosine, sine, seg_row, seg_col
    )
    att = (attended[:half], swap(attended[half:]))

    sum_one = stream_zero + tdot(att[0], w_out[0]) + tdot(att[1], w_out[1])
    hat_one, scale_one = norm_parts(sum_one)
    stream_one = hat_one * norm_params[2] + norm_params[3]
    input_one = stream_one.astype(bf16)
    gates = [mdot(input_one, w_gate[j]) for j in range(2)]
    ups = [mdot(input_one, w_up[j]) for j in range(2)]
    hidden = [glu(gates[j], ups[j]).astype(bf16) for j in range(2)]
    sum_two = stream_one + tdot(hidden[0], w_down[0]) + tdot(hidden[1], w_down[1])
    hat_two, scale_two = norm_parts(sum_two)
    stream_two = hat_two * norm_params[4] + norm_params[5]

    member = (segment[None, :half] == jnp.arange(slot_count, dtype=jnp.int32)[:, None]).astype(f32)
    counts = jnp.maximum(lengths_row, 1).astype(f32)[:, None]
    part = jnp.dot(member, stream_two, precision=highest)
    doc_ok = (seq_lengths[1].reshape(1, -1) > 0).astype(f32)
    query_ok = (seq_lengths[0].reshape(-1, 1) > 0).astype(f32)
    grad_pool, stats = loss_step(
        part, counts, doc_ok, query_ok, positives.reshape(-1, 1), logit_scale.reshape(1, 1)
    )
    loss_sum, query_count, scale_grad = stats[0, 0], stats[1, 0], stats[2, 0]

    grad_two = jnp.dot(member.T, grad_pool, precision=highest)
    grad_sum_two, gain_two, bias_two = norm_back(grad_two, hat_two, scale_two, norm_params[4])
    ffn_low = grad_sum_two.astype(bf16)
    grad_down, grad_gate, grad_up = [], [], []
    grad_stream_one = grad_sum_two
    for j in range(2):
        grad_down.append(jnp.einsum("td,tf->df", ffn_low, hidden[j], preferred_element_type=f32).astype(bf16))
        grad_hidden = mdot(ffn_low, w_down[j])
        d_gate, d_up = jax.vjp(glu, gates[j], ups[j])[1](grad_hidden)
        d_gate, d_up = d_gate.astype(bf16), d_up.astype(bf16)
        grad_gate.append(jnp.einsum("td,tf->df", input_one, d_gate, preferred_element_type=f32).astype(bf16))
        grad_up.append(jnp.einsum("td,tf->df", input_one, d_up, preferred_element_type=f32).astype(bf16))
        grad_stream_one = grad_stream_one + tdot(d_gate, w_gate[j]) + tdot(d_up, w_up[j])
    grad_sum_one, gain_one, bias_one = norm_back(
        grad_stream_one, hat_one, scale_one, norm_params[2]
    )
    attn_low = grad_sum_one.astype(bf16)
    grad_out = [
        jnp.einsum("td,tf->df", attn_low, att[j], preferred_element_type=f32).astype(bf16) for j in range(2)
    ]
    grad_att = jnp.concatenate(
        [mdot(attn_low, w_out[0]).astype(bf16), swap(mdot(attn_low, w_out[1]).astype(bf16))], 0
    )
    grad_proj = backward_attention(
        query, key, value, grad_att, lse, cosine, sine, seg_row, seg_col
    )
    grad_qkv = jnp.einsum("td,tf->df", input_zero, grad_proj, preferred_element_type=f32).astype(bf16)
    back = tdot(grad_proj, w_qkv)
    grad_stream_zero = grad_sum_one + back[:half] + swap(back[half:].astype(bf16)).astype(f32)
    hat_zero, scale_zero = norm_parts(emb.astype(f32))
    grad_embed, gain_zero, bias_zero = norm_back(
        grad_stream_zero, hat_zero, scale_zero, norm_params[0]
    )
    embed_low = grad_embed.astype(bf16)
    norm_part = jnp.stack([gain_zero, bias_zero, gain_one, bias_one, gain_two, bias_two])
    norm_part = jnp.pad(norm_part, ((0, 2), (0, 0)))
    embed_grad, norm_sum = spread_rows(
        embed_low, pos_back[None, :], heard, norm_part, row_count, room
    )
    norm_grad = norm_sum[:6]

    def whole_grads(_):
        column = lax.dynamic_slice_in_dim(embed_low, model_idx * width, width, 1)
        theirs = lax.dynamic_slice_in_dim(embed_low, (1 - model_idx) * width, width, 1)
        theirs = swap(theirs)
        full = jnp.where(
            model_idx == 0,
            jnp.concatenate([column, theirs], 0),
            jnp.concatenate([theirs, column], 0),
        )
        all_ids = lax.all_gather(ids, ("tower", "dp"), axis=0, tiled=True)
        piece = all_ids - data_idx * row_count
        inside = (piece >= 0) & (piece < row_count)
        return jax.ops.segment_sum(
            lax.all_gather(full, ("tower", "dp"), axis=0, tiled=True).astype(f32),
            jnp.where(inside, piece, row_count),
            num_segments=row_count + 1,
        )[:row_count]

    embed_grad = lax.cond(crowded, whole_grads, lambda _: embed_grad, None)
    r_qkv, r_out, r_gate, r_up, r_down = reduce_grads(
        (grad_qkv, grad_out, grad_gate, grad_up, grad_down),
        ("plain", "late", "late", "early", "late"), 4,
    )
    r_qkv = r_qkv.reshape(attn_in.shape)
    r_ffn = jnp.stack([r_gate, r_up], 1)
    shard_grads = (r_qkv, r_out, r_ffn, r_down)
    local_sq = sum((jnp.sum(gradient * gradient) for gradient in shard_grads)) + 0.5 * jnp.sum(
        embed_grad * embed_grad
    )
    total_sq = (
        total_of(jnp.broadcast_to(local_sq, (8, 128)))[0, 0]
        + jnp.sum(norm_grad * norm_grad)
        + scale_grad * scale_grad
    )
    grad_norm = jnp.sqrt(total_sq)
    factor = jnp.minimum(1.0, clip_max / (grad_norm + 1e-06))
    step_num = float(STEP)
    embed_new = adamw(embedding, embed_grad, embed_m, embed_v, factor, step_num, learn_rate)
    qkv_new = adamw(attn_in, shard_grads[0], attn_in_m, attn_in_v, factor, step_num, learn_rate)
    out_new = adamw(attn_out, shard_grads[1], attn_out_m, attn_out_v, factor, step_num, out_rate)
    ffn_new = adamw(ffn_in, shard_grads[2], ffn_in_m, ffn_in_v, factor, step_num, learn_rate)
    down_new = adamw(ffn_out, shard_grads[3], ffn_out_m, ffn_out_v, factor, step_num, learn_rate)
    norms_new = adamw(norm_params, norm_grad, norm_m, norm_v, factor, step_num, norm_rate)
    scale_new = adamw(
        logit_scale, scale_grad.reshape(1), scale_m, scale_v, factor, step_num, learn_rate
    )
    return (
        *embed_new, *qkv_new, *out_new, *ffn_new, *down_new, *norms_new, *scale_new,
        loss_sum.reshape(1), query_count.reshape(1), grad_norm.reshape(1),
    )


def solution(mesh):
    table, rows3, rows2 = P("dp", "mp"), P(("tower", "dp"), None, "mp"), P(("tower", "dp"), "mp")
    weights = (table, rows3, rows2, rows3, rows2)
    moments = tuple(spec for spec in weights for _ in range(2))
    return jax.shard_map(
        local,
        mesh=mesh,
        in_specs=(P("tower", "dp"), P(), P()) + weights + (P(), P()) + moments + (P(),) * 4,
        out_specs=tuple(spec for spec in weights for _ in range(3)) + (P(),) * 9,
        check_vma=False,
    )
```

```python
import jax
import jax.numpy as jnp
from jax import lax
from jax.sharding import PartitionSpec as P
from jax.experimental import pallas as pl
from jax.experimental.pallas import tpu as pltpu

HDIM = 64
STEP = 5

norm_eps = 1e-06
cap_value = 3.4
clip_max = 0.01
beta_one = 0.9
beta_two = 0.999
learn_rate = 0.02
out_rate = 0.05
norm_rate = 0.3
decay_rate = 0.01
adam_eps = 1e-08
neg_large = -1e30
highest = lax.Precision.HIGHEST
f32 = jnp.float32
bf16 = jnp.bfloat16
MESH = pl.DeviceIdType.MESH
ANY = pl.BlockSpec(memory_space=pl.ANY)
VM = pl.BlockSpec(memory_space=pltpu.VMEM)


def sds(shape, dtype):
    return jax.ShapeDtypeStruct(shape, dtype)


def params(ident, limit=58):
    return pltpu.CompilerParams(
        collective_id=ident, has_side_effects=True, vmem_limit_bytes=limit << 20
    )


class Place:
    def __init__(self):
        self.n_dp = lax.axis_size("dp")
        self.count = self.n_dp.bit_length() - 1
        self.t = lax.axis_index("tower")
        self.d = lax.axis_index("dp")
        self.m = lax.axis_index("mp")
        self.bits = [(self.d // (1 << (self.count - 1 - j))) % 2 for j in range(self.count)]

    def across(self, dim):
        if dim == "t":
            return {"tower": 1 - self.t}
        if dim == "y":
            return {"mp": 1 - self.m}
        step = 1 << (self.count - 1 - dim)
        return {"dp": self.d + (1 - 2 * self.bits[dim]) * step}

    def mixed(self, rel):
        out = self.d
        for j in range(self.count):
            step = 1 << (self.count - 1 - j)
            if rel & step:
                out = out + (1 - 2 * self.bits[j]) * step
        return out


def remote(src, dst, send, recv, where):
    return pltpu.make_async_remote_copy(
        src_ref=src, dst_ref=dst, send_sem=send, recv_sem=recv, device_id=where, device_id_type=MESH
    )


def greet(peers):
    barrier = pltpu.get_barrier_semaphore()
    for where in peers:
        pl.semaphore_signal(barrier, inc=1, device_id=where, device_id_type=MESH)
    pl.semaphore_wait(barrier, len(peers))


def tdot(lhs, rhs):
    return lax.dot_general(lhs, rhs, (((1,), (1,)), ((), ())), preferred_element_type=f32)


def mdot(lhs, rhs):
    return jnp.dot(lhs, rhs, preferred_element_type=f32)


def every(ndim, cols):
    return (slice(None),) * (ndim - 1) + (cols,)


class Gather:
    def __init__(self, here, shard, full, other, order, cols, send, recv, local_sem):
        self.here, self.shard, self.full, self.other = here, shard, full, other
        self.order, self.cols, self.send, self.recv = order, cols, send, recv
        self.local_sem = local_sem
        self.last = len(order)
        self.done = set()
        self.live, self.sent = [], []
        self.arrays = [full]
        self.slot = 0

    def view(self):
        here = self.here
        return (
            (here.t,)
            + tuple(slice(None) if j in self.done else here.bits[j] for j in range(here.count))
            + (slice(None), self.cols)
        )

    def stage(self, step):
        here = self.here
        if step == 0:
            self.place = pltpu.make_async_copy(
                self.shard.at[:, self.cols], self.full.at[self.view()], self.local_sem
            )
            self.place.start()
        for copy in self.live:
            copy.wait_recv()
        if step == 1:
            self.place.wait()
        self.sent += self.live
        self.live = []
        if step == self.last:
            for copy in self.sent:
                copy.wait_send()
            return
        dim = self.order[step]
        if dim == "y":
            pairs = [(self.full.at[self.view()], self.other.at[self.view()])]
            self.arrays = [self.full, self.other]
        elif step == 0:
            pairs = [(self.shard.at[:, self.cols], self.full.at[self.view()])]
        else:
            pairs = [(ref.at[self.view()], ref.at[self.view()]) for ref in self.arrays]
        for src, dst in pairs:
            copy = remote(
                src, dst, self.send.at[self.slot], self.recv.at[self.slot], here.across(dim)
            )
            copy.start()
            self.live.append(copy)
            self.slot += 1
        if dim not in ("t", "y"):
            self.done.add(dim)


class Scatter:
    def __init__(self, here, own, other, order, cols, held, landed, out, send, recv, local_sems):
        self.here, self.order, self.cols = here, order, cols
        self.source = [own] if other is None else [own, other]
        self.held, self.landed, self.out = held, landed, out
        self.send, self.recv, self.local_sems = send, recv, local_sems
        self.last = len(order)
        self.fixed = {}
        self.live = []
        self.slot = 0
        self.arrays = list(range(len(self.source)))

    def view(self, extra=None):
        fixed = dict(self.fixed)
        if extra:
            fixed.update(extra)
        return tuple(fixed.get(j, slice(None)) for j in range(self.here.count))

    def start(self, src, where, index):
        copy = remote(
            src, self.landed[self.slot], self.send.at[self.slot], self.recv.at[self.slot], where
        )
        copy.start()
        self.live.append((copy, self.slot, index))
        self.slot += 1

    def stage(self, step):
        here = self.here
        if step > 0:
            self.finish(step - 1)
        if step == self.last:
            return
        dim = self.order[step]
        if dim == "t":
            self.loads = []
            tail = (slice(None),) * (here.count + 1) + (self.cols,)
            for index in self.arrays:
                load = pltpu.make_async_copy(
                    self.source[index].at[(here.t,) + tail], self.held[index],
                    self.local_sems.at[index],
                )
                load.start()
                self.loads.append(load)
                self.start(self.source[index].at[(1 - here.t,) + tail], here.across("t"), index)
        elif dim == "y":
            self.start(self.held[1].at[self.view()], here.across("y"), 0)
            self.arrays = [0]
        else:
            far = self.view({dim: 1 - here.bits[dim]})
            for index in self.arrays:
                self.start(self.held[index].at[far], here.across(dim), index)

    def finish(self, step):
        here = self.here
        dim = self.order[step]
        if dim not in ("t", "y"):
            self.fixed[dim] = here.bits[dim]
        view = self.view()
        if dim == "t":
            for load in self.loads:
                load.wait()
        for copy, slot, index in self.live:
            copy.wait()
            total = self.held[index][view].astype(f32) + self.landed[slot][...].astype(f32)
            if step == self.last - 1:
                self.out[:, self.cols] = total
            else:
                self.held[index][view] = total.astype(bf16)
        self.live = []


class Runner:
    def __init__(self, jobs, lags):
        self.jobs, self.lags, self.tick = jobs, lags, 0
        self.length = max(job.last + lag for job, lag in zip(jobs, lags)) + 1

    def advance(self):
        if self.tick < self.length:
            for job, lag in zip(self.jobs, self.lags):
                if 0 <= self.tick - lag <= job.last:
                    job.stage(self.tick - lag)
            self.tick += 1

    def drain(self):
        while self.tick < self.length:
            self.advance()


def gather_orders(count):
    far, near = list(range(count - 1)), [count - 1]
    return {
        "plain": far + near + ["t"],
        "late": far + near + ["y", "t"],
        "early": far + ["y"] + near + ["t"],
    }


def scatter_orders(count):
    near, far = [count - 1], list(range(count - 2, -1, -1))
    return {
        "plain": ["t"] + near + far,
        "early": ["t", "y"] + near + far,
        "late": ["t"] + near + ["y"] + far,
    }


def scatter_lands(order, count, pair, rows, cols):
    shapes, free, live = [], count, 2 if pair else 1
    for dim in order:
        if dim == "y":
            live = 1
        elif dim != "t":
            free -= 1
        shapes += [(2,) * free + (rows, cols)] * live
    return shapes


def lists_body(lists, heard, flag, send, recv):
    here = Place()
    n = here.n_dp
    peers = []
    for rt in range(2):
        for k in range(n):
            if rt or k:
                peers.append((rt, k, {"tower": here.t + rt * (1 - 2 * here.t), "dp": here.mixed(k)}))
    greet([where for _, _, where in peers])
    copies = []
    for rt, k, where in peers:
        copy = remote(lists.at[k], heard.at[rt, k], send.at[rt, k], recv.at[rt, k], where)
        copy.start()
        copies.append(copy)
    heard[0, 0] = lists[0]
    for copy in copies:
        copy.wait()
    flag[...] = jnp.max(heard[...].reshape((2 * n,) + flag.shape), axis=0)


def exchange_lists(lists):
    n = lists.shape[0]
    dma = pltpu.SemaphoreType.DMA
    return pl.pallas_call(
        lists_body,
        out_shape=[sds((2,) + lists.shape, jnp.int32), sds(lists.shape[1:], jnp.int32)],
        in_specs=[VM],
        out_specs=[VM, VM],
        scratch_shapes=[dma((2, n)), dma((2, n))],
        compiler_params=params(1),
        name="lists",
    )(lists)


def turned(values):
    lanes = lax.broadcasted_iota(jnp.int32, values.shape, 1) % HDIM
    size = values.shape[1]
    return jnp.where(
        lanes < HDIM // 2,
        -pltpu.roll(values, size - HDIM // 2, 1),
        pltpu.roll(values, HDIM // 2, 1),
    )


def norm_parts(stream):
    average = jnp.mean(stream, -1, keepdims=True)
    centered = stream - average
    variance = jnp.mean(centered * centered, -1, keepdims=True)
    scale = lax.rsqrt(variance + norm_eps)
    return centered * scale, scale


def forward_body(room, kinds, pieces, *refs):
    here = Place()
    n, count = here.n_dp, here.count
    table, heard, pos, norm_rows, cosine, sine, seg_row, seg_col = refs[:8]
    shards = refs[8:13]
    emb_out, zero_out, input_out, q_out, k_out, v_out, lse_out, att_own, att_other = refs[13:22]
    fulls, at = [], 22
    for kind in kinds:
        width = 1 if kind == "plain" else 2
        fulls.append((refs[at], None) if width == 1 else (refs[at], refs[at + 1]))
        at += width
    low_table, served, rows, vt, att_far = refs[at : at + 5]
    lows = refs[at + 5 : at + 10]
    rsem, ysem, asem, wsend, wrecv, wlocal = refs[at + 10 :]
    tok = pos.shape[0]
    half = tok // 2
    width = rows.shape[3]
    slots = n * room
    feats = q_out.shape[1]
    groups = feats // 128
    block = 256

    greet(
        [{"dp": here.mixed(k)} for k in range(1, n)] + [here.across("t"), here.across("y")]
    )
    orders = gather_orders(count)
    for low, shard in zip(lows, shards):
        low[...] = shard[...].astype(bf16)
    jobs, lags = [], []
    for number, (which, kind, start, size, lag) in enumerate(pieces):
        jobs.append(
            Gather(
                here, lows[which], fulls[which][0], fulls[which][1], orders[kind],
                pl.ds(start, size), wsend.at[number], wrecv.at[number], wlocal.at[number],
            )
        )
        lags.append(lag)
    runner = Runner(jobs, lags)
    first_ticks = jobs[0].last + 1
    runner.advance()
    low_table[...] = table[...].astype(bf16)
    row_count = table.shape[0]
    out_copies, y_copies = [], []

    def pass_on(k):
        copy = remote(
            rows.at[here.m, k], rows.at[here.m, k], ysem.at[0, k], ysem.at[1, k], here.across("y")
        )
        copy.start()
        y_copies.append(copy)

    for k in list(range(1, n)) + [0]:
        column = jnp.transpose(heard[k])[:room, 0:1]
        hot = (lax.broadcasted_iota(jnp.int32, (room, row_count), 1) == column).astype(f32)
        found = mdot(hot.astype(bf16), low_table[...]).astype(bf16)
        if k == 0:
            rows[here.m, 0] = found
            pass_on(0)
        else:
            served[k] = found
            copy = remote(
                served.at[k], rows.at[here.m, k], rsem.at[0, k], rsem.at[1, k],
                {"dp": here.mixed(k)},
            )
            copy.start()
            out_copies.append(copy)
            if k == n // 2:
                runner.advance()
    for k in range(1, n):
        out_copies[k - 1].wait_recv()
        pass_on(k)
    while runner.tick < first_ticks:
        runner.advance()
    for copy in out_copies:
        copy.wait_send()
    for copy in y_copies:
        copy.wait()

    w_qkv = fulls[0][0]
    for i in range(tok // block):
        at = slice(i * block, (i + 1) * block)
        hot = (lax.broadcasted_iota(jnp.int32, (block, slots), 1) == pos[at, :]).astype(f32)
        hot = hot.astype(bf16)
        emb = jnp.concatenate([mdot(hot, rows[h].reshape(slots, width)) for h in range(2)], 1)
        hat, _scale = norm_parts(emb)
        stream = hat * norm_rows[0:1, :] + norm_rows[1:2, :]
        low = stream.astype(bf16)
        input_out[at, :] = low
        if (i + 1) * block <= half:
            emb_out[at, :] = emb.astype(bf16)
            zero_out[at, :] = stream
        cos, sin = cosine[at, :], sine[at, :]
        proj = mdot(low, w_qkv[...].reshape(2 * width, 3 * feats))
        for c in range(3):
            for g in range(groups):
                cols = slice(g * 128, (g + 1) * 128)
                part = proj[:, c * feats + g * 128 : c * feats + (g + 1) * 128]
                if c < 2:
                    part = part * cos + turned(part) * sin
                part = part.astype(bf16)
                if c == 0:
                    q_out[at, cols] = part * bf16(HDIM**-0.5)
                elif c == 1:
                    k_out[at, cols] = part
                else:
                    v_out[at, cols] = part
        runner.advance()

    lane = lax.broadcasted_iota(jnp.int32, (1, 128), 1)
    att_copies = []
    for g in range(groups):
        cols = slice(g * 128, (g + 1) * 128)
        vt[...] = jnp.transpose(v_out[:, cols].astype(f32)).astype(bf16)
        keys = [jnp.where((lane // HDIM) == h, k_out[:, cols], bf16(0)) for h in range(2)]
        for i in list(range(tok // block // 2, tok // block)) + list(range(tok // block // 2)):
            at = slice(i * block, (i + 1) * block)
            query = q_out[at, cols]
            same = seg_col[...] == seg_row[:, at]
            outs = []
            for h in range(2):
                scores = jnp.where(same, tdot(keys[h], query), neg_large)
                peak = jnp.max(scores, 0, keepdims=True)
                soft = jnp.exp(scores - peak)
                total = jnp.sum(soft, 0, keepdims=True)
                lse_out[2 * g + h, :, at] = peak + jnp.log(total)
                soft = (soft * (1.0 / total)).astype(bf16)
                outs.append(mdot(vt[h * HDIM : (h + 1) * HDIM, :], soft))
            found = jnp.transpose(jnp.concatenate(outs, 0)).astype(bf16)
            if i * block < half:
                att_own[at, cols] = found
            else:
                att_far[slice(i * block - half, (i + 1) * block - half), cols] = found
                if (i + 1) * block == tok:
                    copy = remote(
                        att_far.at[:, cols], att_other.at[:, cols], asem.at[0, g], asem.at[1, g],
                        here.across("y"),
                    )
                    copy.start()
                    att_copies.append(copy)
            runner.advance()
    runner.drain()
    for copy in att_copies:
        copy.wait()


def forward_pass(table, heard, pos, norm_rows, cosine, sine, seg_row, seg_col, shards, kinds, pieces):
    n_dp, room = heard.shape[0], max(32, pos.shape[0] // heard.shape[0])
    count = n_dp.bit_length() - 1
    halves = (2,) * (count + 1)
    tok = pos.shape[0]
    half = tok // 2
    width = table.shape[1]
    feats = shards[0].shape[1] // 3
    outs = [
        sds((half, 2 * width), bf16),
        sds((half, 2 * width), f32),
        sds((tok, 2 * width), bf16),
        sds((tok, feats), bf16),
        sds((tok, feats), bf16),
        sds((tok, feats), bf16),
        sds((feats // HDIM, 1, tok), f32),
        sds((half, feats), bf16),
        sds((half, feats), bf16),
    ]
    specs = [VM] * len(outs)
    for shard, kind in zip(shards, kinds):
        full = sds(halves + shard.shape, bf16)
        outs += [full] if kind == "plain" else [full, full]
        specs += [VM] if kind == "plain" else [ANY, ANY]
    dma = pltpu.SemaphoreType.DMA
    steps = count + 6
    scratch = (
        [
            pltpu.VMEM(table.shape, bf16),
            pltpu.VMEM((n_dp, room, width), bf16),
            pltpu.VMEM((2, n_dp, room, width), bf16),
            pltpu.VMEM((128, tok), bf16),
            pltpu.VMEM((half, feats), bf16),
        ]
        + [pltpu.VMEM(shard.shape, bf16) for shard in shards]
        + [dma((2, n_dp)), dma((2, n_dp)), dma((2, feats // 128))]
        + [dma((len(pieces), steps)), dma((len(pieces), steps)), dma((len(pieces),))]
    )
    out = pl.pallas_call(
        lambda *refs: forward_body(room, kinds, pieces, *refs),
        out_shape=outs,
        in_specs=[VM] * (8 + len(shards)),
        out_specs=specs,
        scratch_shapes=scratch,
        compiler_params=params(2),
        name="forward",
    )(table, heard, pos, norm_rows, cosine, sine, seg_row, seg_col, *shards)
    weights, at = [], 9
    for shard, kind in zip(shards, kinds):
        whole = (2 * n_dp * shard.shape[0], shard.shape[1])
        if kind == "plain":
            weights.append(out[at].reshape(whole))
            at += 1
        else:
            weights.append((out[at].reshape(whole), out[at + 1].reshape(whole)))
            at += 2
    return out[:9], weights


def make_scatters(here, grads, kinds, pieces, outs, held, landed, send, recv, loads):
    orders = scatter_orders(here.count)
    jobs, lags = [], []
    held, landed = list(held), list(landed)
    for number, (which, kind, start, size, lag) in enumerate(pieces):
        own, other = grads[which]
        pair = other is not None
        mine = [held.pop(0) for _ in range(2 if pair else 1)]
        amount = len(scatter_lands(orders[kind], here.count, pair, 1, 1))
        lands = [landed.pop(0) for _ in range(amount)]
        jobs.append(
            Scatter(
                here, own, other, orders[kind], pl.ds(start, size), mine, lands, outs[which],
                send.at[number], recv.at[number], loads.at[number],
            )
        )
        lags.append(lag)
    return Runner(jobs, lags)


def scatter_scratch(count, rows, pairs, pieces):
    orders = scatter_orders(count)
    held, landed = [], []
    for which, kind, _start, size, _lag in pieces:
        pair = pairs[which]
        held += [pltpu.VMEM((2,) * count + (rows, size), bf16)] * (2 if pair else 1)
        landed += [
            pltpu.VMEM(shape, bf16)
            for shape in scatter_lands(orders[kind], count, pair, rows, size)
        ]
    dma = pltpu.SemaphoreType.DMA
    steps = 2 * count + 6
    sems = [dma((len(pieces), steps)), dma((len(pieces), steps)), dma((len(pieces), 2))]
    return held, landed, sems


def square_sum(values):
    return jnp.sum(jnp.sum(values * values, 0, keepdims=True), 1, keepdims=True)


def backward_body(pieces, sizes, *refs):
    here = Place()
    (low, out_own, out_other, query, key, value, lse, cosine, sine, seg_row, seg_col, residual,
     emb, norm_rows, w_qkv) = refs[:15]
    grads = [(refs[15 + 2 * j], refs[16 + 2 * j]) for j in range(3)]
    grad_proj, low_out, norms_out = refs[21:24]
    outs = refs[24:27]
    squares = refs[27]
    kt, dq, dk, dv, grad_att, far_att, far_send, far_recv = refs[28:36]
    at = 36
    held = refs[at : at + sizes[0]]
    landed = refs[at + sizes[0] : at + sizes[0] + sizes[1]]
    asem, bsem, send, recv, loads = refs[at + sizes[0] + sizes[1] :]
    tok, feats = query.shape
    half = tok // 2
    groups = feats // 128
    block = 256
    greet([here.across("t"), here.across("y")] + [here.across(j) for j in range(here.count)])
    runner = make_scatters(here, grads, None, pieces, outs, held, landed, send, recv, loads)
    runner.advance()
    att_copies = []
    far_att[...] = mdot(low[...], out_other[...]).astype(bf16)
    for g in range(groups):
        cols = slice(g * 128, (g + 1) * 128)
        copy = remote(
            far_att.at[:, cols], grad_att.at[half:, cols], asem.at[0, g], asem.at[1, g],
            here.across("y"),
        )
        copy.start()
        att_copies.append(copy)
    grad_att[:half, :] = mdot(low[...], out_own[...]).astype(bf16)
    lane = lax.broadcasted_iota(jnp.int32, (1, 128), 1)
    for g in range(groups):
        cols = slice(g * 128, (g + 1) * 128)
        kt[...] = jnp.transpose(key[:, cols].astype(f32)).astype(bf16)
        keys = [jnp.where((lane // HDIM) == h, key[:, cols], bf16(0)) for h in range(2)]
        values = [jnp.where((lane // HDIM) == h, value[:, cols], bf16(0)) for h in range(2)]
        for i in range(tok // block):
            if i * block == half:
                att_copies[g].wait_recv()
            rows = slice(i * block, (i + 1) * block)
            q_part = query[rows, cols]
            g_part = grad_att[rows, cols]
            same = seg_col[...] == seg_row[:, rows]
            turns = []
            add_k, add_v = None, None
            for h in range(2):
                mine = (lane // HDIM) == h
                scores = jnp.where(same, tdot(keys[h], q_part), neg_large)
                soft = jnp.exp(scores - lse[2 * g + h, :, rows])
                grad_soft = tdot(values[h], g_part)
                inner = jnp.sum(soft * grad_soft, 0, keepdims=True)
                grad_scores = (soft * (grad_soft - inner)).astype(bf16)
                part_v = mdot(soft.astype(bf16), jnp.where(mine, g_part, bf16(0)))
                part_k = mdot(grad_scores, jnp.where(mine, q_part, bf16(0)))
                add_v = part_v if h == 0 else add_v + part_v
                add_k = part_k if h == 0 else add_k + part_k
                turns.append(mdot(kt[h * HDIM : (h + 1) * HDIM, :], grad_scores))
            dq[rows, :] = jnp.transpose(jnp.concatenate(turns, 0)) * (HDIM**-0.5)
            if i == 0:
                dv[...] = add_v
                dk[...] = add_k
            else:
                dv[...] += add_v
                dk[...] += add_k
            if i % 2:
                runner.advance()
        cos, sin = cosine[...], sine[...]
        for c, grad in ((0, dq), (1, dk)):
            whole = grad[...]
            back = whole * cos - turned(whole) * sin
            grad_proj[:, c * feats + g * 128 : c * feats + (g + 1) * 128] = back.astype(bf16)
        grad_proj[:, 2 * feats + g * 128 : 2 * feats + (g + 1) * 128] = dv[...].astype(bf16)
    for copy in att_copies:
        copy.wait_send()
    far_copies = []
    for i in range(half // block):
        rows = slice(i * block, (i + 1) * block)
        far = grad_proj[half + i * block : half + (i + 1) * block, :]
        far_send[rows, :] = tdot(far, w_qkv[...]).astype(bf16)
        copy = remote(
            far_send.at[rows, :], far_recv.at[rows, :], bsem.at[0, i], bsem.at[1, i],
            here.across("y"),
        )
        copy.start()
        far_copies.append(copy)
    norms_out[...] = jnp.zeros_like(norms_out)
    for i in range(half // block):
        rows = slice(i * block, (i + 1) * block)
        near = residual[rows, :] + tdot(grad_proj[rows, :], w_qkv[...])
        far_copies[i].wait()
        near = near + far_recv[rows, :].astype(f32)
        hat, scale = norm_parts(emb[rows, :].astype(f32))
        grad_hat = near * norm_rows[0:1, :]
        first = jnp.mean(grad_hat, -1, keepdims=True)
        second = jnp.mean(grad_hat * hat, -1, keepdims=True)
        low_out[rows, :] = (scale * (grad_hat - first - hat * second)).astype(bf16)
        norms_out[0:1, :] += jnp.sum(near * hat, 0, keepdims=True)
        norms_out[1:2, :] += jnp.sum(near, 0, keepdims=True)
        runner.advance()
    runner.drain()
    total = square_sum(outs[0][...]) + square_sum(outs[1][...]) + square_sum(outs[2][...])
    squares[...] = jnp.broadcast_to(total, squares.shape)


def blocks_of(grad, n_dp):
    count = n_dp.bit_length() - 1
    rows = grad.shape[0] // (2 * n_dp)
    return grad.reshape((2,) * (count + 1) + (rows, grad.shape[1]))


def backward_pass(low, w_out, query, key, value, lse, cosine, sine, seg_row, seg_col, residual,
                  emb, norm_rows, w_qkv, grads, pieces):
    n_dp = lax.axis_size("dp")
    count = n_dp.bit_length() - 1
    tok, feats = query.shape
    half, width = low.shape
    rows, cols = grads[0][0].shape[0] // (2 * n_dp), grads[0][0].shape[1]
    held, landed, sems = scatter_scratch(count, rows, [True] * 3, pieces)
    flat = [blocks_of(g, n_dp) for pair in grads for g in pair]
    dma = pltpu.SemaphoreType.DMA
    vmem = pltpu.VMEM
    return pl.pallas_call(
        lambda *refs: backward_body(pieces, (len(held), len(landed)), *refs),
        out_shape=[
            sds((tok, 3 * feats), bf16), sds((half, width), bf16), sds((8, width), f32),
            sds((rows, cols), f32), sds((rows, cols), f32), sds((rows, cols), f32),
            sds((8, 128), f32),
        ],
        in_specs=[VM] * 15 + [ANY] * 6,
        out_specs=[VM] * 7,
        scratch_shapes=[
            vmem((128, tok), bf16), vmem((tok, 128), f32), vmem((tok, 128), f32),
            vmem((tok, 128), f32), vmem((tok, feats), bf16), vmem((half, feats), bf16),
            vmem((half, width), bf16), vmem((half, width), bf16),
        ] + held + landed + [dma((2, feats // 128)), dma((2, max(1, half // 256)))] + sems,
        compiler_params=params(4),
        name="backward",
    )(low, w_out[0], w_out[1], query, key, value, lse, cosine, sine, seg_row, seg_col, residual,
      emb, norm_rows, w_qkv, *flat)


def spread_body(room, pieces, sizes, *refs):
    here = Place()
    n = here.n_dp
    grad, pos, heard, norm_grad, squares = refs[:5]
    grads = [(refs[5], None), (refs[6], refs[7])]
    out, norms_out, out_qkv, out_proj, total_out = refs[8:13]
    other, packed, mine, theirs, norms, parts, own_part, gathered = refs[13:21]
    at = 21
    held = refs[at : at + sizes[0]]
    landed = refs[at + sizes[0] : at + sizes[0] + sizes[1]]
    ysem, rsem, csem, nsem, tsem, send, recv, loads = refs[at + sizes[0] + sizes[1] :]
    width = grad.shape[1] // 2
    slots = n * room
    peers = []
    for rt in range(2):
        for rd in range(n):
            for rm in range(2):
                if rt or rd or rm:
                    where = {
                        "tower": here.t + rt * (1 - 2 * here.t),
                        "dp": here.mixed(rd),
                        "mp": here.m + rm * (1 - 2 * here.m),
                    }
                    peers.append(((rt * n + rd) * 2 + rm, where))
    greet([where for _, where in peers])
    theirs_at = pl.ds(pl.multiple_of((1 - here.m) * width, 128), width)
    mine_at = pl.ds(pl.multiple_of(here.m * width, 128), width)
    swapped = remote(grad.at[:, theirs_at], other, ysem.at[0], ysem.at[1], here.across("y"))
    swapped.start()
    runner = make_scatters(
        here, grads, None, pieces, (out_qkv, out_proj), held, landed, send, recv, loads
    )
    runner.advance()
    me = (here.t * n + here.d) * 2 + here.m
    norm_copies = []
    for rel, where in peers:
        copy = remote(norm_grad, norms.at[me], nsem.at[0, rel], nsem.at[1, rel], where)
        copy.start()
        norm_copies.append(copy)
    norms[me] = norm_grad[...]
    runner.advance()
    swapped.wait()
    both = jnp.concatenate([grad[:, mine_at], other[...]], 0)
    copies = []
    for k in list(range(1, n)) + [0]:
        hot = (
            lax.broadcasted_iota(jnp.int32, (room, pos.shape[1]), 0) + k * room == pos[...]
        ).astype(f32)
        packed[k] = mdot(hot.astype(bf16), both).astype(bf16)
        if k:
            copy = remote(
                packed.at[k], mine.at[k], rsem.at[0, k], rsem.at[1, k], {"dp": here.mixed(k)}
            )
        else:
            mine[0] = packed[0]
            copy = remote(mine.at[0], theirs.at[0], csem.at[0, 0], csem.at[1, 0], here.across("t"))
        copy.start()
        copies.append(copy)
    passed = [copies.pop()]
    runner.advance()
    for k in range(1, n):
        copies[k - 1].wait_recv()
        copy = remote(mine.at[k], theirs.at[k], csem.at[0, k], csem.at[1, k], here.across("t"))
        copy.start()
        passed.append(copy)
    runner.advance()
    for copy in copies:
        copy.wait_send()
    for copy in passed:
        copy.wait()
    row_count = out.shape[0]
    block = row_count
    for size in range(512, 255, -8):
        if row_count % size == 0:
            block = size
            break
    gathered[0:slots, :] = mine[...].reshape(slots, width)
    gathered[slots:, :] = theirs[...].reshape(slots, width)
    own_part[...] = jnp.zeros_like(own_part)

    @pl.loop(0, row_count // block)
    def _(i):
        rows = pl.ds(pl.multiple_of(i * block, 8) if block != row_count else 0, block)
        base = lax.broadcasted_iota(jnp.int32, (block, room), 0) + i * block
        hots = []
        for source in range(2):
            for k in range(n):
                hots.append((base == heard[source, k, 0:1, :room]).astype(f32).astype(bf16))
        found = mdot(jnp.concatenate(hots, 1), gathered[...])
        out[rows, :] = found
        own_part[0:1, :] += jnp.sum(found * found, 0, keepdims=True)

    runner.drain()
    for copy in norm_copies:
        copy.wait()
    total = norms[0]
    for j in range(1, 4 * n):
        total = total + norms[j]
    norms_out[...] = total
    local_sq = (
        squares[0:1, 0:1]
        + 0.5 * jnp.sum(own_part[...], 1, keepdims=True)[0:1]
        + square_sum(out_qkv[...])
        + square_sum(out_proj[...])
    )
    parts[me] = jnp.broadcast_to(local_sq, parts.shape[1:])
    copies = []
    for rel, where in peers:
        copy = remote(parts.at[me], parts.at[me], tsem.at[0, rel], tsem.at[1, rel], where)
        copy.start()
        copies.append(copy)
    for copy in copies:
        copy.wait()
    total_out[...] = jnp.sum(parts[...], 0) + square_sum(norms_out[...])


def spread_pass(grad, pos_row, heard, norm_grad, squares, grad_qkv, grad_out, row_count, pieces):
    n_dp = lax.axis_size("dp")
    count = n_dp.bit_length() - 1
    half, width = grad.shape[0], grad.shape[1] // 2
    room = max(32, 2 * half // n_dp)
    rows = grad_qkv.shape[0] // (2 * n_dp)
    held, landed, sems = scatter_scratch(count, rows, [False, True], pieces)
    flat = [blocks_of(g, n_dp) for g in (grad_qkv, grad_out[0], grad_out[1])]
    dma = pltpu.SemaphoreType.DMA
    vmem = pltpu.VMEM
    return pl.pallas_call(
        lambda *refs: spread_body(room, pieces, (len(held), len(landed)), *refs),
        out_shape=[
            sds((row_count, width), f32), sds(norm_grad.shape, f32),
            sds((rows, grad_qkv.shape[1]), f32), sds((rows, grad_out[0].shape[1]), f32),
            sds((8, 128), f32),
        ],
        in_specs=[VM] * 5 + [ANY] * 3,
        out_specs=[VM] * 5,
        scratch_shapes=[
            vmem((half, width), bf16),
            vmem((n_dp, room, width), bf16),
            vmem((n_dp, room, width), bf16),
            vmem((n_dp, room, width), bf16),
            vmem((4 * n_dp,) + norm_grad.shape, f32),
            vmem((4 * n_dp, 8, 128), f32),
            vmem((8, width), f32),
            vmem((2 * n_dp * room, width), bf16),
        ] + held + landed
        + [dma((2,)), dma((2, n_dp)), dma((2, n_dp)), dma((2, 4 * n_dp)), dma((2, 4 * n_dp))] + sems,
        compiler_params=params(5),
        name="spread",
    )(grad, pos_row, heard, norm_grad, squares, *flat)


def loss_body(part, counts, doc_ok, query_ok, target, scale, grad_out, stats, other, low_all, turn,
              psend, precv, esend, erecv):
    here = Place()
    n = here.n_dp
    slots, width = part.shape
    peers = []
    for rt in range(2):
        for rd in range(n):
            if rt or rd:
                peers.append(
                    (rt * n + rd, {"tower": here.t + rt * (1 - 2 * here.t), "dp": here.mixed(rd)})
                )
    greet([where for _, where in peers] + [here.across("y")])
    copy = remote(part, other, psend, precv, here.across("y"))
    copy.start()
    copy.wait()
    pooled = (part[...] + other[...]) / counts[...]
    scale_row = lax.rsqrt(jnp.sum(pooled * pooled, 1, keepdims=True) + 1e-06)
    unit = pooled * scale_row
    low_all[here.t, here.d] = unit.astype(bf16)
    copies = []
    for rel, where in peers:
        copy = remote(
            low_all.at[here.t, here.d], low_all.at[here.t, here.d], esend.at[rel], erecv.at[rel], where
        )
        copy.start()
        copies.append(copy)
    for copy in copies:
        copy.wait()
    total = n * slots
    queries = low_all[0].reshape(total, width)
    documents = low_all[1].reshape(total, width)
    cosines = tdot(queries, documents)
    factor = jnp.exp(jnp.minimum(scale[...], cap_value))
    logits = jnp.where(doc_ok[...] > 0, factor * cosines, neg_large)
    peak = jnp.max(logits, 1, keepdims=True)
    log_total = peak + jnp.log(jnp.sum(jnp.exp(logits - peak), 1, keepdims=True))
    soft = jnp.exp(logits - log_total)
    mask = lax.broadcasted_iota(jnp.int32, (total, total), 1) == target[...]
    picked = jnp.sum(jnp.where(mask, logits, 0.0), 1, keepdims=True)
    valid = query_ok[...] > 0
    query_count = jnp.sum(valid.astype(f32), axis=0, keepdims=True)
    loss_sum = jnp.sum(jnp.where(valid, log_total - picked, 0.0), axis=0, keepdims=True)
    grad_logits = jnp.where(valid, soft - mask.astype(f32), 0.0) / query_count
    by_row = jnp.sum(grad_logits * cosines, 1, keepdims=True)
    grad_scale = (
        jnp.sum(by_row, 0, keepdims=True) * factor * (scale[...] < cap_value).astype(f32)
    )
    grad_cos = factor * grad_logits
    at = pl.ds(pl.multiple_of(here.d * slots, slots), slots)
    turn[0] = grad_cos
    turn[1] = jnp.transpose(grad_cos)
    left = turn[here.t, at, :].astype(bf16)
    right = low_all[1 - here.t].reshape(total, width)
    grad_unit = mdot(left, right)
    grad_pooled = scale_row * (
        grad_unit - unit * jnp.sum(unit * grad_unit, 1, keepdims=True)
    )
    grad_out[...] = grad_pooled / counts[...]
    row = lax.broadcasted_iota(jnp.int32, stats.shape, 0)
    stats[...] = jnp.where(row == 0, loss_sum, jnp.where(row == 1, query_count, grad_scale))


def loss_step(part, counts, doc_ok, query_ok, target, scale):
    n_dp = lax.axis_size("dp")
    slots, width = part.shape
    total = n_dp * slots
    dma = pltpu.SemaphoreType.DMA
    return pl.pallas_call(
        loss_body,
        out_shape=[sds(part.shape, f32), sds((8, 128), f32)],
        in_specs=[VM] * 6,
        out_specs=[VM] * 2,
        scratch_shapes=[
            pltpu.VMEM(part.shape, f32),
            pltpu.VMEM((2, n_dp, slots, width), bf16),
            pltpu.VMEM((2, total, total), f32),
            dma, dma, dma((2 * n_dp,)), dma((2 * n_dp,)),
        ],
        compiler_params=params(3),
        name="loss",
    )(part, counts, doc_ok, query_ok, target, scale)


def rotary_tables(positions):
    half_dim = HDIM // 2
    inverse = 1000.0 ** (-2.0 * jnp.arange(half_dim, dtype=f32) / HDIM)
    angles = positions.astype(f32)[:, None] * inverse[None, :]
    angles = jnp.concatenate([angles] * 4, 1)
    return jnp.cos(angles), jnp.sin(angles)


def layout(lengths, places, slot_count):
    end_points = jnp.cumsum(lengths)
    segment = jnp.sum((places[:, None] >= end_points[None, :]).astype(jnp.int32), 1)
    starts = jnp.concatenate([jnp.zeros((1,), jnp.int32), end_points])
    slot_ids = jnp.arange(slot_count + 1, dtype=jnp.int32)
    segment_start = jnp.sum(jnp.where(segment[:, None] == slot_ids[None, :], starts[None, :], 0), 1)
    return segment, places - segment_start


def norm_back(grad, hat, scale, gain):
    grad_hat = grad * gain
    first = jnp.mean(grad_hat, -1, keepdims=True)
    second = jnp.mean(grad_hat * hat, -1, keepdims=True)
    return (
        scale * (grad_hat - first - hat * second),
        jnp.sum(grad * hat, 0),
        jnp.sum(grad, 0),
    )


def glu(gate_vals, up_vals):
    return jax.nn.silu(gate_vals) * up_vals


def adamw(weight_in, gradient, first_mom, second, factor, step_num, rate):
    gradient = gradient * factor
    first_new = beta_one * first_mom + (1.0 - beta_one) * gradient
    second_new = beta_two * second + (1.0 - beta_two) * gradient * gradient
    first_hat = first_new / (1.0 - beta_one**step_num)
    second_hat = second_new / (1.0 - beta_two**step_num)
    weight_new = weight_in - rate * (
        first_hat / (jnp.sqrt(second_hat) + adam_eps) + decay_rate * weight_in
    )
    return (weight_new, first_new, second_new)


def name_rows(ids, d, n_dp, row_count, room):
    tok = ids.shape[0]
    owner = ids // row_count
    local = ids - owner * row_count
    order = jnp.bitwise_xor(owner, d)
    places = jnp.arange(tok, dtype=jnp.int32)
    first_at = jnp.min(
        jnp.where(ids[:, None] == ids[None, :], places[None, :], tok), 1
    )
    is_first = first_at == places
    slot = jnp.sum(
        (
            (places[None, :] < first_at[:, None])
            & is_first[None, :]
            & (owner[None, :] == owner[:, None])
        ).astype(jnp.int32),
        1,
    )
    over = jnp.max(slot) >= room
    pos = order * room + slot
    wanted = jnp.arange(n_dp * room, dtype=jnp.int32)
    listed = jnp.max(
        jnp.where((pos[None, :] == wanted[:, None]) & is_first[None, :], local[None, :], -1), 1
    ).reshape(n_dp, 1, room)
    listed = jnp.pad(listed, ((0, 0), (0, 0), (0, 128 - room)), constant_values=-1)
    flag = jnp.broadcast_to(over.astype(jnp.int32), (n_dp, 7, 128))
    return pos, jnp.concatenate([listed, flag], 1)


def layer_norm(stream, gain_row, bias_row):
    average = jnp.mean(stream, -1, keepdims=True)
    centered = stream - average
    variance = jnp.mean(centered * centered, -1, keepdims=True)
    return centered * lax.rsqrt(variance + norm_eps) * gain_row + bias_row


def rotate(values, cosine, sine_table):
    half_dim = values.shape[-1] // 2
    turned = jnp.concatenate([-values[..., half_dim:], values[..., :half_dim]], -1)
    return values * cosine + turned * sine_table


def plain_rotary_tables(positions, head_dim):
    half_dim = head_dim // 2
    inverse = 1000.0 ** (-2.0 * jnp.arange(half_dim, dtype=jnp.float32) / head_dim)
    angles = positions.astype(jnp.float32)[:, None] * inverse[None, :]
    angles = jnp.concatenate([angles, angles], 1)[:, None, :]
    return (jnp.cos(angles), jnp.sin(angles))


def plain_layout(lengths, tok_count, slot_count):
    end_points = jnp.cumsum(lengths)
    places = jnp.arange(tok_count, dtype=jnp.int32)
    segment = jnp.sum((places[:, None] >= end_points[None, :]).astype(jnp.int32), 1)
    starts = jnp.concatenate([jnp.zeros((1,), jnp.int32), end_points])
    slot_ids = jnp.arange(slot_count + 1, dtype=jnp.int32)
    segment_start = jnp.sum(jnp.where(segment[:, None] == slot_ids[None, :], starts[None, :], 0), 1)
    return (segment, places - segment_start)


def plain_glu(gate_vals, up_vals):
    return jax.nn.silu(gate_vals) * up_vals


def pool_rows(stream_two, member, counts):
    pooled = jnp.dot(member, stream_two, precision=highest) / counts[:, None]
    return pooled * lax.rsqrt(jnp.sum(pooled * pooled, 1, keepdims=True) + 1e-06)


def model_total(values):
    return lax.psum(values.astype(jnp.bfloat16), "mp").astype(jnp.float32)


def block_scores(query_block, seg_block, key_low, segment, factor):
    scores = (
        jnp.einsum("thd,shd->hts", query_block, key_low, preferred_element_type=jnp.float32)
        * factor
    )
    return jnp.where((seg_block[:, None] == segment[None, :])[None], scores, neg_large)


def attention(query_low, key_low, value_low, segment):
    tok_count, heads_local, head_dim = query_low.shape
    block_rows = min(512, tok_count)
    block_count = tok_count // block_rows
    factor = head_dim ** (-0.5)
    query_blocks = query_low.reshape(block_count, block_rows, heads_local, head_dim)
    seg_blocks = segment.reshape(block_count, block_rows)

    def one_block(operands):
        scores = block_scores(operands[0], operands[1], key_low, segment, factor)
        row_peak = jnp.max(scores, 2, keepdims=True)
        row_total = jnp.sum(jnp.exp(scores - row_peak), 2, keepdims=True)
        log_total = row_peak + jnp.log(row_total)
        soft_rows = jnp.exp(scores - log_total)
        attended = jnp.einsum(
            "hts,shd->thd",
            soft_rows.astype(jnp.bfloat16),
            value_low,
            preferred_element_type=jnp.float32,
        )
        return (attended, log_total[..., 0])

    attended, log_total = lax.map(one_block, (query_blocks, seg_blocks))
    return (attended.reshape(tok_count, heads_local * head_dim), log_total)


def attention_back(query_low, key_low, value_low, grad_attended, log_total, segment):
    tok_count, heads_local, head_dim = query_low.shape
    block_rows = min(512, tok_count)
    block_count = tok_count // block_rows
    factor = head_dim ** (-0.5)
    query_blocks = query_low.reshape(block_count, block_rows, heads_local, head_dim)
    grad_blocks = grad_attended.reshape(block_count, block_rows, heads_local, head_dim)
    seg_blocks = segment.reshape(block_count, block_rows)

    def one_block(running, operands):
        query_block, grad_block, seg_block, lse_block = operands
        scores = block_scores(query_block, seg_block, key_low, segment, factor)
        soft_rows = jnp.exp(scores - lse_block[..., None])
        grad_soft = jnp.einsum(
            "thd,shd->hts", grad_block, value_low, preferred_element_type=jnp.float32
        )
        inner = jnp.sum(soft_rows * grad_soft, 2, keepdims=True)
        grad_scores = (soft_rows * (grad_soft - inner)).astype(jnp.bfloat16)
        grad_query = (
            jnp.einsum("hts,shd->thd", grad_scores, key_low, preferred_element_type=jnp.float32)
            * factor
        )
        grad_key = (
            running[0]
            + jnp.einsum(
                "hts,thd->shd", grad_scores, query_block, preferred_element_type=jnp.float32
            )
            * factor
        )
        grad_value = running[1] + jnp.einsum(
            "hts,thd->shd",
            soft_rows.astype(jnp.bfloat16),
            grad_block,
            preferred_element_type=jnp.float32,
        )
        return ((grad_key, grad_value), grad_query)

    zeros_kv = jnp.zeros(key_low.shape, jnp.float32)
    (grad_key, grad_value), grad_query = lax.scan(
        one_block, (zeros_kv, zeros_kv), (query_blocks, grad_blocks, seg_blocks, log_total)
    )
    return (grad_query.reshape(tok_count, heads_local, head_dim), grad_key, grad_value)


def layer_forward(embed_rows, segment, positions, weights, norm_rows):
    w_qkv, w_out, w_ffn, w_down = weights
    tok_count = embed_rows.shape[0]
    heads_local = w_qkv.shape[2] // HDIM
    stream_zero = layer_norm(embed_rows, norm_rows[0], norm_rows[1])
    input_zero = stream_zero.astype(jnp.bfloat16)
    projected = jnp.einsum("td,dcf->tcf", input_zero, w_qkv, preferred_element_type=jnp.float32)
    heads_view = projected.reshape(tok_count, 3, heads_local, HDIM)
    cosine, sine_table = plain_rotary_tables(positions, HDIM)
    query_low = rotate(heads_view[:, 0], cosine, sine_table).astype(jnp.bfloat16)
    key_low = rotate(heads_view[:, 1], cosine, sine_table).astype(jnp.bfloat16)
    value_low = heads_view[:, 2].astype(jnp.bfloat16)
    attended, log_total = attention(query_low, key_low, value_low, segment)
    attended_low = attended.astype(jnp.bfloat16)
    attn_branch = model_total(
        jnp.einsum("tf,df->td", attended_low, w_out, preferred_element_type=jnp.float32)
    )
    sum_one = stream_zero + attn_branch
    stream_one = layer_norm(sum_one, norm_rows[2], norm_rows[3])
    input_one = stream_one.astype(jnp.bfloat16)
    gate_up = jnp.einsum("td,dcf->tcf", input_one, w_ffn, preferred_element_type=jnp.float32)
    hidden_low = plain_glu(gate_up[:, 0], gate_up[:, 1]).astype(jnp.bfloat16)
    ffn_branch = model_total(
        jnp.einsum("tf,df->td", hidden_low, w_down, preferred_element_type=jnp.float32)
    )
    sum_two = stream_one + ffn_branch
    stream_two = layer_norm(sum_two, norm_rows[4], norm_rows[5])
    kept_vals = (
        embed_rows,
        sum_one,
        sum_two,
        input_zero,
        input_one,
        query_low,
        key_low,
        value_low,
        log_total,
        attended_low,
        gate_up,
        hidden_low,
    )
    return (stream_two, kept_vals)


def layer_backward(grad_two, kept_vals, weights, norm_rows, segment, positions):
    w_qkv, w_out, w_ffn, w_down = weights
    (
        embed_rows,
        sum_one,
        sum_two,
        input_zero,
        input_one,
        query_low,
        key_low,
        value_low,
        log_total,
        attended_low,
        gate_up,
        hidden_low,
    ) = kept_vals
    tok_count, heads_local, head_dim = query_low.shape
    grad_sum_two, gain_two, bias_two = jax.vjp(layer_norm, sum_two, norm_rows[4], norm_rows[5])[1](
        grad_two
    )
    ffn_low = grad_sum_two.astype(jnp.bfloat16)
    grad_down = jnp.einsum("td,tf->df", ffn_low, hidden_low, preferred_element_type=jnp.float32)
    grad_hidden = jnp.einsum("td,df->tf", ffn_low, w_down, preferred_element_type=jnp.float32)
    grad_gate, grad_up = jax.vjp(plain_glu, gate_up[:, 0], gate_up[:, 1])[1](grad_hidden)
    gate_grads = jnp.stack([grad_gate, grad_up], 1).astype(jnp.bfloat16)
    grad_ffn = jnp.einsum("td,tcf->dcf", input_one, gate_grads, preferred_element_type=jnp.float32)
    grad_stream_one = grad_sum_two + model_total(
        jnp.einsum("tcf,dcf->td", gate_grads, w_ffn, preferred_element_type=jnp.float32)
    )
    grad_sum_one, gain_one, bias_one = jax.vjp(layer_norm, sum_one, norm_rows[2], norm_rows[3])[1](
        grad_stream_one
    )
    attn_low = grad_sum_one.astype(jnp.bfloat16)
    grad_out = jnp.einsum("td,tf->df", attn_low, attended_low, preferred_element_type=jnp.float32)
    grad_attended = jnp.einsum(
        "td,df->tf", attn_low, w_out, preferred_element_type=jnp.float32
    ).astype(jnp.bfloat16)
    grad_query, grad_key, grad_value = attention_back(
        query_low,
        key_low,
        value_low,
        grad_attended.reshape(tok_count, heads_local, head_dim),
        log_total,
        segment,
    )
    cosine, sine_table = plain_rotary_tables(positions, head_dim)
    turn_back = jax.vjp(lambda values: rotate(values, cosine, sine_table), grad_query)[1]
    grad_projected = jnp.stack([turn_back(grad_query)[0], turn_back(grad_key)[0], grad_value], 1)
    grad_projected = grad_projected.reshape(tok_count, 3, heads_local * head_dim).astype(
        jnp.bfloat16
    )
    grad_qkv = jnp.einsum(
        "td,tcf->dcf", input_zero, grad_projected, preferred_element_type=jnp.float32
    )
    grad_stream_zero = grad_sum_one + model_total(
        jnp.einsum("tcf,dcf->td", grad_projected, w_qkv, preferred_element_type=jnp.float32)
    )
    grad_embed, gain_zero, bias_zero = jax.vjp(layer_norm, embed_rows, norm_rows[0], norm_rows[1])[
        1
    ](grad_stream_zero)
    norm_grads = jnp.stack([gain_zero, bias_zero, gain_one, bias_one, gain_two, bias_two])
    return (grad_embed, (grad_qkv, grad_out, grad_ffn, grad_down), norm_grads)


def plain_adamw(weight_in, gradient, first_mom, second, factor, step_num, rate):
    gradient = gradient * factor
    first_new = beta_one * first_mom + (1.0 - beta_one) * gradient
    second_new = beta_two * second + (1.0 - beta_two) * gradient * gradient
    first_hat = first_new / (1.0 - beta_one**step_num)
    second_hat = second_new / (1.0 - beta_two**step_num)
    weight_new = weight_in - rate * (
        first_hat / (jnp.sqrt(second_hat) + adam_eps) + decay_rate * weight_in
    )
    return (weight_new, first_new, second_new)


def plain_step(
    token_ids,
    seq_lengths,
    positives,
    embedding,
    attn_in,
    attn_out,
    ffn_in,
    ffn_out,
    norm_params,
    logit_scale,
    embed_m,
    embed_v,
    attn_in_m,
    attn_in_v,
    attn_out_m,
    attn_out_v,
    ffn_in_m,
    ffn_in_v,
    ffn_out_m,
    ffn_out_v,
    norm_m,
    norm_v,
    scale_m,
    scale_v,
):
    n_data = lax.axis_size("dp")
    tower_idx = lax.axis_index("tower")
    data_idx = lax.axis_index("dp")
    model_idx = lax.axis_index("mp")
    slot_count = seq_lengths.shape[2]
    token_list = token_ids[0]
    tok_count = token_list.shape[0]
    model_width = norm_params.shape[1]
    local_width = embedding.shape[1]
    row_count = embedding.shape[0]
    weights = (
        lax.all_gather(attn_in.astype(jnp.bfloat16), ("tower", "dp"), axis=0, tiled=True),
        lax.all_gather(attn_out.astype(jnp.bfloat16), ("tower", "dp"), axis=0, tiled=True),
        lax.all_gather(ffn_in.astype(jnp.bfloat16), ("tower", "dp"), axis=0, tiled=True),
        lax.all_gather(ffn_out.astype(jnp.bfloat16), ("tower", "dp"), axis=0, tiled=True),
    )
    shard_piece = lax.all_gather(embedding.astype(jnp.bfloat16), "dp", axis=0, tiled=True)
    inside = (token_list >= 0) & (token_list < shard_piece.shape[0])
    picked = jnp.take(shard_piece, jnp.clip(token_list, 0, shard_piece.shape[0] - 1), axis=0)
    looked = jnp.where(inside[:, None], picked.astype(jnp.float32), 0.0)
    embed_rows = lax.all_gather(looked.astype(jnp.bfloat16), "mp", axis=1, tiled=True).astype(
        jnp.float32
    )
    lengths_row = seq_lengths[tower_idx, data_idx]
    segment, positions = plain_layout(lengths_row, tok_count, slot_count)
    stream_two, kept_vals = layer_forward(embed_rows, segment, positions, weights, norm_params)
    member = (segment[None, :] == jnp.arange(slot_count, dtype=jnp.int32)[:, None]).astype(
        jnp.float32
    )
    counts = jnp.maximum(lengths_row, 1).astype(jnp.float32)
    own_embeds, pool_back = jax.vjp(lambda stream: pool_rows(stream, member, counts), stream_two)
    all_embeds = lax.all_gather(
        own_embeds.astype(jnp.bfloat16), ("tower", "dp"), axis=0, tiled=True
    )
    query_total = n_data * slot_count
    rows_per = slot_count // 2
    first_row = (tower_idx * n_data + data_idx) * rows_per
    query_rows = lax.dynamic_slice_in_dim(all_embeds, first_row, rows_per, 0)
    documents = all_embeds[query_total:]
    cosines = jnp.einsum("qd,kd->qk", query_rows, documents, preferred_element_type=jnp.float32)
    logit_factor = jnp.exp(jnp.minimum(logit_scale[0], cap_value))
    doc_ok = seq_lengths[1].reshape(-1) > 0
    query_ok_all = seq_lengths[0].reshape(-1) > 0
    query_count = jnp.sum(query_ok_all.astype(jnp.float32))
    query_ok = lax.dynamic_slice_in_dim(query_ok_all, first_row, rows_per, 0)
    logits = jnp.where(doc_ok[None, :], logit_factor * cosines, neg_large)
    row_peak = jnp.max(logits, 1, keepdims=True)
    log_total = row_peak + jnp.log(jnp.sum(jnp.exp(logits - row_peak), 1, keepdims=True))
    soft_rows = jnp.exp(logits - log_total)
    targets = lax.dynamic_slice_in_dim(positives.reshape(-1), first_row, rows_per, 0)
    target_mask = jnp.arange(query_total, dtype=jnp.int32)[None, :] == targets[:, None]
    picked = jnp.sum(jnp.where(target_mask, logits, 0.0), 1)
    loss_part = jnp.sum(jnp.where(query_ok, log_total[:, 0] - picked, 0.0))
    grad_logits = (
        jnp.where(query_ok[:, None], soft_rows - target_mask.astype(jnp.float32), 0.0) / query_count
    )
    scale_part = (
        jnp.sum(grad_logits * cosines)
        * logit_factor
        * (logit_scale[0] < cap_value).astype(jnp.float32)
    )
    grad_cos = (logit_factor * grad_logits).astype(jnp.bfloat16)
    grad_queries = jnp.einsum("qk,kd->qd", grad_cos, documents, preferred_element_type=jnp.float32)
    grad_documents = jnp.einsum(
        "qk,qd->kd", grad_cos, query_rows, preferred_element_type=jnp.float32
    )
    grad_term = jnp.concatenate(
        [jnp.zeros((query_total, model_width), jnp.float32), grad_documents], 0
    )
    grad_term = lax.dynamic_update_slice_in_dim(grad_term, grad_queries, first_row, 0)
    own_grad = lax.psum_scatter(grad_term, ("tower", "dp"), scatter_dimension=0, tiled=True)
    grad_two = pool_back(own_grad)[0]
    grad_embed, layer_grads, norm_grads = layer_backward(
        grad_two, kept_vals, weights, norm_params, segment, positions
    )
    embed_low = grad_embed.astype(jnp.bfloat16)
    column_part = lax.dynamic_slice_in_dim(embed_low, model_idx * local_width, local_width, 1)
    row_start = data_idx * row_count
    all_ids = lax.all_gather(token_list, ("tower", "dp"), axis=0, tiled=True)
    piece_ids = all_ids - row_start
    inside = (piece_ids >= 0) & (piece_ids < row_count)
    slot_ids = jnp.where(inside, piece_ids, row_count)
    embed_grad = jax.ops.segment_sum(
        lax.all_gather(column_part, ("tower", "dp"), axis=0, tiled=True).astype(jnp.float32),
        slot_ids,
        num_segments=row_count + 1,
    )[:row_count]
    shard_grads = (
        lax.psum_scatter(layer_grads[0], ("tower", "dp"), scatter_dimension=0, tiled=True),
        lax.psum_scatter(layer_grads[1], ("tower", "dp"), scatter_dimension=0, tiled=True),
        lax.psum_scatter(layer_grads[2], ("tower", "dp"), scatter_dimension=0, tiled=True),
        lax.psum_scatter(layer_grads[3], ("tower", "dp"), scatter_dimension=0, tiled=True),
    )
    norm_grad, loss_sum, scale_grad = lax.psum((norm_grads, loss_part, scale_part), ("tower", "dp"))
    local_sq = sum((jnp.sum(gradient * gradient) for gradient in shard_grads)) + 0.5 * jnp.sum(
        embed_grad * embed_grad
    )
    total_sq = (
        lax.psum(local_sq, ("tower", "dp", "mp"))
        + jnp.sum(norm_grad * norm_grad)
        + scale_grad * scale_grad
    )
    grad_norm = jnp.sqrt(total_sq)
    factor = jnp.minimum(1.0, clip_max / (grad_norm + 1e-06))
    step_num = float(STEP)
    embed_new = plain_adamw(embedding, embed_grad, embed_m, embed_v, factor, step_num, learn_rate)
    qkv_new = plain_adamw(attn_in, shard_grads[0], attn_in_m, attn_in_v, factor, step_num, learn_rate)
    out_new = plain_adamw(attn_out, shard_grads[1], attn_out_m, attn_out_v, factor, step_num, out_rate)
    ffn_new = plain_adamw(ffn_in, shard_grads[2], ffn_in_m, ffn_in_v, factor, step_num, learn_rate)
    down_new = plain_adamw(ffn_out, shard_grads[3], ffn_out_m, ffn_out_v, factor, step_num, learn_rate)
    norms_new = plain_adamw(norm_params, norm_grad, norm_m, norm_v, factor, step_num, norm_rate)
    scale_new = plain_adamw(
        logit_scale, scale_grad.reshape(1), scale_m, scale_v, factor, step_num, learn_rate
    )
    return (
        embed_new[0],
        embed_new[1],
        embed_new[2],
        qkv_new[0],
        qkv_new[1],
        qkv_new[2],
        out_new[0],
        out_new[1],
        out_new[2],
        ffn_new[0],
        ffn_new[1],
        ffn_new[2],
        down_new[0],
        down_new[1],
        down_new[2],
        norms_new[0],
        norms_new[1],
        norms_new[2],
        scale_new[0],
        scale_new[1],
        scale_new[2],
        loss_sum.reshape(1),
        query_count.reshape(1),
        grad_norm.reshape(1),
    )


def lean_step(args, pos, heard):
    (
        token_ids, seq_lengths, positives, embedding, attn_in, attn_out, ffn_in, ffn_out,
        norm_params, logit_scale, embed_m, embed_v, attn_in_m, attn_in_v, attn_out_m, attn_out_v,
        ffn_in_m, ffn_in_v, ffn_out_m, ffn_out_v, norm_m, norm_v, scale_m, scale_v,
    ) = args
    tower_idx = lax.axis_index("tower")
    data_idx = lax.axis_index("dp")
    model_idx = lax.axis_index("mp")
    slot_count = seq_lengths.shape[2]
    tok = token_ids.shape[1]
    half = tok // 2
    row_count = embedding.shape[0]
    feats = attn_out.shape[1]
    ff = ffn_out.shape[1]
    part_ff = ff // 2

    shards = (
        attn_in.reshape(attn_in.shape[0], -1), attn_out, ffn_in[:, 0], ffn_in[:, 1], ffn_out,
    )
    kinds = ("plain", "late", "late", "late", "late")
    gather_pieces = [(0, "plain", 0, 3 * feats, 0), (1, "late", 0, feats, 1)]
    for turn, which in enumerate((2, 3, 4)):
        gather_pieces.append((which, "late", 0, part_ff, 1 + turn))
        gather_pieces.append((which, "early", part_ff, part_ff, 1 + turn))
    places = (jnp.arange(tok, dtype=jnp.int32) + model_idx * half) % tok
    pos_rel = jnp.where(model_idx == 0, pos, jnp.concatenate([pos[half:], pos[:half]]))
    lengths_row = seq_lengths[tower_idx, data_idx]
    segment, positions = layout(lengths_row, places, slot_count)
    cosine, sine = rotary_tables(positions)
    seg_row, seg_col = segment[None, :], segment[:, None]
    kept, weights = forward_pass(
        embedding, heard[0], pos_rel[:, None], norm_params[0:2], cosine, sine, seg_row, seg_col,
        shards, kinds, gather_pieces,
    )
    emb, stream_zero, input_zero, query, key, value, lse = kept[:7]
    att = kept[7:9]
    w_qkv, w_out, w_gate, w_up, w_down = weights

    sum_one = stream_zero + tdot(att[0], w_out[0]) + tdot(att[1], w_out[1])
    hat_one, scale_one = norm_parts(sum_one)
    stream_one = hat_one * norm_params[2] + norm_params[3]
    input_one = stream_one.astype(bf16)
    gates = [mdot(input_one, w_gate[j]) for j in range(2)]
    ups = [mdot(input_one, w_up[j]) for j in range(2)]
    hidden = [glu(gates[j], ups[j]).astype(bf16) for j in range(2)]
    sum_two = stream_one + tdot(hidden[0], w_down[0]) + tdot(hidden[1], w_down[1])
    hat_two, scale_two = norm_parts(sum_two)
    stream_two = hat_two * norm_params[4] + norm_params[5]

    member = (segment[None, :half] == jnp.arange(slot_count, dtype=jnp.int32)[:, None]).astype(f32)
    counts = jnp.maximum(lengths_row, 1).astype(f32)[:, None]
    part = jnp.dot(member, stream_two, precision=highest)
    doc_ok = (seq_lengths[1].reshape(1, -1) > 0).astype(f32)
    query_ok = (seq_lengths[0].reshape(-1, 1) > 0).astype(f32)
    grad_pool, stats = loss_step(
        part, counts, doc_ok, query_ok, positives.reshape(-1, 1), logit_scale.reshape(1, 1)
    )
    loss_sum, query_count, scale_grad = stats[0, 0], stats[1, 0], stats[2, 0]

    grad_two = jnp.dot(member.T, grad_pool, precision=highest)
    grad_sum_two, gain_two, bias_two = norm_back(grad_two, hat_two, scale_two, norm_params[4])
    ffn_low = grad_sum_two.astype(bf16)

    def weight_grad(left, right):
        return jnp.einsum("td,tf->df", left, right, preferred_element_type=f32).astype(bf16)

    grad_down, grad_gate, grad_up = [], [], []
    grad_stream_one = grad_sum_two
    for j in range(2):
        grad_down.append(weight_grad(ffn_low, hidden[j]))
        grad_hidden = mdot(ffn_low, w_down[j])
        d_gate, d_up = jax.vjp(glu, gates[j], ups[j])[1](grad_hidden)
        d_gate, d_up = d_gate.astype(bf16), d_up.astype(bf16)
        grad_gate.append(weight_grad(input_one, d_gate))
        grad_up.append(weight_grad(input_one, d_up))
        grad_stream_one = grad_stream_one + tdot(d_gate, w_gate[j]) + tdot(d_up, w_up[j])
    grad_sum_one, gain_one, bias_one = norm_back(
        grad_stream_one, hat_one, scale_one, norm_params[2]
    )
    attn_low = grad_sum_one.astype(bf16)
    grad_out = [weight_grad(attn_low, att[j]) for j in range(2)]
    pieces = []
    for turn, which in enumerate((2, 0, 1)):
        pieces.append((which, "early", 0, part_ff, turn))
        pieces.append((which, "late", part_ff, part_ff, turn))
    grad_proj, embed_low, zero_norms, r_gate, r_up, r_down, squares = backward_pass(
        attn_low, w_out, query, key, value, lse, cosine, sine, seg_row, seg_col, grad_sum_one,
        emb, norm_params[0:2], w_qkv, (grad_gate, grad_up, grad_down), pieces,
    )
    grad_qkv = weight_grad(input_zero, grad_proj)
    norm_part = jnp.concatenate(
        [zero_norms[0:2], jnp.stack([gain_one, bias_one, gain_two, bias_two]), zero_norms[2:4]]
    )
    pieces = [(0, "plain", 0, 2 * feats, 0), (0, "plain", 2 * feats, feats, 1), (1, "late", 0, feats, 1)]
    embed_grad, norm_sum, r_qkv, r_out, total = spread_pass(
        embed_low, pos_rel[None, :], heard, norm_part, squares, grad_qkv, grad_out, row_count,
        pieces,
    )
    norm_grad = norm_sum[:6]
    r_qkv = r_qkv.reshape(attn_in.shape)
    total_sq = total[0, 0] + scale_grad * scale_grad
    grad_norm = jnp.sqrt(total_sq)
    factor = jnp.minimum(1.0, clip_max / (grad_norm + 1e-06))
    step_num = float(STEP)
    embed_new = adamw(embedding, embed_grad, embed_m, embed_v, factor, step_num, learn_rate)
    qkv_new = adamw(attn_in, r_qkv, attn_in_m, attn_in_v, factor, step_num, learn_rate)
    out_new = adamw(attn_out, r_out, attn_out_m, attn_out_v, factor, step_num, out_rate)
    r_ffn = jnp.stack([r_gate, r_up], 1)
    ffn_new = adamw(ffn_in, r_ffn, ffn_in_m, ffn_in_v, factor, step_num, learn_rate)
    down_new = adamw(ffn_out, r_down, ffn_out_m, ffn_out_v, factor, step_num, learn_rate)
    norms_new = adamw(norm_params, norm_grad, norm_m, norm_v, factor, step_num, norm_rate)
    scale_new = adamw(
        logit_scale, scale_grad.reshape(1), scale_m, scale_v, factor, step_num, learn_rate
    )
    return (
        *embed_new, *qkv_new, *out_new, *ffn_new, *down_new, *norms_new, *scale_new,
        loss_sum.reshape(1), query_count.reshape(1), grad_norm.reshape(1),
    )


def local(*args):
    token_ids, embedding = args[0], args[3]
    n_dp = lax.axis_size("dp")
    room = max(32, token_ids.shape[1] // n_dp)
    pos, lists = name_rows(
        token_ids[0], lax.axis_index("dp"), n_dp, embedding.shape[0], room
    )
    heard, flag = exchange_lists(lists)
    return lax.cond(
        flag[1, 0] > 0,
        lambda values: plain_step(*values),
        lambda values: lean_step(values, pos, heard),
        args,
    )


def solution(mesh):
    table, rows3, rows2 = P("dp", "mp"), P(("tower", "dp"), None, "mp"), P(("tower", "dp"), "mp")
    weights = (table, rows3, rows2, rows3, rows2)
    moments = tuple(spec for spec in weights for _ in range(2))
    return jax.shard_map(
        local,
        mesh=mesh,
        in_specs=(P("tower", "dp"), P(), P()) + weights + (P(), P()) + moments + (P(),) * 4,
        out_specs=tuple(spec for spec in weights for _ in range(3)) + (P(),) * 9,
        check_vma=False,
    )
```

```python
import jax
import jax.numpy as jnp
from jax import lax
from jax.sharding import PartitionSpec as P
from jax.experimental import pallas as pl
from jax.experimental.pallas import tpu as pltpu

HDIM = 64
STEP = 5

norm_eps = 1e-06
cap_value = 3.4
clip_max = 0.01
beta_one = 0.9
beta_two = 0.999
learn_rate = 0.02
out_rate = 0.05
norm_rate = 0.3
decay_rate = 0.01
adam_eps = 1e-08
neg_large = -1e30
highest = lax.Precision.HIGHEST
f32 = jnp.float32
bf16 = jnp.bfloat16
MESH = pl.DeviceIdType.MESH
ANY = pl.BlockSpec(memory_space=pl.ANY)
VM = pl.BlockSpec(memory_space=pltpu.VMEM)


def sds(shape, dtype):
    return jax.ShapeDtypeStruct(shape, dtype)


def params(ident, limit=58):
    return pltpu.CompilerParams(
        collective_id=ident, has_side_effects=True, vmem_limit_bytes=limit << 20
    )


class Place:
    def __init__(self):
        self.n_dp = lax.axis_size("dp")
        self.count = self.n_dp.bit_length() - 1
        self.t = lax.axis_index("tower")
        self.d = lax.axis_index("dp")
        self.m = lax.axis_index("mp")
        self.bits = [(self.d // (1 << (self.count - 1 - j))) % 2 for j in range(self.count)]

    def across(self, dim):
        if dim == "t":
            return {"tower": 1 - self.t}
        if dim == "y":
            return {"mp": 1 - self.m}
        step = 1 << (self.count - 1 - dim)
        return {"dp": self.d + (1 - 2 * self.bits[dim]) * step}

    def mixed(self, rel):
        out = self.d
        for j in range(self.count):
            step = 1 << (self.count - 1 - j)
            if rel & step:
                out = out + (1 - 2 * self.bits[j]) * step
        return out


def remote(src, dst, send, recv, where):
    return pltpu.make_async_remote_copy(
        src_ref=src, dst_ref=dst, send_sem=send, recv_sem=recv, device_id=where, device_id_type=MESH
    )


def greet(peers):
    barrier = pltpu.get_barrier_semaphore()
    for where in peers:
        pl.semaphore_signal(barrier, inc=1, device_id=where, device_id_type=MESH)
    pl.semaphore_wait(barrier, len(peers))


def tdot(lhs, rhs):
    return lax.dot_general(lhs, rhs, (((1,), (1,)), ((), ())), preferred_element_type=f32)


def mdot(lhs, rhs):
    return jnp.dot(lhs, rhs, preferred_element_type=f32)


def every(ndim, cols):
    return (slice(None),) * (ndim - 1) + (cols,)


class Gather:
    def __init__(self, here, shard, full, other, order, cols, send, recv, local_sem):
        self.here, self.shard, self.full, self.other = here, shard, full, other
        self.order, self.cols, self.send, self.recv = order, cols, send, recv
        self.local_sem = local_sem
        self.last = len(order)
        self.done = set()
        self.live, self.sent = [], []
        self.arrays = [full]
        self.slot = 0

    def view(self):
        here = self.here
        return (
            (here.t,)
            + tuple(slice(None) if j in self.done else here.bits[j] for j in range(here.count))
            + (slice(None), self.cols)
        )

    def stage(self, step):
        here = self.here
        if step == 0:
            self.place = pltpu.make_async_copy(
                self.shard.at[:, self.cols], self.full.at[self.view()], self.local_sem
            )
            self.place.start()
        for copy in self.live:
            copy.wait_recv()
        if step == 1:
            self.place.wait()
        self.sent += self.live
        self.live = []
        if step == self.last:
            for copy in self.sent:
                copy.wait_send()
            return
        dim = self.order[step]
        if dim == "y":
            pairs = [(self.full.at[self.view()], self.other.at[self.view()])]
            self.arrays = [self.full, self.other]
        elif step == 0:
            pairs = [(self.shard.at[:, self.cols], self.full.at[self.view()])]
        else:
            pairs = [(ref.at[self.view()], ref.at[self.view()]) for ref in self.arrays]
        for src, dst in pairs:
            copy = remote(
                src, dst, self.send.at[self.slot], self.recv.at[self.slot], here.across(dim)
            )
            copy.start()
            self.live.append(copy)
            self.slot += 1
        if dim not in ("t", "y"):
            self.done.add(dim)


class Scatter:
    def __init__(self, here, own, other, order, cols, held, landed, out, send, recv, local_sems):
        self.here, self.order, self.cols = here, order, cols
        self.source = [own] if other is None else [own, other]
        self.held, self.landed, self.out = held, landed, out
        self.send, self.recv, self.local_sems = send, recv, local_sems
        self.last = len(order)
        self.fixed = {}
        self.live = []
        self.slot = 0
        self.arrays = list(range(len(self.source)))

    def view(self, extra=None):
        fixed = dict(self.fixed)
        if extra:
            fixed.update(extra)
        return tuple(fixed.get(j, slice(None)) for j in range(self.here.count))

    def start(self, src, where, index):
        copy = remote(
            src, self.landed[self.slot], self.send.at[self.slot], self.recv.at[self.slot], where
        )
        copy.start()
        self.live.append((copy, self.slot, index))
        self.slot += 1

    def stage(self, step):
        here = self.here
        if step > 0:
            self.finish(step - 1)
        if step == self.last:
            return
        dim = self.order[step]
        if dim == "t":
            self.loads = []
            tail = (slice(None),) * (here.count + 1) + (self.cols,)
            for index in self.arrays:
                load = pltpu.make_async_copy(
                    self.source[index].at[(here.t,) + tail], self.held[index],
                    self.local_sems.at[index],
                )
                load.start()
                self.loads.append(load)
                self.start(self.source[index].at[(1 - here.t,) + tail], here.across("t"), index)
        elif dim == "y":
            self.start(self.held[1].at[self.view()], here.across("y"), 0)
            self.arrays = [0]
        else:
            far = self.view({dim: 1 - here.bits[dim]})
            for index in self.arrays:
                self.start(self.held[index].at[far], here.across(dim), index)

    def finish(self, step):
        here = self.here
        dim = self.order[step]
        if dim not in ("t", "y"):
            self.fixed[dim] = here.bits[dim]
        view = self.view()
        if dim == "t":
            for load in self.loads:
                load.wait()
        for copy, slot, index in self.live:
            copy.wait()
            total = self.held[index][view].astype(f32) + self.landed[slot][...].astype(f32)
            if step == self.last - 1:
                self.out[:, self.cols] = total
            else:
                self.held[index][view] = total.astype(bf16)
        self.live = []


class Total:
    def __init__(self, here, value, landed, send, recv):
        self.here, self.value, self.landed, self.send, self.recv = here, value, landed, send, recv
        self.order = ["t", "y"] + list(range(here.count))
        self.last = len(self.order)

    def stage(self, step):
        if step > 0:
            self.copy.wait()
            self.value[...] += self.landed[step - 1]
        if step < self.last:
            self.copy = remote(
                self.value, self.landed.at[step], self.send.at[step], self.recv.at[step],
                self.here.across(self.order[step]),
            )
            self.copy.start()


class Runner:
    def __init__(self, jobs, lags, stride=1):
        self.jobs, self.lags, self.stride, self.tick = jobs, lags, stride, 0
        self.length = max(job.last * stride + lag for job, lag in zip(jobs, lags)) + 1

    def advance(self):
        if self.tick < self.length:
            for job, lag in zip(self.jobs, self.lags):
                since = self.tick - lag
                if since % self.stride == 0 and 0 <= since // self.stride <= job.last:
                    job.stage(since // self.stride)
            self.tick += 1

    def drain(self):
        while self.tick < self.length:
            self.advance()


def gather_orders(count):
    far, near = list(range(count - 1)), [count - 1]
    return {
        "plain": far + near + ["t"],
        "late": far + near + ["y", "t"],
        "early": far + ["y"] + near + ["t"],
    }


def scatter_orders(count):
    near, far = [count - 1], list(range(count - 2, -1, -1))
    return {
        "plain": ["t"] + near + far,
        "early": ["t", "y"] + near + far,
        "late": ["t"] + near + ["y"] + far,
    }


def scatter_lands(order, count, pair, rows, cols):
    shapes, free, live = [], count, 2 if pair else 1
    for dim in order:
        if dim == "y":
            live = 1
        elif dim != "t":
            free -= 1
        shapes += [(2,) * free + (rows, cols)] * live
    return shapes


def lists_body(lists, heard, flag, send, recv):
    here = Place()
    n = here.n_dp
    peers = []
    for rt in range(2):
        for k in range(n):
            if rt or k:
                peers.append((rt, k, {"tower": here.t + rt * (1 - 2 * here.t), "dp": here.mixed(k)}))
    greet([where for _, _, where in peers])
    copies = []
    for rt, k, where in peers:
        copy = remote(lists.at[k], heard.at[rt, k], send.at[rt, k], recv.at[rt, k], where)
        copy.start()
        copies.append(copy)
    heard[0, 0] = lists[0]
    for copy in copies:
        copy.wait()
    flag[...] = jnp.max(heard[...].reshape((2 * n,) + flag.shape), axis=0)


def heard_room(tok, n_dp):
    return max(32, tok // n_dp)


def exchange_lists(lists):
    n = lists.shape[0]
    dma = pltpu.SemaphoreType.DMA
    return pl.pallas_call(
        lists_body,
        out_shape=[sds((2,) + lists.shape, jnp.int32), sds(lists.shape[1:], jnp.int32)],
        in_specs=[VM],
        out_specs=[VM, VM],
        scratch_shapes=[dma((2, n)), dma((2, n))],
        compiler_params=params(1),
        name="lists",
    )(lists)


def turned(values):
    lanes = lax.broadcasted_iota(jnp.int32, values.shape, 1) % HDIM
    size = values.shape[1]
    return jnp.where(
        lanes < HDIM // 2,
        -pltpu.roll(values, size - HDIM // 2, 1),
        pltpu.roll(values, HDIM // 2, 1),
    )


def norm_parts(stream):
    average = jnp.mean(stream, -1, keepdims=True)
    centered = stream - average
    variance = jnp.mean(centered * centered, -1, keepdims=True)
    scale = lax.rsqrt(variance + norm_eps)
    return centered * scale, scale


def forward_body(room, kinds, pieces, stride, every, *refs):
    here = Place()
    n, count = here.n_dp, here.count
    table, heard, pos, norm_rows, cosine, sine, seg_row, seg_col = refs[:8]
    shards = refs[8:13]
    emb_out, zero_out, input_out, q_out, k_out, v_out, lse_out, att_own, att_other = refs[13:22]
    fulls, at = [], 22
    for kind in kinds:
        width = 1 if kind == "plain" else 2
        fulls.append((refs[at], None) if width == 1 else (refs[at], refs[at + 1]))
        at += width
    low_table, served, rows, vt, att_far = refs[at : at + 5]
    lows = refs[at + 5 : at + 10]
    rsem, ysem, asem, wsend, wrecv, wlocal = refs[at + 10 :]
    tok = pos.shape[0]
    half = tok // 2
    width = rows.shape[3]
    slots = n * room
    feats = q_out.shape[1]
    groups = feats // 128
    block = 256

    greet(
        [{"dp": here.mixed(k)} for k in range(1, n)] + [here.across("t"), here.across("y")]
    )
    orders = gather_orders(count)
    for low, shard in zip(lows, shards):
        low[...] = shard[...].astype(bf16)
    jobs, lags = [], []
    for number, (which, kind, start, size, lag) in enumerate(pieces):
        jobs.append(
            Gather(
                here, lows[which], fulls[which][0], fulls[which][1], orders[kind],
                pl.ds(start, size), wsend.at[number], wrecv.at[number], wlocal.at[number],
            )
        )
        lags.append(lag)
    first = Runner(jobs[:1], lags[:1])
    runner = Runner(jobs[1:], lags[1:], stride)
    first.advance()
    runner.advance()
    low_table[...] = table[...].astype(bf16)
    row_count = table.shape[0]
    out_copies, y_copies = [], []

    def pass_on(k):
        copy = remote(
            rows.at[here.m, k], rows.at[here.m, k], ysem.at[0, k], ysem.at[1, k], here.across("y")
        )
        copy.start()
        y_copies.append(copy)

    for k in list(range(n - 1, 0, -1)) + [0]:
        column = jnp.transpose(heard[k])[:room, 0:1]
        hot = (lax.broadcasted_iota(jnp.int32, (room, row_count), 1) == column).astype(f32)
        found = mdot(hot.astype(bf16), low_table[...]).astype(bf16)
        if k == 0:
            rows[here.m, 0] = found
            pass_on(0)
        else:
            served[k] = found
            copy = remote(
                served.at[k], rows.at[here.m, k], rsem.at[0, k], rsem.at[1, k],
                {"dp": here.mixed(k)},
            )
            copy.start()
            out_copies.append(copy)
            if k % 2:
                runner.advance()
        if k == n // 2:
            first.advance()
    first.advance()
    for k in range(n - 1, 0, -1):
        out_copies[n - 1 - k].wait_recv()
        pass_on(k)
        if k % 3 == 1:
            runner.advance()
    first.drain()
    for copy in out_copies:
        copy.wait_send()
    for copy in y_copies:
        copy.wait()

    w_qkv = fulls[0][0]
    for i in range(tok // block):
        at = slice(i * block, (i + 1) * block)
        hot = (lax.broadcasted_iota(jnp.int32, (block, slots), 1) == pos[at, :]).astype(f32)
        hot = hot.astype(bf16)
        emb = jnp.concatenate([mdot(hot, rows[h].reshape(slots, width)) for h in range(2)], 1)
        hat, _scale = norm_parts(emb)
        stream = hat * norm_rows[0:1, :] + norm_rows[1:2, :]
        low = stream.astype(bf16)
        input_out[at, :] = low
        if (i + 1) * block <= half:
            emb_out[at, :] = emb.astype(bf16)
            zero_out[at, :] = stream
        cos, sin = cosine[at, :], sine[at, :]
        proj = mdot(low, w_qkv[...].reshape(2 * width, 3 * feats))
        for c in range(3):
            for g in range(groups):
                cols = slice(g * 128, (g + 1) * 128)
                part = proj[:, c * feats + g * 128 : c * feats + (g + 1) * 128]
                if c < 2:
                    part = part * cos + turned(part) * sin
                part = part.astype(bf16)
                if c == 0:
                    q_out[at, cols] = part * bf16(HDIM**-0.5)
                elif c == 1:
                    k_out[at, cols] = part
                else:
                    v_out[at, cols] = part
        if i % every == every - 1:
            runner.advance()

    lane = lax.broadcasted_iota(jnp.int32, (1, 128), 1)
    att_copies = []
    for g in range(groups):
        cols = slice(g * 128, (g + 1) * 128)
        vt[...] = jnp.transpose(v_out[:, cols].astype(f32)).astype(bf16)
        keys = [jnp.where((lane // HDIM) == h, k_out[:, cols], bf16(0)) for h in range(2)]
        for i in list(range(tok // block // 2, tok // block)) + list(range(tok // block // 2)):
            at = slice(i * block, (i + 1) * block)
            query = q_out[at, cols]
            same = seg_col[...] == seg_row[:, at]
            outs = []
            for h in range(2):
                scores = jnp.where(same, tdot(keys[h], query), neg_large)
                peak = jnp.max(scores, 0, keepdims=True)
                soft = jnp.exp(scores - peak)
                total = jnp.sum(soft, 0, keepdims=True)
                lse_out[2 * g + h, :, at] = peak + jnp.log(total)
                soft = (soft * (1.0 / total)).astype(bf16)
                outs.append(mdot(vt[h * HDIM : (h + 1) * HDIM, :], soft))
            found = jnp.transpose(jnp.concatenate(outs, 0)).astype(bf16)
            if i * block < half:
                att_own[at, cols] = found
            else:
                att_far[slice(i * block - half, (i + 1) * block - half), cols] = found
                if (i + 1) * block == tok:
                    copy = remote(
                        att_far.at[:, cols], att_other.at[:, cols], asem.at[0, g], asem.at[1, g],
                        here.across("y"),
                    )
                    copy.start()
                    att_copies.append(copy)
            if i % every == every - 1:
                runner.advance()
    runner.drain()
    for copy in att_copies:
        copy.wait()


def forward_pass(table, heard, pos, norm_rows, cosine, sine, seg_row, seg_col, shards, kinds, pieces,
                 stride=2, every=1):
    n_dp = heard.shape[0]
    room = heard_room(pos.shape[0], n_dp)
    count = n_dp.bit_length() - 1
    halves = (2,) * (count + 1)
    tok = pos.shape[0]
    half = tok // 2
    width = table.shape[1]
    feats = shards[0].shape[1] // 3
    outs = [
        sds((half, 2 * width), bf16),
        sds((half, 2 * width), f32),
        sds((tok, 2 * width), bf16),
        sds((tok, feats), bf16),
        sds((tok, feats), bf16),
        sds((tok, feats), bf16),
        sds((feats // HDIM, 1, tok), f32),
        sds((half, feats), bf16),
        sds((half, feats), bf16),
    ]
    specs = [VM] * len(outs)
    for shard, kind in zip(shards, kinds):
        full = sds(halves + shard.shape, bf16)
        outs += [full] if kind == "plain" else [full, full]
        specs += [VM] if kind == "plain" else [ANY, ANY]
    dma = pltpu.SemaphoreType.DMA
    steps = count + 6
    scratch = (
        [
            pltpu.VMEM(table.shape, bf16),
            pltpu.VMEM((n_dp, room, width), bf16),
            pltpu.VMEM((2, n_dp, room, width), bf16),
            pltpu.VMEM((128, tok), bf16),
            pltpu.VMEM((half, feats), bf16),
        ]
        + [pltpu.VMEM(shard.shape, bf16) for shard in shards]
        + [dma((2, n_dp)), dma((2, n_dp)), dma((2, feats // 128))]
        + [dma((len(pieces), steps)), dma((len(pieces), steps)), dma((len(pieces),))]
    )
    out = pl.pallas_call(
        lambda *refs: forward_body(room, kinds, pieces, stride, every, *refs),
        out_shape=outs,
        in_specs=[VM] * (8 + len(shards)),
        out_specs=specs,
        scratch_shapes=scratch,
        compiler_params=params(2),
        name="forward",
    )(table, heard, pos, norm_rows, cosine, sine, seg_row, seg_col, *shards)
    weights, at = [], 9
    for shard, kind in zip(shards, kinds):
        whole = (2 * n_dp * shard.shape[0], shard.shape[1])
        if kind == "plain":
            weights.append(out[at].reshape(whole))
            at += 1
        else:
            weights.append((out[at].reshape(whole), out[at + 1].reshape(whole)))
            at += 2
    return out[:9], weights


def make_scatters(
    here, grads, kinds, pieces, outs, held, landed, send, recv, loads, stride=1
):
    orders = scatter_orders(here.count)
    jobs, lags = [], []
    held, landed = list(held), list(landed)
    for number, (which, kind, start, size, lag) in enumerate(pieces):
        own, other = grads[which]
        pair = other is not None
        mine = [held.pop(0) for _ in range(2 if pair else 1)]
        amount = len(scatter_lands(orders[kind], here.count, pair, 1, 1))
        lands = [landed.pop(0) for _ in range(amount)]
        jobs.append(
            Scatter(
                here, own, other, orders[kind], pl.ds(start, size), mine, lands, outs[which],
                send.at[number], recv.at[number], loads.at[number],
            )
        )
        lags.append(lag)
    return Runner(jobs, lags, stride)


def scatter_scratch(count, rows, pairs, pieces):
    orders = scatter_orders(count)
    held, landed = [], []
    for which, kind, _start, size, _lag in pieces:
        pair = pairs[which]
        held += [pltpu.VMEM((2,) * count + (rows, size), bf16)] * (2 if pair else 1)
        landed += [
            pltpu.VMEM(shape, bf16)
            for shape in scatter_lands(orders[kind], count, pair, rows, size)
        ]
    dma = pltpu.SemaphoreType.DMA
    steps = 2 * count + 6
    sems = [dma((len(pieces), steps)), dma((len(pieces), steps)), dma((len(pieces), 2))]
    return held, landed, sems


def square_sum(values):
    return jnp.sum(jnp.sum(values * values, 0, keepdims=True), 1, keepdims=True)


def store_blocks(ref, values, count, start):
    rows, cols = ref.shape[-2], values.shape[1]
    for number in range(2 ** (count + 1)):
        at = tuple((number >> (count - j)) & 1 for j in range(count + 1))
        ref[at + (slice(None), slice(start, start + cols))] = values[
            number * rows : (number + 1) * rows, :
        ].astype(bf16)


def hidden_body(pieces, sizes, stride, *refs):
    here = Place()
    count = here.count
    (grad_pool, seg, hat_two, scale_two, norm_rows, low_one, hat_one, scale_one,
     att_own, att_other, hidden_own, hidden_other) = refs[:12]
    weights = refs[12:18]
    residual, low_out, norms_out, wout_own, wout_other = refs[18:23]
    later = refs[23:27]
    out_down, squares = refs[27:29]
    loaded, down, low_two, turned_one, turned_two, total = refs[29:35]
    held = refs[35 : 35 + sizes[0]]
    landed = refs[35 + sizes[0] : 35 + sizes[0] + sizes[1]]
    wsem, send, recv, loads = refs[35 + sizes[0] + sizes[1] :]
    half, width = low_one.shape
    part = weights[0].shape[1] // 2
    copies = {}

    def load(c, j):
        for w in range(3):
            copies[c, j, w] = pltpu.make_async_copy(
                weights[2 * w + j].at[:, pl.ds(c * part, part)], loaded.at[j * 3 + w],
                wsem.at[(c * 2 + j) * 3 + w],
            )
            copies[c, j, w].start()

    load(0, 0)
    load(0, 1)
    greet([here.across("t"), here.across("y")] + [here.across(j) for j in range(count)])
    grads = [(down.at[0], down.at[1])]
    runner = make_scatters(
        here, grads, None, pieces, (out_down,), held, landed, send, recv, loads, stride
    )
    slots = grad_pool.shape[0]
    hot = (lax.broadcasted_iota(jnp.int32, (half, slots), 1) == seg[...]).astype(f32)
    grad_two = jnp.dot(hot, grad_pool[...], precision=highest, preferred_element_type=f32)
    hat = hat_two[...]
    grad_hat = grad_two * norm_rows[4:5, :]
    first = jnp.mean(grad_hat, -1, keepdims=True)
    second = jnp.mean(grad_hat * hat, -1, keepdims=True)
    grad_sum = scale_two[...] * (grad_hat - first - hat * second)
    low_two[...] = grad_sum.astype(bf16)
    turned_two[...] = jnp.transpose(grad_sum).astype(bf16)
    for c in range(2):
        for j, hidden in enumerate((hidden_own, hidden_other)):
            cols = slice(c * part, (c + 1) * part)
            store_blocks(down.at[j], mdot(turned_two[...], hidden[:, cols]), count, c * part)
        runner.advance()
    norms_out[...] = jnp.zeros_like(norms_out)
    norms_out[4:5, :] = jnp.sum(grad_two * hat, 0, keepdims=True)
    norms_out[5:6, :] = jnp.sum(grad_two, 0, keepdims=True)
    turned_one[...] = jnp.transpose(low_one[...].astype(f32)).astype(bf16)
    total[...] = grad_sum
    runner.advance()
    for c in range(2):
        for j in range(2):
            number = j * 3
            for w in range(3):
                copies[c, j, w].wait()
            gate = mdot(low_one[...], loaded[number])
            up = mdot(low_one[...], loaded[number + 1])
            share = 1.0 / (1.0 + jnp.exp(-gate))
            grad_hidden = mdot(low_two[...], loaded[number + 2])
            grad_up = (grad_hidden * (gate * share)).astype(bf16)
            grad_gate = (
                grad_hidden * up * (share * (1.0 + gate * (1.0 - share)))
            ).astype(bf16)
            runner.advance()
            store_blocks(later[j], mdot(turned_one[...], grad_gate), count, c * part)
            store_blocks(later[2 + j], mdot(turned_one[...], grad_up), count, c * part)
            total[...] += tdot(grad_gate, loaded[number]) + tdot(grad_up, loaded[number + 1])
            if c == 0:
                load(1, j)
            runner.advance()
    hat = hat_one[...]
    grad_one = total[...]
    grad_hat = grad_one * norm_rows[2:3, :]
    first = jnp.mean(grad_hat, -1, keepdims=True)
    second = jnp.mean(grad_hat * hat, -1, keepdims=True)
    grad_sum = scale_one[...] * (grad_hat - first - hat * second)
    norms_out[2:3, :] = jnp.sum(grad_one * hat, 0, keepdims=True)
    norms_out[3:4, :] = jnp.sum(grad_one, 0, keepdims=True)
    residual[...] = grad_sum
    low_out[...] = grad_sum.astype(bf16)
    runner.advance()
    turned_two[...] = jnp.transpose(grad_sum).astype(bf16)
    wout_own[...] = mdot(turned_two[...], att_own[...]).astype(bf16)
    runner.advance()
    wout_other[...] = mdot(turned_two[...], att_other[...]).astype(bf16)
    runner.drain()
    squares[...] = jnp.broadcast_to(square_sum(out_down[...]), squares.shape)


def hidden_back(grad_pool, seg, hat_two, scale_two, norm_rows, low_one, hat_one, scale_one, att,
                hidden, w_gate, w_up, w_down, pieces, stride=1):
    n_dp = lax.axis_size("dp")
    count = n_dp.bit_length() - 1
    half, width = low_one.shape
    feats = att[0].shape[1]
    cols = w_gate[0].shape[1]
    rows = width // (2 * n_dp)
    blocks = (2,) * (count + 1) + (rows, cols)
    held, landed, sems = scatter_scratch(count, rows, [True], pieces)
    vmem = pltpu.VMEM
    return pl.pallas_call(
        lambda *refs: hidden_body(pieces, (len(held), len(landed)), stride, *refs),
        out_shape=[
            sds((half, width), f32), sds((half, width), bf16), sds((8, width), f32),
            sds((width, feats), bf16), sds((width, feats), bf16),
        ] + [sds(blocks, bf16)] * 4 + [sds((rows, cols), f32), sds((8, 128), f32)],
        in_specs=[VM] * 12 + [ANY] * 6,
        out_specs=[VM] * 11,
        scratch_shapes=[
            vmem((6, width, cols // 2), bf16), vmem((2,) + blocks, bf16), vmem((half, width), bf16),
            vmem((width, half), bf16), vmem((width, half), bf16), vmem((half, width), f32),
        ] + held + landed + [pltpu.SemaphoreType.DMA((12,))] + sems,
        compiler_params=params(6),
        name="hidden",
    )(grad_pool, seg, hat_two, scale_two, norm_rows, low_one, hat_one, scale_one, *att, *hidden,
      *w_gate, *w_up, *w_down)


def backward_body(room, pieces, late_pieces, sizes, stride, every, *refs):
    here = Place()
    n, count = here.n_dp, here.count
    (low, out_own, out_other, query, key, value, lse, cosine, sine, seg_row, seg_col, residual,
     emb, norm_rows, w_qkv, norms_in, before, inputs, pos, heard) = refs[:20]
    grads = [(refs[20 + 2 * j], refs[21 + 2 * j]) for j in range(3)]
    (table_out, norms_out, out_gate, out_up, out_proj, out_qkv, total_out) = refs[26:33]
    (kt, dq, dk, dv, grad_att, far_att, far_send, far_recv, grad_proj, turned_in, grad_qkv,
     low_out, norm_part, other, packed, mine, theirs, norms, parts, own_part) = refs[33:53]
    at = 53
    cuts = []
    for size in sizes:
        cuts.append(refs[at : at + size])
        at += size
    held, landed, late_held, late_landed = cuts
    (asem, bsem, ysem, rsem, csem, nsem, tsem, send, recv, loads, late_send, late_recv,
     late_loads) = refs[at:]
    tok, feats = query.shape
    half, width = tok // 2, table_out.shape[1]
    groups = feats // 128
    block = 256
    peers = []
    for rt in range(2):
        for rd in range(n):
            for rm in range(2):
                if rt or rd or rm:
                    where = {
                        "tower": here.t + rt * (1 - 2 * here.t),
                        "dp": here.mixed(rd),
                        "mp": here.m + rm * (1 - 2 * here.m),
                    }
                    peers.append(((rt * n + rd) * 2 + rm, where))
    me = (here.t * n + here.d) * 2 + here.m
    greet([where for _, where in peers])
    runner = make_scatters(
        here, grads, None, pieces, (out_gate, out_up, out_proj), held, landed, send, recv, loads,
        stride,
    )
    runner.advance()
    att_copies = []
    far_att[...] = mdot(low[...], out_other[...]).astype(bf16)
    for g in range(groups):
        cols = slice(g * 128, (g + 1) * 128)
        copy = remote(
            far_att.at[:, cols], grad_att.at[half:, cols], asem.at[0, g], asem.at[1, g],
            here.across("y"),
        )
        copy.start()
        att_copies.append(copy)
    grad_att[:half, :] = mdot(low[...], out_own[...]).astype(bf16)
    for i in range(tok // block):
        rows = slice(i * block, (i + 1) * block)
        turned_in[:, rows] = jnp.transpose(inputs[rows, :].astype(f32)).astype(bf16)
    runner.advance()
    lane = lax.broadcasted_iota(jnp.int32, (1, 128), 1)
    for g in range(groups):
        cols = slice(g * 128, (g + 1) * 128)
        kt[...] = jnp.transpose(key[:, cols].astype(f32)).astype(bf16)
        keys = [jnp.where((lane // HDIM) == h, key[:, cols], bf16(0)) for h in range(2)]
        values = [jnp.where((lane // HDIM) == h, value[:, cols], bf16(0)) for h in range(2)]
        for i in range(tok // block):
            if i * block == half:
                att_copies[g].wait_recv()
            rows = slice(i * block, (i + 1) * block)
            q_part = query[rows, cols]
            g_part = grad_att[rows, cols]
            same = seg_col[...] == seg_row[:, rows]
            turns = []
            add_k, add_v = None, None
            for h in range(2):
                inside = (lane // HDIM) == h
                scores = jnp.where(same, tdot(keys[h], q_part), neg_large)
                soft = jnp.exp(scores - lse[2 * g + h, :, rows])
                grad_soft = tdot(values[h], g_part)
                inner = jnp.sum(soft * grad_soft, 0, keepdims=True)
                grad_scores = (soft * (grad_soft - inner)).astype(bf16)
                part_v = mdot(soft.astype(bf16), jnp.where(inside, g_part, bf16(0)))
                part_k = mdot(grad_scores, jnp.where(inside, q_part, bf16(0)))
                add_v = part_v if h == 0 else add_v + part_v
                add_k = part_k if h == 0 else add_k + part_k
                turns.append(mdot(kt[h * HDIM : (h + 1) * HDIM, :], grad_scores))
            dq[rows, :] = jnp.transpose(jnp.concatenate(turns, 0)) * (HDIM**-0.5)
            if i == 0:
                dv[...] = add_v
                dk[...] = add_k
            else:
                dv[...] += add_v
                dk[...] += add_k
            if i % every == every - 1:
                runner.advance()
        cos, sin = cosine[...], sine[...]
        for c, grad in ((0, dq), (1, dk)):
            whole = grad[...]
            back = whole * cos - turned(whole) * sin
            grad_proj[:, c * feats + g * 128 : c * feats + (g + 1) * 128] = back.astype(bf16)
        grad_proj[:, 2 * feats + g * 128 : 2 * feats + (g + 1) * 128] = dv[...].astype(bf16)
    for copy in att_copies:
        copy.wait_send()
    far_copies = []
    for i in range(half // block):
        rows = slice(i * block, (i + 1) * block)
        far = grad_proj[half + i * block : half + (i + 1) * block, :]
        far_send[rows, :] = tdot(far, w_qkv[...]).astype(bf16)
        copy = remote(
            far_send.at[rows, :], far_recv.at[rows, :], bsem.at[0, i], bsem.at[1, i],
            here.across("y"),
        )
        copy.start()
        far_copies.append(copy)
    late = make_scatters(
        here, [(grad_qkv, None)], None, late_pieces, (out_qkv,), late_held, late_landed, late_send,
        late_recv, late_loads, 1,
    )
    jobs = late.jobs
    step = feats if grad_qkv.shape[-2] % 16 == 0 else 128
    for start in range(0, 3 * feats, step):
        cols = slice(start, start + step)
        store_blocks(grad_qkv, mdot(turned_in[...], grad_proj[:, cols]), count, start)
    late.advance()
    runner.advance()
    theirs_at = pl.ds(pl.multiple_of((1 - here.m) * width, 128), width)
    mine_at = pl.ds(pl.multiple_of(here.m * width, 128), width)
    norm_part[...] = norms_in[...]
    swaps = []
    for i in range(half // block):
        rows = slice(i * block, (i + 1) * block)
        near = residual[rows, :] + tdot(grad_proj[rows, :], w_qkv[...])
        if i == 0:
            runner.advance()
        far_copies[i].wait()
        near = near + far_recv[rows, :].astype(f32)
        hat, scale = norm_parts(emb[rows, :].astype(f32))
        grad_hat = near * norm_rows[0:1, :]
        first = jnp.mean(grad_hat, -1, keepdims=True)
        second = jnp.mean(grad_hat * hat, -1, keepdims=True)
        low_out[rows, :] = (scale * (grad_hat - first - hat * second)).astype(bf16)
        copy = remote(
            low_out.at[rows, theirs_at], other.at[rows, :], ysem.at[0, i], ysem.at[1, i],
            here.across("y"),
        )
        copy.start()
        swaps.append(copy)
        norm_part[0:1, :] += jnp.sum(near * hat, 0, keepdims=True)
        norm_part[1:2, :] += jnp.sum(near, 0, keepdims=True)
    jobs.append(Total(here, norm_part, norms, nsem.at[0], nsem.at[1]))
    late.lags.append(late.tick)
    late.length = max(late.length, late.tick + jobs[-1].last + 1)
    late.advance()
    runner.advance()
    for copy in swaps:
        copy.wait()
    both = jnp.concatenate([low_out[:, mine_at], other[...]], 0)
    copies = []
    for k in list(range(n - 1, 0, -1)) + [0]:
        hot = (
            lax.broadcasted_iota(jnp.int32, (room, pos.shape[1]), 0) + k * room == pos[...]
        ).astype(f32)
        packed[k] = mdot(hot.astype(bf16), both).astype(bf16)
        if k:
            copy = remote(
                packed.at[k], mine.at[k], rsem.at[0, k], rsem.at[1, k], {"dp": here.mixed(k)}
            )
        else:
            mine[0] = packed[0]
            copy = remote(mine.at[0], theirs.at[0], csem.at[0, 0], csem.at[1, 0], here.across("t"))
        copy.start()
        copies.append(copy)
    passed = [copies.pop()]
    late.advance()
    runner.advance()
    for k in range(n - 1, 0, -1):
        copies[n - 1 - k].wait_recv()
        copy = remote(mine.at[k], theirs.at[k], csem.at[0, k], csem.at[1, k], here.across("t"))
        copy.start()
        passed.append(copy)
        if k == n // 2:
            late.advance()
            runner.advance()
    late.advance()
    runner.advance()
    for copy in copies:
        copy.wait_send()
    for copy in passed:
        copy.wait()
    slots = n * room
    row_count = table_out.shape[0]
    size = 424 * 1024 // max(slots, 1024) // 8 * 8
    own_part[...] = jnp.zeros_like(own_part)
    for part in range(-(-row_count // size)):
        rows = slice(part * size, min((part + 1) * size, row_count))
        block_rows = rows.stop - rows.start
        base = lax.broadcasted_iota(jnp.int32, (block_rows, slots), 0) + part * size
        found = 0.0
        for source, sums in ((0, mine), (1, theirs)):
            hot = (base == heard[source]).astype(f32).astype(bf16)
            found = found + mdot(hot, sums[...].reshape(slots, width))
        table_out[rows, :] = found
        own_part[0:1, :] += jnp.sum(found * found, 0, keepdims=True)
        if part % 2:
            late.advance()
            runner.advance()
    late.drain()
    runner.drain()
    norms_out[...] = norm_part[...]
    local_sq = (
        before[0:1, 0:1]
        + 0.5 * jnp.sum(own_part[...], 1, keepdims=True)[0:1]
        + square_sum(out_qkv[...])
        + square_sum(out_proj[...])
        + square_sum(out_gate[...])
        + square_sum(out_up[...])
    )
    parts[me] = jnp.broadcast_to(local_sq, parts.shape[1:])
    copies = []
    for rel, where in peers:
        copy = remote(parts.at[me], parts.at[me], tsem.at[0, rel], tsem.at[1, rel], where)
        copy.start()
        copies.append(copy)
    for copy in copies:
        copy.wait()
    total_out[...] = jnp.sum(parts[...], 0) + square_sum(norms_out[...])


def blocks_of(grad, n_dp):
    count = n_dp.bit_length() - 1
    rows = grad.shape[0] // (2 * n_dp)
    return grad.reshape((2,) * (count + 1) + (rows, grad.shape[1]))


def backward_pass(low, w_out, query, key, value, lse, cosine, sine, seg_row, seg_col, residual,
                  emb, norm_rows, w_qkv, norms, before, inputs, pos_row, heard, grads, grad_out,
                  row_count, pieces, late_pieces, stride=2, every=1):
    n_dp = lax.axis_size("dp")
    count = n_dp.bit_length() - 1
    tok, feats = query.shape
    half, width = low.shape
    rows, cols = grads[0].shape[-2:]
    room = heard_room(tok, n_dp)
    held, landed, sems = scatter_scratch(count, rows, [True] * 3, pieces)
    late_held, late_landed, late_sems = scatter_scratch(count, rows, [False], late_pieces)
    flat = list(grads) + [blocks_of(g, n_dp) for g in grad_out]
    dma = pltpu.SemaphoreType.DMA
    vmem = pltpu.VMEM
    sizes = (len(held), len(landed), len(late_held), len(late_landed))
    steps = max(1, half // 256)
    part = width // 2
    return pl.pallas_call(
        lambda *refs: backward_body(room, pieces, late_pieces, sizes, stride, every, *refs),
        out_shape=[
            sds((row_count, part), f32), sds((8, width), f32),
            sds((rows, cols), f32), sds((rows, cols), f32), sds((rows, feats), f32),
            sds((rows, 3 * feats), f32), sds((8, 128), f32),
        ],
        in_specs=[VM] * 20 + [ANY] * 6,
        out_specs=[VM] * 7,
        scratch_shapes=[
            vmem((128, tok), bf16), vmem((tok, 128), f32), vmem((tok, 128), f32),
            vmem((tok, 128), f32), vmem((tok, feats), bf16), vmem((half, feats), bf16),
            vmem((half, width), bf16), vmem((half, width), bf16),
            vmem((tok, 3 * feats), bf16), vmem((width, tok), bf16),
            vmem((2,) * (count + 1) + (rows, 3 * feats), bf16),
            vmem((half, width), bf16), vmem((8, width), f32), vmem((half, part), bf16),
            vmem((n_dp, room, part), bf16), vmem((n_dp, room, part), bf16),
            vmem((n_dp, room, part), bf16), vmem((count + 2, 8, width), f32),
            vmem((4 * n_dp, 8, 128), f32), vmem((8, part), f32),
        ] + held + landed + late_held + late_landed
        + [dma((2, feats // 128)), dma((2, steps)), dma((2, steps)), dma((2, n_dp)),
           dma((2, n_dp)), dma((2, count + 2)), dma((2, 4 * n_dp))] + sems + late_sems,
        compiler_params=params(4, 60),
        name="backward",
    )(low, w_out[0], w_out[1], query, key, value, lse, cosine, sine, seg_row, seg_col, residual,
      emb, norm_rows, w_qkv, norms, before, inputs, pos_row, heard, *flat)


def loss_body(part, counts, doc_ok, query_ok, target, scale, grad_out, stats, other, low_all, turn,
              psend, precv, esend, erecv):
    here = Place()
    n = here.n_dp
    slots, width = part.shape
    peers = []
    for rt in range(2):
        for rd in range(n):
            if rt or rd:
                peers.append(
                    (rt * n + rd, {"tower": here.t + rt * (1 - 2 * here.t), "dp": here.mixed(rd)})
                )
    greet([where for _, where in peers] + [here.across("y")])
    copy = remote(part, other, psend, precv, here.across("y"))
    copy.start()
    copy.wait()
    pooled = (part[...] + other[...]) / counts[...]
    scale_row = lax.rsqrt(jnp.sum(pooled * pooled, 1, keepdims=True) + 1e-06)
    unit = pooled * scale_row
    low_all[here.t, here.d] = unit.astype(bf16)
    copies = []
    for rel, where in peers:
        copy = remote(
            low_all.at[here.t, here.d], low_all.at[here.t, here.d], esend.at[rel], erecv.at[rel], where
        )
        copy.start()
        copies.append(copy)
    for copy in copies:
        copy.wait()
    total = n * slots
    queries = low_all[0].reshape(total, width)
    documents = low_all[1].reshape(total, width)
    cosines = tdot(queries, documents)
    factor = jnp.exp(jnp.minimum(scale[...], cap_value))
    logits = jnp.where(doc_ok[...] > 0, factor * cosines, neg_large)
    peak = jnp.max(logits, 1, keepdims=True)
    log_total = peak + jnp.log(jnp.sum(jnp.exp(logits - peak), 1, keepdims=True))
    soft = jnp.exp(logits - log_total)
    mask = lax.broadcasted_iota(jnp.int32, (total, total), 1) == target[...]
    picked = jnp.sum(jnp.where(mask, logits, 0.0), 1, keepdims=True)
    valid = query_ok[...] > 0
    query_count = jnp.sum(valid.astype(f32), axis=0, keepdims=True)
    loss_sum = jnp.sum(jnp.where(valid, log_total - picked, 0.0), axis=0, keepdims=True)
    grad_logits = jnp.where(valid, soft - mask.astype(f32), 0.0) / query_count
    by_row = jnp.sum(grad_logits * cosines, 1, keepdims=True)
    grad_scale = (
        jnp.sum(by_row, 0, keepdims=True) * factor * (scale[...] < cap_value).astype(f32)
    )
    grad_cos = factor * grad_logits
    at = pl.ds(pl.multiple_of(here.d * slots, slots), slots)
    turn[0] = grad_cos
    turn[1] = jnp.transpose(grad_cos)
    left = turn[here.t, at, :].astype(bf16)
    right = low_all[1 - here.t].reshape(total, width)
    grad_unit = mdot(left, right)
    grad_pooled = scale_row * (
        grad_unit - unit * jnp.sum(unit * grad_unit, 1, keepdims=True)
    )
    grad_out[...] = grad_pooled / counts[...]
    row = lax.broadcasted_iota(jnp.int32, stats.shape, 0)
    stats[...] = jnp.where(row == 0, loss_sum, jnp.where(row == 1, query_count, grad_scale))


def loss_step(part, counts, doc_ok, query_ok, target, scale):
    n_dp = lax.axis_size("dp")
    slots, width = part.shape
    total = n_dp * slots
    dma = pltpu.SemaphoreType.DMA
    return pl.pallas_call(
        loss_body,
        out_shape=[sds(part.shape, f32), sds((8, 128), f32)],
        in_specs=[VM] * 6,
        out_specs=[VM] * 2,
        scratch_shapes=[
            pltpu.VMEM(part.shape, f32),
            pltpu.VMEM((2, n_dp, slots, width), bf16),
            pltpu.VMEM((2, total, total), f32),
            dma, dma, dma((2 * n_dp,)), dma((2 * n_dp,)),
        ],
        compiler_params=params(3),
        name="loss",
    )(part, counts, doc_ok, query_ok, target, scale)


def rotary_tables(positions):
    half_dim = HDIM // 2
    inverse = 1000.0 ** (-2.0 * jnp.arange(half_dim, dtype=f32) / HDIM)
    angles = positions.astype(f32)[:, None] * inverse[None, :]
    angles = jnp.concatenate([angles] * 4, 1)
    return jnp.cos(angles), jnp.sin(angles)


def layout(lengths, places, slot_count):
    end_points = jnp.cumsum(lengths)
    segment = jnp.sum((places[:, None] >= end_points[None, :]).astype(jnp.int32), 1)
    starts = jnp.concatenate([jnp.zeros((1,), jnp.int32), end_points])
    slot_ids = jnp.arange(slot_count + 1, dtype=jnp.int32)
    segment_start = jnp.sum(jnp.where(segment[:, None] == slot_ids[None, :], starts[None, :], 0), 1)
    return segment, places - segment_start


def norm_back(grad, hat, scale, gain):
    grad_hat = grad * gain
    first = jnp.mean(grad_hat, -1, keepdims=True)
    second = jnp.mean(grad_hat * hat, -1, keepdims=True)
    return (
        scale * (grad_hat - first - hat * second),
        jnp.sum(grad * hat, 0),
        jnp.sum(grad, 0),
    )


def glu(gate_vals, up_vals):
    return jax.nn.silu(gate_vals) * up_vals


def adamw(weight_in, gradient, first_mom, second, factor, step_num, rate):
    gradient = gradient * factor
    first_new = beta_one * first_mom + (1.0 - beta_one) * gradient
    second_new = beta_two * second + (1.0 - beta_two) * gradient * gradient
    first_hat = first_new / (1.0 - beta_one**step_num)
    second_hat = second_new / (1.0 - beta_two**step_num)
    weight_new = weight_in - rate * (
        first_hat / (jnp.sqrt(second_hat) + adam_eps) + decay_rate * weight_in
    )
    return (weight_new, first_new, second_new)


def name_rows(ids, d, n_dp, row_count, room):
    tok = ids.shape[0]
    owner = ids // row_count
    local = ids - owner * row_count
    order = jnp.bitwise_xor(owner, d)
    places = jnp.arange(tok, dtype=jnp.int32)
    first_at = jnp.min(
        jnp.where(ids[:, None] == ids[None, :], places[None, :], tok), 1
    )
    is_first = first_at == places
    slot = jnp.sum(
        (
            (places[None, :] < first_at[:, None])
            & is_first[None, :]
            & (owner[None, :] == owner[:, None])
        ).astype(jnp.int32),
        1,
    )
    over = jnp.max(slot) >= room
    pos = order * room + slot
    wanted = jnp.arange(n_dp * room, dtype=jnp.int32)
    listed = jnp.max(
        jnp.where((pos[None, :] == wanted[:, None]) & is_first[None, :], local[None, :], -1), 1
    ).reshape(n_dp, 1, room)
    listed = jnp.pad(listed, ((0, 0), (0, 0), (0, 128 - room)), constant_values=-1)
    flag = jnp.broadcast_to(over.astype(jnp.int32), (n_dp, 7, 128))
    return pos, jnp.concatenate([listed, flag], 1)


def layer_norm(stream, gain_row, bias_row):
    average = jnp.mean(stream, -1, keepdims=True)
    centered = stream - average
    variance = jnp.mean(centered * centered, -1, keepdims=True)
    return centered * lax.rsqrt(variance + norm_eps) * gain_row + bias_row


def rotate(values, cosine, sine_table):
    half_dim = values.shape[-1] // 2
    turned = jnp.concatenate([-values[..., half_dim:], values[..., :half_dim]], -1)
    return values * cosine + turned * sine_table


def plain_rotary_tables(positions, head_dim):
    half_dim = head_dim // 2
    inverse = 1000.0 ** (-2.0 * jnp.arange(half_dim, dtype=jnp.float32) / head_dim)
    angles = positions.astype(jnp.float32)[:, None] * inverse[None, :]
    angles = jnp.concatenate([angles, angles], 1)[:, None, :]
    return (jnp.cos(angles), jnp.sin(angles))


def plain_layout(lengths, tok_count, slot_count):
    end_points = jnp.cumsum(lengths)
    places = jnp.arange(tok_count, dtype=jnp.int32)
    segment = jnp.sum((places[:, None] >= end_points[None, :]).astype(jnp.int32), 1)
    starts = jnp.concatenate([jnp.zeros((1,), jnp.int32), end_points])
    slot_ids = jnp.arange(slot_count + 1, dtype=jnp.int32)
    segment_start = jnp.sum(jnp.where(segment[:, None] == slot_ids[None, :], starts[None, :], 0), 1)
    return (segment, places - segment_start)


def plain_glu(gate_vals, up_vals):
    return jax.nn.silu(gate_vals) * up_vals


def pool_rows(stream_two, member, counts):
    pooled = jnp.dot(member, stream_two, precision=highest) / counts[:, None]
    return pooled * lax.rsqrt(jnp.sum(pooled * pooled, 1, keepdims=True) + 1e-06)


def model_total(values):
    return lax.psum(values.astype(jnp.bfloat16), "mp").astype(jnp.float32)


def block_scores(query_block, seg_block, key_low, segment, factor):
    scores = (
        jnp.einsum("thd,shd->hts", query_block, key_low, preferred_element_type=jnp.float32)
        * factor
    )
    return jnp.where((seg_block[:, None] == segment[None, :])[None], scores, neg_large)


def attention(query_low, key_low, value_low, segment):
    tok_count, heads_local, head_dim = query_low.shape
    block_rows = min(512, tok_count)
    block_count = tok_count // block_rows
    factor = head_dim ** (-0.5)
    query_blocks = query_low.reshape(block_count, block_rows, heads_local, head_dim)
    seg_blocks = segment.reshape(block_count, block_rows)

    def one_block(operands):
        scores = block_scores(operands[0], operands[1], key_low, segment, factor)
        row_peak = jnp.max(scores, 2, keepdims=True)
        row_total = jnp.sum(jnp.exp(scores - row_peak), 2, keepdims=True)
        log_total = row_peak + jnp.log(row_total)
        soft_rows = jnp.exp(scores - log_total)
        attended = jnp.einsum(
            "hts,shd->thd",
            soft_rows.astype(jnp.bfloat16),
            value_low,
            preferred_element_type=jnp.float32,
        )
        return (attended, log_total[..., 0])

    attended, log_total = lax.map(one_block, (query_blocks, seg_blocks))
    return (attended.reshape(tok_count, heads_local * head_dim), log_total)


def attention_back(query_low, key_low, value_low, grad_attended, log_total, segment):
    tok_count, heads_local, head_dim = query_low.shape
    block_rows = min(512, tok_count)
    block_count = tok_count // block_rows
    factor = head_dim ** (-0.5)
    query_blocks = query_low.reshape(block_count, block_rows, heads_local, head_dim)
    grad_blocks = grad_attended.reshape(block_count, block_rows, heads_local, head_dim)
    seg_blocks = segment.reshape(block_count, block_rows)

    def one_block(running, operands):
        query_block, grad_block, seg_block, lse_block = operands
        scores = block_scores(query_block, seg_block, key_low, segment, factor)
        soft_rows = jnp.exp(scores - lse_block[..., None])
        grad_soft = jnp.einsum(
            "thd,shd->hts", grad_block, value_low, preferred_element_type=jnp.float32
        )
        inner = jnp.sum(soft_rows * grad_soft, 2, keepdims=True)
        grad_scores = (soft_rows * (grad_soft - inner)).astype(jnp.bfloat16)
        grad_query = (
            jnp.einsum("hts,shd->thd", grad_scores, key_low, preferred_element_type=jnp.float32)
            * factor
        )
        grad_key = (
            running[0]
            + jnp.einsum(
                "hts,thd->shd", grad_scores, query_block, preferred_element_type=jnp.float32
            )
            * factor
        )
        grad_value = running[1] + jnp.einsum(
            "hts,thd->shd",
            soft_rows.astype(jnp.bfloat16),
            grad_block,
            preferred_element_type=jnp.float32,
        )
        return ((grad_key, grad_value), grad_query)

    zeros_kv = jnp.zeros(key_low.shape, jnp.float32)
    (grad_key, grad_value), grad_query = lax.scan(
        one_block, (zeros_kv, zeros_kv), (query_blocks, grad_blocks, seg_blocks, log_total)
    )
    return (grad_query.reshape(tok_count, heads_local, head_dim), grad_key, grad_value)


def layer_forward(embed_rows, segment, positions, weights, norm_rows):
    w_qkv, w_out, w_ffn, w_down = weights
    tok_count = embed_rows.shape[0]
    heads_local = w_qkv.shape[2] // HDIM
    stream_zero = layer_norm(embed_rows, norm_rows[0], norm_rows[1])
    input_zero = stream_zero.astype(jnp.bfloat16)
    projected = jnp.einsum("td,dcf->tcf", input_zero, w_qkv, preferred_element_type=jnp.float32)
    heads_view = projected.reshape(tok_count, 3, heads_local, HDIM)
    cosine, sine_table = plain_rotary_tables(positions, HDIM)
    query_low = rotate(heads_view[:, 0], cosine, sine_table).astype(jnp.bfloat16)
    key_low = rotate(heads_view[:, 1], cosine, sine_table).astype(jnp.bfloat16)
    value_low = heads_view[:, 2].astype(jnp.bfloat16)
    attended, log_total = attention(query_low, key_low, value_low, segment)
    attended_low = attended.astype(jnp.bfloat16)
    attn_branch = model_total(
        jnp.einsum("tf,df->td", attended_low, w_out, preferred_element_type=jnp.float32)
    )
    sum_one = stream_zero + attn_branch
    stream_one = layer_norm(sum_one, norm_rows[2], norm_rows[3])
    input_one = stream_one.astype(jnp.bfloat16)
    gate_up = jnp.einsum("td,dcf->tcf", input_one, w_ffn, preferred_element_type=jnp.float32)
    hidden_low = plain_glu(gate_up[:, 0], gate_up[:, 1]).astype(jnp.bfloat16)
    ffn_branch = model_total(
        jnp.einsum("tf,df->td", hidden_low, w_down, preferred_element_type=jnp.float32)
    )
    sum_two = stream_one + ffn_branch
    stream_two = layer_norm(sum_two, norm_rows[4], norm_rows[5])
    kept_vals = (
        embed_rows,
        sum_one,
        sum_two,
        input_zero,
        input_one,
        query_low,
        key_low,
        value_low,
        log_total,
        attended_low,
        gate_up,
        hidden_low,
    )
    return (stream_two, kept_vals)


def layer_backward(grad_two, kept_vals, weights, norm_rows, segment, positions):
    w_qkv, w_out, w_ffn, w_down = weights
    (
        embed_rows,
        sum_one,
        sum_two,
        input_zero,
        input_one,
        query_low,
        key_low,
        value_low,
        log_total,
        attended_low,
        gate_up,
        hidden_low,
    ) = kept_vals
    tok_count, heads_local, head_dim = query_low.shape
    grad_sum_two, gain_two, bias_two = jax.vjp(layer_norm, sum_two, norm_rows[4], norm_rows[5])[1](
        grad_two
    )
    ffn_low = grad_sum_two.astype(jnp.bfloat16)
    grad_down = jnp.einsum("td,tf->df", ffn_low, hidden_low, preferred_element_type=jnp.float32)
    grad_hidden = jnp.einsum("td,df->tf", ffn_low, w_down, preferred_element_type=jnp.float32)
    grad_gate, grad_up = jax.vjp(plain_glu, gate_up[:, 0], gate_up[:, 1])[1](grad_hidden)
    gate_grads = jnp.stack([grad_gate, grad_up], 1).astype(jnp.bfloat16)
    grad_ffn = jnp.einsum("td,tcf->dcf", input_one, gate_grads, preferred_element_type=jnp.float32)
    grad_stream_one = grad_sum_two + model_total(
        jnp.einsum("tcf,dcf->td", gate_grads, w_ffn, preferred_element_type=jnp.float32)
    )
    grad_sum_one, gain_one, bias_one = jax.vjp(layer_norm, sum_one, norm_rows[2], norm_rows[3])[1](
        grad_stream_one
    )
    attn_low = grad_sum_one.astype(jnp.bfloat16)
    grad_out = jnp.einsum("td,tf->df", attn_low, attended_low, preferred_element_type=jnp.float32)
    grad_attended = jnp.einsum(
        "td,df->tf", attn_low, w_out, preferred_element_type=jnp.float32
    ).astype(jnp.bfloat16)
    grad_query, grad_key, grad_value = attention_back(
        query_low,
        key_low,
        value_low,
        grad_attended.reshape(tok_count, heads_local, head_dim),
        log_total,
        segment,
    )
    cosine, sine_table = plain_rotary_tables(positions, head_dim)
    turn_back = jax.vjp(lambda values: rotate(values, cosine, sine_table), grad_query)[1]
    grad_projected = jnp.stack([turn_back(grad_query)[0], turn_back(grad_key)[0], grad_value], 1)
    grad_projected = grad_projected.reshape(tok_count, 3, heads_local * head_dim).astype(
        jnp.bfloat16
    )
    grad_qkv = jnp.einsum(
        "td,tcf->dcf", input_zero, grad_projected, preferred_element_type=jnp.float32
    )
    grad_stream_zero = grad_sum_one + model_total(
        jnp.einsum("tcf,dcf->td", grad_projected, w_qkv, preferred_element_type=jnp.float32)
    )
    grad_embed, gain_zero, bias_zero = jax.vjp(layer_norm, embed_rows, norm_rows[0], norm_rows[1])[
        1
    ](grad_stream_zero)
    norm_grads = jnp.stack([gain_zero, bias_zero, gain_one, bias_one, gain_two, bias_two])
    return (grad_embed, (grad_qkv, grad_out, grad_ffn, grad_down), norm_grads)


def plain_adamw(weight_in, gradient, first_mom, second, factor, step_num, rate):
    gradient = gradient * factor
    first_new = beta_one * first_mom + (1.0 - beta_one) * gradient
    second_new = beta_two * second + (1.0 - beta_two) * gradient * gradient
    first_hat = first_new / (1.0 - beta_one**step_num)
    second_hat = second_new / (1.0 - beta_two**step_num)
    weight_new = weight_in - rate * (
        first_hat / (jnp.sqrt(second_hat) + adam_eps) + decay_rate * weight_in
    )
    return (weight_new, first_new, second_new)


def plain_step(
    token_ids,
    seq_lengths,
    positives,
    embedding,
    attn_in,
    attn_out,
    ffn_in,
    ffn_out,
    norm_params,
    logit_scale,
    embed_m,
    embed_v,
    attn_in_m,
    attn_in_v,
    attn_out_m,
    attn_out_v,
    ffn_in_m,
    ffn_in_v,
    ffn_out_m,
    ffn_out_v,
    norm_m,
    norm_v,
    scale_m,
    scale_v,
):
    n_data = lax.axis_size("dp")
    tower_idx = lax.axis_index("tower")
    data_idx = lax.axis_index("dp")
    model_idx = lax.axis_index("mp")
    slot_count = seq_lengths.shape[2]
    token_list = token_ids[0]
    tok_count = token_list.shape[0]
    model_width = norm_params.shape[1]
    local_width = embedding.shape[1]
    row_count = embedding.shape[0]
    weights = (
        lax.all_gather(attn_in.astype(jnp.bfloat16), ("tower", "dp"), axis=0, tiled=True),
        lax.all_gather(attn_out.astype(jnp.bfloat16), ("tower", "dp"), axis=0, tiled=True),
        lax.all_gather(ffn_in.astype(jnp.bfloat16), ("tower", "dp"), axis=0, tiled=True),
        lax.all_gather(ffn_out.astype(jnp.bfloat16), ("tower", "dp"), axis=0, tiled=True),
    )
    shard_piece = lax.all_gather(embedding.astype(jnp.bfloat16), "dp", axis=0, tiled=True)
    inside = (token_list >= 0) & (token_list < shard_piece.shape[0])
    picked = jnp.take(shard_piece, jnp.clip(token_list, 0, shard_piece.shape[0] - 1), axis=0)
    looked = jnp.where(inside[:, None], picked.astype(jnp.float32), 0.0)
    embed_rows = lax.all_gather(looked.astype(jnp.bfloat16), "mp", axis=1, tiled=True).astype(
        jnp.float32
    )
    lengths_row = seq_lengths[tower_idx, data_idx]
    segment, positions = plain_layout(lengths_row, tok_count, slot_count)
    stream_two, kept_vals = layer_forward(embed_rows, segment, positions, weights, norm_params)
    member = (segment[None, :] == jnp.arange(slot_count, dtype=jnp.int32)[:, None]).astype(
        jnp.float32
    )
    counts = jnp.maximum(lengths_row, 1).astype(jnp.float32)
    own_embeds, pool_back = jax.vjp(lambda stream: pool_rows(stream, member, counts), stream_two)
    all_embeds = lax.all_gather(
        own_embeds.astype(jnp.bfloat16), ("tower", "dp"), axis=0, tiled=True
    )
    query_total = n_data * slot_count
    rows_per = slot_count // 2
    first_row = (tower_idx * n_data + data_idx) * rows_per
    query_rows = lax.dynamic_slice_in_dim(all_embeds, first_row, rows_per, 0)
    documents = all_embeds[query_total:]
    cosines = jnp.einsum("qd,kd->qk", query_rows, documents, preferred_element_type=jnp.float32)
    logit_factor = jnp.exp(jnp.minimum(logit_scale[0], cap_value))
    doc_ok = seq_lengths[1].reshape(-1) > 0
    query_ok_all = seq_lengths[0].reshape(-1) > 0
    query_count = jnp.sum(query_ok_all.astype(jnp.float32))
    query_ok = lax.dynamic_slice_in_dim(query_ok_all, first_row, rows_per, 0)
    logits = jnp.where(doc_ok[None, :], logit_factor * cosines, neg_large)
    row_peak = jnp.max(logits, 1, keepdims=True)
    log_total = row_peak + jnp.log(jnp.sum(jnp.exp(logits - row_peak), 1, keepdims=True))
    soft_rows = jnp.exp(logits - log_total)
    targets = lax.dynamic_slice_in_dim(positives.reshape(-1), first_row, rows_per, 0)
    target_mask = jnp.arange(query_total, dtype=jnp.int32)[None, :] == targets[:, None]
    picked = jnp.sum(jnp.where(target_mask, logits, 0.0), 1)
    loss_part = jnp.sum(jnp.where(query_ok, log_total[:, 0] - picked, 0.0))
    grad_logits = (
        jnp.where(query_ok[:, None], soft_rows - target_mask.astype(jnp.float32), 0.0) / query_count
    )
    scale_part = (
        jnp.sum(grad_logits * cosines)
        * logit_factor
        * (logit_scale[0] < cap_value).astype(jnp.float32)
    )
    grad_cos = (logit_factor * grad_logits).astype(jnp.bfloat16)
    grad_queries = jnp.einsum("qk,kd->qd", grad_cos, documents, preferred_element_type=jnp.float32)
    grad_documents = jnp.einsum(
        "qk,qd->kd", grad_cos, query_rows, preferred_element_type=jnp.float32
    )
    grad_term = jnp.concatenate(
        [jnp.zeros((query_total, model_width), jnp.float32), grad_documents], 0
    )
    grad_term = lax.dynamic_update_slice_in_dim(grad_term, grad_queries, first_row, 0)
    own_grad = lax.psum_scatter(grad_term, ("tower", "dp"), scatter_dimension=0, tiled=True)
    grad_two = pool_back(own_grad)[0]
    grad_embed, layer_grads, norm_grads = layer_backward(
        grad_two, kept_vals, weights, norm_params, segment, positions
    )
    embed_low = grad_embed.astype(jnp.bfloat16)
    column_part = lax.dynamic_slice_in_dim(embed_low, model_idx * local_width, local_width, 1)
    row_start = data_idx * row_count
    all_ids = lax.all_gather(token_list, ("tower", "dp"), axis=0, tiled=True)
    piece_ids = all_ids - row_start
    inside = (piece_ids >= 0) & (piece_ids < row_count)
    slot_ids = jnp.where(inside, piece_ids, row_count)
    embed_grad = jax.ops.segment_sum(
        lax.all_gather(column_part, ("tower", "dp"), axis=0, tiled=True).astype(jnp.float32),
        slot_ids,
        num_segments=row_count + 1,
    )[:row_count]
    shard_grads = (
        lax.psum_scatter(layer_grads[0], ("tower", "dp"), scatter_dimension=0, tiled=True),
        lax.psum_scatter(layer_grads[1], ("tower", "dp"), scatter_dimension=0, tiled=True),
        lax.psum_scatter(layer_grads[2], ("tower", "dp"), scatter_dimension=0, tiled=True),
        lax.psum_scatter(layer_grads[3], ("tower", "dp"), scatter_dimension=0, tiled=True),
    )
    norm_grad, loss_sum, scale_grad = lax.psum((norm_grads, loss_part, scale_part), ("tower", "dp"))
    local_sq = sum((jnp.sum(gradient * gradient) for gradient in shard_grads)) + 0.5 * jnp.sum(
        embed_grad * embed_grad
    )
    total_sq = (
        lax.psum(local_sq, ("tower", "dp", "mp"))
        + jnp.sum(norm_grad * norm_grad)
        + scale_grad * scale_grad
    )
    grad_norm = jnp.sqrt(total_sq)
    factor = jnp.minimum(1.0, clip_max / (grad_norm + 1e-06))
    step_num = float(STEP)
    embed_new = plain_adamw(embedding, embed_grad, embed_m, embed_v, factor, step_num, learn_rate)
    qkv_new = plain_adamw(attn_in, shard_grads[0], attn_in_m, attn_in_v, factor, step_num, learn_rate)
    out_new = plain_adamw(attn_out, shard_grads[1], attn_out_m, attn_out_v, factor, step_num, out_rate)
    ffn_new = plain_adamw(ffn_in, shard_grads[2], ffn_in_m, ffn_in_v, factor, step_num, learn_rate)
    down_new = plain_adamw(ffn_out, shard_grads[3], ffn_out_m, ffn_out_v, factor, step_num, learn_rate)
    norms_new = plain_adamw(norm_params, norm_grad, norm_m, norm_v, factor, step_num, norm_rate)
    scale_new = plain_adamw(
        logit_scale, scale_grad.reshape(1), scale_m, scale_v, factor, step_num, learn_rate
    )
    return (
        embed_new[0],
        embed_new[1],
        embed_new[2],
        qkv_new[0],
        qkv_new[1],
        qkv_new[2],
        out_new[0],
        out_new[1],
        out_new[2],
        ffn_new[0],
        ffn_new[1],
        ffn_new[2],
        down_new[0],
        down_new[1],
        down_new[2],
        norms_new[0],
        norms_new[1],
        norms_new[2],
        scale_new[0],
        scale_new[1],
        scale_new[2],
        loss_sum.reshape(1),
        query_count.reshape(1),
        grad_norm.reshape(1),
    )


def lean_step(args, pos, heard):
    (
        token_ids, seq_lengths, positives, embedding, attn_in, attn_out, ffn_in, ffn_out,
        norm_params, logit_scale, embed_m, embed_v, attn_in_m, attn_in_v, attn_out_m, attn_out_v,
        ffn_in_m, ffn_in_v, ffn_out_m, ffn_out_v, norm_m, norm_v, scale_m, scale_v,
    ) = args
    tower_idx = lax.axis_index("tower")
    data_idx = lax.axis_index("dp")
    model_idx = lax.axis_index("mp")
    slot_count = seq_lengths.shape[2]
    tok = token_ids.shape[1]
    half = tok // 2
    row_count = embedding.shape[0]
    feats = attn_out.shape[1]
    ff = ffn_out.shape[1]
    part_ff = ff // 2

    shards = (
        attn_in.reshape(attn_in.shape[0], -1), attn_out, ffn_in[:, 0], ffn_in[:, 1], ffn_out,
    )
    kinds = ("plain", "late", "late", "late", "late")
    gather_pieces = [(0, "plain", 0, 3 * feats, 0)]
    quarter = ff // 4
    for turn, which in enumerate((2, 3, 4)):
        for c in range(4):
            kind = ("late", "early")[c % 2]
            gather_pieces.append((which, kind, c * quarter, quarter, 4 * turn + c))
    gather_pieces.append((1, "late", 0, feats, 6))
    places = (jnp.arange(tok, dtype=jnp.int32) + model_idx * half) % tok
    pos_rel = jnp.where(model_idx == 0, pos, jnp.concatenate([pos[half:], pos[:half]]))
    lengths_row = seq_lengths[tower_idx, data_idx]
    segment, positions = layout(lengths_row, places, slot_count)
    cosine, sine = rotary_tables(positions)
    seg_row, seg_col = segment[None, :], segment[:, None]
    named = heard[:, :, 0, : heard_room(tok, heard.shape[1])].reshape(2, 1, -1)
    kept, weights = forward_pass(
        embedding, heard[0], pos_rel[:, None], norm_params[0:2], cosine, sine, seg_row, seg_col,
        shards, kinds, gather_pieces,
    )
    emb, stream_zero, input_zero, query, key, value, lse = kept[:7]
    att = kept[7:9]
    w_qkv, w_out, w_gate, w_up, w_down = weights

    sum_one = stream_zero + tdot(att[0], w_out[0]) + tdot(att[1], w_out[1])
    hat_one, scale_one = norm_parts(sum_one)
    stream_one = hat_one * norm_params[2] + norm_params[3]
    input_one = stream_one.astype(bf16)
    gates = [mdot(input_one, w_gate[j]) for j in range(2)]
    ups = [mdot(input_one, w_up[j]) for j in range(2)]
    hidden = [glu(gates[j], ups[j]).astype(bf16) for j in range(2)]
    sum_two = stream_one + tdot(hidden[0], w_down[0]) + tdot(hidden[1], w_down[1])
    hat_two, scale_two = norm_parts(sum_two)
    stream_two = hat_two * norm_params[4] + norm_params[5]

    member = (segment[None, :half] == jnp.arange(slot_count, dtype=jnp.int32)[:, None]).astype(f32)
    counts = jnp.maximum(lengths_row, 1).astype(f32)[:, None]
    part = jnp.dot(member, stream_two, precision=highest)
    doc_ok = (seq_lengths[1].reshape(1, -1) > 0).astype(f32)
    query_ok = (seq_lengths[0].reshape(-1, 1) > 0).astype(f32)
    grad_pool, stats = loss_step(
        part, counts, doc_ok, query_ok, positives.reshape(-1, 1), logit_scale.reshape(1, 1)
    )
    loss_sum, query_count, scale_grad = stats[0, 0], stats[1, 0], stats[2, 0]

    def weight_grad(left, right):
        return jnp.einsum("td,tf->df", left, right, preferred_element_type=f32).astype(bf16)

    pieces = [(0, ("early", "late")[c % 2], c * quarter, quarter, c) for c in range(4)]
    out = hidden_back(
        grad_pool, seg_col[:half], hat_two, scale_two, norm_params, input_one, hat_one, scale_one,
        att, hidden, w_gate, w_up, w_down, pieces, 2,
    )
    grad_sum_one, attn_low, norms = out[:3]
    grad_out, later, r_down, squares = out[3:5], out[5:9], out[9], out[10]
    pieces = [
        (c // 4, ("early", "late")[c % 2], (c % 4) * quarter, quarter, c) for c in range(8)
    ] + [(2, "late", 0, feats, 8)]
    late_pieces = [(0, "plain", 0, 2 * feats, 0), (0, "plain", 2 * feats, feats, 0)]
    embed_grad, norm_sum, r_gate, r_up, r_out, r_qkv, total = backward_pass(
        attn_low, w_out, query, key, value, lse, cosine, sine, seg_row, seg_col, grad_sum_one,
        emb, norm_params[0:2], w_qkv, norms, squares, input_zero, pos_rel[None, :], named,
        later, grad_out, row_count, pieces, late_pieces,
    )
    norm_grad = norm_sum[:6]
    r_qkv = r_qkv.reshape(attn_in.shape)
    total_sq = total[0, 0] + scale_grad * scale_grad
    grad_norm = jnp.sqrt(total_sq)
    factor = jnp.minimum(1.0, clip_max / (grad_norm + 1e-06))
    step_num = float(STEP)
    embed_new = adamw(embedding, embed_grad, embed_m, embed_v, factor, step_num, learn_rate)
    qkv_new = adamw(attn_in, r_qkv, attn_in_m, attn_in_v, factor, step_num, learn_rate)
    out_new = adamw(attn_out, r_out, attn_out_m, attn_out_v, factor, step_num, out_rate)
    r_ffn = jnp.stack([r_gate, r_up], 1)
    ffn_new = adamw(ffn_in, r_ffn, ffn_in_m, ffn_in_v, factor, step_num, learn_rate)
    down_new = adamw(ffn_out, r_down, ffn_out_m, ffn_out_v, factor, step_num, learn_rate)
    norms_new = adamw(norm_params, norm_grad, norm_m, norm_v, factor, step_num, norm_rate)
    scale_new = adamw(
        logit_scale, scale_grad.reshape(1), scale_m, scale_v, factor, step_num, learn_rate
    )
    return (
        *embed_new, *qkv_new, *out_new, *ffn_new, *down_new, *norms_new, *scale_new,
        loss_sum.reshape(1), query_count.reshape(1), grad_norm.reshape(1),
    )


def local(*args):
    token_ids, embedding = args[0], args[3]
    n_dp = lax.axis_size("dp")
    room = heard_room(token_ids.shape[1], n_dp)
    pos, lists = name_rows(
        token_ids[0], lax.axis_index("dp"), n_dp, embedding.shape[0], room
    )
    heard, flag = exchange_lists(lists)
    return lax.cond(
        flag[1, 0] > 0,
        lambda values: plain_step(*values),
        lambda values: lean_step(values, pos, heard),
        args,
    )


def solution(mesh):
    table, rows3, rows2 = P("dp", "mp"), P(("tower", "dp"), None, "mp"), P(("tower", "dp"), "mp")
    weights = (table, rows3, rows2, rows3, rows2)
    moments = tuple(spec for spec in weights for _ in range(2))
    return jax.shard_map(
        local,
        mesh=mesh,
        in_specs=(P("tower", "dp"), P(), P()) + weights + (P(), P()) + moments + (P(),) * 4,
        out_specs=tuple(spec for spec in weights for _ in range(3)) + (P(),) * 9,
        check_vma=False,
    )
```

```python
import jax
import jax.numpy as jnp
from jax import lax
from jax.sharding import PartitionSpec as P
from jax.experimental import pallas as pl
from jax.experimental.pallas import tpu as pltpu

HDIM = 64
STEP = 5

norm_eps = 1e-06
cap_value = 3.4
clip_max = 0.01
beta_one = 0.9
beta_two = 0.999
learn_rate = 0.02
out_rate = 0.05
norm_rate = 0.3
decay_rate = 0.01
adam_eps = 1e-08
neg_large = -1e30
highest = lax.Precision.HIGHEST
f32 = jnp.float32
bf16 = jnp.bfloat16
MESH = pl.DeviceIdType.MESH
ANY = pl.BlockSpec(memory_space=pl.ANY)
VM = pl.BlockSpec(memory_space=pltpu.VMEM)


def sds(shape, dtype):
    return jax.ShapeDtypeStruct(shape, dtype)


def params(ident, limit=58):
    return pltpu.CompilerParams(
        collective_id=ident, has_side_effects=True, vmem_limit_bytes=limit << 20
    )


class Place:
    def __init__(self):
        self.n_dp = lax.axis_size("dp")
        self.count = self.n_dp.bit_length() - 1
        self.t = lax.axis_index("tower")
        self.d = lax.axis_index("dp")
        self.m = lax.axis_index("mp")
        self.bits = [(self.d // (1 << (self.count - 1 - j))) % 2 for j in range(self.count)]

    def across(self, dim):
        if dim == "t":
            return {"tower": 1 - self.t}
        if dim == "y":
            return {"mp": 1 - self.m}
        step = 1 << (self.count - 1 - dim)
        return {"dp": self.d + (1 - 2 * self.bits[dim]) * step}

    def mixed(self, rel):
        out = self.d
        for j in range(self.count):
            step = 1 << (self.count - 1 - j)
            if rel & step:
                out = out + (1 - 2 * self.bits[j]) * step
        return out


def remote(src, dst, send, recv, where):
    return pltpu.make_async_remote_copy(
        src_ref=src, dst_ref=dst, send_sem=send, recv_sem=recv, device_id=where, device_id_type=MESH
    )


def greet(peers):
    barrier = pltpu.get_barrier_semaphore()
    for where in peers:
        pl.semaphore_signal(barrier, inc=1, device_id=where, device_id_type=MESH)
    pl.semaphore_wait(barrier, len(peers))


def tdot(lhs, rhs):
    return lax.dot_general(lhs, rhs, (((1,), (1,)), ((), ())), preferred_element_type=f32)


def mdot(lhs, rhs):
    return jnp.dot(lhs, rhs, preferred_element_type=f32)


def every(ndim, cols):
    return (slice(None),) * (ndim - 1) + (cols,)


class Gather:
    def __init__(self, here, shard, full, other, order, cols, send, recv, local_sem):
        self.here, self.shard, self.full, self.other = here, shard, full, other
        self.order, self.cols, self.send, self.recv = order, cols, send, recv
        self.local_sem = local_sem
        self.last = len(order)
        self.done = set()
        self.live, self.sent = [], []
        self.arrays = [full]
        self.slot = 0

    def view(self):
        here = self.here
        return (
            (here.t,)
            + tuple(slice(None) if j in self.done else here.bits[j] for j in range(here.count))
            + (slice(None), self.cols)
        )

    def stage(self, step):
        here = self.here
        if step == 0:
            self.place = pltpu.make_async_copy(
                self.shard.at[:, self.cols], self.full.at[self.view()], self.local_sem
            )
            self.place.start()
        for copy in self.live:
            copy.wait_recv()
        if step == 1:
            self.place.wait()
        self.sent += self.live
        self.live = []
        if step == self.last:
            for copy in self.sent:
                copy.wait_send()
            return
        dim = self.order[step]
        if dim == "y":
            pairs = [(self.full.at[self.view()], self.other.at[self.view()])]
            self.arrays = [self.full, self.other]
        elif step == 0:
            pairs = [(self.shard.at[:, self.cols], self.full.at[self.view()])]
        else:
            pairs = [(ref.at[self.view()], ref.at[self.view()]) for ref in self.arrays]
        for src, dst in pairs:
            copy = remote(
                src, dst, self.send.at[self.slot], self.recv.at[self.slot], here.across(dim)
            )
            copy.start()
            self.live.append(copy)
            self.slot += 1
        if dim not in ("t", "y"):
            self.done.add(dim)


class Scatter:
    def __init__(self, here, own, other, order, cols, held, landed, out, send, recv, local_sems):
        self.here, self.order, self.cols = here, order, cols
        self.source = [own] if other is None else [own, other]
        self.held, self.landed, self.out = held, landed, out
        self.send, self.recv, self.local_sems = send, recv, local_sems
        self.last = len(order)
        self.fixed = {}
        self.live = []
        self.slot = 0
        self.arrays = list(range(len(self.source)))

    def view(self, extra=None):
        fixed = dict(self.fixed)
        if extra:
            fixed.update(extra)
        return tuple(fixed.get(j, slice(None)) for j in range(self.here.count))

    def start(self, src, where, index):
        copy = remote(
            src, self.landed[self.slot], self.send.at[self.slot], self.recv.at[self.slot], where
        )
        copy.start()
        self.live.append((copy, self.slot, index))
        self.slot += 1

    def stage(self, step):
        here = self.here
        if step > 0:
            self.finish(step - 1)
        if step == self.last:
            return
        dim = self.order[step]
        if dim == "t":
            self.loads = []
            tail = (slice(None),) * (here.count + 1) + (self.cols,)
            for index in self.arrays:
                load = pltpu.make_async_copy(
                    self.source[index].at[(here.t,) + tail], self.held[index],
                    self.local_sems.at[index],
                )
                load.start()
                self.loads.append(load)
                self.start(self.source[index].at[(1 - here.t,) + tail], here.across("t"), index)
        elif dim == "y":
            self.start(self.held[1].at[self.view()], here.across("y"), 0)
            self.arrays = [0]
        else:
            far = self.view({dim: 1 - here.bits[dim]})
            for index in self.arrays:
                self.start(self.held[index].at[far], here.across(dim), index)

    def finish(self, step):
        here = self.here
        dim = self.order[step]
        if dim not in ("t", "y"):
            self.fixed[dim] = here.bits[dim]
        view = self.view()
        if dim == "t":
            for load in self.loads:
                load.wait()
        for copy, slot, index in self.live:
            copy.wait()
            total = self.held[index][view].astype(f32) + self.landed[slot][...].astype(f32)
            if step == self.last - 1:
                self.out(self.cols, total)
            else:
                self.held[index][view] = total.astype(bf16)
        self.live = []


class Total:
    def __init__(self, here, value, landed, send, recv):
        self.here, self.value, self.landed, self.send, self.recv = here, value, landed, send, recv
        self.order = ["t", "y"] + list(range(here.count))
        self.last = len(self.order)

    def stage(self, step):
        if step > 0:
            self.copy.wait()
            self.value[...] += self.landed[step - 1]
        if step < self.last:
            self.copy = remote(
                self.value, self.landed.at[step], self.send.at[step], self.recv.at[step],
                self.here.across(self.order[step]),
            )
            self.copy.start()


class Runner:
    def __init__(self, jobs, lags, stride=1):
        self.jobs, self.lags, self.stride, self.tick = jobs, lags, stride, 0
        self.length = max(job.last * stride + lag for job, lag in zip(jobs, lags)) + 1

    def advance(self):
        if self.tick < self.length:
            for job, lag in zip(self.jobs, self.lags):
                since = self.tick - lag
                if since % self.stride == 0 and 0 <= since // self.stride <= job.last:
                    job.stage(since // self.stride)
            self.tick += 1

    def drain(self):
        while self.tick < self.length:
            self.advance()


def gather_orders(count):
    far, near = list(range(count - 1)), [count - 1]
    return {
        "plain": far + near + ["t"],
        "late": far + near + ["y", "t"],
        "early": far + ["y"] + near + ["t"],
        "cross": far[:-1] + near + ["y"] + far[-1:] + ["t"],
    }


def scatter_orders(count):
    near, far = [count - 1], list(range(count - 2, -1, -1))
    return {
        "plain": ["t"] + near + far,
        "early": ["t", "y"] + near + far,
        "late": ["t"] + near + ["y"] + far,
        "cross": ["t"] + far[:1] + ["y"] + near + far[1:],
    }


def scatter_lands(order, count, pair, rows, cols):
    shapes, free, live = [], count, 2 if pair else 1
    for dim in order:
        if dim == "y":
            live = 1
        elif dim != "t":
            free -= 1
        shapes += [(2,) * free + (rows, cols)] * live
    return shapes


def lists_body(lists, heard, flag, send, recv):
    here = Place()
    n = here.n_dp
    peers = []
    for rt in range(2):
        for k in range(n):
            if rt or k:
                peers.append((rt, k, {"tower": here.t + rt * (1 - 2 * here.t), "dp": here.mixed(k)}))
    greet([where for _, _, where in peers])
    copies = []
    for rt, k, where in peers:
        copy = remote(lists.at[k], heard.at[rt, k], send.at[rt, k], recv.at[rt, k], where)
        copy.start()
        copies.append(copy)
    heard[0, 0] = lists[0]
    for copy in copies:
        copy.wait()
    flag[...] = jnp.max(heard[...].reshape((2 * n,) + flag.shape), axis=0)


def heard_room(tok, n_dp):
    return max(32, tok // n_dp)


def exchange_lists(lists):
    n = lists.shape[0]
    dma = pltpu.SemaphoreType.DMA
    return pl.pallas_call(
        lists_body,
        out_shape=[sds((2,) + lists.shape, jnp.int32), sds(lists.shape[1:], jnp.int32)],
        in_specs=[VM],
        out_specs=[VM, VM],
        scratch_shapes=[dma((2, n)), dma((2, n))],
        compiler_params=params(1),
        name="lists",
    )(lists)


def turned(values):
    lanes = lax.broadcasted_iota(jnp.int32, values.shape, 1) % HDIM
    size = values.shape[1]
    return jnp.where(
        lanes < HDIM // 2,
        -pltpu.roll(values, size - HDIM // 2, 1),
        pltpu.roll(values, HDIM // 2, 1),
    )


def norm_parts(stream):
    average = jnp.mean(stream, -1, keepdims=True)
    centered = stream - average
    variance = jnp.mean(centered * centered, -1, keepdims=True)
    scale = lax.rsqrt(variance + norm_eps)
    return centered * scale, scale


def forward_body(room, kinds, pieces, stride, every, *refs):
    here = Place()
    n, count = here.n_dp, here.count
    table, heard, pos, norm_rows, cosine, sine, seg_row, seg_col = refs[:8]
    attn_in, attn_out, ffn_in, ffn_out = refs[8:12]
    emb_out, zero_out, input_out, q_out, k_out, v_out, lse_out, att_own, att_other = refs[12:21]
    fulls, at = [], 21
    for kind in kinds:
        width = 1 if kind == "plain" else 2
        fulls.append((refs[at], None) if width == 1 else (refs[at], refs[at + 1]))
        at += width
    low_table, served, rows, vt, att_far = refs[at : at + 5]
    lows = refs[at + 5 : at + 10]
    rsem, ysem, asem, wsend, wrecv, wlocal = refs[at + 10 :]
    tok = pos.shape[0]
    half = tok // 2
    width = rows.shape[3]
    slots = n * room
    feats = q_out.shape[1]
    groups = feats // 128
    block = 256

    greet(
        [{"dp": here.mixed(k)} for k in range(1, n)] + [here.across("t"), here.across("y")]
    )
    orders = gather_orders(count)
    for c in range(3):
        lows[0][:, c * feats : (c + 1) * feats] = attn_in[:, c, :].astype(bf16)
    lows[1][...] = attn_out[...].astype(bf16)
    for c in range(2):
        lows[2 + c][...] = ffn_in[:, c, :].astype(bf16)
    lows[4][...] = ffn_out[...].astype(bf16)
    jobs, lags = [], []
    for number, (which, kind, start, size, lag) in enumerate(pieces):
        jobs.append(
            Gather(
                here, lows[which], fulls[which][0], fulls[which][1], orders[kind],
                pl.ds(start, size), wsend.at[number], wrecv.at[number], wlocal.at[number],
            )
        )
        lags.append(lag)
    first = Runner(jobs[:1], lags[:1])
    runner = Runner(jobs[1:], lags[1:], stride)
    first.advance()
    runner.advance()
    low_table[...] = table[...].astype(bf16)
    row_count = table.shape[0]
    out_copies, y_copies = [], []

    def pass_on(k):
        copy = remote(
            rows.at[here.m, k], rows.at[here.m, k], ysem.at[0, k], ysem.at[1, k], here.across("y")
        )
        copy.start()
        y_copies.append(copy)

    for k in list(range(n - 1, 0, -1)) + [0]:
        column = jnp.transpose(heard[0, k])[:room, 0:1]
        hot = (lax.broadcasted_iota(jnp.int32, (room, row_count), 1) == column).astype(f32)
        found = mdot(hot.astype(bf16), low_table[...]).astype(bf16)
        if k == 0:
            rows[here.m, 0] = found
            pass_on(0)
        else:
            served[k] = found
            copy = remote(
                served.at[k], rows.at[here.m, k], rsem.at[0, k], rsem.at[1, k],
                {"dp": here.mixed(k)},
            )
            copy.start()
            out_copies.append(copy)
            if k % 2:
                runner.advance()
        if k == n // 2:
            first.advance()
    first.advance()
    for k in range(n - 1, 0, -1):
        out_copies[n - 1 - k].wait_recv()
        pass_on(k)
        if k % 3 == 1:
            runner.advance()
    first.drain()
    for copy in out_copies:
        copy.wait_send()
    for copy in y_copies:
        copy.wait()

    w_qkv = fulls[0][0]
    for i in range(tok // block):
        at = slice(i * block, (i + 1) * block)
        hot = (lax.broadcasted_iota(jnp.int32, (block, slots), 1) == pos[at, :]).astype(f32)
        hot = hot.astype(bf16)
        emb = jnp.concatenate([mdot(hot, rows[h].reshape(slots, width)) for h in range(2)], 1)
        hat, _scale = norm_parts(emb)
        stream = hat * norm_rows[0:1, :] + norm_rows[1:2, :]
        low = stream.astype(bf16)
        input_out[at, :] = low
        if (i + 1) * block <= half:
            emb_out[at, :] = emb.astype(bf16)
            zero_out[at, :] = stream
        cos, sin = cosine[at, :], sine[at, :]
        proj = mdot(low, w_qkv[...].reshape(2 * width, 3 * feats))
        for c in range(3):
            for g in range(groups):
                cols = slice(g * 128, (g + 1) * 128)
                part = proj[:, c * feats + g * 128 : c * feats + (g + 1) * 128]
                if c < 2:
                    part = part * cos + turned(part) * sin
                part = part.astype(bf16)
                if c == 0:
                    q_out[at, cols] = part * bf16(HDIM**-0.5)
                elif c == 1:
                    k_out[at, cols] = part
                else:
                    v_out[at, cols] = part
        if i % every == every - 1:
            runner.advance()

    lane = lax.broadcasted_iota(jnp.int32, (1, 128), 1)
    att_copies = []
    for g in range(groups):
        cols = slice(g * 128, (g + 1) * 128)
        vt[...] = jnp.transpose(v_out[:, cols].astype(f32)).astype(bf16)
        keys = [jnp.where((lane // HDIM) == h, k_out[:, cols], bf16(0)) for h in range(2)]
        for i in list(range(tok // block // 2, tok // block)) + list(range(tok // block // 2)):
            at = slice(i * block, (i + 1) * block)
            query = q_out[at, cols]
            same = seg_col[...] == seg_row[:, at]
            outs = []
            for h in range(2):
                scores = jnp.where(same, tdot(keys[h], query), neg_large)
                peak = jnp.max(scores, 0, keepdims=True)
                soft = jnp.exp(scores - peak)
                total = jnp.sum(soft, 0, keepdims=True)
                lse_out[2 * g + h, :, at] = peak + jnp.log(total)
                soft = (soft * (1.0 / total)).astype(bf16)
                outs.append(mdot(vt[h * HDIM : (h + 1) * HDIM, :], soft))
            found = jnp.transpose(jnp.concatenate(outs, 0)).astype(bf16)
            if i * block < half:
                att_own[at, cols] = found
            else:
                att_far[slice(i * block - half, (i + 1) * block - half), cols] = found
                if (i + 1) * block == tok:
                    copy = remote(
                        att_far.at[:, cols], att_other.at[:, cols], asem.at[0, g], asem.at[1, g],
                        here.across("y"),
                    )
                    copy.start()
                    att_copies.append(copy)
            if i % every == every - 1:
                runner.advance()
    runner.drain()
    for copy in att_copies:
        copy.wait()


def forward_pass(table, heard, pos, norm_rows, cosine, sine, seg_row, seg_col, raw, kinds, pieces,
                 stride=3, every=1):
    n_dp = heard.shape[1]
    attn_in, attn_out, ffn_in, ffn_out = raw
    rows = attn_in.shape[0]
    shards = (
        sds((rows, 3 * attn_in.shape[2]), f32), sds(attn_out.shape, f32),
        sds(ffn_out.shape, f32), sds(ffn_out.shape, f32), sds(ffn_out.shape, f32),
    )
    room = heard_room(pos.shape[0], n_dp)
    count = n_dp.bit_length() - 1
    halves = (2,) * (count + 1)
    tok = pos.shape[0]
    half = tok // 2
    width = table.shape[1]
    feats = shards[0].shape[1] // 3
    outs = [
        sds((half, 2 * width), bf16),
        sds((half, 2 * width), f32),
        sds((tok, 2 * width), bf16),
        sds((tok, feats), bf16),
        sds((tok, feats), bf16),
        sds((tok, feats), bf16),
        sds((feats // HDIM, 1, tok), f32),
        sds((half, feats), bf16),
        sds((half, feats), bf16),
    ]
    specs = [VM] * len(outs)
    for shard, kind in zip(shards, kinds):
        full = sds(halves + shard.shape, bf16)
        outs += [full] if kind == "plain" else [full, full]
        specs += [VM] if kind == "plain" else [ANY, ANY]
    dma = pltpu.SemaphoreType.DMA
    steps = count + 6
    scratch = (
        [
            pltpu.VMEM(table.shape, bf16),
            pltpu.VMEM((n_dp, room, width), bf16),
            pltpu.VMEM((2, n_dp, room, width), bf16),
            pltpu.VMEM((128, tok), bf16),
            pltpu.VMEM((half, feats), bf16),
        ]
        + [pltpu.VMEM(shard.shape, bf16) for shard in shards]
        + [dma((2, n_dp)), dma((2, n_dp)), dma((2, feats // 128))]
        + [dma((len(pieces), steps)), dma((len(pieces), steps)), dma((len(pieces),))]
    )
    out = pl.pallas_call(
        lambda *refs: forward_body(room, kinds, pieces, stride, every, *refs),
        out_shape=outs,
        in_specs=[VM] * 12,
        out_specs=specs,
        scratch_shapes=scratch,
        compiler_params=params(2),
        name="forward",
    )(table, heard, pos, norm_rows, cosine, sine, seg_row, seg_col, *raw)
    weights, at = [], 9
    for shard, kind in zip(shards, kinds):
        whole = (2 * n_dp * shard.shape[0], shard.shape[1])
        if kind == "plain":
            weights.append(out[at].reshape(whole))
            at += 1
        else:
            weights.append((out[at].reshape(whole), out[at + 1].reshape(whole)))
            at += 2
    return out[:9], weights


def writer(ref, kind=None):
    def store(cols, values):
        if kind is None:
            ref[:, cols] = values
        else:
            ref[:, kind, cols] = values

    return store


def make_scatters(
    here, grads, kinds, pieces, outs, held, landed, send, recv, loads, stride=1
):
    orders = scatter_orders(here.count)
    jobs, lags = [], []
    held, landed = list(held), list(landed)
    for number, (which, kind, start, size, lag) in enumerate(pieces):
        own, other = grads[which]
        pair = other is not None
        mine = [held.pop(0) for _ in range(2 if pair else 1)]
        amount = len(scatter_lands(orders[kind], here.count, pair, 1, 1))
        lands = [landed.pop(0) for _ in range(amount)]
        jobs.append(
            Scatter(
                here, own, other, orders[kind], pl.ds(start, size), mine, lands, outs[which],
                send.at[number], recv.at[number], loads.at[number],
            )
        )
        lags.append(lag)
    return Runner(jobs, lags, stride)


def scatter_scratch(count, rows, pairs, pieces):
    orders = scatter_orders(count)
    held, landed = [], []
    for which, kind, _start, size, _lag in pieces:
        pair = pairs[which]
        held += [pltpu.VMEM((2,) * count + (rows, size), bf16)] * (2 if pair else 1)
        landed += [
            pltpu.VMEM(shape, bf16)
            for shape in scatter_lands(orders[kind], count, pair, rows, size)
        ]
    dma = pltpu.SemaphoreType.DMA
    steps = 2 * count + 6
    sems = [dma((len(pieces), steps)), dma((len(pieces), steps)), dma((len(pieces), 2))]
    return held, landed, sems


def square_sum(values):
    return jnp.sum(jnp.sum(values * values, 0, keepdims=True), 1, keepdims=True)


def store_blocks(ref, values, count, start):
    rows, cols = ref.shape[-2], values.shape[1]
    for number in range(2 ** (count + 1)):
        at = tuple((number >> (count - j)) & 1 for j in range(count + 1))
        ref[at + (slice(None), slice(start, start + cols))] = values[
            number * rows : (number + 1) * rows, :
        ].astype(bf16)


def hidden_body(pieces, sizes, stride, *refs):
    here = Place()
    count = here.count
    (grad_pool, seg, sum_two, norm_rows, low_one, sum_one,
     att_own, att_other, hidden_own, hidden_other) = refs[:10]
    weights = refs[10:16]
    residual, low_out, norms_out, wout_own, wout_other = refs[16:21]
    later = refs[21:25]
    out_down, squares = refs[25:27]
    loaded, down, low_two, turned_one, turned_two, total = refs[27:33]
    held = refs[33 : 33 + sizes[0]]
    landed = refs[33 + sizes[0] : 33 + sizes[0] + sizes[1]]
    wsem, send, recv, loads = refs[33 + sizes[0] + sizes[1] :]
    half, width = low_one.shape
    part = weights[0].shape[1] // 2
    copies = {}

    def load(c, j):
        for w in range(3):
            copies[c, j, w] = pltpu.make_async_copy(
                weights[2 * w + j].at[:, pl.ds(c * part, part)], loaded.at[j * 3 + w],
                wsem.at[(c * 2 + j) * 3 + w],
            )
            copies[c, j, w].start()

    load(0, 0)
    load(0, 1)
    greet([here.across("t"), here.across("y")] + [here.across(j) for j in range(count)])
    grads = [(down.at[0], down.at[1])]
    runner = make_scatters(
        here, grads, None, pieces, (writer(out_down),), held, landed, send, recv, loads, stride
    )
    slots = grad_pool.shape[0]
    hot = (lax.broadcasted_iota(jnp.int32, (half, slots), 1) == seg[0:half, :]).astype(f32)
    grad_two = jnp.dot(hot, grad_pool[...], precision=highest, preferred_element_type=f32)
    hat, scale = norm_parts(sum_two[...])
    grad_hat = grad_two * norm_rows[4:5, :]
    first = jnp.mean(grad_hat, -1, keepdims=True)
    second = jnp.mean(grad_hat * hat, -1, keepdims=True)
    grad_sum = scale * (grad_hat - first - hat * second)
    low_two[...] = grad_sum.astype(bf16)
    turned_two[...] = jnp.transpose(grad_sum).astype(bf16)
    for c in range(2):
        for j, hidden in enumerate((hidden_own, hidden_other)):
            cols = slice(c * part, (c + 1) * part)
            store_blocks(down.at[j], mdot(turned_two[...], hidden[:, cols]), count, c * part)
        runner.advance()
    norms_out[...] = jnp.zeros_like(norms_out)
    norms_out[4:5, :] = jnp.sum(grad_two * hat, 0, keepdims=True)
    norms_out[5:6, :] = jnp.sum(grad_two, 0, keepdims=True)
    turned_one[...] = jnp.transpose(low_one[...].astype(f32)).astype(bf16)
    total[...] = grad_sum
    runner.advance()
    for c in range(2):
        for j in range(2):
            number = j * 3
            for w in range(3):
                copies[c, j, w].wait()
            gate = mdot(low_one[...], loaded[number])
            up = mdot(low_one[...], loaded[number + 1])
            share = 1.0 / (1.0 + jnp.exp(-gate))
            grad_hidden = mdot(low_two[...], loaded[number + 2])
            grad_up = (grad_hidden * (gate * share)).astype(bf16)
            grad_gate = (
                grad_hidden * up * (share * (1.0 + gate * (1.0 - share)))
            ).astype(bf16)
            runner.advance()
            store_blocks(later[j], mdot(turned_one[...], grad_gate), count, c * part)
            store_blocks(later[2 + j], mdot(turned_one[...], grad_up), count, c * part)
            total[...] += tdot(grad_gate, loaded[number]) + tdot(grad_up, loaded[number + 1])
            if c == 0:
                load(1, j)
            runner.advance()
    hat, scale = norm_parts(sum_one[...])
    grad_one = total[...]
    grad_hat = grad_one * norm_rows[2:3, :]
    first = jnp.mean(grad_hat, -1, keepdims=True)
    second = jnp.mean(grad_hat * hat, -1, keepdims=True)
    grad_sum = scale * (grad_hat - first - hat * second)
    norms_out[2:3, :] = jnp.sum(grad_one * hat, 0, keepdims=True)
    norms_out[3:4, :] = jnp.sum(grad_one, 0, keepdims=True)
    residual[...] = grad_sum
    low_out[...] = grad_sum.astype(bf16)
    runner.advance()
    turned_two[...] = jnp.transpose(grad_sum).astype(bf16)
    wout_own[...] = mdot(turned_two[...], att_own[...]).astype(bf16)
    runner.advance()
    wout_other[...] = mdot(turned_two[...], att_other[...]).astype(bf16)
    runner.drain()
    squares[...] = jnp.broadcast_to(square_sum(out_down[...]), squares.shape)


def hidden_back(grad_pool, seg, sum_two, norm_rows, low_one, sum_one, att, hidden, w_gate, w_up,
                w_down, pieces, stride=1):
    n_dp = lax.axis_size("dp")
    count = n_dp.bit_length() - 1
    half, width = low_one.shape
    feats = att[0].shape[1]
    cols = w_gate[0].shape[1]
    rows = width // (2 * n_dp)
    blocks = (2,) * (count + 1) + (rows, cols)
    held, landed, sems = scatter_scratch(count, rows, [True], pieces)
    vmem = pltpu.VMEM
    return pl.pallas_call(
        lambda *refs: hidden_body(pieces, (len(held), len(landed)), stride, *refs),
        out_shape=[
            sds((half, width), f32), sds((half, width), bf16), sds((8, width), f32),
            sds((width, feats), bf16), sds((width, feats), bf16),
        ] + [sds(blocks, bf16)] * 4 + [sds((rows, cols), f32), sds((8, 128), f32)],
        in_specs=[VM] * 10 + [ANY] * 6,
        out_specs=[VM] * 11,
        scratch_shapes=[
            vmem((6, width, cols // 2), bf16), vmem((2,) + blocks, bf16), vmem((half, width), bf16),
            vmem((width, half), bf16), vmem((width, half), bf16), vmem((half, width), f32),
        ] + held + landed + [pltpu.SemaphoreType.DMA((12,))] + sems,
        compiler_params=params(6),
        name="hidden",
    )(grad_pool, seg, sum_two, norm_rows, low_one, sum_one, *att, *hidden,
      *w_gate, *w_up, *w_down)


def backward_body(room, pieces, late_pieces, sizes, stride, every, *refs):
    here = Place()
    n, count = here.n_dp, here.count
    (low, out_own, out_other, query, key, value, lse, cosine, sine, seg_row, seg_col, residual,
     emb, norm_rows, w_qkv, norms_in, before, inputs, pos, heard) = refs[:20]
    grads = [(refs[20 + 2 * j], refs[21 + 2 * j]) for j in range(3)]
    (table_out, norms_out, out_ffn, out_proj, out_qkv, total_out) = refs[26:32]
    refs = refs[:26] + (None,) + refs[26:]
    (kt, dq, dk, dv, grad_att, far_att, far_send, far_recv, grad_proj, turned_in, grad_qkv,
     low_out, norm_part, other, packed, mine, theirs, norms, parts, own_part) = refs[33:53]
    at = 53
    cuts = []
    for size in sizes:
        cuts.append(refs[at : at + size])
        at += size
    held, landed, late_held, late_landed = cuts
    (asem, bsem, ysem, rsem, csem, nsem, tsem, send, recv, loads, late_send, late_recv,
     late_loads) = refs[at:]
    tok, feats = query.shape
    half, width = tok // 2, table_out.shape[1]
    groups = feats // 128
    block = 256
    peers = []
    for rt in range(2):
        for rd in range(n):
            for rm in range(2):
                if rt or rd or rm:
                    where = {
                        "tower": here.t + rt * (1 - 2 * here.t),
                        "dp": here.mixed(rd),
                        "mp": here.m + rm * (1 - 2 * here.m),
                    }
                    peers.append(((rt * n + rd) * 2 + rm, where))
    me = (here.t * n + here.d) * 2 + here.m
    greet([where for _, where in peers])
    runner = make_scatters(
        here, grads, None, pieces, (writer(out_ffn, 0), writer(out_ffn, 1), writer(out_proj)), held,
        landed, send, recv, loads, stride,
    )
    runner.advance()
    att_copies = []
    far_att[...] = mdot(low[...], out_other[...]).astype(bf16)
    for g in range(groups):
        cols = slice(g * 128, (g + 1) * 128)
        copy = remote(
            far_att.at[:, cols], grad_att.at[half:, cols], asem.at[0, g], asem.at[1, g],
            here.across("y"),
        )
        copy.start()
        att_copies.append(copy)
    grad_att[:half, :] = mdot(low[...], out_own[...]).astype(bf16)
    for i in range(tok // block):
        rows = slice(i * block, (i + 1) * block)
        turned_in[:, rows] = jnp.transpose(inputs[rows, :].astype(f32)).astype(bf16)
    runner.advance()
    lane = lax.broadcasted_iota(jnp.int32, (1, 128), 1)
    for g in range(groups):
        cols = slice(g * 128, (g + 1) * 128)
        kt[...] = jnp.transpose(key[:, cols].astype(f32)).astype(bf16)
        keys = [jnp.where((lane // HDIM) == h, key[:, cols], bf16(0)) for h in range(2)]
        values = [jnp.where((lane // HDIM) == h, value[:, cols], bf16(0)) for h in range(2)]
        for i in range(tok // block):
            if i * block == half:
                att_copies[g].wait_recv()
            rows = slice(i * block, (i + 1) * block)
            q_part = query[rows, cols]
            g_part = grad_att[rows, cols]
            same = seg_col[...] == seg_row[:, rows]
            turns = []
            add_k, add_v = None, None
            for h in range(2):
                inside = (lane // HDIM) == h
                scores = jnp.where(same, tdot(keys[h], q_part), neg_large)
                soft = jnp.exp(scores - lse[2 * g + h, :, rows])
                grad_soft = tdot(values[h], g_part)
                inner = jnp.sum(soft * grad_soft, 0, keepdims=True)
                grad_scores = (soft * (grad_soft - inner)).astype(bf16)
                part_v = mdot(soft.astype(bf16), jnp.where(inside, g_part, bf16(0)))
                part_k = mdot(grad_scores, jnp.where(inside, q_part, bf16(0)))
                add_v = part_v if h == 0 else add_v + part_v
                add_k = part_k if h == 0 else add_k + part_k
                turns.append(mdot(kt[h * HDIM : (h + 1) * HDIM, :], grad_scores))
            dq[rows, :] = jnp.transpose(jnp.concatenate(turns, 0)) * (HDIM**-0.5)
            if i == 0:
                dv[...] = add_v
                dk[...] = add_k
            else:
                dv[...] += add_v
                dk[...] += add_k
            if i % every == every - 1:
                runner.advance()
        cos, sin = cosine[...], sine[...]
        for c, grad in ((0, dq), (1, dk)):
            whole = grad[...]
            back = whole * cos - turned(whole) * sin
            grad_proj[:, c * feats + g * 128 : c * feats + (g + 1) * 128] = back.astype(bf16)
        grad_proj[:, 2 * feats + g * 128 : 2 * feats + (g + 1) * 128] = dv[...].astype(bf16)
    for copy in att_copies:
        copy.wait_send()
    far_copies = []
    for i in range(half // block):
        rows = slice(i * block, (i + 1) * block)
        far = grad_proj[half + i * block : half + (i + 1) * block, :]
        far_send[rows, :] = tdot(far, w_qkv[...]).astype(bf16)
        copy = remote(
            far_send.at[rows, :], far_recv.at[rows, :], bsem.at[0, i], bsem.at[1, i],
            here.across("y"),
        )
        copy.start()
        far_copies.append(copy)
    grad_parts = [grad_qkv.at[c] for c in range(3)]
    late = make_scatters(
        here, [(part, None) for part in grad_parts], None, late_pieces,
        [writer(out_qkv, c) for c in range(3)], late_held, late_landed, late_send, late_recv,
        late_loads, 1,
    )
    jobs = late.jobs
    step = feats if grad_qkv.shape[-2] % 16 == 0 else 128
    for start in range(0, 3 * feats, step):
        cols = slice(start, start + step)
        store_blocks(
            grad_parts[start // feats], mdot(turned_in[...], grad_proj[:, cols]), count,
            start % feats,
        )
    late.advance()
    runner.advance()
    theirs_at = pl.ds(pl.multiple_of((1 - here.m) * width, 128), width)
    mine_at = pl.ds(pl.multiple_of(here.m * width, 128), width)
    norm_part[...] = norms_in[...]
    swaps = []
    for i in range(half // block):
        rows = slice(i * block, (i + 1) * block)
        near = residual[rows, :] + tdot(grad_proj[rows, :], w_qkv[...])
        if i == 0:
            runner.advance()
        far_copies[i].wait()
        near = near + far_recv[rows, :].astype(f32)
        hat, scale = norm_parts(emb[rows, :].astype(f32))
        grad_hat = near * norm_rows[0:1, :]
        first = jnp.mean(grad_hat, -1, keepdims=True)
        second = jnp.mean(grad_hat * hat, -1, keepdims=True)
        low_out[rows, :] = (scale * (grad_hat - first - hat * second)).astype(bf16)
        copy = remote(
            low_out.at[rows, theirs_at], other.at[rows, :], ysem.at[0, i], ysem.at[1, i],
            here.across("y"),
        )
        copy.start()
        swaps.append(copy)
        norm_part[0:1, :] += jnp.sum(near * hat, 0, keepdims=True)
        norm_part[1:2, :] += jnp.sum(near, 0, keepdims=True)
    jobs.append(Total(here, norm_part, norms, nsem.at[0], nsem.at[1]))
    late.lags.append(late.tick)
    late.length = max(late.length, late.tick + jobs[-1].last + 1)
    late.advance()
    runner.advance()
    for copy in swaps:
        copy.wait()
    both = jnp.concatenate([low_out[:, mine_at], other[...]], 0)
    copies = []
    for k in list(range(n - 1, 0, -1)) + [0]:
        hot = (
            lax.broadcasted_iota(jnp.int32, (room, pos.shape[1]), 0) + k * room == pos[...]
        ).astype(f32)
        packed[k] = mdot(hot.astype(bf16), both).astype(bf16)
        if k:
            copy = remote(
                packed.at[k], mine.at[k], rsem.at[0, k], rsem.at[1, k], {"dp": here.mixed(k)}
            )
        else:
            mine[0] = packed[0]
            copy = remote(mine.at[0], theirs.at[0], csem.at[0, 0], csem.at[1, 0], here.across("t"))
        copy.start()
        copies.append(copy)
    passed = [copies.pop()]
    late.advance()
    runner.advance()
    for k in range(n - 1, 0, -1):
        copies[n - 1 - k].wait_recv()
        copy = remote(mine.at[k], theirs.at[k], csem.at[0, k], csem.at[1, k], here.across("t"))
        copy.start()
        passed.append(copy)
        if k == n // 2:
            late.advance()
            runner.advance()
    late.advance()
    runner.advance()
    for copy in copies:
        copy.wait_send()
    for copy in passed:
        copy.wait()
    slots = n * room
    row_count = table_out.shape[0]
    size = 424 * 1024 // max(slots, 1024) // 8 * 8
    own_part[...] = jnp.zeros_like(own_part)
    for part in range(-(-row_count // size)):
        rows = slice(part * size, min((part + 1) * size, row_count))
        block_rows = rows.stop - rows.start
        base = lax.broadcasted_iota(jnp.int32, (block_rows, slots), 0) + part * size
        found = 0.0
        for source, sums in ((0, mine), (1, theirs)):
            hot = (base == heard[source]).astype(f32).astype(bf16)
            found = found + mdot(hot, sums[...].reshape(slots, width))
        table_out[rows, :] = found
        own_part[0:1, :] += jnp.sum(found * found, 0, keepdims=True)
        if part % 2:
            late.advance()
            runner.advance()
    late.drain()
    runner.drain()
    norms_out[...] = norm_part[...]
    local_sq = (
        before[0:1, 0:1]
        + 0.5 * jnp.sum(own_part[...], 1, keepdims=True)[0:1]
        + square_sum(out_proj[...])
        + sum(square_sum(out_qkv[:, c, :]) for c in range(3))
        + sum(square_sum(out_ffn[:, c, :]) for c in range(2))
    )
    parts[me] = jnp.broadcast_to(local_sq, parts.shape[1:])
    copies = []
    for rel, where in peers:
        copy = remote(parts.at[me], parts.at[me], tsem.at[0, rel], tsem.at[1, rel], where)
        copy.start()
        copies.append(copy)
    for copy in copies:
        copy.wait()
    total_out[...] = jnp.sum(parts[...], 0) + square_sum(norms_out[...])


def blocks_of(grad, n_dp):
    count = n_dp.bit_length() - 1
    rows = grad.shape[0] // (2 * n_dp)
    return grad.reshape((2,) * (count + 1) + (rows, grad.shape[1]))


def backward_pass(low, w_out, query, key, value, lse, cosine, sine, seg_row, seg_col, residual,
                  emb, norm_rows, w_qkv, norms, before, inputs, pos_row, heard, grads, grad_out,
                  row_count, pieces, late_pieces, stride=3, every=1):
    n_dp = lax.axis_size("dp")
    count = n_dp.bit_length() - 1
    tok, feats = query.shape
    half, width = low.shape
    rows, cols = grads[0].shape[-2:]
    room = heard_room(tok, n_dp)
    held, landed, sems = scatter_scratch(count, rows, [True] * 3, pieces)
    late_held, late_landed, late_sems = scatter_scratch(count, rows, [False] * 3, late_pieces)
    flat = list(grads) + [blocks_of(g, n_dp) for g in grad_out]
    dma = pltpu.SemaphoreType.DMA
    vmem = pltpu.VMEM
    sizes = (len(held), len(landed), len(late_held), len(late_landed))
    steps = max(1, half // 256)
    part = width // 2
    return pl.pallas_call(
        lambda *refs: backward_body(room, pieces, late_pieces, sizes, stride, every, *refs),
        out_shape=[
            sds((row_count, part), f32), sds((8, width), f32),
            sds((rows, 2, cols), f32), sds((rows, feats), f32), sds((rows, 3, feats), f32),
            sds((8, 128), f32),
        ],
        in_specs=[VM] * 20 + [ANY] * 6,
        out_specs=[VM] * 6,
        scratch_shapes=[
            vmem((128, tok), bf16), vmem((tok, 128), f32), vmem((tok, 128), f32),
            vmem((tok, 128), f32), vmem((tok, feats), bf16), vmem((half, feats), bf16),
            vmem((half, width), bf16), vmem((half, width), bf16),
            vmem((tok, 3 * feats), bf16), vmem((width, tok), bf16),
            vmem((3,) + (2,) * (count + 1) + (rows, feats), bf16),
            vmem((half, width), bf16), vmem((8, width), f32), vmem((half, part), bf16),
            vmem((n_dp, room, part), bf16), vmem((n_dp, room, part), bf16),
            vmem((n_dp, room, part), bf16), vmem((count + 2, 8, width), f32),
            vmem((4 * n_dp, 8, 128), f32), vmem((8, part), f32),
        ] + held + landed + late_held + late_landed
        + [dma((2, feats // 128)), dma((2, steps)), dma((2, steps)), dma((2, n_dp)),
           dma((2, n_dp)), dma((2, count + 2)), dma((2, 4 * n_dp))] + sems + late_sems,
        compiler_params=params(4, 60),
        name="backward",
    )(low, w_out[0], w_out[1], query, key, value, lse, cosine, sine, seg_row, seg_col, residual,
      emb, norm_rows, w_qkv, norms, before, inputs, pos_row, heard, *flat)


def loss_body(part, counts, doc_ok, query_ok, target, scale, grad_out, stats, other, low_all, turn,
              psend, precv, esend, erecv):
    here = Place()
    n = here.n_dp
    slots, width = part.shape
    peers = []
    for rt in range(2):
        for rd in range(n):
            if rt or rd:
                peers.append(
                    (rt * n + rd, {"tower": here.t + rt * (1 - 2 * here.t), "dp": here.mixed(rd)})
                )
    greet([where for _, where in peers] + [here.across("y")])
    copy = remote(part, other, psend, precv, here.across("y"))
    copy.start()
    copy.wait()
    pooled = (part[...] + other[...]) / counts[...]
    scale_row = lax.rsqrt(jnp.sum(pooled * pooled, 1, keepdims=True) + 1e-06)
    unit = pooled * scale_row
    low_all[here.t, here.d] = unit.astype(bf16)
    copies = []
    for rel, where in peers:
        copy = remote(
            low_all.at[here.t, here.d], low_all.at[here.t, here.d], esend.at[rel], erecv.at[rel], where
        )
        copy.start()
        copies.append(copy)
    for copy in copies:
        copy.wait()
    total = n * slots
    queries = low_all[0].reshape(total, width)
    documents = low_all[1].reshape(total, width)
    cosines = tdot(queries, documents)
    factor = jnp.exp(jnp.minimum(scale[...], cap_value))
    logits = jnp.where(doc_ok[...] > 0, factor * cosines, neg_large)
    peak = jnp.max(logits, 1, keepdims=True)
    log_total = peak + jnp.log(jnp.sum(jnp.exp(logits - peak), 1, keepdims=True))
    soft = jnp.exp(logits - log_total)
    mask = lax.broadcasted_iota(jnp.int32, (total, total), 1) == target[...]
    picked = jnp.sum(jnp.where(mask, logits, 0.0), 1, keepdims=True)
    valid = query_ok[...] > 0
    query_count = jnp.sum(valid.astype(f32), axis=0, keepdims=True)
    loss_sum = jnp.sum(jnp.where(valid, log_total - picked, 0.0), axis=0, keepdims=True)
    grad_logits = jnp.where(valid, soft - mask.astype(f32), 0.0) / query_count
    by_row = jnp.sum(grad_logits * cosines, 1, keepdims=True)
    grad_scale = (
        jnp.sum(by_row, 0, keepdims=True) * factor * (scale[...] < cap_value).astype(f32)
    )
    grad_cos = factor * grad_logits
    at = pl.ds(pl.multiple_of(here.d * slots, slots), slots)
    turn[0] = grad_cos
    turn[1] = jnp.transpose(grad_cos)
    left = turn[here.t, at, :].astype(bf16)
    right = low_all[1 - here.t].reshape(total, width)
    grad_unit = mdot(left, right)
    grad_pooled = scale_row * (
        grad_unit - unit * jnp.sum(unit * grad_unit, 1, keepdims=True)
    )
    grad_out[...] = grad_pooled / counts[...]
    row = lax.broadcasted_iota(jnp.int32, stats.shape, 0)
    stats[...] = jnp.where(row == 0, loss_sum, jnp.where(row == 1, query_count, grad_scale))


def loss_step(part, counts, doc_ok, query_ok, target, scale):
    n_dp = lax.axis_size("dp")
    slots, width = part.shape
    total = n_dp * slots
    dma = pltpu.SemaphoreType.DMA
    return pl.pallas_call(
        loss_body,
        out_shape=[sds(part.shape, f32), sds((8, 128), f32)],
        in_specs=[VM] * 6,
        out_specs=[VM] * 2,
        scratch_shapes=[
            pltpu.VMEM(part.shape, f32),
            pltpu.VMEM((2, n_dp, slots, width), bf16),
            pltpu.VMEM((2, total, total), f32),
            dma, dma, dma((2 * n_dp,)), dma((2 * n_dp,)),
        ],
        compiler_params=params(3),
        name="loss",
    )(part, counts, doc_ok, query_ok, target, scale)


def rotary_tables(positions):
    half_dim = HDIM // 2
    inverse = 1000.0 ** (-2.0 * jnp.arange(half_dim, dtype=f32) / HDIM)
    angles = positions.astype(f32)[:, None] * inverse[None, :]
    angles = jnp.concatenate([angles] * 4, 1)
    return jnp.cos(angles), jnp.sin(angles)


def layout(lengths, places, slot_count):
    end_points = jnp.cumsum(lengths)
    segment = jnp.sum((places[:, None] >= end_points[None, :]).astype(jnp.int32), 1)
    starts = jnp.concatenate([jnp.zeros((1,), jnp.int32), end_points])
    slot_ids = jnp.arange(slot_count + 1, dtype=jnp.int32)
    segment_start = jnp.sum(jnp.where(segment[:, None] == slot_ids[None, :], starts[None, :], 0), 1)
    return segment, places - segment_start


def norm_back(grad, hat, scale, gain):
    grad_hat = grad * gain
    first = jnp.mean(grad_hat, -1, keepdims=True)
    second = jnp.mean(grad_hat * hat, -1, keepdims=True)
    return (
        scale * (grad_hat - first - hat * second),
        jnp.sum(grad * hat, 0),
        jnp.sum(grad, 0),
    )


def glu(gate_vals, up_vals):
    return jax.nn.silu(gate_vals) * up_vals


def adamw(weight_in, gradient, first_mom, second, factor, step_num, rate):
    gradient = gradient * factor
    first_new = beta_one * first_mom + (1.0 - beta_one) * gradient
    second_new = beta_two * second + (1.0 - beta_two) * gradient * gradient
    first_hat = first_new / (1.0 - beta_one**step_num)
    second_hat = second_new / (1.0 - beta_two**step_num)
    weight_new = weight_in - rate * (
        first_hat / (jnp.sqrt(second_hat) + adam_eps) + decay_rate * weight_in
    )
    return (weight_new, first_new, second_new)


def name_rows(ids, d, n_dp, row_count, room):
    tok = ids.shape[0]
    owner = ids // row_count
    local = ids - owner * row_count
    order = jnp.bitwise_xor(owner, d)
    places = jnp.arange(tok, dtype=jnp.int32)
    first_at = jnp.min(
        jnp.where(ids[:, None] == ids[None, :], places[None, :], tok), 1
    )
    is_first = first_at == places
    slot = jnp.sum(
        (
            (places[None, :] < first_at[:, None])
            & is_first[None, :]
            & (owner[None, :] == owner[:, None])
        ).astype(jnp.int32),
        1,
    )
    over = jnp.max(slot) >= room
    pos = order * room + slot
    wanted = jnp.arange(n_dp * room, dtype=jnp.int32)
    listed = jnp.max(
        jnp.where((pos[None, :] == wanted[:, None]) & is_first[None, :], local[None, :], -1), 1
    ).reshape(n_dp, 1, room)
    listed = jnp.pad(listed, ((0, 0), (0, 0), (0, 128 - room)), constant_values=-1)
    flag = jnp.broadcast_to(over.astype(jnp.int32), (n_dp, 7, 128))
    return pos, jnp.concatenate([listed, flag], 1)


def layer_norm(stream, gain_row, bias_row):
    average = jnp.mean(stream, -1, keepdims=True)
    centered = stream - average
    variance = jnp.mean(centered * centered, -1, keepdims=True)
    return centered * lax.rsqrt(variance + norm_eps) * gain_row + bias_row


def rotate(values, cosine, sine_table):
    half_dim = values.shape[-1] // 2
    turned = jnp.concatenate([-values[..., half_dim:], values[..., :half_dim]], -1)
    return values * cosine + turned * sine_table


def plain_rotary_tables(positions, head_dim):
    half_dim = head_dim // 2
    inverse = 1000.0 ** (-2.0 * jnp.arange(half_dim, dtype=jnp.float32) / head_dim)
    angles = positions.astype(jnp.float32)[:, None] * inverse[None, :]
    angles = jnp.concatenate([angles, angles], 1)[:, None, :]
    return (jnp.cos(angles), jnp.sin(angles))


def plain_layout(lengths, tok_count, slot_count):
    end_points = jnp.cumsum(lengths)
    places = jnp.arange(tok_count, dtype=jnp.int32)
    segment = jnp.sum((places[:, None] >= end_points[None, :]).astype(jnp.int32), 1)
    starts = jnp.concatenate([jnp.zeros((1,), jnp.int32), end_points])
    slot_ids = jnp.arange(slot_count + 1, dtype=jnp.int32)
    segment_start = jnp.sum(jnp.where(segment[:, None] == slot_ids[None, :], starts[None, :], 0), 1)
    return (segment, places - segment_start)


def plain_glu(gate_vals, up_vals):
    return jax.nn.silu(gate_vals) * up_vals


def pool_rows(stream_two, member, counts):
    pooled = jnp.dot(member, stream_two, precision=highest) / counts[:, None]
    return pooled * lax.rsqrt(jnp.sum(pooled * pooled, 1, keepdims=True) + 1e-06)


def model_total(values):
    return lax.psum(values.astype(jnp.bfloat16), "mp").astype(jnp.float32)


def block_scores(query_block, seg_block, key_low, segment, factor):
    scores = (
        jnp.einsum("thd,shd->hts", query_block, key_low, preferred_element_type=jnp.float32)
        * factor
    )
    return jnp.where((seg_block[:, None] == segment[None, :])[None], scores, neg_large)


def attention(query_low, key_low, value_low, segment):
    tok_count, heads_local, head_dim = query_low.shape
    block_rows = min(512, tok_count)
    block_count = tok_count // block_rows
    factor = head_dim ** (-0.5)
    query_blocks = query_low.reshape(block_count, block_rows, heads_local, head_dim)
    seg_blocks = segment.reshape(block_count, block_rows)

    def one_block(operands):
        scores = block_scores(operands[0], operands[1], key_low, segment, factor)
        row_peak = jnp.max(scores, 2, keepdims=True)
        row_total = jnp.sum(jnp.exp(scores - row_peak), 2, keepdims=True)
        log_total = row_peak + jnp.log(row_total)
        soft_rows = jnp.exp(scores - log_total)
        attended = jnp.einsum(
            "hts,shd->thd",
            soft_rows.astype(jnp.bfloat16),
            value_low,
            preferred_element_type=jnp.float32,
        )
        return (attended, log_total[..., 0])

    attended, log_total = lax.map(one_block, (query_blocks, seg_blocks))
    return (attended.reshape(tok_count, heads_local * head_dim), log_total)


def attention_back(query_low, key_low, value_low, grad_attended, log_total, segment):
    tok_count, heads_local, head_dim = query_low.shape
    block_rows = min(512, tok_count)
    block_count = tok_count // block_rows
    factor = head_dim ** (-0.5)
    query_blocks = query_low.reshape(block_count, block_rows, heads_local, head_dim)
    grad_blocks = grad_attended.reshape(block_count, block_rows, heads_local, head_dim)
    seg_blocks = segment.reshape(block_count, block_rows)

    def one_block(running, operands):
        query_block, grad_block, seg_block, lse_block = operands
        scores = block_scores(query_block, seg_block, key_low, segment, factor)
        soft_rows = jnp.exp(scores - lse_block[..., None])
        grad_soft = jnp.einsum(
            "thd,shd->hts", grad_block, value_low, preferred_element_type=jnp.float32
        )
        inner = jnp.sum(soft_rows * grad_soft, 2, keepdims=True)
        grad_scores = (soft_rows * (grad_soft - inner)).astype(jnp.bfloat16)
        grad_query = (
            jnp.einsum("hts,shd->thd", grad_scores, key_low, preferred_element_type=jnp.float32)
            * factor
        )
        grad_key = (
            running[0]
            + jnp.einsum(
                "hts,thd->shd", grad_scores, query_block, preferred_element_type=jnp.float32
            )
            * factor
        )
        grad_value = running[1] + jnp.einsum(
            "hts,thd->shd",
            soft_rows.astype(jnp.bfloat16),
            grad_block,
            preferred_element_type=jnp.float32,
        )
        return ((grad_key, grad_value), grad_query)

    zeros_kv = jnp.zeros(key_low.shape, jnp.float32)
    (grad_key, grad_value), grad_query = lax.scan(
        one_block, (zeros_kv, zeros_kv), (query_blocks, grad_blocks, seg_blocks, log_total)
    )
    return (grad_query.reshape(tok_count, heads_local, head_dim), grad_key, grad_value)


def layer_forward(embed_rows, segment, positions, weights, norm_rows):
    w_qkv, w_out, w_ffn, w_down = weights
    tok_count = embed_rows.shape[0]
    heads_local = w_qkv.shape[2] // HDIM
    stream_zero = layer_norm(embed_rows, norm_rows[0], norm_rows[1])
    input_zero = stream_zero.astype(jnp.bfloat16)
    projected = jnp.einsum("td,dcf->tcf", input_zero, w_qkv, preferred_element_type=jnp.float32)
    heads_view = projected.reshape(tok_count, 3, heads_local, HDIM)
    cosine, sine_table = plain_rotary_tables(positions, HDIM)
    query_low = rotate(heads_view[:, 0], cosine, sine_table).astype(jnp.bfloat16)
    key_low = rotate(heads_view[:, 1], cosine, sine_table).astype(jnp.bfloat16)
    value_low = heads_view[:, 2].astype(jnp.bfloat16)
    attended, log_total = attention(query_low, key_low, value_low, segment)
    attended_low = attended.astype(jnp.bfloat16)
    attn_branch = model_total(
        jnp.einsum("tf,df->td", attended_low, w_out, preferred_element_type=jnp.float32)
    )
    sum_one = stream_zero + attn_branch
    stream_one = layer_norm(sum_one, norm_rows[2], norm_rows[3])
    input_one = stream_one.astype(jnp.bfloat16)
    gate_up = jnp.einsum("td,dcf->tcf", input_one, w_ffn, preferred_element_type=jnp.float32)
    hidden_low = plain_glu(gate_up[:, 0], gate_up[:, 1]).astype(jnp.bfloat16)
    ffn_branch = model_total(
        jnp.einsum("tf,df->td", hidden_low, w_down, preferred_element_type=jnp.float32)
    )
    sum_two = stream_one + ffn_branch
    stream_two = layer_norm(sum_two, norm_rows[4], norm_rows[5])
    kept_vals = (
        embed_rows,
        sum_one,
        sum_two,
        input_zero,
        input_one,
        query_low,
        key_low,
        value_low,
        log_total,
        attended_low,
        gate_up,
        hidden_low,
    )
    return (stream_two, kept_vals)


def layer_backward(grad_two, kept_vals, weights, norm_rows, segment, positions):
    w_qkv, w_out, w_ffn, w_down = weights
    (
        embed_rows,
        sum_one,
        sum_two,
        input_zero,
        input_one,
        query_low,
        key_low,
        value_low,
        log_total,
        attended_low,
        gate_up,
        hidden_low,
    ) = kept_vals
    tok_count, heads_local, head_dim = query_low.shape
    grad_sum_two, gain_two, bias_two = jax.vjp(layer_norm, sum_two, norm_rows[4], norm_rows[5])[1](
        grad_two
    )
    ffn_low = grad_sum_two.astype(jnp.bfloat16)
    grad_down = jnp.einsum("td,tf->df", ffn_low, hidden_low, preferred_element_type=jnp.float32)
    grad_hidden = jnp.einsum("td,df->tf", ffn_low, w_down, preferred_element_type=jnp.float32)
    grad_gate, grad_up = jax.vjp(plain_glu, gate_up[:, 0], gate_up[:, 1])[1](grad_hidden)
    gate_grads = jnp.stack([grad_gate, grad_up], 1).astype(jnp.bfloat16)
    grad_ffn = jnp.einsum("td,tcf->dcf", input_one, gate_grads, preferred_element_type=jnp.float32)
    grad_stream_one = grad_sum_two + model_total(
        jnp.einsum("tcf,dcf->td", gate_grads, w_ffn, preferred_element_type=jnp.float32)
    )
    grad_sum_one, gain_one, bias_one = jax.vjp(layer_norm, sum_one, norm_rows[2], norm_rows[3])[1](
        grad_stream_one
    )
    attn_low = grad_sum_one.astype(jnp.bfloat16)
    grad_out = jnp.einsum("td,tf->df", attn_low, attended_low, preferred_element_type=jnp.float32)
    grad_attended = jnp.einsum(
        "td,df->tf", attn_low, w_out, preferred_element_type=jnp.float32
    ).astype(jnp.bfloat16)
    grad_query, grad_key, grad_value = attention_back(
        query_low,
        key_low,
        value_low,
        grad_attended.reshape(tok_count, heads_local, head_dim),
        log_total,
        segment,
    )
    cosine, sine_table = plain_rotary_tables(positions, head_dim)
    turn_back = jax.vjp(lambda values: rotate(values, cosine, sine_table), grad_query)[1]
    grad_projected = jnp.stack([turn_back(grad_query)[0], turn_back(grad_key)[0], grad_value], 1)
    grad_projected = grad_projected.reshape(tok_count, 3, heads_local * head_dim).astype(
        jnp.bfloat16
    )
    grad_qkv = jnp.einsum(
        "td,tcf->dcf", input_zero, grad_projected, preferred_element_type=jnp.float32
    )
    grad_stream_zero = grad_sum_one + model_total(
        jnp.einsum("tcf,dcf->td", grad_projected, w_qkv, preferred_element_type=jnp.float32)
    )
    grad_embed, gain_zero, bias_zero = jax.vjp(layer_norm, embed_rows, norm_rows[0], norm_rows[1])[
        1
    ](grad_stream_zero)
    norm_grads = jnp.stack([gain_zero, bias_zero, gain_one, bias_one, gain_two, bias_two])
    return (grad_embed, (grad_qkv, grad_out, grad_ffn, grad_down), norm_grads)


def plain_adamw(weight_in, gradient, first_mom, second, factor, step_num, rate):
    gradient = gradient * factor
    first_new = beta_one * first_mom + (1.0 - beta_one) * gradient
    second_new = beta_two * second + (1.0 - beta_two) * gradient * gradient
    first_hat = first_new / (1.0 - beta_one**step_num)
    second_hat = second_new / (1.0 - beta_two**step_num)
    weight_new = weight_in - rate * (
        first_hat / (jnp.sqrt(second_hat) + adam_eps) + decay_rate * weight_in
    )
    return (weight_new, first_new, second_new)


def plain_step(
    token_ids,
    seq_lengths,
    positives,
    embedding,
    attn_in,
    attn_out,
    ffn_in,
    ffn_out,
    norm_params,
    logit_scale,
    embed_m,
    embed_v,
    attn_in_m,
    attn_in_v,
    attn_out_m,
    attn_out_v,
    ffn_in_m,
    ffn_in_v,
    ffn_out_m,
    ffn_out_v,
    norm_m,
    norm_v,
    scale_m,
    scale_v,
):
    n_data = lax.axis_size("dp")
    tower_idx = lax.axis_index("tower")
    data_idx = lax.axis_index("dp")
    model_idx = lax.axis_index("mp")
    slot_count = seq_lengths.shape[2]
    token_list = token_ids[0]
    tok_count = token_list.shape[0]
    model_width = norm_params.shape[1]
    local_width = embedding.shape[1]
    row_count = embedding.shape[0]
    weights = (
        lax.all_gather(attn_in.astype(jnp.bfloat16), ("tower", "dp"), axis=0, tiled=True),
        lax.all_gather(attn_out.astype(jnp.bfloat16), ("tower", "dp"), axis=0, tiled=True),
        lax.all_gather(ffn_in.astype(jnp.bfloat16), ("tower", "dp"), axis=0, tiled=True),
        lax.all_gather(ffn_out.astype(jnp.bfloat16), ("tower", "dp"), axis=0, tiled=True),
    )
    shard_piece = lax.all_gather(embedding.astype(jnp.bfloat16), "dp", axis=0, tiled=True)
    inside = (token_list >= 0) & (token_list < shard_piece.shape[0])
    picked = jnp.take(shard_piece, jnp.clip(token_list, 0, shard_piece.shape[0] - 1), axis=0)
    looked = jnp.where(inside[:, None], picked.astype(jnp.float32), 0.0)
    embed_rows = lax.all_gather(looked.astype(jnp.bfloat16), "mp", axis=1, tiled=True).astype(
        jnp.float32
    )
    lengths_row = seq_lengths[tower_idx, data_idx]
    segment, positions = plain_layout(lengths_row, tok_count, slot_count)
    stream_two, kept_vals = layer_forward(embed_rows, segment, positions, weights, norm_params)
    member = (segment[None, :] == jnp.arange(slot_count, dtype=jnp.int32)[:, None]).astype(
        jnp.float32
    )
    counts = jnp.maximum(lengths_row, 1).astype(jnp.float32)
    own_embeds, pool_back = jax.vjp(lambda stream: pool_rows(stream, member, counts), stream_two)
    all_embeds = lax.all_gather(
        own_embeds.astype(jnp.bfloat16), ("tower", "dp"), axis=0, tiled=True
    )
    query_total = n_data * slot_count
    rows_per = slot_count // 2
    first_row = (tower_idx * n_data + data_idx) * rows_per
    query_rows = lax.dynamic_slice_in_dim(all_embeds, first_row, rows_per, 0)
    documents = all_embeds[query_total:]
    cosines = jnp.einsum("qd,kd->qk", query_rows, documents, preferred_element_type=jnp.float32)
    logit_factor = jnp.exp(jnp.minimum(logit_scale[0], cap_value))
    doc_ok = seq_lengths[1].reshape(-1) > 0
    query_ok_all = seq_lengths[0].reshape(-1) > 0
    query_count = jnp.sum(query_ok_all.astype(jnp.float32))
    query_ok = lax.dynamic_slice_in_dim(query_ok_all, first_row, rows_per, 0)
    logits = jnp.where(doc_ok[None, :], logit_factor * cosines, neg_large)
    row_peak = jnp.max(logits, 1, keepdims=True)
    log_total = row_peak + jnp.log(jnp.sum(jnp.exp(logits - row_peak), 1, keepdims=True))
    soft_rows = jnp.exp(logits - log_total)
    targets = lax.dynamic_slice_in_dim(positives.reshape(-1), first_row, rows_per, 0)
    target_mask = jnp.arange(query_total, dtype=jnp.int32)[None, :] == targets[:, None]
    picked = jnp.sum(jnp.where(target_mask, logits, 0.0), 1)
    loss_part = jnp.sum(jnp.where(query_ok, log_total[:, 0] - picked, 0.0))
    grad_logits = (
        jnp.where(query_ok[:, None], soft_rows - target_mask.astype(jnp.float32), 0.0) / query_count
    )
    scale_part = (
        jnp.sum(grad_logits * cosines)
        * logit_factor
        * (logit_scale[0] < cap_value).astype(jnp.float32)
    )
    grad_cos = (logit_factor * grad_logits).astype(jnp.bfloat16)
    grad_queries = jnp.einsum("qk,kd->qd", grad_cos, documents, preferred_element_type=jnp.float32)
    grad_documents = jnp.einsum(
        "qk,qd->kd", grad_cos, query_rows, preferred_element_type=jnp.float32
    )
    grad_term = jnp.concatenate(
        [jnp.zeros((query_total, model_width), jnp.float32), grad_documents], 0
    )
    grad_term = lax.dynamic_update_slice_in_dim(grad_term, grad_queries, first_row, 0)
    own_grad = lax.psum_scatter(grad_term, ("tower", "dp"), scatter_dimension=0, tiled=True)
    grad_two = pool_back(own_grad)[0]
    grad_embed, layer_grads, norm_grads = layer_backward(
        grad_two, kept_vals, weights, norm_params, segment, positions
    )
    embed_low = grad_embed.astype(jnp.bfloat16)
    column_part = lax.dynamic_slice_in_dim(embed_low, model_idx * local_width, local_width, 1)
    row_start = data_idx * row_count
    all_ids = lax.all_gather(token_list, ("tower", "dp"), axis=0, tiled=True)
    piece_ids = all_ids - row_start
    inside = (piece_ids >= 0) & (piece_ids < row_count)
    slot_ids = jnp.where(inside, piece_ids, row_count)
    embed_grad = jax.ops.segment_sum(
        lax.all_gather(column_part, ("tower", "dp"), axis=0, tiled=True).astype(jnp.float32),
        slot_ids,
        num_segments=row_count + 1,
    )[:row_count]
    shard_grads = (
        lax.psum_scatter(layer_grads[0], ("tower", "dp"), scatter_dimension=0, tiled=True),
        lax.psum_scatter(layer_grads[1], ("tower", "dp"), scatter_dimension=0, tiled=True),
        lax.psum_scatter(layer_grads[2], ("tower", "dp"), scatter_dimension=0, tiled=True),
        lax.psum_scatter(layer_grads[3], ("tower", "dp"), scatter_dimension=0, tiled=True),
    )
    norm_grad, loss_sum, scale_grad = lax.psum((norm_grads, loss_part, scale_part), ("tower", "dp"))
    local_sq = sum((jnp.sum(gradient * gradient) for gradient in shard_grads)) + 0.5 * jnp.sum(
        embed_grad * embed_grad
    )
    total_sq = (
        lax.psum(local_sq, ("tower", "dp", "mp"))
        + jnp.sum(norm_grad * norm_grad)
        + scale_grad * scale_grad
    )
    grad_norm = jnp.sqrt(total_sq)
    factor = jnp.minimum(1.0, clip_max / (grad_norm + 1e-06))
    step_num = float(STEP)
    embed_new = plain_adamw(embedding, embed_grad, embed_m, embed_v, factor, step_num, learn_rate)
    qkv_new = plain_adamw(attn_in, shard_grads[0], attn_in_m, attn_in_v, factor, step_num, learn_rate)
    out_new = plain_adamw(attn_out, shard_grads[1], attn_out_m, attn_out_v, factor, step_num, out_rate)
    ffn_new = plain_adamw(ffn_in, shard_grads[2], ffn_in_m, ffn_in_v, factor, step_num, learn_rate)
    down_new = plain_adamw(ffn_out, shard_grads[3], ffn_out_m, ffn_out_v, factor, step_num, learn_rate)
    norms_new = plain_adamw(norm_params, norm_grad, norm_m, norm_v, factor, step_num, norm_rate)
    scale_new = plain_adamw(
        logit_scale, scale_grad.reshape(1), scale_m, scale_v, factor, step_num, learn_rate
    )
    return (
        embed_new[0],
        embed_new[1],
        embed_new[2],
        qkv_new[0],
        qkv_new[1],
        qkv_new[2],
        out_new[0],
        out_new[1],
        out_new[2],
        ffn_new[0],
        ffn_new[1],
        ffn_new[2],
        down_new[0],
        down_new[1],
        down_new[2],
        norms_new[0],
        norms_new[1],
        norms_new[2],
        scale_new[0],
        scale_new[1],
        scale_new[2],
        loss_sum.reshape(1),
        query_count.reshape(1),
        grad_norm.reshape(1),
    )


def lean_step(args, pos, heard):
    (
        token_ids, seq_lengths, positives, embedding, attn_in, attn_out, ffn_in, ffn_out,
        norm_params, logit_scale, embed_m, embed_v, attn_in_m, attn_in_v, attn_out_m, attn_out_v,
        ffn_in_m, ffn_in_v, ffn_out_m, ffn_out_v, norm_m, norm_v, scale_m, scale_v,
    ) = args
    tower_idx = lax.axis_index("tower")
    data_idx = lax.axis_index("dp")
    model_idx = lax.axis_index("mp")
    slot_count = seq_lengths.shape[2]
    tok = token_ids.shape[1]
    half = tok // 2
    row_count = embedding.shape[0]
    feats = attn_out.shape[1]
    ff = ffn_out.shape[1]
    part_ff = ff // 2

    kinds = ("plain", "late", "late", "late", "late")
    gather_pieces = [(0, "plain", 0, 3 * feats, 0)]
    quarter = ff // 4
    for turn, which in enumerate((2, 3, 4)):
        for c in range(4):
            kind = ("late", "early", "cross")[(4 * turn + c) % 3]
            gather_pieces.append((which, kind, c * quarter, quarter, 4 * turn + c))
    gather_pieces.append((1, "early", 0, feats, 6))
    places = (jnp.arange(tok, dtype=jnp.int32) + model_idx * half) % tok
    pos_rel = jnp.where(model_idx == 0, pos, jnp.concatenate([pos[half:], pos[:half]]))
    lengths_row = seq_lengths[tower_idx, data_idx]
    segment, positions = layout(lengths_row, places, slot_count)
    cosine, sine = rotary_tables(positions)
    seg_row, seg_col = segment[None, :], segment[:, None]
    named = heard[:, :, 0, : heard_room(tok, heard.shape[1])].reshape(2, 1, -1)
    kept, weights = forward_pass(
        embedding, heard, pos_rel[:, None], norm_params, cosine, sine, seg_row, seg_col,
        (attn_in, attn_out, ffn_in, ffn_out), kinds, gather_pieces,
    )
    emb, stream_zero, input_zero, query, key, value, lse = kept[:7]
    att = kept[7:9]
    w_qkv, w_out, w_gate, w_up, w_down = weights

    sum_one = stream_zero + tdot(att[0], w_out[0]) + tdot(att[1], w_out[1])
    hat_one, scale_one = norm_parts(sum_one)
    stream_one = hat_one * norm_params[2] + norm_params[3]
    input_one = stream_one.astype(bf16)
    gates = [mdot(input_one, w_gate[j]) for j in range(2)]
    ups = [mdot(input_one, w_up[j]) for j in range(2)]
    hidden = [glu(gates[j], ups[j]).astype(bf16) for j in range(2)]
    sum_two = stream_one + tdot(hidden[0], w_down[0]) + tdot(hidden[1], w_down[1])
    hat_two, scale_two = norm_parts(sum_two)
    stream_two = hat_two * norm_params[4] + norm_params[5]

    member = (segment[None, :half] == jnp.arange(slot_count, dtype=jnp.int32)[:, None]).astype(f32)
    counts = jnp.maximum(lengths_row, 1).astype(f32)[:, None]
    part = jnp.dot(member, stream_two, precision=highest)
    doc_ok = (seq_lengths[1].reshape(1, -1) > 0).astype(f32)
    query_ok = (seq_lengths[0].reshape(-1, 1) > 0).astype(f32)
    grad_pool, stats = loss_step(
        part, counts, doc_ok, query_ok, positives.reshape(-1, 1), logit_scale.reshape(1, 1)
    )
    loss_sum, query_count, scale_grad = stats[0, 0], stats[1, 0], stats[2, 0]

    def weight_grad(left, right):
        return jnp.einsum("td,tf->df", left, right, preferred_element_type=f32).astype(bf16)

    pieces = [(0, ("early", "late")[c % 2], c * quarter, quarter, c) for c in range(4)]
    out = hidden_back(
        grad_pool, seg_col, sum_two, norm_params, input_one, sum_one, att, hidden, w_gate, w_up, w_down, pieces, 2,
    )
    grad_sum_one, attn_low, norms = out[:3]
    grad_out, later, r_down, squares = out[3:5], out[5:9], out[9], out[10]
    pieces = [
        (c // 4, ("early", "late", "cross")[c % 3], (c % 4) * quarter, quarter, c)
        for c in range(8)
    ] + [(2, "late", 0, feats, 8)]
    late_pieces = [(c, "plain", 0, feats, 0) for c in range(3)]
    embed_grad, norm_sum, r_ffn, r_out, r_qkv, total = backward_pass(
        attn_low, w_out, query, key, value, lse, cosine, sine, seg_row, seg_col, grad_sum_one,
        emb, norm_params, w_qkv, norms, squares, input_zero, pos_rel[None, :], named,
        later, grad_out, row_count, pieces, late_pieces,
    )
    norm_grad = norm_sum[:6]
    total_sq = total[0, 0] + scale_grad * scale_grad
    grad_norm = jnp.sqrt(total_sq)
    factor = jnp.minimum(1.0, clip_max / (grad_norm + 1e-06))
    step_num = float(STEP)
    embed_new = adamw(embedding, embed_grad, embed_m, embed_v, factor, step_num, learn_rate)
    qkv_new = adamw(attn_in, r_qkv, attn_in_m, attn_in_v, factor, step_num, learn_rate)
    out_new = adamw(attn_out, r_out, attn_out_m, attn_out_v, factor, step_num, out_rate)
    ffn_new = adamw(ffn_in, r_ffn, ffn_in_m, ffn_in_v, factor, step_num, learn_rate)
    down_new = adamw(ffn_out, r_down, ffn_out_m, ffn_out_v, factor, step_num, learn_rate)
    norms_new = adamw(norm_params, norm_grad, norm_m, norm_v, factor, step_num, norm_rate)
    scale_new = adamw(
        logit_scale, scale_grad.reshape(1), scale_m, scale_v, factor, step_num, learn_rate
    )
    return (
        *embed_new, *qkv_new, *out_new, *ffn_new, *down_new, *norms_new, *scale_new,
        loss_sum.reshape(1), query_count.reshape(1), grad_norm.reshape(1),
    )


def local(*args):
    token_ids, embedding = args[0], args[3]
    n_dp = lax.axis_size("dp")
    room = heard_room(token_ids.shape[1], n_dp)
    pos, lists = name_rows(
        token_ids[0], lax.axis_index("dp"), n_dp, embedding.shape[0], room
    )
    heard, flag = exchange_lists(lists)
    return lax.cond(
        flag[1, 0] > 0,
        lambda values: plain_step(*values),
        lambda values: lean_step(values, pos, heard),
        args,
    )


def solution(mesh):
    table, rows3, rows2 = P("dp", "mp"), P(("tower", "dp"), None, "mp"), P(("tower", "dp"), "mp")
    weights = (table, rows3, rows2, rows3, rows2)
    moments = tuple(spec for spec in weights for _ in range(2))
    return jax.shard_map(
        local,
        mesh=mesh,
        in_specs=(P("tower", "dp"), P(), P()) + weights + (P(), P()) + moments + (P(),) * 4,
        out_specs=tuple(spec for spec in weights for _ in range(3)) + (P(),) * 9,
        check_vma=False,
    )
```

```python
import jax
import jax.numpy as jnp
from jax import lax
from jax.sharding import PartitionSpec as P
from jax.experimental import pallas as pl
from jax.experimental.pallas import tpu as pltpu

HDIM = 64
STEP = 5

norm_eps = 1e-06
cap_value = 3.4
clip_max = 0.01
beta_one = 0.9
beta_two = 0.999
learn_rate = 0.02
out_rate = 0.05
norm_rate = 0.3
decay_rate = 0.01
adam_eps = 1e-08
neg_large = -1e30
highest = lax.Precision.HIGHEST
f32 = jnp.float32
bf16 = jnp.bfloat16
MESH = pl.DeviceIdType.MESH
ANY = pl.BlockSpec(memory_space=pl.ANY)
VM = pl.BlockSpec(memory_space=pltpu.VMEM)


def sds(shape, dtype):
    return jax.ShapeDtypeStruct(shape, dtype)


def params(ident, limit=58):
    return pltpu.CompilerParams(
        collective_id=ident, has_side_effects=True, vmem_limit_bytes=limit << 20
    )


class Place:
    def __init__(self):
        self.n_dp = lax.axis_size("dp")
        self.count = self.n_dp.bit_length() - 1
        self.t = lax.axis_index("tower")
        self.d = lax.axis_index("dp")
        self.m = lax.axis_index("mp")
        self.bits = [(self.d // (1 << (self.count - 1 - j))) % 2 for j in range(self.count)]

    def across(self, dim):
        if dim == "t":
            return {"tower": 1 - self.t}
        if dim == "y":
            return {"mp": 1 - self.m}
        step = 1 << (self.count - 1 - dim)
        return {"dp": self.d + (1 - 2 * self.bits[dim]) * step}

    def mixed(self, rel):
        out = self.d
        for j in range(self.count):
            step = 1 << (self.count - 1 - j)
            if rel & step:
                out = out + (1 - 2 * self.bits[j]) * step
        return out


def remote(src, dst, send, recv, where):
    return pltpu.make_async_remote_copy(
        src_ref=src, dst_ref=dst, send_sem=send, recv_sem=recv, device_id=where, device_id_type=MESH
    )


def greet(peers):
    barrier = pltpu.get_barrier_semaphore()
    for where in peers:
        pl.semaphore_signal(barrier, inc=1, device_id=where, device_id_type=MESH)
    pl.semaphore_wait(barrier, len(peers))


def tdot(lhs, rhs):
    return lax.dot_general(lhs, rhs, (((1,), (1,)), ((), ())), preferred_element_type=f32)


def mdot(lhs, rhs):
    return jnp.dot(lhs, rhs, preferred_element_type=f32)


def every(ndim, cols):
    return (slice(None),) * (ndim - 1) + (cols,)


class Gather:
    def __init__(self, here, shard, full, other, order, cols, send, recv, local_sem):
        self.here, self.shard, self.full, self.other = here, shard, full, other
        self.order, self.cols, self.send, self.recv = order, cols, send, recv
        self.local_sem = local_sem
        self.last = len(order)
        self.done = set()
        self.live, self.sent = [], []
        self.arrays = [full]
        self.slot = 0

    def view(self):
        here = self.here
        return (
            (here.t,)
            + tuple(slice(None) if j in self.done else here.bits[j] for j in range(here.count))
            + (slice(None), self.cols)
        )

    def stage(self, step):
        here = self.here
        if step == 0:
            self.place = pltpu.make_async_copy(
                self.shard.at[:, self.cols], self.full.at[self.view()], self.local_sem
            )
            self.place.start()
        for copy in self.live:
            copy.wait_recv()
        if step == 1:
            self.place.wait()
        self.sent += self.live
        self.live = []
        if step == self.last:
            for copy in self.sent:
                copy.wait_send()
            return
        dim = self.order[step]
        if dim == "y":
            pairs = [(self.full.at[self.view()], self.other.at[self.view()])]
            self.arrays = [self.full, self.other]
        elif step == 0:
            pairs = [(self.shard.at[:, self.cols], self.full.at[self.view()])]
        else:
            pairs = [(ref.at[self.view()], ref.at[self.view()]) for ref in self.arrays]
        for src, dst in pairs:
            copy = remote(
                src, dst, self.send.at[self.slot], self.recv.at[self.slot], here.across(dim)
            )
            copy.start()
            self.live.append(copy)
            self.slot += 1
        if dim not in ("t", "y"):
            self.done.add(dim)


class Scatter:
    def __init__(self, here, own, other, order, cols, held, landed, out, send, recv, local_sems):
        self.here, self.order, self.cols = here, order, cols
        self.source = [own] if other is None else [own, other]
        self.held, self.landed, self.out = held, landed, out
        self.send, self.recv, self.local_sems = send, recv, local_sems
        self.last = len(order)
        self.fixed = {}
        self.live = []
        self.slot = 0
        self.arrays = list(range(len(self.source)))

    def view(self, extra=None):
        fixed = dict(self.fixed)
        if extra:
            fixed.update(extra)
        return tuple(fixed.get(j, slice(None)) for j in range(self.here.count))

    def start(self, src, where, index):
        copy = remote(
            src, self.landed[self.slot], self.send.at[self.slot], self.recv.at[self.slot], where
        )
        copy.start()
        self.live.append((copy, self.slot, index))
        self.slot += 1

    def stage(self, step):
        here = self.here
        if step > 0:
            self.finish(step - 1)
        if step == self.last:
            return
        dim = self.order[step]
        if dim == "t":
            self.loads = []
            tail = (slice(None),) * (here.count + 1) + (self.cols,)
            for index in self.arrays:
                load = pltpu.make_async_copy(
                    self.source[index].at[(here.t,) + tail], self.held[index],
                    self.local_sems.at[index],
                )
                load.start()
                self.loads.append(load)
                self.start(self.source[index].at[(1 - here.t,) + tail], here.across("t"), index)
        elif dim == "y":
            self.start(self.held[1].at[self.view()], here.across("y"), 0)
            self.arrays = [0]
        else:
            far = self.view({dim: 1 - here.bits[dim]})
            for index in self.arrays:
                self.start(self.held[index].at[far], here.across(dim), index)

    def finish(self, step):
        here = self.here
        dim = self.order[step]
        if dim not in ("t", "y"):
            self.fixed[dim] = here.bits[dim]
        view = self.view()
        if dim == "t":
            for load in self.loads:
                load.wait()
        for copy, slot, index in self.live:
            copy.wait()
            total = self.held[index][view].astype(f32) + self.landed[slot][...].astype(f32)
            if step == self.last - 1:
                self.out(self.cols, total)
            else:
                self.held[index][view] = total.astype(bf16)
        self.live = []


class Total:
    def __init__(self, here, value, landed, send, recv):
        self.here, self.value, self.landed, self.send, self.recv = here, value, landed, send, recv
        self.order = ["t", "y"] + list(range(here.count))
        self.last = len(self.order)

    def stage(self, step):
        if step > 0:
            self.copy.wait()
            self.value[...] += self.landed[step - 1]
        if step < self.last:
            self.copy = remote(
                self.value, self.landed.at[step], self.send.at[step], self.recv.at[step],
                self.here.across(self.order[step]),
            )
            self.copy.start()


class Runner:
    def __init__(self, jobs, lags, stride=1):
        self.jobs, self.lags, self.stride, self.tick = jobs, lags, stride, 0
        self.length = max(job.last * stride + lag for job, lag in zip(jobs, lags)) + 1

    def advance(self):
        if self.tick < self.length:
            for job, lag in zip(self.jobs, self.lags):
                since = self.tick - lag
                if since % self.stride == 0 and 0 <= since // self.stride <= job.last:
                    job.stage(since // self.stride)
            self.tick += 1

    def drain(self):
        while self.tick < self.length:
            self.advance()


def gather_orders(count):
    far, near = list(range(count - 1)), [count - 1]
    return {
        "plain": far + near + ["t"],
        "late": far + near + ["y", "t"],
        "early": far + ["y"] + near + ["t"],
        "cross": far[:-1] + near + ["y"] + far[-1:] + ["t"],
    }


def scatter_orders(count):
    near, far = [count - 1], list(range(count - 2, -1, -1))
    return {
        "plain": ["t"] + near + far,
        "early": ["t", "y"] + near + far,
        "late": ["t"] + near + ["y"] + far,
        "cross": ["t"] + far[:1] + ["y"] + near + far[1:],
    }


def scatter_lands(order, count, pair, rows, cols):
    shapes, free, live = [], count, 2 if pair else 1
    for dim in order:
        if dim == "y":
            live = 1
        elif dim != "t":
            free -= 1
        shapes += [(2,) * free + (rows, cols)] * live
    return shapes


def lists_body(lists, heard, flag, send, recv):
    here = Place()
    n = here.n_dp
    peers = []
    for rt in range(2):
        for k in range(n):
            if rt or k:
                peers.append((rt, k, {"tower": here.t + rt * (1 - 2 * here.t), "dp": here.mixed(k)}))
    greet([where for _, _, where in peers])
    copies = []
    for rt, k, where in peers:
        copy = remote(lists.at[k], heard.at[rt, k], send.at[rt, k], recv.at[rt, k], where)
        copy.start()
        copies.append(copy)
    heard[0, 0] = lists[0]
    for copy in copies:
        copy.wait()
    flag[...] = jnp.max(heard[...].reshape((2 * n,) + flag.shape), axis=0)


def heard_room(tok, n_dp):
    return max(32, tok // n_dp)


def exchange_lists(lists):
    n = lists.shape[0]
    dma = pltpu.SemaphoreType.DMA
    return pl.pallas_call(
        lists_body,
        out_shape=[sds((2,) + lists.shape, jnp.int32), sds(lists.shape[1:], jnp.int32)],
        in_specs=[VM],
        out_specs=[VM, VM],
        scratch_shapes=[dma((2, n)), dma((2, n))],
        compiler_params=params(1),
        name="lists",
    )(lists)


def turned(values):
    lanes = lax.broadcasted_iota(jnp.int32, values.shape, 1) % HDIM
    size = values.shape[1]
    return jnp.where(
        lanes < HDIM // 2,
        -pltpu.roll(values, size - HDIM // 2, 1),
        pltpu.roll(values, HDIM // 2, 1),
    )


def norm_parts(stream):
    average = jnp.mean(stream, -1, keepdims=True)
    centered = stream - average
    variance = jnp.mean(centered * centered, -1, keepdims=True)
    scale = lax.rsqrt(variance + norm_eps)
    return centered * scale, scale


def forward_body(room, kinds, pieces, stride, every, *refs):
    here = Place()
    n, count = here.n_dp, here.count
    table, heard, pos, norm_rows, cosine, sine, seg_row, seg_col = refs[:8]
    attn_in, attn_out, ffn_in, ffn_out = refs[8:12]
    emb_out, zero_out, input_out, q_out, k_out, v_out, lse_out, att_own, att_other = refs[12:21]
    fulls, at = [], 21
    for kind in kinds:
        width = 1 if kind == "plain" else 2
        fulls.append((refs[at], None) if width == 1 else (refs[at], refs[at + 1]))
        at += width
    low_table, served, rows, vt, att_far = refs[at : at + 5]
    lows = refs[at + 5 : at + 10]
    rsem, ysem, asem, wsend, wrecv, wlocal = refs[at + 10 :]
    tok = pos.shape[0]
    half = tok // 2
    width = rows.shape[3]
    slots = n * room
    feats = q_out.shape[1]
    groups = feats // 128
    block = 256

    greet(
        [{"dp": here.mixed(k)} for k in range(1, n)] + [here.across("t"), here.across("y")]
    )
    orders = gather_orders(count)
    for c in range(3):
        lows[0][:, c * feats : (c + 1) * feats] = attn_in[:, c, :].astype(bf16)
    lows[1][...] = attn_out[...].astype(bf16)
    for c in range(2):
        lows[2 + c][...] = ffn_in[:, c, :].astype(bf16)
    lows[4][...] = ffn_out[...].astype(bf16)
    jobs, lags = [], []
    for number, (which, kind, start, size, lag) in enumerate(pieces):
        jobs.append(
            Gather(
                here, lows[which], fulls[which][0], fulls[which][1], orders[kind],
                pl.ds(start, size), wsend.at[number], wrecv.at[number], wlocal.at[number],
            )
        )
        lags.append(lag)
    first = Runner(jobs[:1], lags[:1])
    runner = Runner(jobs[1:], lags[1:], stride)
    first.advance()
    runner.advance()
    low_table[...] = table[...].astype(bf16)
    row_count = table.shape[0]
    out_copies, y_copies = [], []

    def pass_on(k):
        copy = remote(
            rows.at[here.m, k], rows.at[here.m, k], ysem.at[0, k], ysem.at[1, k], here.across("y")
        )
        copy.start()
        y_copies.append(copy)

    for k in list(range(n - 1, 0, -1)) + [0]:
        column = jnp.transpose(heard[0, k])[:room, 0:1]
        hot = (lax.broadcasted_iota(jnp.int32, (room, row_count), 1) == column).astype(f32)
        found = mdot(hot.astype(bf16), low_table[...]).astype(bf16)
        if k == 0:
            rows[here.m, 0] = found
            pass_on(0)
        else:
            served[k] = found
            copy = remote(
                served.at[k], rows.at[here.m, k], rsem.at[0, k], rsem.at[1, k],
                {"dp": here.mixed(k)},
            )
            copy.start()
            out_copies.append(copy)
            if k % 2:
                runner.advance()
        if k == n // 2:
            first.advance()
    first.advance()
    for k in range(n - 1, 0, -1):
        out_copies[n - 1 - k].wait_recv()
        pass_on(k)
        if k % 3 == 1:
            runner.advance()
    first.drain()
    for copy in out_copies:
        copy.wait_send()
    for copy in y_copies:
        copy.wait()

    w_qkv = fulls[0][0]
    for i in range(tok // block):
        at = slice(i * block, (i + 1) * block)
        hot = (lax.broadcasted_iota(jnp.int32, (block, slots), 1) == pos[at, :]).astype(f32)
        hot = hot.astype(bf16)
        emb = jnp.concatenate([mdot(hot, rows[h].reshape(slots, width)) for h in range(2)], 1)
        hat, _scale = norm_parts(emb)
        stream = hat * norm_rows[0:1, :] + norm_rows[1:2, :]
        low = stream.astype(bf16)
        input_out[at, :] = low
        if (i + 1) * block <= half:
            emb_out[at, :] = emb.astype(bf16)
            zero_out[at, :] = stream
        cos, sin = cosine[at, :], sine[at, :]
        proj = mdot(low, w_qkv[...].reshape(2 * width, 3 * feats))
        for c in range(3):
            for g in range(groups):
                cols = slice(g * 128, (g + 1) * 128)
                part = proj[:, c * feats + g * 128 : c * feats + (g + 1) * 128]
                if c < 2:
                    part = part * cos + turned(part) * sin
                part = part.astype(bf16)
                if c == 0:
                    q_out[at, cols] = part * bf16(HDIM**-0.5)
                elif c == 1:
                    k_out[at, cols] = part
                else:
                    v_out[at, cols] = part
        if i % every == every - 1:
            runner.advance()

    lane = lax.broadcasted_iota(jnp.int32, (1, 128), 1)
    att_copies = []
    for g in range(groups):
        cols = slice(g * 128, (g + 1) * 128)
        vt[...] = jnp.transpose(v_out[:, cols].astype(f32)).astype(bf16)
        keys = [jnp.where((lane // HDIM) == h, k_out[:, cols], bf16(0)) for h in range(2)]
        for i in list(range(tok // block // 2, tok // block)) + list(range(tok // block // 2)):
            at = slice(i * block, (i + 1) * block)
            query = q_out[at, cols]
            same = seg_col[...] == seg_row[:, at]
            outs = []
            for h in range(2):
                scores = jnp.where(same, tdot(keys[h], query), neg_large)
                peak = jnp.max(scores, 0, keepdims=True)
                soft = jnp.exp(scores - peak)
                total = jnp.sum(soft, 0, keepdims=True)
                lse_out[2 * g + h, :, at] = peak + jnp.log(total)
                soft = (soft * (1.0 / total)).astype(bf16)
                outs.append(mdot(vt[h * HDIM : (h + 1) * HDIM, :], soft))
            found = jnp.transpose(jnp.concatenate(outs, 0)).astype(bf16)
            if i * block < half:
                att_own[at, cols] = found
            else:
                att_far[slice(i * block - half, (i + 1) * block - half), cols] = found
                if (i + 1) * block == tok:
                    copy = remote(
                        att_far.at[:, cols], att_other.at[:, cols], asem.at[0, g], asem.at[1, g],
                        here.across("y"),
                    )
                    copy.start()
                    att_copies.append(copy)
            if i % every == every - 1:
                runner.advance()
    runner.drain()
    for copy in att_copies:
        copy.wait()


def forward_pass(table, heard, pos, norm_rows, cosine, sine, seg_row, seg_col, raw, kinds, pieces,
                 stride=3, every=1):
    n_dp = heard.shape[1]
    attn_in, attn_out, ffn_in, ffn_out = raw
    rows = attn_in.shape[0]
    shards = (
        sds((rows, 3 * attn_in.shape[2]), f32), sds(attn_out.shape, f32),
        sds(ffn_out.shape, f32), sds(ffn_out.shape, f32), sds(ffn_out.shape, f32),
    )
    room = heard_room(pos.shape[0], n_dp)
    count = n_dp.bit_length() - 1
    halves = (2,) * (count + 1)
    tok = pos.shape[0]
    half = tok // 2
    width = table.shape[1]
    feats = shards[0].shape[1] // 3
    outs = [
        sds((half, 2 * width), bf16),
        sds((half, 2 * width), f32),
        sds((tok, 2 * width), bf16),
        sds((tok, feats), bf16),
        sds((tok, feats), bf16),
        sds((tok, feats), bf16),
        sds((feats // HDIM, 1, tok), f32),
        sds((half, feats), bf16),
        sds((half, feats), bf16),
    ]
    specs = [VM] * len(outs)
    for shard, kind in zip(shards, kinds):
        full = sds(halves + shard.shape, bf16)
        outs += [full] if kind == "plain" else [full, full]
        specs += [VM] if kind == "plain" else [ANY, ANY]
    dma = pltpu.SemaphoreType.DMA
    steps = count + 6
    scratch = (
        [
            pltpu.VMEM(table.shape, bf16),
            pltpu.VMEM((n_dp, room, width), bf16),
            pltpu.VMEM((2, n_dp, room, width), bf16),
            pltpu.VMEM((128, tok), bf16),
            pltpu.VMEM((half, feats), bf16),
        ]
        + [pltpu.VMEM(shard.shape, bf16) for shard in shards]
        + [dma((2, n_dp)), dma((2, n_dp)), dma((2, feats // 128))]
        + [dma((len(pieces), steps)), dma((len(pieces), steps)), dma((len(pieces),))]
    )
    out = pl.pallas_call(
        lambda *refs: forward_body(room, kinds, pieces, stride, every, *refs),
        out_shape=outs,
        in_specs=[VM] * 12,
        out_specs=specs,
        scratch_shapes=scratch,
        compiler_params=params(2),
        name="forward",
    )(table, heard, pos, norm_rows, cosine, sine, seg_row, seg_col, *raw)
    weights, at = [], 9
    for shard, kind in zip(shards, kinds):
        whole = (2 * n_dp * shard.shape[0], shard.shape[1])
        if kind == "plain":
            weights.append(out[at].reshape(whole))
            at += 1
        else:
            weights.append((out[at].reshape(whole), out[at + 1].reshape(whole)))
            at += 2
    return out[:9], weights


def writer(ref, kind=None):
    def store(cols, values):
        if kind is None:
            ref[:, cols] = values
        else:
            ref[:, kind, cols] = values

    return store


def make_scatters(
    here, grads, kinds, pieces, outs, held, landed, send, recv, loads, stride=1
):
    orders = scatter_orders(here.count)
    jobs, lags = [], []
    held, landed = list(held), list(landed)
    for number, (which, kind, start, size, lag) in enumerate(pieces):
        own, other = grads[which]
        pair = other is not None
        mine = [held.pop(0) for _ in range(2 if pair else 1)]
        amount = len(scatter_lands(orders[kind], here.count, pair, 1, 1))
        lands = [landed.pop(0) for _ in range(amount)]
        jobs.append(
            Scatter(
                here, own, other, orders[kind], pl.ds(start, size), mine, lands, outs[which],
                send.at[number], recv.at[number], loads.at[number],
            )
        )
        lags.append(lag)
    return Runner(jobs, lags, stride)


def scatter_scratch(count, rows, pairs, pieces):
    orders = scatter_orders(count)
    held, landed = [], []
    for which, kind, _start, size, _lag in pieces:
        pair = pairs[which]
        held += [pltpu.VMEM((2,) * count + (rows, size), bf16)] * (2 if pair else 1)
        landed += [
            pltpu.VMEM(shape, bf16)
            for shape in scatter_lands(orders[kind], count, pair, rows, size)
        ]
    dma = pltpu.SemaphoreType.DMA
    steps = 2 * count + 6
    sems = [dma((len(pieces), steps)), dma((len(pieces), steps)), dma((len(pieces), 2))]
    return held, landed, sems


def square_sum(values):
    return jnp.sum(jnp.sum(values * values, 0, keepdims=True), 1, keepdims=True)


def store_blocks(ref, values, count, start):
    rows, cols = ref.shape[-2], values.shape[1]
    for number in range(2 ** (count + 1)):
        at = tuple((number >> (count - j)) & 1 for j in range(count + 1))
        ref[at + (slice(None), slice(start, start + cols))] = values[
            number * rows : (number + 1) * rows, :
        ].astype(bf16)


def hidden_body(pieces, sizes, stride, *refs):
    here = Place()
    count = here.count
    (grad_pool, seg, sum_two, norm_rows, low_one, sum_one,
     att_own, att_other, hidden_own, hidden_other) = refs[:10]
    weights = refs[10:16]
    residual, low_out, norms_out, wout_own, wout_other = refs[16:21]
    later = refs[21:25]
    out_down, squares = refs[25:27]
    loaded, down, low_two, turned_one, turned_two, total = refs[27:33]
    held = refs[33 : 33 + sizes[0]]
    landed = refs[33 + sizes[0] : 33 + sizes[0] + sizes[1]]
    wsem, send, recv, loads = refs[33 + sizes[0] + sizes[1] :]
    half, width = low_one.shape
    part = weights[0].shape[1] // 2
    copies = {}

    def load(c, j):
        for w in range(3):
            copies[c, j, w] = pltpu.make_async_copy(
                weights[2 * w + j].at[:, pl.ds(c * part, part)], loaded.at[j * 3 + w],
                wsem.at[(c * 2 + j) * 3 + w],
            )
            copies[c, j, w].start()

    load(0, 0)
    load(0, 1)
    greet([here.across("t"), here.across("y")] + [here.across(j) for j in range(count)])
    grads = [(down.at[0], down.at[1])]
    runner = make_scatters(
        here, grads, None, pieces, (writer(out_down),), held, landed, send, recv, loads, stride
    )
    slots = grad_pool.shape[0]
    hot = (lax.broadcasted_iota(jnp.int32, (half, slots), 1) == seg[0:half, :]).astype(f32)
    grad_two = jnp.dot(hot, grad_pool[...], precision=highest, preferred_element_type=f32)
    hat, scale = norm_parts(sum_two[...])
    grad_hat = grad_two * norm_rows[4:5, :]
    first = jnp.mean(grad_hat, -1, keepdims=True)
    second = jnp.mean(grad_hat * hat, -1, keepdims=True)
    grad_sum = scale * (grad_hat - first - hat * second)
    low_two[...] = grad_sum.astype(bf16)
    turned_two[...] = jnp.transpose(grad_sum).astype(bf16)
    for c in range(2):
        for j, hidden in enumerate((hidden_own, hidden_other)):
            cols = slice(c * part, (c + 1) * part)
            store_blocks(down.at[j], mdot(turned_two[...], hidden[:, cols]), count, c * part)
        runner.advance()
    norms_out[...] = jnp.zeros_like(norms_out)
    norms_out[4:5, :] = jnp.sum(grad_two * hat, 0, keepdims=True)
    norms_out[5:6, :] = jnp.sum(grad_two, 0, keepdims=True)
    turned_one[...] = jnp.transpose(low_one[...].astype(f32)).astype(bf16)
    total[...] = grad_sum
    runner.advance()
    for c in range(2):
        for j in range(2):
            number = j * 3
            for w in range(3):
                copies[c, j, w].wait()
            gate = mdot(low_one[...], loaded[number])
            up = mdot(low_one[...], loaded[number + 1])
            share = 1.0 / (1.0 + jnp.exp(-gate))
            grad_hidden = mdot(low_two[...], loaded[number + 2])
            grad_up = (grad_hidden * (gate * share)).astype(bf16)
            grad_gate = (
                grad_hidden * up * (share * (1.0 + gate * (1.0 - share)))
            ).astype(bf16)
            runner.advance()
            store_blocks(later[j], mdot(turned_one[...], grad_gate), count, c * part)
            store_blocks(later[2 + j], mdot(turned_one[...], grad_up), count, c * part)
            total[...] += tdot(grad_gate, loaded[number]) + tdot(grad_up, loaded[number + 1])
            if c == 0:
                load(1, j)
            runner.advance()
    hat, scale = norm_parts(sum_one[...])
    grad_one = total[...]
    grad_hat = grad_one * norm_rows[2:3, :]
    first = jnp.mean(grad_hat, -1, keepdims=True)
    second = jnp.mean(grad_hat * hat, -1, keepdims=True)
    grad_sum = scale * (grad_hat - first - hat * second)
    norms_out[2:3, :] = jnp.sum(grad_one * hat, 0, keepdims=True)
    norms_out[3:4, :] = jnp.sum(grad_one, 0, keepdims=True)
    residual[...] = grad_sum
    low_out[...] = grad_sum.astype(bf16)
    runner.advance()
    turned_two[...] = jnp.transpose(grad_sum).astype(bf16)
    wout_own[...] = mdot(turned_two[...], att_own[...]).astype(bf16)
    runner.advance()
    wout_other[...] = mdot(turned_two[...], att_other[...]).astype(bf16)
    runner.drain()
    squares[...] = jnp.broadcast_to(square_sum(out_down[...]), squares.shape)


def hidden_back(grad_pool, seg, sum_two, norm_rows, low_one, sum_one, att, hidden, w_gate, w_up,
                w_down, pieces, stride=1):
    n_dp = lax.axis_size("dp")
    count = n_dp.bit_length() - 1
    half, width = low_one.shape
    feats = att[0].shape[1]
    cols = w_gate[0].shape[1]
    rows = width // (2 * n_dp)
    blocks = (2,) * (count + 1) + (rows, cols)
    held, landed, sems = scatter_scratch(count, rows, [True], pieces)
    vmem = pltpu.VMEM
    return pl.pallas_call(
        lambda *refs: hidden_body(pieces, (len(held), len(landed)), stride, *refs),
        out_shape=[
            sds((half, width), f32), sds((half, width), bf16), sds((8, width), f32),
            sds((width, feats), bf16), sds((width, feats), bf16),
        ] + [sds(blocks, bf16)] * 4 + [sds((rows, cols), f32), sds((8, 128), f32)],
        in_specs=[VM] * 10 + [ANY] * 6,
        out_specs=[VM] * 11,
        scratch_shapes=[
            vmem((6, width, cols // 2), bf16), vmem((2,) + blocks, bf16), vmem((half, width), bf16),
            vmem((width, half), bf16), vmem((width, half), bf16), vmem((half, width), f32),
        ] + held + landed + [pltpu.SemaphoreType.DMA((12,))] + sems,
        compiler_params=params(6),
        name="hidden",
    )(grad_pool, seg, sum_two, norm_rows, low_one, sum_one, *att, *hidden,
      *w_gate, *w_up, *w_down)


def backward_body(room, pieces, late_pieces, sizes, stride, every, *refs):
    here = Place()
    n, count = here.n_dp, here.count
    (low, out_own, out_other, query, key, value, lse, cosine, sine, seg_row, seg_col, residual,
     emb, norm_rows, w_qkv, norms_in, before, inputs, pos, heard) = refs[:20]
    grads = [(refs[20 + 2 * j], refs[21 + 2 * j]) for j in range(3)]
    (table_out, norms_out, out_ffn, out_proj, out_qkv, total_out) = refs[26:32]
    refs = refs[:26] + (None,) + refs[26:]
    (kt, dq, dk, dv, grad_att, far_att, far_send, far_recv, grad_proj, turned_in, grad_qkv,
     low_out, norm_part, other, packed, mine, theirs, norms, parts, own_part) = refs[33:53]
    at = 53
    cuts = []
    for size in sizes:
        cuts.append(refs[at : at + size])
        at += size
    held, landed, late_held, late_landed = cuts
    (asem, bsem, ysem, rsem, csem, nsem, tsem, send, recv, loads, late_send, late_recv,
     late_loads) = refs[at:]
    tok, feats = query.shape
    half, width = tok // 2, table_out.shape[1]
    groups = feats // 128
    block = 256
    peers = []
    for rt in range(2):
        for rd in range(n):
            for rm in range(2):
                if rt or rd or rm:
                    where = {
                        "tower": here.t + rt * (1 - 2 * here.t),
                        "dp": here.mixed(rd),
                        "mp": here.m + rm * (1 - 2 * here.m),
                    }
                    peers.append(((rt * n + rd) * 2 + rm, where))
    me = (here.t * n + here.d) * 2 + here.m
    greet([where for _, where in peers])
    runner = make_scatters(
        here, grads, None, pieces, (writer(out_ffn, 0), writer(out_ffn, 1), writer(out_proj)), held,
        landed, send, recv, loads, stride,
    )
    runner.advance()
    att_copies = []
    far_att[...] = mdot(low[...], out_other[...]).astype(bf16)
    for g in range(groups):
        cols = slice(g * 128, (g + 1) * 128)
        copy = remote(
            far_att.at[:, cols], grad_att.at[half:, cols], asem.at[0, g], asem.at[1, g],
            here.across("y"),
        )
        copy.start()
        att_copies.append(copy)
    grad_att[:half, :] = mdot(low[...], out_own[...]).astype(bf16)
    for i in range(tok // block):
        rows = slice(i * block, (i + 1) * block)
        turned_in[:, rows] = jnp.transpose(inputs[rows, :].astype(f32)).astype(bf16)
    runner.advance()
    lane = lax.broadcasted_iota(jnp.int32, (1, 128), 1)
    for g in range(groups):
        cols = slice(g * 128, (g + 1) * 128)
        kt[...] = jnp.transpose(key[:, cols].astype(f32)).astype(bf16)
        keys = [jnp.where((lane // HDIM) == h, key[:, cols], bf16(0)) for h in range(2)]
        values = [jnp.where((lane // HDIM) == h, value[:, cols], bf16(0)) for h in range(2)]
        for i in range(tok // block):
            if i * block == half:
                att_copies[g].wait_recv()
            rows = slice(i * block, (i + 1) * block)
            q_part = query[rows, cols]
            g_part = grad_att[rows, cols]
            same = seg_col[...] == seg_row[:, rows]
            turns = []
            add_k, add_v = None, None
            for h in range(2):
                inside = (lane // HDIM) == h
                scores = jnp.where(same, tdot(keys[h], q_part), neg_large)
                soft = jnp.exp(scores - lse[2 * g + h, :, rows])
                grad_soft = tdot(values[h], g_part)
                inner = jnp.sum(soft * grad_soft, 0, keepdims=True)
                grad_scores = (soft * (grad_soft - inner)).astype(bf16)
                part_v = mdot(soft.astype(bf16), jnp.where(inside, g_part, bf16(0)))
                part_k = mdot(grad_scores, jnp.where(inside, q_part, bf16(0)))
                add_v = part_v if h == 0 else add_v + part_v
                add_k = part_k if h == 0 else add_k + part_k
                turns.append(mdot(kt[h * HDIM : (h + 1) * HDIM, :], grad_scores))
            dq[rows, :] = jnp.transpose(jnp.concatenate(turns, 0)) * (HDIM**-0.5)
            if i == 0:
                dv[...] = add_v
                dk[...] = add_k
            else:
                dv[...] += add_v
                dk[...] += add_k
            if i % every == every - 1:
                runner.advance()
        cos, sin = cosine[...], sine[...]
        for c, grad in ((0, dq), (1, dk)):
            whole = grad[...]
            back = whole * cos - turned(whole) * sin
            grad_proj[:, c * feats + g * 128 : c * feats + (g + 1) * 128] = back.astype(bf16)
        grad_proj[:, 2 * feats + g * 128 : 2 * feats + (g + 1) * 128] = dv[...].astype(bf16)
    for copy in att_copies:
        copy.wait_send()
    far_copies = []
    for i in range(half // block):
        rows = slice(i * block, (i + 1) * block)
        far = grad_proj[half + i * block : half + (i + 1) * block, :]
        far_send[rows, :] = tdot(far, w_qkv[...]).astype(bf16)
        copy = remote(
            far_send.at[rows, :], far_recv.at[rows, :], bsem.at[0, i], bsem.at[1, i],
            here.across("y"),
        )
        copy.start()
        far_copies.append(copy)
    grad_parts = [grad_qkv.at[c] for c in range(3)]
    late = make_scatters(
        here, [(part, None) for part in grad_parts], None, late_pieces,
        [writer(out_qkv, c) for c in range(3)], late_held, late_landed, late_send, late_recv,
        late_loads, 1,
    )
    jobs = late.jobs
    step = feats if grad_qkv.shape[-2] % 16 == 0 else 128
    for start in range(0, 3 * feats, step):
        cols = slice(start, start + step)
        store_blocks(
            grad_parts[start // feats], mdot(turned_in[...], grad_proj[:, cols]), count,
            start % feats,
        )
    late.advance()
    runner.advance()
    theirs_at = pl.ds(pl.multiple_of((1 - here.m) * width, 128), width)
    mine_at = pl.ds(pl.multiple_of(here.m * width, 128), width)
    norm_part[...] = norms_in[...]
    swaps = []
    for i in range(half // block):
        rows = slice(i * block, (i + 1) * block)
        near = residual[rows, :] + tdot(grad_proj[rows, :], w_qkv[...])
        if i == 0:
            runner.advance()
        far_copies[i].wait()
        near = near + far_recv[rows, :].astype(f32)
        hat, scale = norm_parts(emb[rows, :].astype(f32))
        grad_hat = near * norm_rows[0:1, :]
        first = jnp.mean(grad_hat, -1, keepdims=True)
        second = jnp.mean(grad_hat * hat, -1, keepdims=True)
        low_out[rows, :] = (scale * (grad_hat - first - hat * second)).astype(bf16)
        copy = remote(
            low_out.at[rows, theirs_at], other.at[rows, :], ysem.at[0, i], ysem.at[1, i],
            here.across("y"),
        )
        copy.start()
        swaps.append(copy)
        norm_part[0:1, :] += jnp.sum(near * hat, 0, keepdims=True)
        norm_part[1:2, :] += jnp.sum(near, 0, keepdims=True)
    jobs.append(Total(here, norm_part, norms, nsem.at[0], nsem.at[1]))
    late.lags.append(late.tick)
    late.length = max(late.length, late.tick + jobs[-1].last + 1)
    late.advance()
    runner.advance()
    for copy in swaps:
        copy.wait()
    both = jnp.concatenate([low_out[:, mine_at], other[...]], 0)
    copies = []
    for k in list(range(n - 1, 0, -1)) + [0]:
        hot = (
            lax.broadcasted_iota(jnp.int32, (room, pos.shape[1]), 0) + k * room == pos[...]
        ).astype(f32)
        packed[k] = mdot(hot.astype(bf16), both).astype(bf16)
        if k:
            copy = remote(
                packed.at[k], mine.at[k], rsem.at[0, k], rsem.at[1, k], {"dp": here.mixed(k)}
            )
        else:
            mine[0] = packed[0]
            copy = remote(mine.at[0], theirs.at[0], csem.at[0, 0], csem.at[1, 0], here.across("t"))
        copy.start()
        copies.append(copy)
    passed = [copies.pop()]
    late.advance()
    runner.advance()
    for k in range(n - 1, 0, -1):
        copies[n - 1 - k].wait_recv()
        copy = remote(mine.at[k], theirs.at[k], csem.at[0, k], csem.at[1, k], here.across("t"))
        copy.start()
        passed.append(copy)
        if k == n // 2:
            late.advance()
            runner.advance()
    late.advance()
    runner.advance()
    for copy in copies:
        copy.wait_send()
    for copy in passed:
        copy.wait()
    slots = n * room
    row_count = table_out.shape[0]
    size = 424 * 1024 // max(slots, 1024) // 8 * 8
    own_part[...] = jnp.zeros_like(own_part)
    for part in range(-(-row_count // size)):
        rows = slice(part * size, min((part + 1) * size, row_count))
        block_rows = rows.stop - rows.start
        base = lax.broadcasted_iota(jnp.int32, (block_rows, slots), 0) + part * size
        found = 0.0
        for source, sums in ((0, mine), (1, theirs)):
            hot = (base == heard[source]).astype(f32).astype(bf16)
            found = found + mdot(hot, sums[...].reshape(slots, width))
        table_out[rows, :] = found
        own_part[0:1, :] += jnp.sum(found * found, 0, keepdims=True)
        if part % 2:
            late.advance()
            runner.advance()
    late.drain()
    runner.drain()
    norms_out[...] = norm_part[...]
    local_sq = (
        before[0:1, 0:1]
        + 0.5 * jnp.sum(own_part[...], 1, keepdims=True)[0:1]
        + square_sum(out_proj[...])
        + sum(square_sum(out_qkv[:, c, :]) for c in range(3))
        + sum(square_sum(out_ffn[:, c, :]) for c in range(2))
    )
    parts[me] = jnp.broadcast_to(local_sq, parts.shape[1:])
    copies = []
    for rel, where in peers:
        copy = remote(parts.at[me], parts.at[me], tsem.at[0, rel], tsem.at[1, rel], where)
        copy.start()
        copies.append(copy)
    for copy in copies:
        copy.wait()
    total_out[...] = jnp.sum(parts[...], 0) + square_sum(norms_out[...])


def blocks_of(grad, n_dp):
    count = n_dp.bit_length() - 1
    rows = grad.shape[0] // (2 * n_dp)
    return grad.reshape((2,) * (count + 1) + (rows, grad.shape[1]))


def backward_pass(low, w_out, query, key, value, lse, cosine, sine, seg_row, seg_col, residual,
                  emb, norm_rows, w_qkv, norms, before, inputs, pos_row, heard, grads, grad_out,
                  row_count, pieces, late_pieces, stride=3, every=1):
    n_dp = lax.axis_size("dp")
    count = n_dp.bit_length() - 1
    tok, feats = query.shape
    half, width = low.shape
    rows, cols = grads[0].shape[-2:]
    room = heard_room(tok, n_dp)
    held, landed, sems = scatter_scratch(count, rows, [True] * 3, pieces)
    late_held, late_landed, late_sems = scatter_scratch(count, rows, [False] * 3, late_pieces)
    flat = list(grads) + [blocks_of(g, n_dp) for g in grad_out]
    dma = pltpu.SemaphoreType.DMA
    vmem = pltpu.VMEM
    sizes = (len(held), len(landed), len(late_held), len(late_landed))
    steps = max(1, half // 256)
    part = width // 2
    return pl.pallas_call(
        lambda *refs: backward_body(room, pieces, late_pieces, sizes, stride, every, *refs),
        out_shape=[
            sds((row_count, part), f32), sds((8, width), f32),
            sds((rows, 2, cols), f32), sds((rows, feats), f32), sds((rows, 3, feats), f32),
            sds((8, 128), f32),
        ],
        in_specs=[VM] * 20 + [ANY] * 6,
        out_specs=[VM] * 6,
        scratch_shapes=[
            vmem((128, tok), bf16), vmem((tok, 128), f32), vmem((tok, 128), f32),
            vmem((tok, 128), f32), vmem((tok, feats), bf16), vmem((half, feats), bf16),
            vmem((half, width), bf16), vmem((half, width), bf16),
            vmem((tok, 3 * feats), bf16), vmem((width, tok), bf16),
            vmem((3,) + (2,) * (count + 1) + (rows, feats), bf16),
            vmem((half, width), bf16), vmem((8, width), f32), vmem((half, part), bf16),
            vmem((n_dp, room, part), bf16), vmem((n_dp, room, part), bf16),
            vmem((n_dp, room, part), bf16), vmem((count + 2, 8, width), f32),
            vmem((4 * n_dp, 8, 128), f32), vmem((8, part), f32),
        ] + held + landed + late_held + late_landed
        + [dma((2, feats // 128)), dma((2, steps)), dma((2, steps)), dma((2, n_dp)),
           dma((2, n_dp)), dma((2, count + 2)), dma((2, 4 * n_dp))] + sems + late_sems,
        compiler_params=params(4, 60),
        name="backward",
    )(low, w_out[0], w_out[1], query, key, value, lse, cosine, sine, seg_row, seg_col, residual,
      emb, norm_rows, w_qkv, norms, before, inputs, pos_row, heard, *flat)


def loss_body(part, counts, doc_ok, query_ok, target, scale, grad_out, stats, other, low_all, turn,
              psend, precv, esend, erecv):
    here = Place()
    n = here.n_dp
    slots, width = part.shape
    peers = []
    for rt in range(2):
        for rd in range(n):
            if rt or rd:
                peers.append(
                    (rt * n + rd, {"tower": here.t + rt * (1 - 2 * here.t), "dp": here.mixed(rd)})
                )
    greet([where for _, where in peers] + [here.across("y")])
    copy = remote(part, other, psend, precv, here.across("y"))
    copy.start()
    copy.wait()
    pooled = (part[...] + other[...]) / counts[...]
    scale_row = lax.rsqrt(jnp.sum(pooled * pooled, 1, keepdims=True) + 1e-06)
    unit = pooled * scale_row
    low_all[here.t, here.d] = unit.astype(bf16)
    copies = []
    for rel, where in peers:
        copy = remote(
            low_all.at[here.t, here.d], low_all.at[here.t, here.d], esend.at[rel], erecv.at[rel], where
        )
        copy.start()
        copies.append(copy)
    for copy in copies:
        copy.wait()
    total = n * slots
    queries = low_all[0].reshape(total, width)
    documents = low_all[1].reshape(total, width)
    cosines = tdot(queries, documents)
    factor = jnp.exp(jnp.minimum(scale[...], cap_value))
    logits = jnp.where(doc_ok[...] > 0, factor * cosines, neg_large)
    peak = jnp.max(logits, 1, keepdims=True)
    log_total = peak + jnp.log(jnp.sum(jnp.exp(logits - peak), 1, keepdims=True))
    soft = jnp.exp(logits - log_total)
    mask = lax.broadcasted_iota(jnp.int32, (total, total), 1) == target[...]
    picked = jnp.sum(jnp.where(mask, logits, 0.0), 1, keepdims=True)
    valid = query_ok[...] > 0
    query_count = jnp.sum(valid.astype(f32), axis=0, keepdims=True)
    loss_sum = jnp.sum(jnp.where(valid, log_total - picked, 0.0), axis=0, keepdims=True)
    grad_logits = jnp.where(valid, soft - mask.astype(f32), 0.0) / query_count
    by_row = jnp.sum(grad_logits * cosines, 1, keepdims=True)
    grad_scale = (
        jnp.sum(by_row, 0, keepdims=True) * factor * (scale[...] < cap_value).astype(f32)
    )
    grad_cos = factor * grad_logits
    at = pl.ds(pl.multiple_of(here.d * slots, slots), slots)
    turn[0] = grad_cos
    turn[1] = jnp.transpose(grad_cos)
    left = turn[here.t, at, :].astype(bf16)
    right = low_all[1 - here.t].reshape(total, width)
    grad_unit = mdot(left, right)
    grad_pooled = scale_row * (
        grad_unit - unit * jnp.sum(unit * grad_unit, 1, keepdims=True)
    )
    grad_out[...] = grad_pooled / counts[...]
    row = lax.broadcasted_iota(jnp.int32, stats.shape, 0)
    stats[...] = jnp.where(row == 0, loss_sum, jnp.where(row == 1, query_count, grad_scale))


def loss_step(part, counts, doc_ok, query_ok, target, scale):
    n_dp = lax.axis_size("dp")
    slots, width = part.shape
    total = n_dp * slots
    dma = pltpu.SemaphoreType.DMA
    return pl.pallas_call(
        loss_body,
        out_shape=[sds(part.shape, f32), sds((8, 128), f32)],
        in_specs=[VM] * 6,
        out_specs=[VM] * 2,
        scratch_shapes=[
            pltpu.VMEM(part.shape, f32),
            pltpu.VMEM((2, n_dp, slots, width), bf16),
            pltpu.VMEM((2, total, total), f32),
            dma, dma, dma((2 * n_dp,)), dma((2 * n_dp,)),
        ],
        compiler_params=params(3),
        name="loss",
    )(part, counts, doc_ok, query_ok, target, scale)


def rotary_tables(positions):
    half_dim = HDIM // 2
    inverse = 1000.0 ** (-2.0 * jnp.arange(half_dim, dtype=f32) / HDIM)
    angles = positions.astype(f32)[:, None] * inverse[None, :]
    angles = jnp.concatenate([angles] * 4, 1)
    return jnp.cos(angles), jnp.sin(angles)


def layout(lengths, places, slot_count):
    end_points = jnp.cumsum(lengths)
    segment = jnp.sum((places[:, None] >= end_points[None, :]).astype(jnp.int32), 1)
    starts = jnp.concatenate([jnp.zeros((1,), jnp.int32), end_points])
    slot_ids = jnp.arange(slot_count + 1, dtype=jnp.int32)
    segment_start = jnp.sum(jnp.where(segment[:, None] == slot_ids[None, :], starts[None, :], 0), 1)
    return segment, places - segment_start


def norm_back(grad, hat, scale, gain):
    grad_hat = grad * gain
    first = jnp.mean(grad_hat, -1, keepdims=True)
    second = jnp.mean(grad_hat * hat, -1, keepdims=True)
    return (
        scale * (grad_hat - first - hat * second),
        jnp.sum(grad * hat, 0),
        jnp.sum(grad, 0),
    )


def glu(gate_vals, up_vals):
    return jax.nn.silu(gate_vals) * up_vals


def adamw(weight_in, gradient, first_mom, second, factor, step_num, rate):
    gradient = gradient * factor
    first_new = beta_one * first_mom + (1.0 - beta_one) * gradient
    second_new = beta_two * second + (1.0 - beta_two) * gradient * gradient
    first_hat = first_new / (1.0 - beta_one**step_num)
    second_hat = second_new / (1.0 - beta_two**step_num)
    weight_new = weight_in - rate * (
        first_hat / (jnp.sqrt(second_hat) + adam_eps) + decay_rate * weight_in
    )
    return (weight_new, first_new, second_new)


def name_rows(ids, d, n_dp, row_count, room):
    tok = ids.shape[0]
    owner = ids // row_count
    local = ids - owner * row_count
    order = jnp.bitwise_xor(owner, d)
    places = jnp.arange(tok, dtype=jnp.int32)
    first_at = jnp.min(
        jnp.where(ids[:, None] == ids[None, :], places[None, :], tok), 1
    )
    is_first = first_at == places
    slot = jnp.sum(
        (
            (places[None, :] < first_at[:, None])
            & is_first[None, :]
            & (owner[None, :] == owner[:, None])
        ).astype(jnp.int32),
        1,
    )
    over = jnp.max(slot) >= room
    pos = order * room + slot
    wanted = jnp.arange(n_dp * room, dtype=jnp.int32)
    listed = jnp.max(
        jnp.where((pos[None, :] == wanted[:, None]) & is_first[None, :], local[None, :], -1), 1
    ).reshape(n_dp, 1, room)
    listed = jnp.pad(listed, ((0, 0), (0, 0), (0, 128 - room)), constant_values=-1)
    flag = jnp.broadcast_to(over.astype(jnp.int32), (n_dp, 7, 128))
    return pos, jnp.concatenate([listed, flag], 1)


def layer_norm(stream, gain_row, bias_row):
    average = jnp.mean(stream, -1, keepdims=True)
    centered = stream - average
    variance = jnp.mean(centered * centered, -1, keepdims=True)
    return centered * lax.rsqrt(variance + norm_eps) * gain_row + bias_row


def rotate(values, cosine, sine_table):
    half_dim = values.shape[-1] // 2
    turned = jnp.concatenate([-values[..., half_dim:], values[..., :half_dim]], -1)
    return values * cosine + turned * sine_table


def plain_rotary_tables(positions, head_dim):
    half_dim = head_dim // 2
    inverse = 1000.0 ** (-2.0 * jnp.arange(half_dim, dtype=jnp.float32) / head_dim)
    angles = positions.astype(jnp.float32)[:, None] * inverse[None, :]
    angles = jnp.concatenate([angles, angles], 1)[:, None, :]
    return (jnp.cos(angles), jnp.sin(angles))


def plain_layout(lengths, tok_count, slot_count):
    end_points = jnp.cumsum(lengths)
    places = jnp.arange(tok_count, dtype=jnp.int32)
    segment = jnp.sum((places[:, None] >= end_points[None, :]).astype(jnp.int32), 1)
    starts = jnp.concatenate([jnp.zeros((1,), jnp.int32), end_points])
    slot_ids = jnp.arange(slot_count + 1, dtype=jnp.int32)
    segment_start = jnp.sum(jnp.where(segment[:, None] == slot_ids[None, :], starts[None, :], 0), 1)
    return (segment, places - segment_start)


def plain_glu(gate_vals, up_vals):
    return jax.nn.silu(gate_vals) * up_vals


def pool_rows(stream_two, member, counts):
    pooled = jnp.dot(member, stream_two, precision=highest) / counts[:, None]
    return pooled * lax.rsqrt(jnp.sum(pooled * pooled, 1, keepdims=True) + 1e-06)


def model_total(values):
    return lax.psum(values.astype(jnp.bfloat16), "mp").astype(jnp.float32)


def block_scores(query_block, seg_block, key_low, segment, factor):
    scores = (
        jnp.einsum("thd,shd->hts", query_block, key_low, preferred_element_type=jnp.float32)
        * factor
    )
    return jnp.where((seg_block[:, None] == segment[None, :])[None], scores, neg_large)


def attention(query_low, key_low, value_low, segment):
    tok_count, heads_local, head_dim = query_low.shape
    block_rows = min(512, tok_count)
    block_count = tok_count // block_rows
    factor = head_dim ** (-0.5)
    query_blocks = query_low.reshape(block_count, block_rows, heads_local, head_dim)
    seg_blocks = segment.reshape(block_count, block_rows)

    def one_block(operands):
        scores = block_scores(operands[0], operands[1], key_low, segment, factor)
        row_peak = jnp.max(scores, 2, keepdims=True)
        row_total = jnp.sum(jnp.exp(scores - row_peak), 2, keepdims=True)
        log_total = row_peak + jnp.log(row_total)
        soft_rows = jnp.exp(scores - log_total)
        attended = jnp.einsum(
            "hts,shd->thd",
            soft_rows.astype(jnp.bfloat16),
            value_low,
            preferred_element_type=jnp.float32,
        )
        return (attended, log_total[..., 0])

    attended, log_total = lax.map(one_block, (query_blocks, seg_blocks))
    return (attended.reshape(tok_count, heads_local * head_dim), log_total)


def attention_back(query_low, key_low, value_low, grad_attended, log_total, segment):
    tok_count, heads_local, head_dim = query_low.shape
    block_rows = min(512, tok_count)
    block_count = tok_count // block_rows
    factor = head_dim ** (-0.5)
    query_blocks = query_low.reshape(block_count, block_rows, heads_local, head_dim)
    grad_blocks = grad_attended.reshape(block_count, block_rows, heads_local, head_dim)
    seg_blocks = segment.reshape(block_count, block_rows)

    def one_block(running, operands):
        query_block, grad_block, seg_block, lse_block = operands
        scores = block_scores(query_block, seg_block, key_low, segment, factor)
        soft_rows = jnp.exp(scores - lse_block[..., None])
        grad_soft = jnp.einsum(
            "thd,shd->hts", grad_block, value_low, preferred_element_type=jnp.float32
        )
        inner = jnp.sum(soft_rows * grad_soft, 2, keepdims=True)
        grad_scores = (soft_rows * (grad_soft - inner)).astype(jnp.bfloat16)
        grad_query = (
            jnp.einsum("hts,shd->thd", grad_scores, key_low, preferred_element_type=jnp.float32)
            * factor
        )
        grad_key = (
            running[0]
            + jnp.einsum(
                "hts,thd->shd", grad_scores, query_block, preferred_element_type=jnp.float32
            )
            * factor
        )
        grad_value = running[1] + jnp.einsum(
            "hts,thd->shd",
            soft_rows.astype(jnp.bfloat16),
            grad_block,
            preferred_element_type=jnp.float32,
        )
        return ((grad_key, grad_value), grad_query)

    zeros_kv = jnp.zeros(key_low.shape, jnp.float32)
    (grad_key, grad_value), grad_query = lax.scan(
        one_block, (zeros_kv, zeros_kv), (query_blocks, grad_blocks, seg_blocks, log_total)
    )
    return (grad_query.reshape(tok_count, heads_local, head_dim), grad_key, grad_value)


def layer_forward(embed_rows, segment, positions, weights, norm_rows):
    w_qkv, w_out, w_ffn, w_down = weights
    tok_count = embed_rows.shape[0]
    heads_local = w_qkv.shape[2] // HDIM
    stream_zero = layer_norm(embed_rows, norm_rows[0], norm_rows[1])
    input_zero = stream_zero.astype(jnp.bfloat16)
    projected = jnp.einsum("td,dcf->tcf", input_zero, w_qkv, preferred_element_type=jnp.float32)
    heads_view = projected.reshape(tok_count, 3, heads_local, HDIM)
    cosine, sine_table = plain_rotary_tables(positions, HDIM)
    query_low = rotate(heads_view[:, 0], cosine, sine_table).astype(jnp.bfloat16)
    key_low = rotate(heads_view[:, 1], cosine, sine_table).astype(jnp.bfloat16)
    value_low = heads_view[:, 2].astype(jnp.bfloat16)
    attended, log_total = attention(query_low, key_low, value_low, segment)
    attended_low = attended.astype(jnp.bfloat16)
    attn_branch = model_total(
        jnp.einsum("tf,df->td", attended_low, w_out, preferred_element_type=jnp.float32)
    )
    sum_one = stream_zero + attn_branch
    stream_one = layer_norm(sum_one, norm_rows[2], norm_rows[3])
    input_one = stream_one.astype(jnp.bfloat16)
    gate_up = jnp.einsum("td,dcf->tcf", input_one, w_ffn, preferred_element_type=jnp.float32)
    hidden_low = plain_glu(gate_up[:, 0], gate_up[:, 1]).astype(jnp.bfloat16)
    ffn_branch = model_total(
        jnp.einsum("tf,df->td", hidden_low, w_down, preferred_element_type=jnp.float32)
    )
    sum_two = stream_one + ffn_branch
    stream_two = layer_norm(sum_two, norm_rows[4], norm_rows[5])
    kept_vals = (
        embed_rows,
        sum_one,
        sum_two,
        input_zero,
        input_one,
        query_low,
        key_low,
        value_low,
        log_total,
        attended_low,
        gate_up,
        hidden_low,
    )
    return (stream_two, kept_vals)


def layer_backward(grad_two, kept_vals, weights, norm_rows, segment, positions):
    w_qkv, w_out, w_ffn, w_down = weights
    (
        embed_rows,
        sum_one,
        sum_two,
        input_zero,
        input_one,
        query_low,
        key_low,
        value_low,
        log_total,
        attended_low,
        gate_up,
        hidden_low,
    ) = kept_vals
    tok_count, heads_local, head_dim = query_low.shape
    grad_sum_two, gain_two, bias_two = jax.vjp(layer_norm, sum_two, norm_rows[4], norm_rows[5])[1](
        grad_two
    )
    ffn_low = grad_sum_two.astype(jnp.bfloat16)
    grad_down = jnp.einsum("td,tf->df", ffn_low, hidden_low, preferred_element_type=jnp.float32)
    grad_hidden = jnp.einsum("td,df->tf", ffn_low, w_down, preferred_element_type=jnp.float32)
    grad_gate, grad_up = jax.vjp(plain_glu, gate_up[:, 0], gate_up[:, 1])[1](grad_hidden)
    gate_grads = jnp.stack([grad_gate, grad_up], 1).astype(jnp.bfloat16)
    grad_ffn = jnp.einsum("td,tcf->dcf", input_one, gate_grads, preferred_element_type=jnp.float32)
    grad_stream_one = grad_sum_two + model_total(
        jnp.einsum("tcf,dcf->td", gate_grads, w_ffn, preferred_element_type=jnp.float32)
    )
    grad_sum_one, gain_one, bias_one = jax.vjp(layer_norm, sum_one, norm_rows[2], norm_rows[3])[1](
        grad_stream_one
    )
    attn_low = grad_sum_one.astype(jnp.bfloat16)
    grad_out = jnp.einsum("td,tf->df", attn_low, attended_low, preferred_element_type=jnp.float32)
    grad_attended = jnp.einsum(
        "td,df->tf", attn_low, w_out, preferred_element_type=jnp.float32
    ).astype(jnp.bfloat16)
    grad_query, grad_key, grad_value = attention_back(
        query_low,
        key_low,
        value_low,
        grad_attended.reshape(tok_count, heads_local, head_dim),
        log_total,
        segment,
    )
    cosine, sine_table = plain_rotary_tables(positions, head_dim)
    turn_back = jax.vjp(lambda values: rotate(values, cosine, sine_table), grad_query)[1]
    grad_projected = jnp.stack([turn_back(grad_query)[0], turn_back(grad_key)[0], grad_value], 1)
    grad_projected = grad_projected.reshape(tok_count, 3, heads_local * head_dim).astype(
        jnp.bfloat16
    )
    grad_qkv = jnp.einsum(
        "td,tcf->dcf", input_zero, grad_projected, preferred_element_type=jnp.float32
    )
    grad_stream_zero = grad_sum_one + model_total(
        jnp.einsum("tcf,dcf->td", grad_projected, w_qkv, preferred_element_type=jnp.float32)
    )
    grad_embed, gain_zero, bias_zero = jax.vjp(layer_norm, embed_rows, norm_rows[0], norm_rows[1])[
        1
    ](grad_stream_zero)
    norm_grads = jnp.stack([gain_zero, bias_zero, gain_one, bias_one, gain_two, bias_two])
    return (grad_embed, (grad_qkv, grad_out, grad_ffn, grad_down), norm_grads)


def plain_adamw(weight_in, gradient, first_mom, second, factor, step_num, rate):
    gradient = gradient * factor
    first_new = beta_one * first_mom + (1.0 - beta_one) * gradient
    second_new = beta_two * second + (1.0 - beta_two) * gradient * gradient
    first_hat = first_new / (1.0 - beta_one**step_num)
    second_hat = second_new / (1.0 - beta_two**step_num)
    weight_new = weight_in - rate * (
        first_hat / (jnp.sqrt(second_hat) + adam_eps) + decay_rate * weight_in
    )
    return (weight_new, first_new, second_new)


def plain_step(
    token_ids,
    seq_lengths,
    positives,
    embedding,
    attn_in,
    attn_out,
    ffn_in,
    ffn_out,
    norm_params,
    logit_scale,
    embed_m,
    embed_v,
    attn_in_m,
    attn_in_v,
    attn_out_m,
    attn_out_v,
    ffn_in_m,
    ffn_in_v,
    ffn_out_m,
    ffn_out_v,
    norm_m,
    norm_v,
    scale_m,
    scale_v,
):
    n_data = lax.axis_size("dp")
    tower_idx = lax.axis_index("tower")
    data_idx = lax.axis_index("dp")
    model_idx = lax.axis_index("mp")
    slot_count = seq_lengths.shape[2]
    token_list = token_ids[0]
    tok_count = token_list.shape[0]
    model_width = norm_params.shape[1]
    local_width = embedding.shape[1]
    row_count = embedding.shape[0]
    weights = (
        lax.all_gather(attn_in.astype(jnp.bfloat16), ("tower", "dp"), axis=0, tiled=True),
        lax.all_gather(attn_out.astype(jnp.bfloat16), ("tower", "dp"), axis=0, tiled=True),
        lax.all_gather(ffn_in.astype(jnp.bfloat16), ("tower", "dp"), axis=0, tiled=True),
        lax.all_gather(ffn_out.astype(jnp.bfloat16), ("tower", "dp"), axis=0, tiled=True),
    )
    shard_piece = lax.all_gather(embedding.astype(jnp.bfloat16), "dp", axis=0, tiled=True)
    inside = (token_list >= 0) & (token_list < shard_piece.shape[0])
    picked = jnp.take(shard_piece, jnp.clip(token_list, 0, shard_piece.shape[0] - 1), axis=0)
    looked = jnp.where(inside[:, None], picked.astype(jnp.float32), 0.0)
    embed_rows = lax.all_gather(looked.astype(jnp.bfloat16), "mp", axis=1, tiled=True).astype(
        jnp.float32
    )
    lengths_row = seq_lengths[tower_idx, data_idx]
    segment, positions = plain_layout(lengths_row, tok_count, slot_count)
    stream_two, kept_vals = layer_forward(embed_rows, segment, positions, weights, norm_params)
    member = (segment[None, :] == jnp.arange(slot_count, dtype=jnp.int32)[:, None]).astype(
        jnp.float32
    )
    counts = jnp.maximum(lengths_row, 1).astype(jnp.float32)
    own_embeds, pool_back = jax.vjp(lambda stream: pool_rows(stream, member, counts), stream_two)
    all_embeds = lax.all_gather(
        own_embeds.astype(jnp.bfloat16), ("tower", "dp"), axis=0, tiled=True
    )
    query_total = n_data * slot_count
    rows_per = slot_count // 2
    first_row = (tower_idx * n_data + data_idx) * rows_per
    query_rows = lax.dynamic_slice_in_dim(all_embeds, first_row, rows_per, 0)
    documents = all_embeds[query_total:]
    cosines = jnp.einsum("qd,kd->qk", query_rows, documents, preferred_element_type=jnp.float32)
    logit_factor = jnp.exp(jnp.minimum(logit_scale[0], cap_value))
    doc_ok = seq_lengths[1].reshape(-1) > 0
    query_ok_all = seq_lengths[0].reshape(-1) > 0
    query_count = jnp.sum(query_ok_all.astype(jnp.float32))
    query_ok = lax.dynamic_slice_in_dim(query_ok_all, first_row, rows_per, 0)
    logits = jnp.where(doc_ok[None, :], logit_factor * cosines, neg_large)
    row_peak = jnp.max(logits, 1, keepdims=True)
    log_total = row_peak + jnp.log(jnp.sum(jnp.exp(logits - row_peak), 1, keepdims=True))
    soft_rows = jnp.exp(logits - log_total)
    targets = lax.dynamic_slice_in_dim(positives.reshape(-1), first_row, rows_per, 0)
    target_mask = jnp.arange(query_total, dtype=jnp.int32)[None, :] == targets[:, None]
    picked = jnp.sum(jnp.where(target_mask, logits, 0.0), 1)
    loss_part = jnp.sum(jnp.where(query_ok, log_total[:, 0] - picked, 0.0))
    grad_logits = (
        jnp.where(query_ok[:, None], soft_rows - target_mask.astype(jnp.float32), 0.0) / query_count
    )
    scale_part = (
        jnp.sum(grad_logits * cosines)
        * logit_factor
        * (logit_scale[0] < cap_value).astype(jnp.float32)
    )
    grad_cos = (logit_factor * grad_logits).astype(jnp.bfloat16)
    grad_queries = jnp.einsum("qk,kd->qd", grad_cos, documents, preferred_element_type=jnp.float32)
    grad_documents = jnp.einsum(
        "qk,qd->kd", grad_cos, query_rows, preferred_element_type=jnp.float32
    )
    grad_term = jnp.concatenate(
        [jnp.zeros((query_total, model_width), jnp.float32), grad_documents], 0
    )
    grad_term = lax.dynamic_update_slice_in_dim(grad_term, grad_queries, first_row, 0)
    own_grad = lax.psum_scatter(grad_term, ("tower", "dp"), scatter_dimension=0, tiled=True)
    grad_two = pool_back(own_grad)[0]
    grad_embed, layer_grads, norm_grads = layer_backward(
        grad_two, kept_vals, weights, norm_params, segment, positions
    )
    embed_low = grad_embed.astype(jnp.bfloat16)
    column_part = lax.dynamic_slice_in_dim(embed_low, model_idx * local_width, local_width, 1)
    row_start = data_idx * row_count
    all_ids = lax.all_gather(token_list, ("tower", "dp"), axis=0, tiled=True)
    piece_ids = all_ids - row_start
    inside = (piece_ids >= 0) & (piece_ids < row_count)
    slot_ids = jnp.where(inside, piece_ids, row_count)
    embed_grad = jax.ops.segment_sum(
        lax.all_gather(column_part, ("tower", "dp"), axis=0, tiled=True).astype(jnp.float32),
        slot_ids,
        num_segments=row_count + 1,
    )[:row_count]
    shard_grads = (
        lax.psum_scatter(layer_grads[0], ("tower", "dp"), scatter_dimension=0, tiled=True),
        lax.psum_scatter(layer_grads[1], ("tower", "dp"), scatter_dimension=0, tiled=True),
        lax.psum_scatter(layer_grads[2], ("tower", "dp"), scatter_dimension=0, tiled=True),
        lax.psum_scatter(layer_grads[3], ("tower", "dp"), scatter_dimension=0, tiled=True),
    )
    norm_grad, loss_sum, scale_grad = lax.psum((norm_grads, loss_part, scale_part), ("tower", "dp"))
    local_sq = sum((jnp.sum(gradient * gradient) for gradient in shard_grads)) + 0.5 * jnp.sum(
        embed_grad * embed_grad
    )
    total_sq = (
        lax.psum(local_sq, ("tower", "dp", "mp"))
        + jnp.sum(norm_grad * norm_grad)
        + scale_grad * scale_grad
    )
    grad_norm = jnp.sqrt(total_sq)
    factor = jnp.minimum(1.0, clip_max / (grad_norm + 1e-06))
    step_num = float(STEP)
    embed_new = plain_adamw(embedding, embed_grad, embed_m, embed_v, factor, step_num, learn_rate)
    qkv_new = plain_adamw(attn_in, shard_grads[0], attn_in_m, attn_in_v, factor, step_num, learn_rate)
    out_new = plain_adamw(attn_out, shard_grads[1], attn_out_m, attn_out_v, factor, step_num, out_rate)
    ffn_new = plain_adamw(ffn_in, shard_grads[2], ffn_in_m, ffn_in_v, factor, step_num, learn_rate)
    down_new = plain_adamw(ffn_out, shard_grads[3], ffn_out_m, ffn_out_v, factor, step_num, learn_rate)
    norms_new = plain_adamw(norm_params, norm_grad, norm_m, norm_v, factor, step_num, norm_rate)
    scale_new = plain_adamw(
        logit_scale, scale_grad.reshape(1), scale_m, scale_v, factor, step_num, learn_rate
    )
    return (
        embed_new[0],
        embed_new[1],
        embed_new[2],
        qkv_new[0],
        qkv_new[1],
        qkv_new[2],
        out_new[0],
        out_new[1],
        out_new[2],
        ffn_new[0],
        ffn_new[1],
        ffn_new[2],
        down_new[0],
        down_new[1],
        down_new[2],
        norms_new[0],
        norms_new[1],
        norms_new[2],
        scale_new[0],
        scale_new[1],
        scale_new[2],
        loss_sum.reshape(1),
        query_count.reshape(1),
        grad_norm.reshape(1),
    )


def lean_step(args, pos, heard):
    (
        token_ids, seq_lengths, positives, embedding, attn_in, attn_out, ffn_in, ffn_out,
        norm_params, logit_scale, embed_m, embed_v, attn_in_m, attn_in_v, attn_out_m, attn_out_v,
        ffn_in_m, ffn_in_v, ffn_out_m, ffn_out_v, norm_m, norm_v, scale_m, scale_v,
    ) = args
    tower_idx = lax.axis_index("tower")
    data_idx = lax.axis_index("dp")
    model_idx = lax.axis_index("mp")
    slot_count = seq_lengths.shape[2]
    tok = token_ids.shape[1]
    half = tok // 2
    row_count = embedding.shape[0]
    feats = attn_out.shape[1]
    ff = ffn_out.shape[1]
    part_ff = ff // 2

    kinds = ("plain", "late", "late", "late", "late")
    gather_pieces = [(0, "plain", 0, 3 * feats, 0)]
    quarter = ff // 4
    for turn, which in enumerate((2, 3, 4)):
        for c in range(4):
            kind = ("late", "early", "cross")[(4 * turn + c) % 3]
            gather_pieces.append((which, kind, c * quarter, quarter, 4 * turn + c))
    gather_pieces.append((1, "early", 0, feats, 6))
    places = (jnp.arange(tok, dtype=jnp.int32) + model_idx * half) % tok
    pos_rel = jnp.where(model_idx == 0, pos, jnp.concatenate([pos[half:], pos[:half]]))
    lengths_row = seq_lengths[tower_idx, data_idx]
    segment, positions = layout(lengths_row, places, slot_count)
    cosine, sine = rotary_tables(positions)
    seg_row, seg_col = segment[None, :], segment[:, None]
    named = heard[:, :, 0, : heard_room(tok, heard.shape[1])].reshape(2, 1, -1)
    kept, weights = forward_pass(
        embedding, heard, pos_rel[:, None], norm_params, cosine, sine, seg_row, seg_col,
        (attn_in, attn_out, ffn_in, ffn_out), kinds, gather_pieces,
    )
    emb, stream_zero, input_zero, query, key, value, lse = kept[:7]
    att = kept[7:9]
    w_qkv, w_out, w_gate, w_up, w_down = weights

    sum_one = stream_zero + tdot(att[0], w_out[0]) + tdot(att[1], w_out[1])
    hat_one, scale_one = norm_parts(sum_one)
    stream_one = hat_one * norm_params[2] + norm_params[3]
    input_one = stream_one.astype(bf16)
    gates = [mdot(input_one, w_gate[j]) for j in range(2)]
    ups = [mdot(input_one, w_up[j]) for j in range(2)]
    hidden = [glu(gates[j], ups[j]).astype(bf16) for j in range(2)]
    sum_two = stream_one + tdot(hidden[0], w_down[0]) + tdot(hidden[1], w_down[1])
    hat_two, scale_two = norm_parts(sum_two)
    stream_two = hat_two * norm_params[4] + norm_params[5]

    member = (segment[None, :half] == jnp.arange(slot_count, dtype=jnp.int32)[:, None]).astype(f32)
    counts = jnp.maximum(lengths_row, 1).astype(f32)[:, None]
    part = jnp.dot(member, stream_two, precision=highest)
    doc_ok = (seq_lengths[1].reshape(1, -1) > 0).astype(f32)
    query_ok = (seq_lengths[0].reshape(-1, 1) > 0).astype(f32)
    grad_pool, stats = loss_step(
        part, counts, doc_ok, query_ok, positives.reshape(-1, 1), logit_scale.reshape(1, 1)
    )
    loss_sum, query_count, scale_grad = stats[0, 0], stats[1, 0], stats[2, 0]

    def weight_grad(left, right):
        return jnp.einsum("td,tf->df", left, right, preferred_element_type=f32).astype(bf16)

    pieces = [
        (0, kind, c * quarter, quarter, c // 2)
        for c, kind in enumerate(("early", "cross", "early", "late"))
    ]
    out = hidden_back(
        grad_pool, seg_col, sum_two, norm_params, input_one, sum_one, att, hidden, w_gate, w_up, w_down, pieces, 2,
    )
    grad_sum_one, attn_low, norms = out[:3]
    grad_out, later, r_down, squares = out[3:5], out[5:9], out[9], out[10]
    pieces = [
        (c // 4, ("early", "late", "cross")[c % 3], (c % 4) * quarter, quarter, c)
        for c in range(8)
    ] + [(2, "early", 0, feats, 3)]
    late_pieces = [(c, "plain", 0, feats, 0) for c in range(3)]
    embed_grad, norm_sum, r_ffn, r_out, r_qkv, total = backward_pass(
        attn_low, w_out, query, key, value, lse, cosine, sine, seg_row, seg_col, grad_sum_one,
        emb, norm_params, w_qkv, norms, squares, input_zero, pos_rel[None, :], named,
        later, grad_out, row_count, pieces, late_pieces,
    )
    norm_grad = norm_sum[:6]
    total_sq = total[0, 0] + scale_grad * scale_grad
    grad_norm = jnp.sqrt(total_sq)
    factor = jnp.minimum(1.0, clip_max / (grad_norm + 1e-06))
    step_num = float(STEP)
    embed_new = adamw(embedding, embed_grad, embed_m, embed_v, factor, step_num, learn_rate)
    qkv_new = adamw(attn_in, r_qkv, attn_in_m, attn_in_v, factor, step_num, learn_rate)
    out_new = adamw(attn_out, r_out, attn_out_m, attn_out_v, factor, step_num, out_rate)
    ffn_new = adamw(ffn_in, r_ffn, ffn_in_m, ffn_in_v, factor, step_num, learn_rate)
    down_new = adamw(ffn_out, r_down, ffn_out_m, ffn_out_v, factor, step_num, learn_rate)
    norms_new = adamw(norm_params, norm_grad, norm_m, norm_v, factor, step_num, norm_rate)
    scale_new = adamw(
        logit_scale, scale_grad.reshape(1), scale_m, scale_v, factor, step_num, learn_rate
    )
    return (
        *embed_new, *qkv_new, *out_new, *ffn_new, *down_new, *norms_new, *scale_new,
        loss_sum.reshape(1), query_count.reshape(1), grad_norm.reshape(1),
    )


def local(*args):
    token_ids, embedding = args[0], args[3]
    n_dp = lax.axis_size("dp")
    room = heard_room(token_ids.shape[1], n_dp)
    pos, lists = name_rows(
        token_ids[0], lax.axis_index("dp"), n_dp, embedding.shape[0], room
    )
    heard, flag = exchange_lists(lists)
    return lax.cond(
        flag[1, 0] > 0,
        lambda values: plain_step(*values),
        lambda values: lean_step(values, pos, heard),
        args,
    )


def solution(mesh):
    table, rows3, rows2 = P("dp", "mp"), P(("tower", "dp"), None, "mp"), P(("tower", "dp"), "mp")
    weights = (table, rows3, rows2, rows3, rows2)
    moments = tuple(spec for spec in weights for _ in range(2))
    return jax.shard_map(
        local,
        mesh=mesh,
        in_specs=(P("tower", "dp"), P(), P()) + weights + (P(), P()) + moments + (P(),) * 4,
        out_specs=tuple(spec for spec in weights for _ in range(3)) + (P(),) * 9,
        check_vma=False,
    )
```

```python
import jax
import jax.numpy as jnp
from jax import lax
from jax.sharding import PartitionSpec as P
from jax.experimental import pallas as pl
from jax.experimental.pallas import tpu as pltpu

HDIM = 64
STEP = 5

norm_eps = 1e-06
cap_value = 3.4
clip_max = 0.01
beta_one = 0.9
beta_two = 0.999
learn_rate = 0.02
out_rate = 0.05
norm_rate = 0.3
decay_rate = 0.01
adam_eps = 1e-08
neg_large = -1e30
highest = lax.Precision.HIGHEST
f32 = jnp.float32
bf16 = jnp.bfloat16
MESH = pl.DeviceIdType.MESH
ANY = pl.BlockSpec(memory_space=pl.ANY)
VM = pl.BlockSpec(memory_space=pltpu.VMEM)


def sds(shape, dtype):
    return jax.ShapeDtypeStruct(shape, dtype)


def params(ident, limit=58):
    return pltpu.CompilerParams(
        collective_id=ident, has_side_effects=True, vmem_limit_bytes=limit << 20
    )


class Place:
    def __init__(self):
        self.n_dp = lax.axis_size("dp")
        self.count = self.n_dp.bit_length() - 1
        self.t = lax.axis_index("tower")
        self.d = lax.axis_index("dp")
        self.m = lax.axis_index("mp")
        self.bits = [(self.d // (1 << (self.count - 1 - j))) % 2 for j in range(self.count)]

    def across(self, dim):
        if dim == "t":
            return {"tower": 1 - self.t}
        if dim == "y":
            return {"mp": 1 - self.m}
        step = 1 << (self.count - 1 - dim)
        return {"dp": self.d + (1 - 2 * self.bits[dim]) * step}

    def mixed(self, rel):
        out = self.d
        for j in range(self.count):
            step = 1 << (self.count - 1 - j)
            if rel & step:
                out = out + (1 - 2 * self.bits[j]) * step
        return out


def remote(src, dst, send, recv, where):
    return pltpu.make_async_remote_copy(
        src_ref=src, dst_ref=dst, send_sem=send, recv_sem=recv, device_id=where, device_id_type=MESH
    )


def greet(peers):
    barrier = pltpu.get_barrier_semaphore()
    for where in peers:
        pl.semaphore_signal(barrier, inc=1, device_id=where, device_id_type=MESH)
    pl.semaphore_wait(barrier, len(peers))


def tdot(lhs, rhs):
    return lax.dot_general(lhs, rhs, (((1,), (1,)), ((), ())), preferred_element_type=f32)


def mdot(lhs, rhs):
    return jnp.dot(lhs, rhs, preferred_element_type=f32)


def every(ndim, cols):
    return (slice(None),) * (ndim - 1) + (cols,)


class Gather:
    def __init__(self, here, shard, full, other, order, cols, send, recv, local_sem):
        self.here, self.shard, self.full, self.other = here, shard, full, other
        self.order, self.cols, self.send, self.recv = order, cols, send, recv
        self.local_sem = local_sem
        self.last = len(order)
        self.done = set()
        self.live, self.sent = [], []
        self.arrays = [full]
        self.slot = 0

    def view(self):
        here = self.here
        return (
            (here.t,)
            + tuple(slice(None) if j in self.done else here.bits[j] for j in range(here.count))
            + (slice(None), self.cols)
        )

    def stage(self, step):
        here = self.here
        if step == 0:
            self.place = pltpu.make_async_copy(
                self.shard.at[:, self.cols], self.full.at[self.view()], self.local_sem
            )
            self.place.start()
        for copy in self.live:
            copy.wait_recv()
        if step == 1:
            self.place.wait()
        self.sent += self.live
        self.live = []
        if step == self.last:
            for copy in self.sent:
                copy.wait_send()
            return
        dim = self.order[step]
        if dim == "y":
            pairs = [(self.full.at[self.view()], self.other.at[self.view()])]
            self.arrays = [self.full, self.other]
        elif step == 0:
            pairs = [(self.shard.at[:, self.cols], self.full.at[self.view()])]
        else:
            pairs = [(ref.at[self.view()], ref.at[self.view()]) for ref in self.arrays]
        for src, dst in pairs:
            copy = remote(
                src, dst, self.send.at[self.slot], self.recv.at[self.slot], here.across(dim)
            )
            copy.start()
            self.live.append(copy)
            self.slot += 1
        if dim not in ("t", "y"):
            self.done.add(dim)


class Scatter:
    def __init__(self, here, own, other, order, cols, held, landed, out, send, recv, local_sems):
        self.here, self.order, self.cols = here, order, cols
        self.source = [own] if other is None else [own, other]
        self.held, self.landed, self.out = held, landed, out
        self.send, self.recv, self.local_sems = send, recv, local_sems
        self.last = len(order)
        self.fixed = {}
        self.live = []
        self.slot = 0
        self.arrays = list(range(len(self.source)))

    def view(self, extra=None):
        fixed = dict(self.fixed)
        if extra:
            fixed.update(extra)
        return tuple(fixed.get(j, slice(None)) for j in range(self.here.count))

    def start(self, src, where, index):
        copy = remote(
            src, self.landed[self.slot], self.send.at[self.slot], self.recv.at[self.slot], where
        )
        copy.start()
        self.live.append((copy, self.slot, index))
        self.slot += 1

    def stage(self, step):
        here = self.here
        if step > 0:
            self.finish(step - 1)
        if step == self.last:
            return
        dim = self.order[step]
        if dim == "t":
            self.loads = []
            tail = (slice(None),) * (here.count + 1) + (self.cols,)
            for index in self.arrays:
                load = pltpu.make_async_copy(
                    self.source[index].at[(here.t,) + tail], self.held[index],
                    self.local_sems.at[index],
                )
                load.start()
                self.loads.append(load)
                self.start(self.source[index].at[(1 - here.t,) + tail], here.across("t"), index)
        elif dim == "y":
            self.start(self.held[1].at[self.view()], here.across("y"), 0)
            self.arrays = [0]
        else:
            far = self.view({dim: 1 - here.bits[dim]})
            for index in self.arrays:
                self.start(self.held[index].at[far], here.across(dim), index)

    def finish(self, step):
        here = self.here
        dim = self.order[step]
        if dim not in ("t", "y"):
            self.fixed[dim] = here.bits[dim]
        view = self.view()
        if dim == "t":
            for load in self.loads:
                load.wait()
        for copy, slot, index in self.live:
            copy.wait()
            total = self.held[index][view].astype(f32) + self.landed[slot][...].astype(f32)
            if step == self.last - 1:
                self.out(self.cols, total)
            else:
                self.held[index][view] = total.astype(bf16)
        self.live = []


class Total:
    def __init__(self, here, value, landed, send, recv):
        self.here, self.value, self.landed, self.send, self.recv = here, value, landed, send, recv
        self.order = ["t", "y"] + list(range(here.count))
        self.last = len(self.order)

    def stage(self, step):
        if step > 0:
            self.copy.wait()
            self.value[...] += self.landed[step - 1]
        if step < self.last:
            self.copy = remote(
                self.value, self.landed.at[step], self.send.at[step], self.recv.at[step],
                self.here.across(self.order[step]),
            )
            self.copy.start()


class Runner:
    def __init__(self, jobs, lags, stride=1):
        self.jobs, self.lags, self.stride, self.tick = jobs, lags, stride, 0
        self.length = max(job.last * stride + lag for job, lag in zip(jobs, lags)) + 1

    def advance(self):
        if self.tick < self.length:
            for job, lag in zip(self.jobs, self.lags):
                since = self.tick - lag
                if since % self.stride == 0 and 0 <= since // self.stride <= job.last:
                    job.stage(since // self.stride)
            self.tick += 1

    def drain(self):
        while self.tick < self.length:
            self.advance()


def gather_orders(count):
    far, near = list(range(count - 1)), [count - 1]
    return {
        "plain": far + near + ["t"],
        "late": far + near + ["y", "t"],
        "early": far + ["y"] + near + ["t"],
        "cross": far[:-1] + near + ["y"] + far[-1:] + ["t"],
    }


def scatter_orders(count):
    near, far = [count - 1], list(range(count - 2, -1, -1))
    return {
        "plain": ["t"] + near + far,
        "early": ["t", "y"] + near + far,
        "late": ["t"] + near + ["y"] + far,
        "cross": ["t"] + far[:1] + ["y"] + near + far[1:],
    }


def scatter_lands(order, count, pair, rows, cols):
    shapes, free, live = [], count, 2 if pair else 1
    for dim in order:
        if dim == "y":
            live = 1
        elif dim != "t":
            free -= 1
        shapes += [(2,) * free + (rows, cols)] * live
    return shapes


def lists_body(lists, heard, flag, send, recv):
    here = Place()
    n = here.n_dp
    peers = []
    for rt in range(2):
        for k in range(n):
            if rt or k:
                peers.append((rt, k, {"tower": here.t + rt * (1 - 2 * here.t), "dp": here.mixed(k)}))
    greet([where for _, _, where in peers])
    copies = []
    for rt, k, where in peers:
        copy = remote(lists.at[k], heard.at[rt, k], send.at[rt, k], recv.at[rt, k], where)
        copy.start()
        copies.append(copy)
    heard[0, 0] = lists[0]
    for copy in copies:
        copy.wait()
    flag[...] = jnp.max(heard[...].reshape((2 * n,) + flag.shape), axis=0)


def heard_room(tok, n_dp):
    return max(32, tok // n_dp)


def exchange_lists(lists):
    n = lists.shape[0]
    dma = pltpu.SemaphoreType.DMA
    return pl.pallas_call(
        lists_body,
        out_shape=[sds((2,) + lists.shape, jnp.int32), sds(lists.shape[1:], jnp.int32)],
        in_specs=[VM],
        out_specs=[VM, VM],
        scratch_shapes=[dma((2, n)), dma((2, n))],
        compiler_params=params(1),
        name="lists",
    )(lists)


def turned(values):
    lanes = lax.broadcasted_iota(jnp.int32, values.shape, 1) % HDIM
    size = values.shape[1]
    return jnp.where(
        lanes < HDIM // 2,
        -pltpu.roll(values, size - HDIM // 2, 1),
        pltpu.roll(values, HDIM // 2, 1),
    )


def norm_parts(stream):
    average = jnp.mean(stream, -1, keepdims=True)
    centered = stream - average
    variance = jnp.mean(centered * centered, -1, keepdims=True)
    scale = lax.rsqrt(variance + norm_eps)
    return centered * scale, scale


def forward_body(room, kinds, pieces, stride, every, *refs):
    here = Place()
    n, count = here.n_dp, here.count
    table, heard, pos, norm_rows, cosine, sine, seg_row, seg_col = refs[:8]
    attn_in, attn_out, ffn_in, ffn_out = refs[8:12]
    emb_out, zero_out, input_out, q_out, k_out, v_out, lse_out, att_own, att_other = refs[12:21]
    fulls, at = [], 21
    for kind in kinds:
        width = 1 if kind == "plain" else 2
        fulls.append((refs[at], None) if width == 1 else (refs[at], refs[at + 1]))
        at += width
    low_table, served, rows, vt, att_far = refs[at : at + 5]
    lows = refs[at + 5 : at + 10]
    rsem, ysem, asem, wsend, wrecv, wlocal = refs[at + 10 :]
    tok = pos.shape[0]
    half = tok // 2
    width = rows.shape[3]
    slots = n * room
    feats = q_out.shape[1]
    groups = feats // 128
    block = 256

    greet(
        [{"dp": here.mixed(k)} for k in range(1, n)] + [here.across("t"), here.across("y")]
    )
    orders = gather_orders(count)
    for c in range(3):
        lows[0][:, c * feats : (c + 1) * feats] = attn_in[:, c, :].astype(bf16)
    lows[1][...] = attn_out[...].astype(bf16)
    for c in range(2):
        lows[2 + c][...] = ffn_in[:, c, :].astype(bf16)
    lows[4][...] = ffn_out[...].astype(bf16)
    jobs, lags = [], []
    for number, (which, kind, start, size, lag) in enumerate(pieces):
        jobs.append(
            Gather(
                here, lows[which], fulls[which][0], fulls[which][1], orders[kind],
                pl.ds(start, size), wsend.at[number], wrecv.at[number], wlocal.at[number],
            )
        )
        lags.append(lag)
    first = Runner(jobs[:1], lags[:1])
    runner = Runner(jobs[1:], lags[1:], stride)
    first.advance()
    runner.advance()
    low_table[...] = table[...].astype(bf16)
    row_count = table.shape[0]
    out_copies, y_copies = [], []

    def pass_on(k):
        copy = remote(
            rows.at[here.m, k], rows.at[here.m, k], ysem.at[0, k], ysem.at[1, k], here.across("y")
        )
        copy.start()
        y_copies.append(copy)

    for k in list(range(n - 1, 0, -1)) + [0]:
        column = jnp.transpose(heard[0, k])[:room, 0:1]
        hot = (lax.broadcasted_iota(jnp.int32, (room, row_count), 1) == column).astype(f32)
        found = mdot(hot.astype(bf16), low_table[...]).astype(bf16)
        if k == 0:
            rows[here.m, 0] = found
            pass_on(0)
        else:
            served[k] = found
            copy = remote(
                served.at[k], rows.at[here.m, k], rsem.at[0, k], rsem.at[1, k],
                {"dp": here.mixed(k)},
            )
            copy.start()
            out_copies.append(copy)
            if k % 2:
                runner.advance()
        if k == n // 2:
            first.advance()
    first.advance()
    for k in range(n - 1, 0, -1):
        out_copies[n - 1 - k].wait_recv()
        pass_on(k)
        if k % 3 == 1:
            runner.advance()
    first.drain()
    for copy in out_copies:
        copy.wait_send()
    for copy in y_copies:
        copy.wait()

    w_qkv = fulls[0][0]
    for i in range(tok // block):
        at = slice(i * block, (i + 1) * block)
        hot = (lax.broadcasted_iota(jnp.int32, (block, slots), 1) == pos[at, :]).astype(f32)
        hot = hot.astype(bf16)
        emb = jnp.concatenate([mdot(hot, rows[h].reshape(slots, width)) for h in range(2)], 1)
        hat, _scale = norm_parts(emb)
        stream = hat * norm_rows[0:1, :] + norm_rows[1:2, :]
        low = stream.astype(bf16)
        input_out[at, :] = low
        if (i + 1) * block <= half:
            emb_out[at, :] = emb.astype(bf16)
            zero_out[at, :] = stream
        cos, sin = cosine[at, :], sine[at, :]
        proj = mdot(low, w_qkv[...].reshape(2 * width, 3 * feats))
        for c in range(3):
            for g in range(groups):
                cols = slice(g * 128, (g + 1) * 128)
                part = proj[:, c * feats + g * 128 : c * feats + (g + 1) * 128]
                if c < 2:
                    part = part * cos + turned(part) * sin
                part = part.astype(bf16)
                if c == 0:
                    q_out[at, cols] = part * bf16(HDIM**-0.5)
                elif c == 1:
                    k_out[at, cols] = part
                else:
                    v_out[at, cols] = part
        if i % every == every - 1:
            runner.advance()

    lane = lax.broadcasted_iota(jnp.int32, (1, 128), 1)
    att_copies = []
    for g in range(groups):
        cols = slice(g * 128, (g + 1) * 128)
        vt[...] = jnp.transpose(v_out[:, cols].astype(f32)).astype(bf16)
        keys = [jnp.where((lane // HDIM) == h, k_out[:, cols], bf16(0)) for h in range(2)]
        for i in list(range(tok // block // 2, tok // block)) + list(range(tok // block // 2)):
            at = slice(i * block, (i + 1) * block)
            query = q_out[at, cols]
            same = seg_col[...] == seg_row[:, at]
            outs = []
            for h in range(2):
                scores = jnp.where(same, tdot(keys[h], query), neg_large)
                peak = jnp.max(scores, 0, keepdims=True)
                soft = jnp.exp(scores - peak)
                total = jnp.sum(soft, 0, keepdims=True)
                lse_out[2 * g + h, :, at] = peak + jnp.log(total)
                soft = (soft * (1.0 / total)).astype(bf16)
                outs.append(mdot(vt[h * HDIM : (h + 1) * HDIM, :], soft))
            found = jnp.transpose(jnp.concatenate(outs, 0)).astype(bf16)
            if i * block < half:
                att_own[at, cols] = found
            else:
                att_far[slice(i * block - half, (i + 1) * block - half), cols] = found
                if (i + 1) * block == tok:
                    copy = remote(
                        att_far.at[:, cols], att_other.at[:, cols], asem.at[0, g], asem.at[1, g],
                        here.across("y"),
                    )
                    copy.start()
                    att_copies.append(copy)
            if i % every == every - 1:
                runner.advance()
    runner.drain()
    for copy in att_copies:
        copy.wait()


def forward_pass(table, heard, pos, norm_rows, cosine, sine, seg_row, seg_col, raw, kinds, pieces,
                 stride=3, every=1):
    n_dp = heard.shape[1]
    attn_in, attn_out, ffn_in, ffn_out = raw
    rows = attn_in.shape[0]
    shards = (
        sds((rows, 3 * attn_in.shape[2]), f32), sds(attn_out.shape, f32),
        sds(ffn_out.shape, f32), sds(ffn_out.shape, f32), sds(ffn_out.shape, f32),
    )
    room = heard_room(pos.shape[0], n_dp)
    count = n_dp.bit_length() - 1
    halves = (2,) * (count + 1)
    tok = pos.shape[0]
    half = tok // 2
    width = table.shape[1]
    feats = shards[0].shape[1] // 3
    outs = [
        sds((half, 2 * width), bf16),
        sds((half, 2 * width), f32),
        sds((tok, 2 * width), bf16),
        sds((tok, feats), bf16),
        sds((tok, feats), bf16),
        sds((tok, feats), bf16),
        sds((feats // HDIM, 1, tok), f32),
        sds((half, feats), bf16),
        sds((half, feats), bf16),
    ]
    specs = [VM] * len(outs)
    for shard, kind in zip(shards, kinds):
        full = sds(halves + shard.shape, bf16)
        outs += [full] if kind == "plain" else [full, full]
        specs += [VM] if kind == "plain" else [ANY, ANY]
    dma = pltpu.SemaphoreType.DMA
    steps = count + 6
    scratch = (
        [
            pltpu.VMEM(table.shape, bf16),
            pltpu.VMEM((n_dp, room, width), bf16),
            pltpu.VMEM((2, n_dp, room, width), bf16),
            pltpu.VMEM((128, tok), bf16),
            pltpu.VMEM((half, feats), bf16),
        ]
        + [pltpu.VMEM(shard.shape, bf16) for shard in shards]
        + [dma((2, n_dp)), dma((2, n_dp)), dma((2, feats // 128))]
        + [dma((len(pieces), steps)), dma((len(pieces), steps)), dma((len(pieces),))]
    )
    out = pl.pallas_call(
        lambda *refs: forward_body(room, kinds, pieces, stride, every, *refs),
        out_shape=outs,
        in_specs=[VM] * 12,
        out_specs=specs,
        scratch_shapes=scratch,
        compiler_params=params(2),
        name="forward",
    )(table, heard, pos, norm_rows, cosine, sine, seg_row, seg_col, *raw)
    weights, at = [], 9
    for shard, kind in zip(shards, kinds):
        whole = (2 * n_dp * shard.shape[0], shard.shape[1])
        if kind == "plain":
            weights.append(out[at].reshape(whole))
            at += 1
        else:
            weights.append((out[at].reshape(whole), out[at + 1].reshape(whole)))
            at += 2
    return out[:9], weights


def writer(ref, kind=None):
    def store(cols, values):
        if kind is None:
            ref[:, cols] = values
        else:
            ref[:, kind, cols] = values

    return store


def make_scatters(
    here, grads, kinds, pieces, outs, held, landed, send, recv, loads, stride=1
):
    orders = scatter_orders(here.count)
    jobs, lags = [], []
    held, landed = list(held), list(landed)
    for number, (which, kind, start, size, lag) in enumerate(pieces):
        own, other = grads[which]
        pair = other is not None
        mine = [held.pop(0) for _ in range(2 if pair else 1)]
        amount = len(scatter_lands(orders[kind], here.count, pair, 1, 1))
        lands = [landed.pop(0) for _ in range(amount)]
        jobs.append(
            Scatter(
                here, own, other, orders[kind], pl.ds(start, size), mine, lands, outs[which],
                send.at[number], recv.at[number], loads.at[number],
            )
        )
        lags.append(lag)
    return Runner(jobs, lags, stride)


def scatter_scratch(count, rows, pairs, pieces):
    orders = scatter_orders(count)
    held, landed = [], []
    for which, kind, _start, size, _lag in pieces:
        pair = pairs[which]
        held += [pltpu.VMEM((2,) * count + (rows, size), bf16)] * (2 if pair else 1)
        landed += [
            pltpu.VMEM(shape, bf16)
            for shape in scatter_lands(orders[kind], count, pair, rows, size)
        ]
    dma = pltpu.SemaphoreType.DMA
    steps = 2 * count + 6
    sems = [dma((len(pieces), steps)), dma((len(pieces), steps)), dma((len(pieces), 2))]
    return held, landed, sems


def square_sum(values):
    return jnp.sum(jnp.sum(values * values, 0, keepdims=True), 1, keepdims=True)


def store_blocks(ref, values, count, start):
    rows, cols = ref.shape[-2], values.shape[1]
    for number in range(2 ** (count + 1)):
        at = tuple((number >> (count - j)) & 1 for j in range(count + 1))
        ref[at + (slice(None), slice(start, start + cols))] = values[
            number * rows : (number + 1) * rows, :
        ].astype(bf16)


def hidden_body(pieces, sizes, stride, *refs):
    here = Place()
    count = here.count
    (grad_pool, seg, sum_two, norm_rows, low_one, sum_one,
     att_own, att_other, hidden_own, hidden_other) = refs[:10]
    weights = refs[10:16]
    residual, low_out, norms_out, wout_own, wout_other = refs[16:21]
    later = refs[21:25]
    out_down, squares = refs[25:27]
    loaded, down, low_two, turned_one, turned_two, total = refs[27:33]
    held = refs[33 : 33 + sizes[0]]
    landed = refs[33 + sizes[0] : 33 + sizes[0] + sizes[1]]
    wsem, send, recv, loads = refs[33 + sizes[0] + sizes[1] :]
    half, width = low_one.shape
    part = weights[0].shape[1] // 2
    copies = {}

    def load(c, j):
        for w in range(3):
            copies[c, j, w] = pltpu.make_async_copy(
                weights[2 * w + j].at[:, pl.ds(c * part, part)], loaded.at[j * 3 + w],
                wsem.at[(c * 2 + j) * 3 + w],
            )
            copies[c, j, w].start()

    load(0, 0)
    load(0, 1)
    greet([here.across("t"), here.across("y")] + [here.across(j) for j in range(count)])
    grads = [(down.at[0], down.at[1])]
    runner = make_scatters(
        here, grads, None, pieces, (writer(out_down),), held, landed, send, recv, loads, stride
    )
    slots = grad_pool.shape[0]
    hot = (lax.broadcasted_iota(jnp.int32, (half, slots), 1) == seg[0:half, :]).astype(f32)
    grad_two = jnp.dot(hot, grad_pool[...], precision=highest, preferred_element_type=f32)
    hat, scale = norm_parts(sum_two[...])
    grad_hat = grad_two * norm_rows[4:5, :]
    first = jnp.mean(grad_hat, -1, keepdims=True)
    second = jnp.mean(grad_hat * hat, -1, keepdims=True)
    grad_sum = scale * (grad_hat - first - hat * second)
    low_two[...] = grad_sum.astype(bf16)
    turned_two[...] = jnp.transpose(grad_sum).astype(bf16)
    for c in range(2):
        for j, hidden in enumerate((hidden_own, hidden_other)):
            cols = slice(c * part, (c + 1) * part)
            store_blocks(down.at[j], mdot(turned_two[...], hidden[:, cols]), count, c * part)
        runner.advance()
    norms_out[...] = jnp.zeros_like(norms_out)
    norms_out[4:5, :] = jnp.sum(grad_two * hat, 0, keepdims=True)
    norms_out[5:6, :] = jnp.sum(grad_two, 0, keepdims=True)
    turned_one[...] = jnp.transpose(low_one[...].astype(f32)).astype(bf16)
    total[...] = grad_sum
    runner.advance()
    for c in range(2):
        for j in range(2):
            number = j * 3
            for w in range(3):
                copies[c, j, w].wait()
            gate = mdot(low_one[...], loaded[number])
            up = mdot(low_one[...], loaded[number + 1])
            share = 1.0 / (1.0 + jnp.exp(-gate))
            grad_hidden = mdot(low_two[...], loaded[number + 2])
            grad_up = (grad_hidden * (gate * share)).astype(bf16)
            grad_gate = (
                grad_hidden * up * (share * (1.0 + gate * (1.0 - share)))
            ).astype(bf16)
            runner.advance()
            store_blocks(later[j], mdot(turned_one[...], grad_gate), count, c * part)
            store_blocks(later[2 + j], mdot(turned_one[...], grad_up), count, c * part)
            total[...] += tdot(grad_gate, loaded[number]) + tdot(grad_up, loaded[number + 1])
            if c == 0:
                load(1, j)
            runner.advance()
    hat, scale = norm_parts(sum_one[...])
    grad_one = total[...]
    grad_hat = grad_one * norm_rows[2:3, :]
    first = jnp.mean(grad_hat, -1, keepdims=True)
    second = jnp.mean(grad_hat * hat, -1, keepdims=True)
    grad_sum = scale * (grad_hat - first - hat * second)
    norms_out[2:3, :] = jnp.sum(grad_one * hat, 0, keepdims=True)
    norms_out[3:4, :] = jnp.sum(grad_one, 0, keepdims=True)
    residual[...] = grad_sum
    low_out[...] = grad_sum.astype(bf16)
    runner.advance()
    turned_two[...] = jnp.transpose(grad_sum).astype(bf16)
    wout_own[...] = mdot(turned_two[...], att_own[...]).astype(bf16)
    runner.advance()
    wout_other[...] = mdot(turned_two[...], att_other[...]).astype(bf16)
    runner.drain()
    squares[...] = jnp.broadcast_to(square_sum(out_down[...]), squares.shape)


def hidden_back(grad_pool, seg, sum_two, norm_rows, low_one, sum_one, att, hidden, w_gate, w_up,
                w_down, pieces, stride=1):
    n_dp = lax.axis_size("dp")
    count = n_dp.bit_length() - 1
    half, width = low_one.shape
    feats = att[0].shape[1]
    cols = w_gate[0].shape[1]
    rows = width // (2 * n_dp)
    blocks = (2,) * (count + 1) + (rows, cols)
    held, landed, sems = scatter_scratch(count, rows, [True], pieces)
    vmem = pltpu.VMEM
    return pl.pallas_call(
        lambda *refs: hidden_body(pieces, (len(held), len(landed)), stride, *refs),
        out_shape=[
            sds((half, width), f32), sds((half, width), bf16), sds((8, width), f32),
            sds((width, feats), bf16), sds((width, feats), bf16),
        ] + [sds(blocks, bf16)] * 4 + [sds((rows, cols), f32), sds((8, 128), f32)],
        in_specs=[VM] * 10 + [ANY] * 6,
        out_specs=[VM] * 11,
        scratch_shapes=[
            vmem((6, width, cols // 2), bf16), vmem((2,) + blocks, bf16), vmem((half, width), bf16),
            vmem((width, half), bf16), vmem((width, half), bf16), vmem((half, width), f32),
        ] + held + landed + [pltpu.SemaphoreType.DMA((12,))] + sems,
        compiler_params=params(6),
        name="hidden",
    )(grad_pool, seg, sum_two, norm_rows, low_one, sum_one, *att, *hidden,
      *w_gate, *w_up, *w_down)


def backward_body(room, pieces, late_pieces, sizes, stride, every, *refs):
    here = Place()
    n, count = here.n_dp, here.count
    (low, out_own, out_other, query, key, value, lse, cosine, sine, seg_row, seg_col, residual,
     emb, norm_rows, w_qkv, norms_in, before, inputs, pos, heard) = refs[:20]
    grads = [(refs[20 + 2 * j], refs[21 + 2 * j]) for j in range(3)]
    (table_out, norms_out, out_ffn, out_proj, out_qkv, total_out) = refs[26:32]
    refs = refs[:26] + (None,) + refs[26:]
    (kt, dq, dk, dv, grad_att, far_att, far_send, far_recv, grad_proj, turned_in, grad_qkv,
     low_out, norm_part, other, packed, mine, theirs, norms, parts, own_part) = refs[33:53]
    at = 53
    cuts = []
    for size in sizes:
        cuts.append(refs[at : at + size])
        at += size
    held, landed, late_held, late_landed = cuts
    (asem, bsem, ysem, rsem, csem, nsem, tsem, send, recv, loads, late_send, late_recv,
     late_loads) = refs[at:]
    tok, feats = query.shape
    half, width = tok // 2, table_out.shape[1]
    groups = feats // 128
    block = 256
    peers = []
    for rt in range(2):
        for rd in range(n):
            for rm in range(2):
                if rt or rd or rm:
                    where = {
                        "tower": here.t + rt * (1 - 2 * here.t),
                        "dp": here.mixed(rd),
                        "mp": here.m + rm * (1 - 2 * here.m),
                    }
                    peers.append(((rt * n + rd) * 2 + rm, where))
    me = (here.t * n + here.d) * 2 + here.m
    greet([where for _, where in peers])
    runner = make_scatters(
        here, grads, None, pieces, (writer(out_ffn, 0), writer(out_ffn, 1), writer(out_proj)), held,
        landed, send, recv, loads, stride,
    )
    runner.advance()
    att_copies = []
    far_att[...] = mdot(low[...], out_other[...]).astype(bf16)
    for g in range(groups):
        cols = slice(g * 128, (g + 1) * 128)
        copy = remote(
            far_att.at[:, cols], grad_att.at[half:, cols], asem.at[0, g], asem.at[1, g],
            here.across("y"),
        )
        copy.start()
        att_copies.append(copy)
    grad_att[:half, :] = mdot(low[...], out_own[...]).astype(bf16)
    for i in range(tok // block):
        rows = slice(i * block, (i + 1) * block)
        turned_in[:, rows] = jnp.transpose(inputs[rows, :].astype(f32)).astype(bf16)
    runner.advance()
    lane = lax.broadcasted_iota(jnp.int32, (1, 128), 1)
    for g in range(groups):
        cols = slice(g * 128, (g + 1) * 128)
        kt[...] = jnp.transpose(key[:, cols].astype(f32)).astype(bf16)
        keys = [jnp.where((lane // HDIM) == h, key[:, cols], bf16(0)) for h in range(2)]
        values = [jnp.where((lane // HDIM) == h, value[:, cols], bf16(0)) for h in range(2)]
        for i in range(tok // block):
            if i * block == half:
                att_copies[g].wait_recv()
            rows = slice(i * block, (i + 1) * block)
            q_part = query[rows, cols]
            g_part = grad_att[rows, cols]
            same = seg_col[...] == seg_row[:, rows]
            turns = []
            add_k, add_v = None, None
            for h in range(2):
                inside = (lane // HDIM) == h
                scores = jnp.where(same, tdot(keys[h], q_part), neg_large)
                soft = jnp.exp(scores - lse[2 * g + h, :, rows])
                grad_soft = tdot(values[h], g_part)
                inner = jnp.sum(soft * grad_soft, 0, keepdims=True)
                grad_scores = (soft * (grad_soft - inner)).astype(bf16)
                part_v = mdot(soft.astype(bf16), jnp.where(inside, g_part, bf16(0)))
                part_k = mdot(grad_scores, jnp.where(inside, q_part, bf16(0)))
                add_v = part_v if h == 0 else add_v + part_v
                add_k = part_k if h == 0 else add_k + part_k
                turns.append(mdot(kt[h * HDIM : (h + 1) * HDIM, :], grad_scores))
            dq[rows, :] = jnp.transpose(jnp.concatenate(turns, 0)) * (HDIM**-0.5)
            if i == 0:
                dv[...] = add_v
                dk[...] = add_k
            else:
                dv[...] += add_v
                dk[...] += add_k
            if i % every == every - 1:
                runner.advance()
        cos, sin = cosine[...], sine[...]
        for c, grad in ((0, dq), (1, dk)):
            whole = grad[...]
            back = whole * cos - turned(whole) * sin
            grad_proj[:, c * feats + g * 128 : c * feats + (g + 1) * 128] = back.astype(bf16)
        grad_proj[:, 2 * feats + g * 128 : 2 * feats + (g + 1) * 128] = dv[...].astype(bf16)
    for copy in att_copies:
        copy.wait_send()
    far_copies = []
    for i in range(half // block):
        rows = slice(i * block, (i + 1) * block)
        far = grad_proj[half + i * block : half + (i + 1) * block, :]
        far_send[rows, :] = tdot(far, w_qkv[...]).astype(bf16)
        copy = remote(
            far_send.at[rows, :], far_recv.at[rows, :], bsem.at[0, i], bsem.at[1, i],
            here.across("y"),
        )
        copy.start()
        far_copies.append(copy)
    grad_parts = [grad_qkv.at[c] for c in range(3)]
    late = make_scatters(
        here, [(part, None) for part in grad_parts], None, late_pieces,
        [writer(out_qkv, c) for c in range(3)], late_held, late_landed, late_send, late_recv,
        late_loads, 1,
    )
    jobs = late.jobs
    step = feats if grad_qkv.shape[-2] % 16 == 0 else 128
    for start in range(0, 3 * feats, step):
        cols = slice(start, start + step)
        store_blocks(
            grad_parts[start // feats], mdot(turned_in[...], grad_proj[:, cols]), count,
            start % feats,
        )
    late.advance()
    runner.advance()
    theirs_at = pl.ds(pl.multiple_of((1 - here.m) * width, 128), width)
    mine_at = pl.ds(pl.multiple_of(here.m * width, 128), width)
    norm_part[...] = norms_in[...]
    swaps = []
    for i in range(half // block):
        rows = slice(i * block, (i + 1) * block)
        near = residual[rows, :] + tdot(grad_proj[rows, :], w_qkv[...])
        if i == 0:
            runner.advance()
        far_copies[i].wait()
        near = near + far_recv[rows, :].astype(f32)
        hat, scale = norm_parts(emb[rows, :].astype(f32))
        grad_hat = near * norm_rows[0:1, :]
        first = jnp.mean(grad_hat, -1, keepdims=True)
        second = jnp.mean(grad_hat * hat, -1, keepdims=True)
        low_out[rows, :] = (scale * (grad_hat - first - hat * second)).astype(bf16)
        copy = remote(
            low_out.at[rows, theirs_at], other.at[rows, :], ysem.at[0, i], ysem.at[1, i],
            here.across("y"),
        )
        copy.start()
        swaps.append(copy)
        norm_part[0:1, :] += jnp.sum(near * hat, 0, keepdims=True)
        norm_part[1:2, :] += jnp.sum(near, 0, keepdims=True)
    jobs.append(Total(here, norm_part, norms, nsem.at[0], nsem.at[1]))
    late.lags.append(late.tick)
    late.length = max(late.length, late.tick + jobs[-1].last + 1)
    late.advance()
    runner.advance()
    for copy in swaps:
        copy.wait()
    both = jnp.concatenate([low_out[:, mine_at], other[...]], 0)
    copies = []
    for k in list(range(n - 1, 0, -1)) + [0]:
        hot = (
            lax.broadcasted_iota(jnp.int32, (room, pos.shape[1]), 0) + k * room == pos[...]
        ).astype(f32)
        packed[k] = mdot(hot.astype(bf16), both).astype(bf16)
        if k:
            copy = remote(
                packed.at[k], mine.at[k], rsem.at[0, k], rsem.at[1, k], {"dp": here.mixed(k)}
            )
        else:
            mine[0] = packed[0]
            copy = remote(mine.at[0], theirs.at[0], csem.at[0, 0], csem.at[1, 0], here.across("t"))
        copy.start()
        copies.append(copy)
    passed = [copies.pop()]
    late.advance()
    runner.advance()
    for k in range(n - 1, 0, -1):
        copies[n - 1 - k].wait_recv()
        copy = remote(mine.at[k], theirs.at[k], csem.at[0, k], csem.at[1, k], here.across("t"))
        copy.start()
        passed.append(copy)
        if k == n // 2:
            late.advance()
            runner.advance()
    late.advance()
    runner.advance()
    for copy in copies:
        copy.wait_send()
    for copy in passed:
        copy.wait()
    slots = n * room
    row_count = table_out.shape[0]
    size = 424 * 1024 // max(slots, 1024) // 8 * 8
    own_part[...] = jnp.zeros_like(own_part)
    for part in range(-(-row_count // size)):
        rows = slice(part * size, min((part + 1) * size, row_count))
        block_rows = rows.stop - rows.start
        base = lax.broadcasted_iota(jnp.int32, (block_rows, slots), 0) + part * size
        found = 0.0
        for source, sums in ((0, mine), (1, theirs)):
            hot = (base == heard[source]).astype(f32).astype(bf16)
            found = found + mdot(hot, sums[...].reshape(slots, width))
        table_out[rows, :] = found
        own_part[0:1, :] += jnp.sum(found * found, 0, keepdims=True)
        if part % 2:
            late.advance()
            runner.advance()
    late.drain()
    runner.drain()
    norms_out[...] = norm_part[...]
    local_sq = (
        before[0:1, 0:1]
        + 0.5 * jnp.sum(own_part[...], 1, keepdims=True)[0:1]
        + square_sum(out_proj[...])
        + sum(square_sum(out_qkv[:, c, :]) for c in range(3))
        + sum(square_sum(out_ffn[:, c, :]) for c in range(2))
    )
    parts[me] = jnp.broadcast_to(local_sq, parts.shape[1:])
    copies = []
    for rel, where in peers:
        copy = remote(parts.at[me], parts.at[me], tsem.at[0, rel], tsem.at[1, rel], where)
        copy.start()
        copies.append(copy)
    for copy in copies:
        copy.wait()
    total_out[...] = jnp.sum(parts[...], 0) + square_sum(norms_out[...])


def blocks_of(grad, n_dp):
    count = n_dp.bit_length() - 1
    rows = grad.shape[0] // (2 * n_dp)
    return grad.reshape((2,) * (count + 1) + (rows, grad.shape[1]))


def backward_pass(low, w_out, query, key, value, lse, cosine, sine, seg_row, seg_col, residual,
                  emb, norm_rows, w_qkv, norms, before, inputs, pos_row, heard, grads, grad_out,
                  row_count, pieces, late_pieces, stride=3, every=1):
    n_dp = lax.axis_size("dp")
    count = n_dp.bit_length() - 1
    tok, feats = query.shape
    half, width = low.shape
    rows, cols = grads[0].shape[-2:]
    room = heard_room(tok, n_dp)
    held, landed, sems = scatter_scratch(count, rows, [True] * 3, pieces)
    late_held, late_landed, late_sems = scatter_scratch(count, rows, [False] * 3, late_pieces)
    flat = list(grads) + [blocks_of(g, n_dp) for g in grad_out]
    dma = pltpu.SemaphoreType.DMA
    vmem = pltpu.VMEM
    sizes = (len(held), len(landed), len(late_held), len(late_landed))
    steps = max(1, half // 256)
    part = width // 2
    return pl.pallas_call(
        lambda *refs: backward_body(room, pieces, late_pieces, sizes, stride, every, *refs),
        out_shape=[
            sds((row_count, part), f32), sds((8, width), f32),
            sds((rows, 2, cols), f32), sds((rows, feats), f32), sds((rows, 3, feats), f32),
            sds((8, 128), f32),
        ],
        in_specs=[VM] * 20 + [ANY] * 6,
        out_specs=[VM] * 6,
        scratch_shapes=[
            vmem((128, tok), bf16), vmem((tok, 128), f32), vmem((tok, 128), f32),
            vmem((tok, 128), f32), vmem((tok, feats), bf16), vmem((half, feats), bf16),
            vmem((half, width), bf16), vmem((half, width), bf16),
            vmem((tok, 3 * feats), bf16), vmem((width, tok), bf16),
            vmem((3,) + (2,) * (count + 1) + (rows, feats), bf16),
            vmem((half, width), bf16), vmem((8, width), f32), vmem((half, part), bf16),
            vmem((n_dp, room, part), bf16), vmem((n_dp, room, part), bf16),
            vmem((n_dp, room, part), bf16), vmem((count + 2, 8, width), f32),
            vmem((4 * n_dp, 8, 128), f32), vmem((8, part), f32),
        ] + held + landed + late_held + late_landed
        + [dma((2, feats // 128)), dma((2, steps)), dma((2, steps)), dma((2, n_dp)),
           dma((2, n_dp)), dma((2, count + 2)), dma((2, 4 * n_dp))] + sems + late_sems,
        compiler_params=params(4, 60),
        name="backward",
    )(low, w_out[0], w_out[1], query, key, value, lse, cosine, sine, seg_row, seg_col, residual,
      emb, norm_rows, w_qkv, norms, before, inputs, pos_row, heard, *flat)


def loss_body(part, counts, doc_ok, query_ok, target, scale, grad_out, stats, other, low_all, turn,
              psend, precv, esend, erecv):
    here = Place()
    n = here.n_dp
    slots, width = part.shape
    peers = []
    for rt in range(2):
        for rd in range(n):
            if rt or rd:
                peers.append(
                    (rt * n + rd, {"tower": here.t + rt * (1 - 2 * here.t), "dp": here.mixed(rd)})
                )
    greet([where for _, where in peers] + [here.across("y")])
    copy = remote(part, other, psend, precv, here.across("y"))
    copy.start()
    copy.wait()
    pooled = (part[...] + other[...]) / counts[...]
    scale_row = lax.rsqrt(jnp.sum(pooled * pooled, 1, keepdims=True) + 1e-06)
    unit = pooled * scale_row
    low_all[here.t, here.d] = unit.astype(bf16)
    copies = []
    for rel, where in peers:
        copy = remote(
            low_all.at[here.t, here.d], low_all.at[here.t, here.d], esend.at[rel], erecv.at[rel], where
        )
        copy.start()
        copies.append(copy)
    for copy in copies:
        copy.wait()
    total = n * slots
    queries = low_all[0].reshape(total, width)
    documents = low_all[1].reshape(total, width)
    cosines = tdot(queries, documents)
    factor = jnp.exp(jnp.minimum(scale[...], cap_value))
    logits = jnp.where(doc_ok[...] > 0, factor * cosines, neg_large)
    peak = jnp.max(logits, 1, keepdims=True)
    log_total = peak + jnp.log(jnp.sum(jnp.exp(logits - peak), 1, keepdims=True))
    soft = jnp.exp(logits - log_total)
    mask = lax.broadcasted_iota(jnp.int32, (total, total), 1) == target[...]
    picked = jnp.sum(jnp.where(mask, logits, 0.0), 1, keepdims=True)
    valid = query_ok[...] > 0
    query_count = jnp.sum(valid.astype(f32), axis=0, keepdims=True)
    loss_sum = jnp.sum(jnp.where(valid, log_total - picked, 0.0), axis=0, keepdims=True)
    grad_logits = jnp.where(valid, soft - mask.astype(f32), 0.0) / query_count
    by_row = jnp.sum(grad_logits * cosines, 1, keepdims=True)
    grad_scale = (
        jnp.sum(by_row, 0, keepdims=True) * factor * (scale[...] < cap_value).astype(f32)
    )
    grad_cos = factor * grad_logits
    at = pl.ds(pl.multiple_of(here.d * slots, slots), slots)
    turn[0] = grad_cos
    turn[1] = jnp.transpose(grad_cos)
    left = turn[here.t, at, :].astype(bf16)
    right = low_all[1 - here.t].reshape(total, width)
    grad_unit = mdot(left, right)
    grad_pooled = scale_row * (
        grad_unit - unit * jnp.sum(unit * grad_unit, 1, keepdims=True)
    )
    grad_out[...] = grad_pooled / counts[...]
    row = lax.broadcasted_iota(jnp.int32, stats.shape, 0)
    stats[...] = jnp.where(row == 0, loss_sum, jnp.where(row == 1, query_count, grad_scale))


def loss_step(part, counts, doc_ok, query_ok, target, scale):
    n_dp = lax.axis_size("dp")
    slots, width = part.shape
    total = n_dp * slots
    dma = pltpu.SemaphoreType.DMA
    return pl.pallas_call(
        loss_body,
        out_shape=[sds(part.shape, f32), sds((8, 128), f32)],
        in_specs=[VM] * 6,
        out_specs=[VM] * 2,
        scratch_shapes=[
            pltpu.VMEM(part.shape, f32),
            pltpu.VMEM((2, n_dp, slots, width), bf16),
            pltpu.VMEM((2, total, total), f32),
            dma, dma, dma((2 * n_dp,)), dma((2 * n_dp,)),
        ],
        compiler_params=params(3),
        name="loss",
    )(part, counts, doc_ok, query_ok, target, scale)


def rotary_tables(positions):
    half_dim = HDIM // 2
    inverse = 1000.0 ** (-2.0 * jnp.arange(half_dim, dtype=f32) / HDIM)
    angles = positions.astype(f32)[:, None] * inverse[None, :]
    angles = jnp.concatenate([angles] * 4, 1)
    return jnp.cos(angles), jnp.sin(angles)


def layout(lengths, places, slot_count):
    end_points = jnp.cumsum(lengths)
    segment = jnp.sum((places[:, None] >= end_points[None, :]).astype(jnp.int32), 1)
    starts = jnp.concatenate([jnp.zeros((1,), jnp.int32), end_points])
    slot_ids = jnp.arange(slot_count + 1, dtype=jnp.int32)
    segment_start = jnp.sum(jnp.where(segment[:, None] == slot_ids[None, :], starts[None, :], 0), 1)
    return segment, places - segment_start


def norm_back(grad, hat, scale, gain):
    grad_hat = grad * gain
    first = jnp.mean(grad_hat, -1, keepdims=True)
    second = jnp.mean(grad_hat * hat, -1, keepdims=True)
    return (
        scale * (grad_hat - first - hat * second),
        jnp.sum(grad * hat, 0),
        jnp.sum(grad, 0),
    )


def glu(gate_vals, up_vals):
    return jax.nn.silu(gate_vals) * up_vals


def adamw(weight_in, gradient, first_mom, second, factor, step_num, rate):
    gradient = gradient * factor
    first_new = beta_one * first_mom + (1.0 - beta_one) * gradient
    second_new = beta_two * second + (1.0 - beta_two) * gradient * gradient
    first_hat = first_new / (1.0 - beta_one**step_num)
    second_hat = second_new / (1.0 - beta_two**step_num)
    weight_new = weight_in - rate * (
        first_hat / (jnp.sqrt(second_hat) + adam_eps) + decay_rate * weight_in
    )
    return (weight_new, first_new, second_new)


def name_rows(ids, d, n_dp, row_count, room):
    tok = ids.shape[0]
    owner = ids // row_count
    local = ids - owner * row_count
    order = jnp.bitwise_xor(owner, d)
    places = jnp.arange(tok, dtype=jnp.int32)
    first_at = jnp.min(
        jnp.where(ids[:, None] == ids[None, :], places[None, :], tok), 1
    )
    is_first = first_at == places
    slot = jnp.sum(
        (
            (places[None, :] < first_at[:, None])
            & is_first[None, :]
            & (owner[None, :] == owner[:, None])
        ).astype(jnp.int32),
        1,
    )
    over = jnp.max(slot) >= room
    pos = order * room + slot
    wanted = jnp.arange(n_dp * room, dtype=jnp.int32)
    listed = jnp.max(
        jnp.where((pos[None, :] == wanted[:, None]) & is_first[None, :], local[None, :], -1), 1
    ).reshape(n_dp, 1, room)
    listed = jnp.pad(listed, ((0, 0), (0, 0), (0, 128 - room)), constant_values=-1)
    flag = jnp.broadcast_to(over.astype(jnp.int32), (n_dp, 7, 128))
    return pos, jnp.concatenate([listed, flag], 1)


def layer_norm(stream, gain_row, bias_row):
    average = jnp.mean(stream, -1, keepdims=True)
    centered = stream - average
    variance = jnp.mean(centered * centered, -1, keepdims=True)
    return centered * lax.rsqrt(variance + norm_eps) * gain_row + bias_row


def rotate(values, cosine, sine_table):
    half_dim = values.shape[-1] // 2
    turned = jnp.concatenate([-values[..., half_dim:], values[..., :half_dim]], -1)
    return values * cosine + turned * sine_table


def plain_rotary_tables(positions, head_dim):
    half_dim = head_dim // 2
    inverse = 1000.0 ** (-2.0 * jnp.arange(half_dim, dtype=jnp.float32) / head_dim)
    angles = positions.astype(jnp.float32)[:, None] * inverse[None, :]
    angles = jnp.concatenate([angles, angles], 1)[:, None, :]
    return (jnp.cos(angles), jnp.sin(angles))


def plain_layout(lengths, tok_count, slot_count):
    end_points = jnp.cumsum(lengths)
    places = jnp.arange(tok_count, dtype=jnp.int32)
    segment = jnp.sum((places[:, None] >= end_points[None, :]).astype(jnp.int32), 1)
    starts = jnp.concatenate([jnp.zeros((1,), jnp.int32), end_points])
    slot_ids = jnp.arange(slot_count + 1, dtype=jnp.int32)
    segment_start = jnp.sum(jnp.where(segment[:, None] == slot_ids[None, :], starts[None, :], 0), 1)
    return (segment, places - segment_start)


def plain_glu(gate_vals, up_vals):
    return jax.nn.silu(gate_vals) * up_vals


def pool_rows(stream_two, member, counts):
    pooled = jnp.dot(member, stream_two, precision=highest) / counts[:, None]
    return pooled * lax.rsqrt(jnp.sum(pooled * pooled, 1, keepdims=True) + 1e-06)


def model_total(values):
    return lax.psum(values.astype(jnp.bfloat16), "mp").astype(jnp.float32)


def block_scores(query_block, seg_block, key_low, segment, factor):
    scores = (
        jnp.einsum("thd,shd->hts", query_block, key_low, preferred_element_type=jnp.float32)
        * factor
    )
    return jnp.where((seg_block[:, None] == segment[None, :])[None], scores, neg_large)


def attention(query_low, key_low, value_low, segment):
    tok_count, heads_local, head_dim = query_low.shape
    block_rows = min(512, tok_count)
    block_count = tok_count // block_rows
    factor = head_dim ** (-0.5)
    query_blocks = query_low.reshape(block_count, block_rows, heads_local, head_dim)
    seg_blocks = segment.reshape(block_count, block_rows)

    def one_block(operands):
        scores = block_scores(operands[0], operands[1], key_low, segment, factor)
        row_peak = jnp.max(scores, 2, keepdims=True)
        row_total = jnp.sum(jnp.exp(scores - row_peak), 2, keepdims=True)
        log_total = row_peak + jnp.log(row_total)
        soft_rows = jnp.exp(scores - log_total)
        attended = jnp.einsum(
            "hts,shd->thd",
            soft_rows.astype(jnp.bfloat16),
            value_low,
            preferred_element_type=jnp.float32,
        )
        return (attended, log_total[..., 0])

    attended, log_total = lax.map(one_block, (query_blocks, seg_blocks))
    return (attended.reshape(tok_count, heads_local * head_dim), log_total)


def attention_back(query_low, key_low, value_low, grad_attended, log_total, segment):
    tok_count, heads_local, head_dim = query_low.shape
    block_rows = min(512, tok_count)
    block_count = tok_count // block_rows
    factor = head_dim ** (-0.5)
    query_blocks = query_low.reshape(block_count, block_rows, heads_local, head_dim)
    grad_blocks = grad_attended.reshape(block_count, block_rows, heads_local, head_dim)
    seg_blocks = segment.reshape(block_count, block_rows)

    def one_block(running, operands):
        query_block, grad_block, seg_block, lse_block = operands
        scores = block_scores(query_block, seg_block, key_low, segment, factor)
        soft_rows = jnp.exp(scores - lse_block[..., None])
        grad_soft = jnp.einsum(
            "thd,shd->hts", grad_block, value_low, preferred_element_type=jnp.float32
        )
        inner = jnp.sum(soft_rows * grad_soft, 2, keepdims=True)
        grad_scores = (soft_rows * (grad_soft - inner)).astype(jnp.bfloat16)
        grad_query = (
            jnp.einsum("hts,shd->thd", grad_scores, key_low, preferred_element_type=jnp.float32)
            * factor
        )
        grad_key = (
            running[0]
            + jnp.einsum(
                "hts,thd->shd", grad_scores, query_block, preferred_element_type=jnp.float32
            )
            * factor
        )
        grad_value = running[1] + jnp.einsum(
            "hts,thd->shd",
            soft_rows.astype(jnp.bfloat16),
            grad_block,
            preferred_element_type=jnp.float32,
        )
        return ((grad_key, grad_value), grad_query)

    zeros_kv = jnp.zeros(key_low.shape, jnp.float32)
    (grad_key, grad_value), grad_query = lax.scan(
        one_block, (zeros_kv, zeros_kv), (query_blocks, grad_blocks, seg_blocks, log_total)
    )
    return (grad_query.reshape(tok_count, heads_local, head_dim), grad_key, grad_value)


def layer_forward(embed_rows, segment, positions, weights, norm_rows):
    w_qkv, w_out, w_ffn, w_down = weights
    tok_count = embed_rows.shape[0]
    heads_local = w_qkv.shape[2] // HDIM
    stream_zero = layer_norm(embed_rows, norm_rows[0], norm_rows[1])
    input_zero = stream_zero.astype(jnp.bfloat16)
    projected = jnp.einsum("td,dcf->tcf", input_zero, w_qkv, preferred_element_type=jnp.float32)
    heads_view = projected.reshape(tok_count, 3, heads_local, HDIM)
    cosine, sine_table = plain_rotary_tables(positions, HDIM)
    query_low = rotate(heads_view[:, 0], cosine, sine_table).astype(jnp.bfloat16)
    key_low = rotate(heads_view[:, 1], cosine, sine_table).astype(jnp.bfloat16)
    value_low = heads_view[:, 2].astype(jnp.bfloat16)
    attended, log_total = attention(query_low, key_low, value_low, segment)
    attended_low = attended.astype(jnp.bfloat16)
    attn_branch = model_total(
        jnp.einsum("tf,df->td", attended_low, w_out, preferred_element_type=jnp.float32)
    )
    sum_one = stream_zero + attn_branch
    stream_one = layer_norm(sum_one, norm_rows[2], norm_rows[3])
    input_one = stream_one.astype(jnp.bfloat16)
    gate_up = jnp.einsum("td,dcf->tcf", input_one, w_ffn, preferred_element_type=jnp.float32)
    hidden_low = plain_glu(gate_up[:, 0], gate_up[:, 1]).astype(jnp.bfloat16)
    ffn_branch = model_total(
        jnp.einsum("tf,df->td", hidden_low, w_down, preferred_element_type=jnp.float32)
    )
    sum_two = stream_one + ffn_branch
    stream_two = layer_norm(sum_two, norm_rows[4], norm_rows[5])
    kept_vals = (
        embed_rows,
        sum_one,
        sum_two,
        input_zero,
        input_one,
        query_low,
        key_low,
        value_low,
        log_total,
        attended_low,
        gate_up,
        hidden_low,
    )
    return (stream_two, kept_vals)


def layer_backward(grad_two, kept_vals, weights, norm_rows, segment, positions):
    w_qkv, w_out, w_ffn, w_down = weights
    (
        embed_rows,
        sum_one,
        sum_two,
        input_zero,
        input_one,
        query_low,
        key_low,
        value_low,
        log_total,
        attended_low,
        gate_up,
        hidden_low,
    ) = kept_vals
    tok_count, heads_local, head_dim = query_low.shape
    grad_sum_two, gain_two, bias_two = jax.vjp(layer_norm, sum_two, norm_rows[4], norm_rows[5])[1](
        grad_two
    )
    ffn_low = grad_sum_two.astype(jnp.bfloat16)
    grad_down = jnp.einsum("td,tf->df", ffn_low, hidden_low, preferred_element_type=jnp.float32)
    grad_hidden = jnp.einsum("td,df->tf", ffn_low, w_down, preferred_element_type=jnp.float32)
    grad_gate, grad_up = jax.vjp(plain_glu, gate_up[:, 0], gate_up[:, 1])[1](grad_hidden)
    gate_grads = jnp.stack([grad_gate, grad_up], 1).astype(jnp.bfloat16)
    grad_ffn = jnp.einsum("td,tcf->dcf", input_one, gate_grads, preferred_element_type=jnp.float32)
    grad_stream_one = grad_sum_two + model_total(
        jnp.einsum("tcf,dcf->td", gate_grads, w_ffn, preferred_element_type=jnp.float32)
    )
    grad_sum_one, gain_one, bias_one = jax.vjp(layer_norm, sum_one, norm_rows[2], norm_rows[3])[1](
        grad_stream_one
    )
    attn_low = grad_sum_one.astype(jnp.bfloat16)
    grad_out = jnp.einsum("td,tf->df", attn_low, attended_low, preferred_element_type=jnp.float32)
    grad_attended = jnp.einsum(
        "td,df->tf", attn_low, w_out, preferred_element_type=jnp.float32
    ).astype(jnp.bfloat16)
    grad_query, grad_key, grad_value = attention_back(
        query_low,
        key_low,
        value_low,
        grad_attended.reshape(tok_count, heads_local, head_dim),
        log_total,
        segment,
    )
    cosine, sine_table = plain_rotary_tables(positions, head_dim)
    turn_back = jax.vjp(lambda values: rotate(values, cosine, sine_table), grad_query)[1]
    grad_projected = jnp.stack([turn_back(grad_query)[0], turn_back(grad_key)[0], grad_value], 1)
    grad_projected = grad_projected.reshape(tok_count, 3, heads_local * head_dim).astype(
        jnp.bfloat16
    )
    grad_qkv = jnp.einsum(
        "td,tcf->dcf", input_zero, grad_projected, preferred_element_type=jnp.float32
    )
    grad_stream_zero = grad_sum_one + model_total(
        jnp.einsum("tcf,dcf->td", grad_projected, w_qkv, preferred_element_type=jnp.float32)
    )
    grad_embed, gain_zero, bias_zero = jax.vjp(layer_norm, embed_rows, norm_rows[0], norm_rows[1])[
        1
    ](grad_stream_zero)
    norm_grads = jnp.stack([gain_zero, bias_zero, gain_one, bias_one, gain_two, bias_two])
    return (grad_embed, (grad_qkv, grad_out, grad_ffn, grad_down), norm_grads)


def plain_adamw(weight_in, gradient, first_mom, second, factor, step_num, rate):
    gradient = gradient * factor
    first_new = beta_one * first_mom + (1.0 - beta_one) * gradient
    second_new = beta_two * second + (1.0 - beta_two) * gradient * gradient
    first_hat = first_new / (1.0 - beta_one**step_num)
    second_hat = second_new / (1.0 - beta_two**step_num)
    weight_new = weight_in - rate * (
        first_hat / (jnp.sqrt(second_hat) + adam_eps) + decay_rate * weight_in
    )
    return (weight_new, first_new, second_new)


def plain_step(
    token_ids,
    seq_lengths,
    positives,
    embedding,
    attn_in,
    attn_out,
    ffn_in,
    ffn_out,
    norm_params,
    logit_scale,
    embed_m,
    embed_v,
    attn_in_m,
    attn_in_v,
    attn_out_m,
    attn_out_v,
    ffn_in_m,
    ffn_in_v,
    ffn_out_m,
    ffn_out_v,
    norm_m,
    norm_v,
    scale_m,
    scale_v,
):
    n_data = lax.axis_size("dp")
    tower_idx = lax.axis_index("tower")
    data_idx = lax.axis_index("dp")
    model_idx = lax.axis_index("mp")
    slot_count = seq_lengths.shape[2]
    token_list = token_ids[0]
    tok_count = token_list.shape[0]
    model_width = norm_params.shape[1]
    local_width = embedding.shape[1]
    row_count = embedding.shape[0]
    weights = (
        lax.all_gather(attn_in.astype(jnp.bfloat16), ("tower", "dp"), axis=0, tiled=True),
        lax.all_gather(attn_out.astype(jnp.bfloat16), ("tower", "dp"), axis=0, tiled=True),
        lax.all_gather(ffn_in.astype(jnp.bfloat16), ("tower", "dp"), axis=0, tiled=True),
        lax.all_gather(ffn_out.astype(jnp.bfloat16), ("tower", "dp"), axis=0, tiled=True),
    )
    shard_piece = lax.all_gather(embedding.astype(jnp.bfloat16), "dp", axis=0, tiled=True)
    inside = (token_list >= 0) & (token_list < shard_piece.shape[0])
    picked = jnp.take(shard_piece, jnp.clip(token_list, 0, shard_piece.shape[0] - 1), axis=0)
    looked = jnp.where(inside[:, None], picked.astype(jnp.float32), 0.0)
    embed_rows = lax.all_gather(looked.astype(jnp.bfloat16), "mp", axis=1, tiled=True).astype(
        jnp.float32
    )
    lengths_row = seq_lengths[tower_idx, data_idx]
    segment, positions = plain_layout(lengths_row, tok_count, slot_count)
    stream_two, kept_vals = layer_forward(embed_rows, segment, positions, weights, norm_params)
    member = (segment[None, :] == jnp.arange(slot_count, dtype=jnp.int32)[:, None]).astype(
        jnp.float32
    )
    counts = jnp.maximum(lengths_row, 1).astype(jnp.float32)
    own_embeds, pool_back = jax.vjp(lambda stream: pool_rows(stream, member, counts), stream_two)
    all_embeds = lax.all_gather(
        own_embeds.astype(jnp.bfloat16), ("tower", "dp"), axis=0, tiled=True
    )
    query_total = n_data * slot_count
    rows_per = slot_count // 2
    first_row = (tower_idx * n_data + data_idx) * rows_per
    query_rows = lax.dynamic_slice_in_dim(all_embeds, first_row, rows_per, 0)
    documents = all_embeds[query_total:]
    cosines = jnp.einsum("qd,kd->qk", query_rows, documents, preferred_element_type=jnp.float32)
    logit_factor = jnp.exp(jnp.minimum(logit_scale[0], cap_value))
    doc_ok = seq_lengths[1].reshape(-1) > 0
    query_ok_all = seq_lengths[0].reshape(-1) > 0
    query_count = jnp.sum(query_ok_all.astype(jnp.float32))
    query_ok = lax.dynamic_slice_in_dim(query_ok_all, first_row, rows_per, 0)
    logits = jnp.where(doc_ok[None, :], logit_factor * cosines, neg_large)
    row_peak = jnp.max(logits, 1, keepdims=True)
    log_total = row_peak + jnp.log(jnp.sum(jnp.exp(logits - row_peak), 1, keepdims=True))
    soft_rows = jnp.exp(logits - log_total)
    targets = lax.dynamic_slice_in_dim(positives.reshape(-1), first_row, rows_per, 0)
    target_mask = jnp.arange(query_total, dtype=jnp.int32)[None, :] == targets[:, None]
    picked = jnp.sum(jnp.where(target_mask, logits, 0.0), 1)
    loss_part = jnp.sum(jnp.where(query_ok, log_total[:, 0] - picked, 0.0))
    grad_logits = (
        jnp.where(query_ok[:, None], soft_rows - target_mask.astype(jnp.float32), 0.0) / query_count
    )
    scale_part = (
        jnp.sum(grad_logits * cosines)
        * logit_factor
        * (logit_scale[0] < cap_value).astype(jnp.float32)
    )
    grad_cos = (logit_factor * grad_logits).astype(jnp.bfloat16)
    grad_queries = jnp.einsum("qk,kd->qd", grad_cos, documents, preferred_element_type=jnp.float32)
    grad_documents = jnp.einsum(
        "qk,qd->kd", grad_cos, query_rows, preferred_element_type=jnp.float32
    )
    grad_term = jnp.concatenate(
        [jnp.zeros((query_total, model_width), jnp.float32), grad_documents], 0
    )
    grad_term = lax.dynamic_update_slice_in_dim(grad_term, grad_queries, first_row, 0)
    own_grad = lax.psum_scatter(grad_term, ("tower", "dp"), scatter_dimension=0, tiled=True)
    grad_two = pool_back(own_grad)[0]
    grad_embed, layer_grads, norm_grads = layer_backward(
        grad_two, kept_vals, weights, norm_params, segment, positions
    )
    embed_low = grad_embed.astype(jnp.bfloat16)
    column_part = lax.dynamic_slice_in_dim(embed_low, model_idx * local_width, local_width, 1)
    row_start = data_idx * row_count
    all_ids = lax.all_gather(token_list, ("tower", "dp"), axis=0, tiled=True)
    piece_ids = all_ids - row_start
    inside = (piece_ids >= 0) & (piece_ids < row_count)
    slot_ids = jnp.where(inside, piece_ids, row_count)
    embed_grad = jax.ops.segment_sum(
        lax.all_gather(column_part, ("tower", "dp"), axis=0, tiled=True).astype(jnp.float32),
        slot_ids,
        num_segments=row_count + 1,
    )[:row_count]
    shard_grads = (
        lax.psum_scatter(layer_grads[0], ("tower", "dp"), scatter_dimension=0, tiled=True),
        lax.psum_scatter(layer_grads[1], ("tower", "dp"), scatter_dimension=0, tiled=True),
        lax.psum_scatter(layer_grads[2], ("tower", "dp"), scatter_dimension=0, tiled=True),
        lax.psum_scatter(layer_grads[3], ("tower", "dp"), scatter_dimension=0, tiled=True),
    )
    norm_grad, loss_sum, scale_grad = lax.psum((norm_grads, loss_part, scale_part), ("tower", "dp"))
    local_sq = sum((jnp.sum(gradient * gradient) for gradient in shard_grads)) + 0.5 * jnp.sum(
        embed_grad * embed_grad
    )
    total_sq = (
        lax.psum(local_sq, ("tower", "dp", "mp"))
        + jnp.sum(norm_grad * norm_grad)
        + scale_grad * scale_grad
    )
    grad_norm = jnp.sqrt(total_sq)
    factor = jnp.minimum(1.0, clip_max / (grad_norm + 1e-06))
    step_num = float(STEP)
    embed_new = plain_adamw(embedding, embed_grad, embed_m, embed_v, factor, step_num, learn_rate)
    qkv_new = plain_adamw(attn_in, shard_grads[0], attn_in_m, attn_in_v, factor, step_num, learn_rate)
    out_new = plain_adamw(attn_out, shard_grads[1], attn_out_m, attn_out_v, factor, step_num, out_rate)
    ffn_new = plain_adamw(ffn_in, shard_grads[2], ffn_in_m, ffn_in_v, factor, step_num, learn_rate)
    down_new = plain_adamw(ffn_out, shard_grads[3], ffn_out_m, ffn_out_v, factor, step_num, learn_rate)
    norms_new = plain_adamw(norm_params, norm_grad, norm_m, norm_v, factor, step_num, norm_rate)
    scale_new = plain_adamw(
        logit_scale, scale_grad.reshape(1), scale_m, scale_v, factor, step_num, learn_rate
    )
    return (
        embed_new[0],
        embed_new[1],
        embed_new[2],
        qkv_new[0],
        qkv_new[1],
        qkv_new[2],
        out_new[0],
        out_new[1],
        out_new[2],
        ffn_new[0],
        ffn_new[1],
        ffn_new[2],
        down_new[0],
        down_new[1],
        down_new[2],
        norms_new[0],
        norms_new[1],
        norms_new[2],
        scale_new[0],
        scale_new[1],
        scale_new[2],
        loss_sum.reshape(1),
        query_count.reshape(1),
        grad_norm.reshape(1),
    )


def lean_step(args, pos, heard):
    (
        token_ids, seq_lengths, positives, embedding, attn_in, attn_out, ffn_in, ffn_out,
        norm_params, logit_scale, embed_m, embed_v, attn_in_m, attn_in_v, attn_out_m, attn_out_v,
        ffn_in_m, ffn_in_v, ffn_out_m, ffn_out_v, norm_m, norm_v, scale_m, scale_v,
    ) = args
    tower_idx = lax.axis_index("tower")
    data_idx = lax.axis_index("dp")
    model_idx = lax.axis_index("mp")
    slot_count = seq_lengths.shape[2]
    tok = token_ids.shape[1]
    half = tok // 2
    row_count = embedding.shape[0]
    feats = attn_out.shape[1]
    ff = ffn_out.shape[1]
    part_ff = ff // 2

    kinds = ("plain", "late", "late", "late", "late")
    gather_pieces = [(0, "plain", 0, 3 * feats, 0)]
    quarter = ff // 4
    for turn, which in enumerate((2, 3, 4)):
        for c in range(4):
            kind = ("late", "early", "cross")[(4 * turn + c) % 3]
            gather_pieces.append((which, kind, c * quarter, quarter, 4 * turn + c))
    gather_pieces.append((1, "early", 0, feats, 6))
    places = (jnp.arange(tok, dtype=jnp.int32) + model_idx * half) % tok
    pos_rel = jnp.where(model_idx == 0, pos, jnp.concatenate([pos[half:], pos[:half]]))
    lengths_row = seq_lengths[tower_idx, data_idx]
    segment, positions = layout(lengths_row, places, slot_count)
    cosine, sine = rotary_tables(positions)
    seg_row, seg_col = segment[None, :], segment[:, None]
    named = heard[:, :, 0, : heard_room(tok, heard.shape[1])].reshape(2, 1, -1)
    kept, weights = forward_pass(
        embedding, heard, pos_rel[:, None], norm_params, cosine, sine, seg_row, seg_col,
        (attn_in, attn_out, ffn_in, ffn_out), kinds, gather_pieces,
    )
    emb, stream_zero, input_zero, query, key, value, lse = kept[:7]
    att = kept[7:9]
    w_qkv, w_out, w_gate, w_up, w_down = weights

    sum_one = stream_zero + tdot(att[0], w_out[0]) + tdot(att[1], w_out[1])
    hat_one, scale_one = norm_parts(sum_one)
    stream_one = hat_one * norm_params[2] + norm_params[3]
    input_one = stream_one.astype(bf16)
    gates = [mdot(input_one, w_gate[j]) for j in range(2)]
    ups = [mdot(input_one, w_up[j]) for j in range(2)]
    hidden = [glu(gates[j], ups[j]).astype(bf16) for j in range(2)]
    sum_two = stream_one + tdot(hidden[0], w_down[0]) + tdot(hidden[1], w_down[1])
    hat_two, scale_two = norm_parts(sum_two)
    stream_two = hat_two * norm_params[4] + norm_params[5]

    member = (segment[None, :half] == jnp.arange(slot_count, dtype=jnp.int32)[:, None]).astype(f32)
    counts = jnp.maximum(lengths_row, 1).astype(f32)[:, None]
    part = jnp.dot(member, stream_two, precision=highest)
    doc_ok = (seq_lengths[1].reshape(1, -1) > 0).astype(f32)
    query_ok = (seq_lengths[0].reshape(-1, 1) > 0).astype(f32)
    grad_pool, stats = loss_step(
        part, counts, doc_ok, query_ok, positives.reshape(-1, 1), logit_scale.reshape(1, 1)
    )
    loss_sum, query_count, scale_grad = stats[0, 0], stats[1, 0], stats[2, 0]

    def weight_grad(left, right):
        return jnp.einsum("td,tf->df", left, right, preferred_element_type=f32).astype(bf16)

    pieces = [(0, ("early", "late")[c % 2], c * quarter, quarter, c) for c in range(4)]
    out = hidden_back(
        grad_pool, seg_col, sum_two, norm_params, input_one, sum_one, att, hidden, w_gate, w_up, w_down, pieces, 2,
    )
    grad_sum_one, attn_low, norms = out[:3]
    grad_out, later, r_down, squares = out[3:5], out[5:9], out[9], out[10]
    pieces = [
        (c // 4, ("early", "late", "cross")[c % 3], (c % 4) * quarter, quarter, c)
        for c in range(8)
    ] + [(2, "early", 0, feats, 3)]
    late_pieces = [(c, "plain", 0, feats, 0) for c in range(3)]
    embed_grad, norm_sum, r_ffn, r_out, r_qkv, total = backward_pass(
        attn_low, w_out, query, key, value, lse, cosine, sine, seg_row, seg_col, grad_sum_one,
        emb, norm_params, w_qkv, norms, squares, input_zero, pos_rel[None, :], named,
        later, grad_out, row_count, pieces, late_pieces,
    )
    norm_grad = norm_sum[:6]
    total_sq = total[0, 0] + scale_grad * scale_grad
    grad_norm = jnp.sqrt(total_sq)
    factor = jnp.minimum(1.0, clip_max / (grad_norm + 1e-06))
    step_num = float(STEP)
    embed_new = adamw(embedding, embed_grad, embed_m, embed_v, factor, step_num, learn_rate)
    qkv_new = adamw(attn_in, r_qkv, attn_in_m, attn_in_v, factor, step_num, learn_rate)
    out_new = adamw(attn_out, r_out, attn_out_m, attn_out_v, factor, step_num, out_rate)
    ffn_new = adamw(ffn_in, r_ffn, ffn_in_m, ffn_in_v, factor, step_num, learn_rate)
    down_new = adamw(ffn_out, r_down, ffn_out_m, ffn_out_v, factor, step_num, learn_rate)
    norms_new = adamw(norm_params, norm_grad, norm_m, norm_v, factor, step_num, norm_rate)
    scale_new = adamw(
        logit_scale, scale_grad.reshape(1), scale_m, scale_v, factor, step_num, learn_rate
    )
    return (
        *embed_new, *qkv_new, *out_new, *ffn_new, *down_new, *norms_new, *scale_new,
        loss_sum.reshape(1), query_count.reshape(1), grad_norm.reshape(1),
    )


def local(*args):
    token_ids, embedding = args[0], args[3]
    n_dp = lax.axis_size("dp")
    room = heard_room(token_ids.shape[1], n_dp)
    pos, lists = name_rows(
        token_ids[0], lax.axis_index("dp"), n_dp, embedding.shape[0], room
    )
    heard, flag = exchange_lists(lists)
    return lax.cond(
        flag[1, 0] > 0,
        lambda values: plain_step(*values),
        lambda values: lean_step(values, pos, heard),
        args,
    )


def solution(mesh):
    table, rows3, rows2 = P("dp", "mp"), P(("tower", "dp"), None, "mp"), P(("tower", "dp"), "mp")
    weights = (table, rows3, rows2, rows3, rows2)
    moments = tuple(spec for spec in weights for _ in range(2))
    return jax.shard_map(
        local,
        mesh=mesh,
        in_specs=(P("tower", "dp"), P(), P()) + weights + (P(), P()) + moments + (P(),) * 4,
        out_specs=tuple(spec for spec in weights for _ in range(3)) + (P(),) * 9,
        check_vma=False,
    )
```
